32 devices in a mesh: dp: 8 (over y, x, core), hist: 4 (over z).
Axes of the slice: x: 2, y: 2, z: 4, core: 2. Of those that a mesh axis runs over, the one named last changes fastest.
Arguments:
- history: bfloat16 [16, 24, 256, 2048], P('hist', 'dp'), may hold values from -6 to 6
- history_layer_index: int32 [16], replicated, may hold values from 0 to 15, each once
- lengths: int32 [24], P('dp'), may hold values from 32 to 256, as said below
- norm_gains: bfloat16 [5, 2048], P(None, 'dp'), may hold values from 0.099609375 to 1.8984375
- mix_in: bfloat16 [2048, 64], P('dp'), may hold values from -0.125 to 0.125
- mix_out: bfloat16 [64, 64], P('dp'), may hold values from -0.25 to 0.25
- w_attn: bfloat16 [3, 2048, 2048], P(None, 'dp'), may hold values from -0.125 to 0.125
- w_out: bfloat16 [2048, 2048], P('dp'), may hold values from -1 to 1
- w_up: bfloat16 [2048, 8192], P('dp'), may hold values from -0.125 to 0.125
- w_down: bfloat16 [8192, 2048], P('dp'), may hold values from -0.0625 to 0.0625
- cotangent: bfloat16 [24, 256, 2048], P('dp', 'hist'), may hold values from -6 to 6
Outputs:
- block_out: bfloat16 [24, 256, 2048], P('dp', 'hist')
- history_grad: bfloat16 [16, 24, 256, 2048], P('hist', 'dp')
- norm_gains_grad: float32 [5, 2048], P(None, 'dp')
- mix_in_grad: float32 [2048, 64], P('dp')
- mix_out_grad: float32 [64, 64], P('dp')
- w_attn_grad: float32 [3, 2048, 2048], P(None, 'dp')
- w_out_grad: float32 [2048, 2048], P('dp')
- w_up_grad: float32 [2048, 8192], P('dp')
- w_down_grad: float32 [8192, 2048], P('dp')
The draws below stay inside these ranges and needn't reach their ends.
Inputs may be any that keep to these rules, and one draw needn't show every extreme that they name: Slot s holds the output of layer history_layer_index[s]; each layer once. `lengths`: positions at or past a sequence's length are padding; some sequence has the full 256 tokens and some has 32.
All inputs are finite; a program needn't handle non-finite values.
Results may differ from the reference program's by a relative error of at most 0.018.
Values may be sent and summed in bfloat16 or wider, within the bound.
A program may use at most 704 MiB of HBM per device.

```python
import math
import jax
import jax.numpy as jnp
from jax import lax

MODEL_WIDTH = 2048
HEADS = 16
HEAD_DIM = 128
FF = 8192
HISTORY_SLOTS = 16
STREAM_COUNT = 4
PADDED_LENGTH = 256
MIXH = 64
SEQUENCE_COUNT = 24


def draw_lengths(key, part):
    key = jax.random.fold_in(key, 11)
    key_values, key_longest, key_short = jax.random.split(key, 3)
    shortest = max(PADDED_LENGTH // 8, 1)
    values = jax.random.randint(key_values, (SEQUENCE_COUNT,), shortest, PADDED_LENGTH + 1)
    longest_at = jax.random.randint(key_longest, (), 0, SEQUENCE_COUNT)
    shortest_at = (longest_at + 1 + jax.random.randint(key_short, (), 0, SEQUENCE_COUNT - 1)) % SEQUENCE_COUNT
    values = values.at[longest_at].set(PADDED_LENGTH)
    values = values.at[shortest_at].set(shortest)
    return values.astype(jnp.int32)


def level_of(key, extent, shards, low, largest):
    def one(dim, blocks):
        heights = jax.random.uniform(jax.random.fold_in(jax.random.fold_in(key, 6), dim), (blocks,), jnp.float32, low / len(shards), largest / len(shards))
        return jnp.repeat(jnp.exp(heights), extent[dim] // blocks).reshape((-1,) + (1,) * (len(extent) - dim - 1))

    gain = one(*shards[0])
    for cut in shards[1:]:
        gain = gain * one(*cut)
    return gain


def bell_draw(stream_key, dims, deviation, limit, shards=(), held_as=jnp.bfloat16):
    level = level_of(stream_key, dims, shards, -0.22, 0.18) if shards else 1.0
    values = jax.random.normal(stream_key, dims, jnp.float32) * deviation * level
    return jnp.minimum(jnp.maximum(values, -limit), limit).astype(held_as)


def setup_inputs(seed: int = 0) -> dict:
    splits = jax.random.split(jax.random.key(seed), 12)
    return {
        "history": bell_draw(splits[0], (HISTORY_SLOTS, SEQUENCE_COUNT, PADDED_LENGTH, MODEL_WIDTH), 1.0, 6.0, ((0, 4), (1, 8))),
        "history_layer_index": jax.random.permutation(splits[1], HISTORY_SLOTS).astype(jnp.int32),
        "lengths": draw_lengths(jax.random.fold_in(splits[11], 71), 0),
        "norm_gains": jnp.clip(1.0 + 0.18 * jax.random.normal(splits[3], (5, MODEL_WIDTH), jnp.float32), 0.099609375, 1.8984375).astype(jnp.bfloat16),
        "mix_in": bell_draw(splits[4], (MODEL_WIDTH, MIXH), MODEL_WIDTH ** -0.5, 0.125, ((0, 8),)),
        "mix_out": bell_draw(splits[5], (MIXH, MIXH), (MIXH * 8) ** -0.5, 0.25, ((0, 8),)),
        "w_attn": bell_draw(splits[6], (3, MODEL_WIDTH, MODEL_WIDTH), MODEL_WIDTH ** -0.5, 0.125, ((1, 8),)),
        "w_out": bell_draw(splits[7], (MODEL_WIDTH, MODEL_WIDTH), (max(MODEL_WIDTH // 64, 1)) ** -0.5, 1.0, ((0, 8),)),
        "w_up": bell_draw(splits[8], (MODEL_WIDTH, FF), MODEL_WIDTH ** -0.5, 0.125, ((0, 8),)),
        "w_down": bell_draw(splits[9], (FF, MODEL_WIDTH), FF ** -0.5, 0.0625, ((0, 8),)),
        "cotangent": bell_draw(splits[10], (SEQUENCE_COUNT, PADDED_LENGTH, MODEL_WIDTH), 1.0, 6.0, ((0, 8), (1, 4))),
    }


@jax.custom_vjp
def low(v):
    return lax.optimization_barrier(v.astype(jnp.bfloat16)).astype(jnp.float32)

@jax.custom_vjp
def low_back(v):
    return v

def low_keep(v):
    return (low(v), None)

def low_pass(kept, grad):
    return (grad,)

def back_keep(v):
    return (v, None)

def back_low(kept, grad):
    return (low(grad),)
low.defvjp(low_keep, low_pass)
low_back.defvjp(back_keep, back_low)
epsilon = 1e-06
masked_out = -1e+30

def weighted_product(left_side, right_side):
    return jnp.dot(left_side, right_side, precision=lax.Precision.HIGHEST, preferred_element_type=jnp.float32)

def rms_scale(values, gain_row):
    return values * lax.rsqrt(lax.optimization_barrier(jnp.mean(values * values, axis=-1, keepdims=True)) + epsilon) * gain_row

def rotate(values, positions):
    half_dim = values.shape[-1] // 2
    frequency = jnp.exp(jnp.arange(half_dim, dtype=jnp.float32) * (-2.0 * math.log(10000.0) / values.shape[-1]))
    angles = positions.astype(jnp.float32)[:, None] * frequency[None, :]
    cosine = jnp.cos(angles)[:, None, :]
    sine_part = jnp.sin(angles)[:, None, :]
    lower_half = values[..., :half_dim]
    upper_half = values[..., half_dim:]
    return jnp.concatenate([lower_half * cosine - upper_half * sine_part, upper_half * cosine + lower_half * sine_part], axis=-1)

def sequence_forward(earlier_block_results, length, layer_lookup, newest_output, gains_wide, mix_in_wide, mixer_output_wide, attn_wide, out_wide, up_wide, down_wide):
    sequence_length = earlier_block_results.shape[1]
    latest_rows = lax.dynamic_index_in_dim(earlier_block_results, newest_output, 0, keepdims=False)
    mix_norm = low(rms_scale(latest_rows, gains_wide[0]))
    mixer_preactivation = weighted_product(mix_norm, mix_in_wide)
    dynamic_weights = weighted_product(jax.nn.gelu(mixer_preactivation, approximate=False), mixer_output_wide).reshape(sequence_length, STREAM_COUNT, HISTORY_SLOTS)
    depth_combination_factors = jnp.einsum('nza,ra->nzr', dynamic_weights, layer_lookup, precision=lax.Precision.HIGHEST)
    blended_residual_inputs = jnp.einsum('tjr,rti->jti', depth_combination_factors, earlier_block_results, precision=lax.Precision.HIGHEST)
    normed = [low(rms_scale(blended_residual_inputs[stream_idx], gains_wide[stream_idx + 1])) for stream_idx in range(STREAM_COUNT)]
    positions = jnp.arange(sequence_length, dtype=jnp.int32)
    head_shape = (sequence_length, HEADS, HEAD_DIM)
    attention_asker_vectors = low(rotate(low_back(weighted_product(normed[0], attn_wide[0])).reshape(head_shape), positions))
    keys_rot = low(rotate(low_back(weighted_product(normed[1], attn_wide[1])).reshape(head_shape), positions))
    values_low = low(low_back(weighted_product(normed[2], attn_wide[2]))).reshape(head_shape)
    scores = jnp.einsum('qhd,khd->hqk', attention_asker_vectors, keys_rot, precision=lax.Precision.HIGHEST) * (1.0 / math.sqrt(HEAD_DIM))
    allowed = (positions[None, :] <= positions[:, None]) & (positions[None, :] < length)
    scores = jnp.where(allowed[None], scores, masked_out)
    soft_weights = jax.nn.softmax(scores, axis=-1)
    attended = jnp.einsum('hqk,khd->qhd', soft_weights, values_low, precision=lax.Precision.HIGHEST).reshape(sequence_length, MODEL_WIDTH)
    attended = low(low_back(attended))
    up_pre = low_back(weighted_product(normed[3], up_wide))
    hidden = low(jax.nn.gelu(up_pre, approximate=False))
    branch = low_back(weighted_product(attended, out_wide) + weighted_product(hidden, down_wide))
    valid_rows = (positions < length).astype(jnp.float32)[:, None]
    return (blended_residual_inputs[3] + branch) * valid_rows

def reference(history, history_layer_index, lengths, norm_gains, mix_in, mix_out, w_attn, w_out, w_up, w_down, cotangent):
    layer_lookup = (history_layer_index[:, None] == jnp.arange(HISTORY_SLOTS, dtype=jnp.int32)[None, :]).astype(jnp.float32)
    newest_output = jnp.sum(jnp.arange(HISTORY_SLOTS, dtype=jnp.int32) * (history_layer_index == HISTORY_SLOTS - 1).astype(jnp.int32))
    weights = tuple((weight.astype(jnp.float32) for weight in (norm_gains, mix_in, mix_out, w_attn, w_out, w_up, w_down)))

    def step_one(carried, seq_idx):
        grad_sums, history_grad, block_out = carried
        earlier_block_results = lax.dynamic_index_in_dim(history, seq_idx, 1, keepdims=False).astype(jnp.float32)
        cot_rows = lax.dynamic_index_in_dim(cotangent, seq_idx, 0, keepdims=False).astype(jnp.float32)
        length = lax.dynamic_index_in_dim(lengths, seq_idx, 0, keepdims=False)

        def forward(slot_part, gains_wide, mix_in_wide, mixer_output_wide, attn_wide, out_wide, up_wide, down_wide):
            return sequence_forward(slot_part, length, layer_lookup, newest_output, gains_wide, mix_in_wide, mixer_output_wide, attn_wide, out_wide, up_wide, down_wide)
        result, pullback = jax.vjp(forward, earlier_block_results, weights[0], weights[1], weights[2], weights[3], weights[4], weights[5], weights[6])
        pieces = pullback(cot_rows)
        history_grad = lax.dynamic_update_index_in_dim(history_grad, pieces[0].astype(jnp.bfloat16), seq_idx, 1)
        block_out = lax.dynamic_update_index_in_dim(block_out, result.astype(jnp.bfloat16), seq_idx, 0)
        grad_sums = tuple((total_sum + piece_grad for total_sum, piece_grad in zip(grad_sums, pieces[1:])))
        return ((grad_sums, history_grad, block_out), None)
    initial = (tuple((jnp.zeros(weight.shape, jnp.float32) for weight in weights)), jnp.zeros(history.shape, jnp.bfloat16), jnp.zeros(cotangent.shape, jnp.bfloat16))
    finished, unused = lax.scan(step_one, initial, jnp.arange(SEQUENCE_COUNT, dtype=jnp.int32))
    grad_sums, history_grad, block_out = finished
    return (block_out, history_grad, grad_sums[0], grad_sums[1], grad_sums[2], grad_sums[3], grad_sums[4], grad_sums[5], grad_sums[6])
```

```python
import functools
import math

import jax
import jax.numpy as jnp
from jax import lax
from jax.experimental import pallas as pl
from jax.experimental.pallas import tpu as pltpu
from jax.sharding import PartitionSpec as P

MODEL_WIDTH = 2048
HEADS = 16
HEAD_DIM = 128
FF = 8192
STREAM_COUNT = 4


epsilon = 1e-06
masked_out = -1e30
highest = lax.Precision.HIGHEST
contract_rows = (((0,), (0,)), ((), ()))
contract_cols = (((1,), (1,)), ((), ()))


def broadcast(value, axis, source):
    kept = jnp.where(lax.axis_index(axis) == source, value, 0).astype(value.dtype)
    return lax.psum(kept, axis)


def matmul(left_side, right_side):
    return jnp.dot(left_side, right_side, preferred_element_type=jnp.float32)


def precise(left_side, right_side):
    return jnp.dot(left_side, right_side, precision=highest, preferred_element_type=jnp.float32)


def gelu_slope(values):
    return 0.5 * (1.0 + lax.erf(values * (1.0 / math.sqrt(2.0)))) + values * jnp.exp(
        -0.5 * values * values
    ) * (1.0 / math.sqrt(2.0 * math.pi))


def rms_scale(values, gain_row):
    inverse = lax.rsqrt(jnp.mean(values * values, axis=-1, keepdims=True) + epsilon)
    return (values * inverse * gain_row, inverse)


def rms_back(values, inverse, gain_row, grad_in):
    scaled = grad_in * gain_row
    gain_grad = jnp.sum(grad_in * values * inverse, axis=0)
    inner_mean = jnp.mean(scaled * values, axis=-1, keepdims=True)
    return (inverse * scaled - values * (inverse * inverse * inverse) * inner_mean, gain_grad)


def rotate(values, positions, turn_sign):
    half_dim = values.shape[-1] // 2
    frequency = jnp.exp(
        jnp.arange(half_dim, dtype=jnp.float32) * (-2.0 * math.log(10000.0) / values.shape[-1])
    )
    angles = positions.astype(jnp.float32)[:, None] * frequency[None, :]
    cosine = jnp.cos(angles)[:, None, :]
    sine_part = jnp.sin(angles)[:, None, :] * turn_sign
    lower_half = values[..., :half_dim]
    upper_half = values[..., half_dim:]
    return jnp.concatenate(
        [
            lower_half * cosine - upper_half * sine_part,
            upper_half * cosine + lower_half * sine_part,
        ],
        axis=-1,
    )


def first_rows(weights, lefts):

    def add_piece(totals, pieces, start_at):
        return tuple(
            (matmul(left_side, piece_rows) for left_side, piece_rows in zip(lefts, pieces))
        )

    initial = tuple(
        (jnp.zeros((lefts[0].shape[0], weight.shape[1]), jnp.float32) for weight in weights)
    )
    return add_piece(
        initial,
        (
            lax.all_gather(weights[0], "dp", axis=0, tiled=True),
            lax.all_gather(weights[1], "dp", axis=0, tiled=True),
            lax.all_gather(weights[2], "dp", axis=0, tiled=True),
            lax.all_gather(weights[3], "dp", axis=0, tiled=True),
        ),
        jnp.int32(0),
    )


def second_rows(w_out, down_folded, attended_low, hidden, ratio):

    def add_piece(total_sum, pieces, start_at):
        count = pieces[0].shape[0]
        down_rows = pieces[1].reshape(count * ratio, pieces[1].shape[1] // ratio)
        return matmul(attended_low, pieces[0]) + matmul(hidden, down_rows)

    initial = jnp.zeros((attended_low.shape[0], w_out.shape[1]), jnp.float32)
    return add_piece(
        initial,
        (
            lax.all_gather(w_out, "dp", axis=0, tiled=True),
            lax.all_gather(down_folded, "dp", axis=0, tiled=True),
        ),
        jnp.int32(0),
    )


def back_first(w_out, down_folded, grad_low, ratio):

    def add_piece(totals, pieces, start_at):
        count = pieces[0].shape[0]
        out_part = lax.dot_general(
            grad_low, pieces[0], contract_cols, preferred_element_type=jnp.float32
        )
        down_rows = pieces[1].reshape(count * ratio, pieces[1].shape[1] // ratio)
        down_part = lax.dot_general(
            grad_low, down_rows, contract_cols, preferred_element_type=jnp.float32
        )
        return (out_part, down_part)

    features = w_out.shape[1]
    initial = (
        jnp.zeros((grad_low.shape[0], features), jnp.float32),
        jnp.zeros((grad_low.shape[0], features * ratio), jnp.float32),
    )
    return add_piece(
        initial,
        (
            lax.all_gather(w_out, "dp", axis=0, tiled=True),
            lax.all_gather(down_folded, "dp", axis=0, tiled=True),
        ),
        jnp.int32(0),
    )


def back_second(weights, rights):

    def add_piece(totals, pieces, start_at):
        return tuple(
            (
                lax.dot_general(
                    right_side, piece_rows, contract_cols, preferred_element_type=jnp.float32
                )
                for right_side, piece_rows in zip(rights, pieces)
            )
        )

    features = weights[1].shape[1]
    initial = tuple((jnp.zeros((rights[0].shape[0], features), jnp.float32) for weight in weights))
    return add_piece(
        initial,
        (
            lax.all_gather(weights[0], "dp", axis=0, tiled=True),
            lax.all_gather(weights[1], "dp", axis=0, tiled=True),
            lax.all_gather(weights[2], "dp", axis=0, tiled=True),
            lax.all_gather(weights[3], "dp", axis=0, tiled=True),
        ),
        jnp.int32(0),
    )


def mix_forward(values_low, gain_row, mix_in_all, mixer_output_wide):
    values = values_low.astype(jnp.float32)
    scaled, inverse = rms_scale(values, gain_row)
    normed_mix = scaled.astype(jnp.bfloat16)
    mixer_preactivation = matmul(normed_mix, mix_in_all)
    mix_act = jax.nn.gelu(mixer_preactivation, approximate=False)
    return (
        precise(mix_act, mixer_output_wide),
        (values, inverse, normed_mix, mixer_preactivation, mix_act),
    )


def mix_backward(kept_mix, act_grad, gain_row, mix_in_all):
    values, inverse, normed_mix, mixer_preactivation, mix_act = kept_mix
    pre_grad = act_grad * gelu_slope(mixer_preactivation)
    in_grad = precise(normed_mix.astype(jnp.float32).T, pre_grad)
    normed_grad = precise(pre_grad, mix_in_all.astype(jnp.float32).T)
    latest_grad, gain_grad = rms_back(values, inverse, gain_row, normed_grad)
    return (latest_grad, gain_grad, in_grad)


def shards(
    history,
    history_layer_index,
    lengths,
    norm_gains,
    mix_in,
    mix_out,
    w_attn,
    w_out,
    w_up,
    w_down,
    cotangent,
):
    local_slots, micro_count, sequence_length, features = history.shape
    hist_count = lax.axis_size("hist")
    dp_count = lax.axis_size("dp")
    hist_place = lax.axis_index("hist")
    slot_count = local_slots * hist_count
    ratio = FF // MODEL_WIDTH
    gains_all, mix_in_all, mix_out_all = (
        lax.all_gather(norm_gains, "dp", axis=1, tiled=True),
        lax.all_gather(mix_in, "dp", axis=0, tiled=True),
        lax.all_gather(mix_out, "dp", axis=0, tiled=True),
    )
    gains_all = gains_all.astype(jnp.float32)
    mixer_output_wide = mix_out_all.astype(jnp.float32)
    mix_width = mixer_output_wide.shape[0]
    layer_lookup = (
        history_layer_index[:, None] == jnp.arange(slot_count, dtype=jnp.int32)[None, :]
    ).astype(jnp.float32)
    newest_output = jnp.sum(
        jnp.arange(slot_count, dtype=jnp.int32)
        * (history_layer_index == slot_count - 1).astype(jnp.int32)
    )
    down_folded = w_down.reshape(w_down.shape[0] // ratio, ratio * w_down.shape[1])
    quarter = cotangent.shape[1]
    own_rows = micro_count * quarter
    positions = hist_place * quarter + jnp.arange(quarter, dtype=jnp.int32)
    valid_rows = (positions[None, :] < lengths[:, None]).astype(jnp.float32).reshape(own_rows, 1)
    root = newest_output // local_slots
    latest_local = lax.dynamic_index_in_dim(history, newest_output % local_slots, 0, keepdims=False)
    latest_rows = broadcast(latest_local, "hist", root)
    dynamic_weights, kept_mix = mix_forward(
        latest_rows.reshape(micro_count * sequence_length, features),
        gains_all[0],
        mix_in_all,
        mixer_output_wide,
    )
    dynamic_weights = dynamic_weights.reshape(
        micro_count, sequence_length, STREAM_COUNT, slot_count
    )
    own_table = lax.dynamic_slice_in_dim(layer_lookup, hist_place * local_slots, local_slots, 0)
    depth_combination_factors = jnp.einsum(
        "mtcj,sj->scmt", dynamic_weights, own_table, precision=highest
    )
    partial_sums = jnp.zeros((STREAM_COUNT, micro_count, sequence_length, features), jnp.float32)
    for depth_position_number in range(local_slots):
        partial_sums = (
            partial_sums
            + depth_combination_factors[depth_position_number][..., None]
            * history[depth_position_number].astype(jnp.float32)[None]
        )
    blended_residual_inputs = lax.psum_scatter(
        partial_sums, "hist", scatter_dimension=2, tiled=True
    )
    stream_rows = blended_residual_inputs.reshape(STREAM_COUNT, own_rows, features)
    normed = []
    inverses = []
    for stream_idx in range(STREAM_COUNT):
        scaled, inverse = rms_scale(stream_rows[stream_idx], gains_all[stream_idx + 1])
        normed.append(scaled.astype(jnp.bfloat16))
        inverses.append(inverse)
    head_shape = (micro_count, quarter, HEADS, HEAD_DIM)
    query_pre, key_pre, value_pre, up_pre = first_rows(
        (w_attn[0], w_attn[1], w_attn[2], w_up), (normed[0], normed[1], normed[2], normed[3])
    )
    attention_asker_vectors = rotate(query_pre.reshape(head_shape), positions, 1.0).astype(
        jnp.bfloat16
    )
    keys_rot = rotate(key_pre.reshape(head_shape), positions, 1.0).astype(jnp.bfloat16)
    values_low = value_pre.astype(jnp.bfloat16)
    keys_all, values_all = (
        lax.all_gather(
            keys_rot.reshape(micro_count, quarter, features), "hist", axis=1, tiled=True
        ),
        lax.all_gather(
            values_low.reshape(micro_count, quarter, features), "hist", axis=1, tiled=True
        ),
    )
    key_heads = keys_all.reshape(micro_count, sequence_length, HEADS, HEAD_DIM)
    value_wide = values_all.reshape(micro_count, sequence_length, HEADS, HEAD_DIM).astype(
        jnp.float32
    )
    score_scale = 1.0 / math.sqrt(HEAD_DIM)
    scores = (
        jnp.einsum(
            "mqhd,mkhd->mhqk",
            attention_asker_vectors,
            key_heads,
            preferred_element_type=jnp.float32,
        )
        * score_scale
    )
    key_positions = jnp.arange(sequence_length, dtype=jnp.int32)
    allowed = (key_positions[None, None, :] <= positions[None, :, None]) & (
        key_positions[None, None, :] < lengths[:, None, None]
    )
    scores = jnp.where(allowed[:, None], scores, masked_out)
    row_top = jnp.max(scores, axis=-1, keepdims=True)
    raised = jnp.exp(scores - row_top)
    soft_weights = raised / jnp.sum(raised, axis=-1, keepdims=True)
    attended = jnp.einsum("mhqk,mkhd->mqhd", soft_weights, value_wide, precision=highest)
    attended_low = attended.reshape(own_rows, features).astype(jnp.bfloat16)
    hidden = jax.nn.gelu(up_pre, approximate=False).astype(jnp.bfloat16)
    branch = second_rows(w_out, down_folded, attended_low, hidden, ratio)
    block_out = (
        ((stream_rows[3] + branch) * valid_rows)
        .astype(jnp.bfloat16)
        .reshape(micro_count, quarter, features)
    )
    grad_rows = cotangent.reshape(own_rows, features).astype(jnp.float32) * valid_rows
    grad_low = grad_rows.astype(jnp.bfloat16)
    attended_back, hidden_grad = back_first(w_out, down_folded, grad_low, ratio)
    up_grad = (hidden_grad * gelu_slope(up_pre)).astype(jnp.bfloat16)
    attended_grad = attended_back.astype(jnp.bfloat16)
    attended_wide = attended_grad.astype(jnp.float32).reshape(head_shape)
    prob_grad = jnp.einsum("mqhd,mkhd->mhqk", attended_wide, value_wide, precision=highest)
    inner_rows = jnp.sum(attended_wide * attended, axis=-1)
    logit_derivative = (
        soft_weights * (prob_grad - jnp.transpose(inner_rows, (0, 2, 1))[..., None]) * score_scale
    )
    query_grad = jnp.einsum(
        "mhqk,mkhd->mqhd", logit_derivative, key_heads.astype(jnp.float32), precision=highest
    )
    key_grad_all = jnp.einsum(
        "mhqk,mqhd->mkhd",
        logit_derivative,
        attention_asker_vectors.astype(jnp.float32),
        precision=highest,
    )
    value_grad_all = jnp.einsum("mhqk,mqhd->mkhd", soft_weights, attended_wide, precision=highest)
    key_grad, value_grad = (
        lax.psum_scatter(
            key_grad_all.reshape(micro_count, sequence_length, features).astype(jnp.bfloat16),
            "hist",
            scatter_dimension=1,
            tiled=True,
        ).astype(jnp.float32),
        lax.psum_scatter(
            value_grad_all.reshape(micro_count, sequence_length, features).astype(jnp.bfloat16),
            "hist",
            scatter_dimension=1,
            tiled=True,
        ).astype(jnp.float32),
    )
    projection_grads = [
        rotate(query_grad, positions, -1.0).reshape(own_rows, features).astype(jnp.bfloat16),
        rotate(key_grad.reshape(head_shape), positions, -1.0)
        .reshape(own_rows, features)
        .astype(jnp.bfloat16),
        value_grad.reshape(own_rows, features).astype(jnp.bfloat16),
    ]
    resid_normed_grad, query_normed_grad, key_normed_grad, value_normed_grad = back_second(
        (w_up, w_attn[0], w_attn[1], w_attn[2]),
        (up_grad, projection_grads[0], projection_grads[1], projection_grads[2]),
    )
    normed_grads = [query_normed_grad, key_normed_grad, value_normed_grad]
    stream_grads = []
    gain_grads = []
    for stream_idx in range(3):
        stream_grad, gain_grad = rms_back(
            stream_rows[stream_idx],
            inverses[stream_idx],
            gains_all[stream_idx + 1],
            normed_grads[stream_idx],
        )
        stream_grads.append(stream_grad)
        gain_grads.append(gain_grad)
    resid_grad, skip_scaling_derivative = rms_back(
        stream_rows[3], inverses[3], gains_all[4], resid_normed_grad
    )
    stream_grads.append(resid_grad + grad_rows)
    gain_grads.append(skip_scaling_derivative)
    stream_grads_all = jnp.stack(stream_grads).reshape(STREAM_COUNT, micro_count, quarter, features)
    full_grads = lax.all_gather(
        stream_grads_all.astype(jnp.bfloat16), "hist", axis=2, tiled=True
    ).astype(stream_grads_all.dtype)
    slot_grads = []
    dyn_grad = jnp.zeros((micro_count, sequence_length, STREAM_COUNT, slot_count), jnp.float32)
    for depth_position_number in range(local_slots):
        rows_now = history[depth_position_number].astype(jnp.float32)
        slot_grads.append(
            jnp.sum(
                depth_combination_factors[depth_position_number][..., None] * full_grads, axis=0
            )
        )
        inner_now = jnp.sum(full_grads * rows_now[None], axis=-1)
        dyn_grad = dyn_grad + jnp.einsum("cmt,j->mtcj", inner_now, own_table[depth_position_number])
    dyn_grad = dyn_grad.reshape(micro_count * sequence_length, STREAM_COUNT * slot_count)
    act_part = precise(dyn_grad, mixer_output_wide.T)
    mix_out_grad = precise(kept_mix[4].T, dyn_grad)
    act_grad = lax.psum(act_part.astype(jnp.bfloat16), "hist").astype(jnp.float32)
    on_root = (hist_place == root).astype(jnp.float32)
    latest_grad, gain_zero, mix_in_grad = mix_backward(kept_mix, act_grad, gains_all[0], mix_in_all)
    gain_zero = gain_zero * on_root
    mix_in_grad = mix_in_grad * on_root
    latest_grad = latest_grad.reshape(micro_count, sequence_length, features)
    marked = []
    for depth_position_number in range(local_slots):
        is_latest = (hist_place * local_slots + depth_position_number == newest_output).astype(
            jnp.float32
        )
        marked.append(slot_grads[depth_position_number] + latest_grad * is_latest)
    history_grad = jnp.stack(marked).astype(jnp.bfloat16)
    gains_grad_full = jnp.stack(
        [gain_zero, gain_grads[0], gain_grads[1], gain_grads[2], gain_grads[3]]
    )
    share_rows = w_out.shape[0]
    per_device = mix_width // dp_count
    mix_out_padded = jnp.pad(
        mix_out_grad.reshape(dp_count, per_device, mix_width),
        ((0, 0), (0, share_rows - per_device), (0, 0)),
    ).reshape(dp_count * share_rows, mix_width)
    small_wide = jnp.concatenate([mix_in_grad, gains_grad_full.T, mix_out_padded], axis=1)
    attn_lefts = (normed[0], normed[1], normed[2], attended_low)
    attn_rights = (projection_grads[0], projection_grads[1], projection_grads[2], grad_low)
    attn_share = lax.psum_scatter(
        jnp.concatenate(
            [
                lax.dot_general(
                    left_side, right_side, contract_rows, preferred_element_type=jnp.float32
                )
                for left_side, right_side in zip(attn_lefts, attn_rights)
            ],
            axis=1,
        ).astype(jnp.bfloat16),
        "dp",
        scatter_dimension=0,
        tiled=True,
    )
    up_term = lax.dot_general(normed[3], up_grad, contract_rows, preferred_element_type=jnp.float32)
    down_term = lax.dot_general(
        hidden, grad_low, contract_rows, preferred_element_type=jnp.float32
    ).reshape(share_rows * lax.axis_size("dp"), ratio * features)
    ffn_share = lax.psum_scatter(
        jnp.concatenate([up_term, down_term, small_wide], axis=1).astype(jnp.bfloat16),
        "dp",
        scatter_dimension=0,
        tiled=True,
    )
    attn_total, ffn_total = (
        lax.psum(attn_share, "hist").astype(jnp.float32),
        lax.psum(ffn_share, "hist").astype(jnp.float32),
    )
    ff_width = ratio * features
    w_attn_grad = jnp.stack(
        [
            attn_total[:, 0:features],
            attn_total[:, features : 2 * features],
            attn_total[:, 2 * features : 3 * features],
        ]
    )
    w_out_grad = attn_total[:, 3 * features : 4 * features]
    w_up_grad = ffn_total[:, 0:ff_width]
    w_down_grad = ffn_total[:, ff_width : 2 * ff_width].reshape(share_rows * ratio, features)
    mix_in_share = ffn_total[:, 2 * ff_width : 2 * ff_width + mix_width]
    gains_share = ffn_total[:, 2 * ff_width + mix_width : 2 * ff_width + mix_width + 5].T
    mix_out_share = ffn_total[0:per_device, 2 * ff_width + mix_width + 5 :]
    return (
        block_out,
        history_grad,
        gains_share,
        mix_in_share,
        mix_out_share,
        w_attn_grad,
        w_out_grad,
        w_up_grad,
        w_down_grad,
    )


DEVICE_MESH = pl.DeviceIdType.MESH
CORE, ACROSS_X, ACROSS_Y = 1, 2, 4


def partner(column, mask):
    moved = column
    for bit in (1, 2, 4):
        if mask & bit:
            on = lax.rem(lax.div(moved, bit), 2)
            moved = moved + bit - 2 * bit * on
    return moved


def greet(column, masks):
    barrier = pltpu.get_barrier_semaphore()
    for mask in masks:
        pl.semaphore_signal(
            barrier, inc=1, device_id={"dp": partner(column, mask)}, device_id_type=DEVICE_MESH
        )
    pl.semaphore_wait(barrier, len(masks))


def push(source, target, send_sem, recv_sem, place):
    copy = pltpu.make_async_remote_copy(
        src_ref=source,
        dst_ref=target,
        send_sem=send_sem,
        recv_sem=recv_sem,
        device_id={"dp": place},
        device_id_type=DEVICE_MESH,
    )
    copy.start()
    return copy


def gather_kernel(own_ref, all_ref, send_sem, recv_sem, local_sem):
    column = lax.axis_index("dp")
    rows = own_ref.shape[0]
    half = rows // 2
    greet(column, (CORE, ACROSS_X, ACROSS_Y))
    across = partner(column, ACROSS_X)
    along = partner(column, ACROSS_Y)
    beside = partner(column, CORE)
    corner = partner(column, ACROSS_X + ACROSS_Y)

    def place(owner, part):
        start = owner * rows + (half if part == 1 else 0)
        count = rows if part is None else half
        return all_ref.at[pl.ds(pl.multiple_of(start, 16), count)]

    def own(part):
        return own_ref.at[pl.ds(half if part == 1 else 0, rows if part is None else half)]

    local = pltpu.make_async_copy(own_ref, place(column, None), local_sem)
    local.start()

    def send(index, source, owner, part, to):
        return push(source, place(owner, part), send_sem.at[index], recv_sem.at[index], to)

    x_second = send(0, own(1), column, 1, across)
    y_first = send(1, own(0), column, 0, along)
    x_first = send(2, own(0), column, 0, across)
    y_second = send(3, own(1), column, 1, along)
    sibling = send(4, own(None), column, None, beside)
    y_first.wait_recv()
    x_corner = send(5, place(along, 0), along, 0, across)
    x_second.wait_recv()
    y_corner = send(6, place(across, 1), across, 1, along)
    x_first.wait_recv()
    sibling_x = send(7, place(across, None), across, None, beside)
    y_second.wait_recv()
    sibling_y = send(8, place(along, None), along, None, beside)
    x_corner.wait_recv()
    sibling_first = send(9, place(corner, 0), corner, 0, beside)
    y_corner.wait_recv()
    sibling_second = send(10, place(corner, 1), corner, 1, beside)
    for copy in (sibling, sibling_x, sibling_y, sibling_first, sibling_second):
        copy.wait_recv()
    for copy in (x_second, y_first, x_first, y_second, sibling, x_corner, y_corner):
        copy.wait_send()
    for copy in (sibling_x, sibling_y, sibling_first, sibling_second):
        copy.wait_send()
    local.wait()


def plane_gather(own):
    rows, features = own.shape
    return pl.pallas_call(
        gather_kernel,
        out_shape=jax.ShapeDtypeStruct((8 * rows, features), own.dtype),
        in_specs=[pl.BlockSpec(memory_space=pl.ANY)],
        out_specs=pl.BlockSpec(memory_space=pl.ANY),
        scratch_shapes=[
            pltpu.SemaphoreType.DMA((11,)),
            pltpu.SemaphoreType.DMA((11,)),
            pltpu.SemaphoreType.DMA,
        ],
        compiler_params=pltpu.CompilerParams(collective_id=1, has_side_effects=True),
        cost_estimate=pl.CostEstimate(
            flops=0, bytes_accessed=64 * 8 * rows * features, transcendentals=0
        ),
    )(own)


def scatter_kernel(*refs, pairs, dims):
    inputs = refs[: 2 * pairs]
    out_ref, out_buf, side, chip, from_x, from_y, last, send_sem, recv_sem = refs[2 * pairs :]
    column = lax.axis_index("dp")
    rows, features = out_ref.shape
    half = rows // 2
    tile = 512
    across = partner(column, ACROSS_X)
    along = partner(column, ACROSS_Y)
    beside = partner(column, CORE)
    blocks = (6, 2, 4, 0)

    def product(owner, target):
        left_rows = pl.ds(pl.multiple_of(owner * rows, 16), rows)

        def one_tile(t, carry):
            lanes = pl.ds(pl.multiple_of(t * tile, tile), tile)
            total = None
            for p in range(pairs):
                left = inputs[2 * p][left_rows, :]
                if dims[p] == 1:
                    term = lax.dot_general(
                        left,
                        inputs[2 * p + 1][lanes, :],
                        contract_cols,
                        preferred_element_type=jnp.float32,
                    )
                else:
                    term = jnp.dot(
                        left, inputs[2 * p + 1][:, lanes], preferred_element_type=jnp.float32
                    )
                total = term if total is None else total + term
            target[:, lanes] = total.astype(jnp.bfloat16)
            return carry

        lax.fori_loop(0, features // tile, one_tile, 0)

    def added(target, other):
        target[...] = (
            target[...].astype(jnp.float32) + other[...].astype(jnp.float32)
        ).astype(jnp.bfloat16)

    def sibling_copy(i):
        return pltpu.make_async_remote_copy(
            src_ref=out_buf.at[i],
            dst_ref=side.at[i],
            send_sem=send_sem.at[i],
            recv_sem=recv_sem.at[i],
            device_id={"dp": beside},
            device_id_type=DEVICE_MESH,
        )

    first, second = pl.ds(0, half), pl.ds(half, half)
    product(partner(column, 6 + CORE), out_buf.at[0])
    greet(column, (CORE, ACROSS_X, ACROSS_Y))
    siblings = []
    sends = []
    for i, mask in enumerate(blocks):
        if i > 0:
            product(partner(column, mask + CORE), out_buf.at[i])
        copy = sibling_copy(i)
        copy.start()
        siblings.append(copy)
        product(partner(column, mask), chip.at[i])
        copy.wait_recv()
        added(chip.at[i], side.at[i])
        if mask == 6:
            sends.append(
                push(chip.at[0, first], from_x.at[0], send_sem.at[4], recv_sem.at[4], across)
            )
            sends.append(
                push(chip.at[0, second], from_y.at[0], send_sem.at[5], recv_sem.at[5], along)
            )
        if mask == 2:
            sends.append(
                push(chip.at[1, first], from_x.at[1], send_sem.at[6], recv_sem.at[6], across)
            )
        if mask == 4:
            sends.append(
                push(chip.at[2, second], from_y.at[1], send_sem.at[7], recv_sem.at[7], along)
            )
    sends[0].wait_recv()
    added(chip.at[2, first], from_x.at[0])
    sends.append(push(chip.at[2, first], last.at[0], send_sem.at[8], recv_sem.at[8], along))
    sends[1].wait_recv()
    added(chip.at[1, second], from_y.at[0])
    sends.append(push(chip.at[1, second], last.at[1], send_sem.at[9], recv_sem.at[9], across))
    sends[2].wait_recv()
    added(chip.at[3, first], from_x.at[1])
    sends[3].wait_recv()
    added(chip.at[3, second], from_y.at[1])
    sends[4].wait_recv()
    added(chip.at[3, first], last.at[0])
    sends[5].wait_recv()
    added(chip.at[3, second], last.at[1])
    out_ref[...] = chip[3]
    for copy in siblings + sends:
        copy.wait_send()


def plane_scatter(terms, collective):
    total, features = terms[0][0].shape[0], 0
    rows = total // 8
    operands, dims, flops = [], [], 0
    for left, right, dim in terms:
        operands += [left, right]
        dims.append(dim)
        features = right.shape[0] if dim == 1 else right.shape[1]
        flops += 2 * total * left.shape[1] * features
    block = (rows, features)
    return pl.pallas_call(
        functools.partial(scatter_kernel, pairs=len(terms), dims=tuple(dims)),
        out_shape=jax.ShapeDtypeStruct(block, jnp.bfloat16),
        in_specs=[pl.BlockSpec(memory_space=pltpu.VMEM)] * len(operands),
        out_specs=pl.BlockSpec(memory_space=pltpu.VMEM),
        scratch_shapes=[
            pltpu.VMEM((4,) + block, jnp.bfloat16),
            pltpu.VMEM((4,) + block, jnp.bfloat16),
            pltpu.VMEM((4,) + block, jnp.bfloat16),
            pltpu.VMEM((2, rows // 2, features), jnp.bfloat16),
            pltpu.VMEM((2, rows // 2, features), jnp.bfloat16),
            pltpu.VMEM((2, rows // 2, features), jnp.bfloat16),
            pltpu.SemaphoreType.DMA((10,)),
            pltpu.SemaphoreType.DMA((10,)),
        ],
        compiler_params=pltpu.CompilerParams(
            collective_id=collective, has_side_effects=True, vmem_limit_bytes=48 * 1024 * 1024
        ),
        cost_estimate=pl.CostEstimate(
            flops=flops, bytes_accessed=64 * total * features, transcendentals=0
        ),
    )(*operands)


def rotary_table(row_positions, head_dim):
    half_dim = head_dim // 2
    frequency = jnp.exp(
        jnp.arange(half_dim, dtype=jnp.float32) * (-2.0 * math.log(10000.0) / head_dim)
    )
    angles = row_positions.astype(jnp.float32)[:, None] * frequency[None, :]
    cosine = jnp.cos(angles)
    sine_part = jnp.sin(angles)
    return (
        jnp.concatenate([cosine, cosine], axis=-1),
        jnp.concatenate([-sine_part, sine_part], axis=-1),
    )


def attention_kernel(
    length_ref,
    plane_ref,
    cos_ref,
    sin_ref,
    q_ref,
    k_ref,
    v_ref,
    kv_before_ref,
    out_grad_ref,
    att_ref,
    q_grad_ref,
    kv_grad_ref,
    kv_before_grad_ref,
    *,
    heads,
    micro_count,
    sequence_length,
):
    column = pl.program_id(0)
    plane = plane_ref[0]
    rows = q_ref.shape[0]
    scale = 1.0 / math.sqrt(HEAD_DIM)
    row = plane * rows + lax.broadcasted_iota(jnp.int32, (rows, 1), 0)
    start = jnp.zeros((rows, 1), jnp.int32)
    limit = jnp.zeros((rows, 1), jnp.int32)
    for m in range(micro_count):
        here = (row >= m * sequence_length) & (row < (m + 1) * sequence_length)
        start = jnp.where(here, m * sequence_length, start)
        limit = jnp.where(here, m * sequence_length + length_ref[column * micro_count + m], limit)
    limit = jnp.minimum(limit, row + 1)
    key_row = (plane - 1) * rows + lax.broadcasted_iota(jnp.int32, (1, 2 * rows), 1)
    allowed = (key_row >= start) & (key_row < limit)
    cosine = cos_ref[...]
    sine_part = sin_ref[...]
    width = heads * HEAD_DIM
    for head in range(heads):
        lanes = slice(head * HEAD_DIM, (head + 1) * HEAD_DIM)
        value_lanes = slice(width + head * HEAD_DIM, width + (head + 1) * HEAD_DIM)
        query = q_ref[:, lanes]
        keys = jnp.concatenate([kv_before_ref[:, lanes], k_ref[:, lanes]], axis=0)
        values = jnp.concatenate([kv_before_ref[:, value_lanes], v_ref[:, lanes]], axis=0)
        out_grad = out_grad_ref[:, lanes]
        scores = (
            lax.dot_general(query, keys, contract_cols, preferred_element_type=jnp.float32) * scale
        )
        scores = jnp.where(allowed, scores, masked_out)
        raised = jnp.exp(scores - jnp.max(scores, axis=-1, keepdims=True))
        weights = raised / jnp.sum(raised, axis=-1, keepdims=True)
        weights_low = weights.astype(jnp.bfloat16)
        att_ref[:, lanes] = matmul(weights_low, values).astype(jnp.bfloat16)
        weight_grad = lax.dot_general(
            out_grad, values, contract_cols, preferred_element_type=jnp.float32
        )
        inner = jnp.sum(weights * weight_grad, axis=-1, keepdims=True)
        score_grad = (weights * (weight_grad - inner) * scale).astype(jnp.bfloat16)
        query_grad = matmul(score_grad, keys)
        swapped = jnp.concatenate(
            [query_grad[:, HEAD_DIM // 2 :], query_grad[:, : HEAD_DIM // 2]], axis=1
        )
        q_grad_ref[:, lanes] = (query_grad * cosine - swapped * sine_part).astype(jnp.bfloat16)
        key_grad = lax.dot_general(
            score_grad, query, contract_rows, preferred_element_type=jnp.float32
        )
        value_grad = lax.dot_general(
            weights_low, out_grad, contract_rows, preferred_element_type=jnp.float32
        )
        kv_before_grad_ref[:, lanes] = key_grad[:rows].astype(jnp.bfloat16)
        kv_before_grad_ref[:, value_lanes] = value_grad[:rows].astype(jnp.bfloat16)
        kv_grad_ref[:, lanes] = key_grad[rows:]
        kv_grad_ref[:, value_lanes] = value_grad[rows:]


def attention(
    lengths_all, plane, cosine, sine_part, q, k, v, kv_before, out_grad, rows, micro_count, length
):
    total, width = q.shape
    heads = width // HEAD_DIM
    block = lambda columns: pl.BlockSpec((rows, columns), lambda m: (m, 0))
    whole = pl.BlockSpec(memory_space=pltpu.SMEM)
    table = pl.BlockSpec((rows, HEAD_DIM), lambda m: (0, 0))
    return pl.pallas_call(
        functools.partial(
            attention_kernel, heads=heads, micro_count=micro_count, sequence_length=length
        ),
        grid=(total // rows,),
        in_specs=[whole, whole, table, table]
        + [block(width)] * 3
        + [block(2 * width), block(width)],
        out_specs=[block(width), block(width), block(2 * width), block(2 * width)],
        out_shape=[
            jax.ShapeDtypeStruct((total, width), jnp.bfloat16),
            jax.ShapeDtypeStruct((total, width), jnp.bfloat16),
            jax.ShapeDtypeStruct((total, 2 * width), jnp.float32),
            jax.ShapeDtypeStruct((total, 2 * width), jnp.bfloat16),
        ],
        compiler_params=pltpu.CompilerParams(vmem_limit_bytes=32 * 1024 * 1024),
        cost_estimate=pl.CostEstimate(
            flops=28 * total * rows * width, bytes_accessed=24 * total * width, transcendentals=0
        ),
    )(lengths_all, plane, cosine, sine_part, q, k, v, kv_before, out_grad)


def turned(values, cosine, sine_part, rows, sign):
    total, width = values.shape
    heads = values.reshape(total // rows, rows, width // HEAD_DIM, HEAD_DIM)
    swapped = jnp.concatenate(
        [heads[..., HEAD_DIM // 2 :], heads[..., : HEAD_DIM // 2]], axis=-1
    )
    return (
        heads * cosine[None, :, None, :] + sign * swapped * sine_part[None, :, None, :]
    ).reshape(total, width)


def shards_split(
    history,
    history_layer_index,
    lengths,
    norm_gains,
    mix_in,
    mix_out,
    w_attn,
    w_out,
    w_up,
    w_down,
    cotangent,
):
    local_slots, micro_count, sequence_length, features = history.shape
    planes = lax.axis_size("hist")
    columns = lax.axis_size("dp")
    plane = lax.axis_index("hist")
    slot_count = local_slots * planes
    all_rows = micro_count * sequence_length
    rows = all_rows // planes
    share = features // columns
    mix_width = mix_in.shape[1]
    ff_share = w_down.shape[0]
    low = lambda values: values.astype(jnp.bfloat16)

    top = jnp.concatenate(
        [mix_in, norm_gains.T, jnp.zeros((share, 128 - mix_width - 5), jnp.bfloat16)], axis=1
    )
    mix_rows = mix_out.shape[0]
    bottom = jnp.zeros((16, 128), jnp.bfloat16)
    bottom = bottom.at[:mix_rows, :mix_width].set(mix_out)
    bottom = bottom.at[0, mix_width : mix_width + micro_count].set(low(lengths))
    packed = lax.all_gather(jnp.concatenate([top, bottom], axis=0), "dp", axis=0, tiled=False)
    mix_in_all = packed[:, :share, :mix_width].reshape(features, mix_width)
    gains_all = (
        packed[:, :share, mix_width : mix_width + 5].reshape(features, 5).astype(jnp.float32).T
    )
    mixer_output_wide = (
        packed[:, share : share + mix_rows, :mix_width]
        .reshape(mix_width, mix_width)
        .astype(jnp.float32)
    )
    lengths_all = (
        packed[:, share, mix_width : mix_width + micro_count].reshape(-1).astype(jnp.int32)
    )

    up_columns = lax.all_to_all(
        w_up.reshape(share, columns, ff_share), "dp", split_axis=1, concat_axis=0, tiled=True
    ).reshape(features, ff_share)
    attn_columns = lax.all_to_all(
        w_attn.reshape(3, share, columns, share).transpose(1, 2, 0, 3),
        "dp",
        split_axis=1,
        concat_axis=0,
        tiled=True,
    ).reshape(features, 3, share)

    chunk = sequence_length // planes
    inverse_step = pow(micro_count, -1, planes)
    received = []
    for i in range(micro_count):
        target = lax.rem((plane - i + planes * micro_count) * inverse_step, planes)
        which = lax.div(target * micro_count + i, planes)
        piece = lax.dynamic_index_in_dim(cotangent, which, 0, keepdims=False)
        pairs = [(t, ((t - i) * inverse_step) % planes) for t in range(planes)]
        received.append(lax.ppermute(piece, "hist", pairs))
    my_row = plane * rows + jnp.arange(rows, dtype=jnp.int32)
    my_position = lax.rem(my_row, sequence_length)
    my_sequence = lax.div(my_row, sequence_length)
    my_length = jnp.sum(
        jnp.where(
            my_sequence[:, None] == jnp.arange(micro_count, dtype=jnp.int32)[None, :],
            lengths[None, :],
            0,
        ),
        axis=1,
    )
    valid_rows = (my_position < my_length).astype(jnp.float32)[:, None]
    grad_rows = jnp.concatenate(received, axis=0).astype(jnp.float32) * valid_rows
    grad_all = plane_gather(low(grad_rows))

    layer_lookup = (
        history_layer_index[:, None] == jnp.arange(slot_count, dtype=jnp.int32)[None, :]
    ).astype(jnp.float32)
    newest_output = jnp.sum(
        jnp.arange(slot_count, dtype=jnp.int32)
        * (history_layer_index == slot_count - 1).astype(jnp.int32)
    )
    root = newest_output // local_slots
    on_root = (plane == root).astype(jnp.float32)
    latest_local = lax.dynamic_index_in_dim(history, newest_output % local_slots, 0, keepdims=False)
    dyn_local, kept_mix = mix_forward(
        latest_local.reshape(all_rows, features), gains_all[0], mix_in_all, mixer_output_wide
    )
    dyn_every = lax.all_gather(dyn_local, "hist", axis=0, tiled=False)
    dyn = lax.dynamic_index_in_dim(dyn_every, root, 0, keepdims=False)
    own_table = lax.dynamic_slice_in_dim(layer_lookup, plane * local_slots, local_slots, 0)
    factors = jnp.einsum(
        "tcj,sj->sct",
        dyn.reshape(all_rows, STREAM_COUNT, slot_count),
        own_table,
        precision=highest,
    )
    flat_history = history.reshape(local_slots, all_rows, features)

    def mixed(stream):
        total = jnp.zeros((all_rows, features), jnp.float32)
        for slot in range(local_slots):
            total = total + factors[slot, stream][:, None] * flat_history[slot].astype(jnp.float32)
        return lax.psum_scatter(low(total), "hist", scatter_dimension=0, tiled=True).astype(
            jnp.float32
        )

    stream_rows = [None] * STREAM_COUNT
    inverses = [None] * STREAM_COUNT
    normed = [None] * STREAM_COUNT
    for stream in (3, 0, 1, 2):
        stream_rows[stream] = mixed(stream)
        scaled, inverses[stream] = rms_scale(stream_rows[stream], gains_all[stream + 1])
        normed[stream] = plane_gather(low(scaled))

    up_pre = matmul(normed[3], up_columns)
    hidden = low(jax.nn.gelu(up_pre, approximate=False))
    hidden_grad = lax.dot_general(
        grad_all, w_down, contract_cols, preferred_element_type=jnp.float32
    )
    up_grad = low(hidden_grad * gelu_slope(up_pre))
    normed_grads = [None] * STREAM_COUNT
    normed_grads[3] = plane_scatter([(up_grad, up_columns, 1)], 2)
    down_term = low(
        lax.dot_general(hidden, grad_all, contract_rows, preferred_element_type=jnp.float32)
    )
    up_term = low(
        lax.dot_general(normed[3], up_grad, contract_rows, preferred_element_type=jnp.float32)
    )

    cosine, sine_part = rotary_table(my_position, HEAD_DIM)
    q = low(turned(matmul(normed[0], attn_columns[:, 0]), cosine, sine_part, rows, 1.0))
    k = low(turned(matmul(normed[1], attn_columns[:, 1]), cosine, sine_part, rows, 1.0))
    v = low(matmul(normed[2], attn_columns[:, 2]))
    onward = [(p, p + 1) for p in range(planes - 1)]
    back = [(p + 1, p) for p in range(planes - 1)]
    kv_before = lax.ppermute(jnp.concatenate([k, v], axis=1), "hist", onward)
    att_grad = low(
        lax.dot_general(grad_all, w_out, contract_cols, preferred_element_type=jnp.float32)
    )
    att, q_grad, kv_grad, kv_before_grad = attention(
        lengths_all,
        plane.reshape(1),
        cosine,
        sine_part,
        q,
        k,
        v,
        kv_before,
        att_grad,
        rows,
        micro_count,
        sequence_length,
    )
    kv_grad = kv_grad + lax.ppermute(kv_before_grad, "hist", back).astype(jnp.float32)
    k_grad = low(turned(kv_grad[:, :share], cosine, sine_part, rows, -1.0))
    v_grad = low(kv_grad[:, share:])
    branch = plane_scatter([(att, w_out, 0), (hidden, w_down, 0)], 3)
    block_rows = low((stream_rows[3] + branch.astype(jnp.float32)) * valid_rows)
    block_out = jnp.zeros((micro_count, chunk, features), jnp.bfloat16)
    for i in range(micro_count):
        pairs = [(p, (micro_count * p + i) % planes) for p in range(planes)]
        piece = lax.ppermute(block_rows[i * chunk : (i + 1) * chunk], "hist", pairs)
        source = lax.rem((plane - i + planes * micro_count) * inverse_step, planes)
        which = lax.div(source * micro_count + i, planes)
        block_out = lax.dynamic_update_index_in_dim(block_out, piece, which, 0)
    out_term = low(
        lax.dot_general(att, grad_all, contract_rows, preferred_element_type=jnp.float32)
    )
    projection_grads = (q_grad, k_grad, v_grad)
    attn_terms = []
    for stream in range(3):
        normed_grads[stream] = plane_scatter(
            [(projection_grads[stream], attn_columns[:, stream], 1)], 4
        )
        attn_terms.append(
            low(
                lax.dot_general(
                    normed[stream],
                    projection_grads[stream],
                    contract_rows,
                    preferred_element_type=jnp.float32,
                )
            )
        )

    full_grads = [None] * STREAM_COUNT
    gain_grads = [None] * STREAM_COUNT
    for stream in (3, 0, 1, 2):
        stream_grad, gain_grads[stream] = rms_back(
            stream_rows[stream],
            inverses[stream],
            gains_all[stream + 1],
            normed_grads[stream].astype(jnp.float32),
        )
        if stream == 3:
            stream_grad = stream_grad + grad_rows
        full_grads[stream] = lax.all_gather(low(stream_grad), "hist", axis=0, tiled=True).astype(
            jnp.float32
        )
    inner = jnp.stack(
        [
            jnp.stack(
                [
                    jnp.sum(full_grads[stream] * flat_history[slot].astype(jnp.float32), axis=-1)
                    for slot in range(local_slots)
                ],
                axis=-1,
            )
            for stream in range(STREAM_COUNT)
        ],
        axis=1,
    )
    dyn_part = jnp.einsum("tcs,sj->tcj", inner, own_table, precision=highest)
    dyn_grad = jnp.sum(
        lax.all_gather(
            dyn_part.reshape(all_rows, STREAM_COUNT * slot_count), "hist", axis=0, tiled=False
        ),
        axis=0,
    )
    act_grad = precise(dyn_grad, mixer_output_wide.T)
    mix_out_grad = precise(kept_mix[4].T, dyn_grad) * on_root
    latest_grad, gain_zero, mix_in_grad = mix_backward(kept_mix, act_grad, gains_all[0], mix_in_all)
    slot_grads = []
    for slot in range(local_slots):
        is_latest = (plane * local_slots + slot == newest_output).astype(jnp.float32)
        slot_grad = latest_grad * is_latest
        for stream in range(STREAM_COUNT):
            slot_grad = slot_grad + factors[slot, stream][:, None] * full_grads[stream]
        slot_grads.append(low(slot_grad))
    history_grad = jnp.stack(slot_grads).reshape(history.shape)

    def scattered(term):
        return lax.psum_scatter(term, "hist", scatter_dimension=0, tiled=True)

    def gathered(term, axis):
        return lax.all_gather(term, "hist", axis=axis, tiled=True).astype(jnp.float32)

    part = share // planes
    w_down_grad = gathered(scattered(down_term), 0)
    w_out_grad = gathered(scattered(out_term), 0)

    def by_plane(term):
        return (
            term.reshape(columns, planes, part, term.shape[1])
            .transpose(1, 0, 2, 3)
            .reshape(features, term.shape[1])
        )

    up_own = scattered(by_plane(up_term)).reshape(columns, part, ff_share)
    up_own = lax.all_to_all(up_own, "dp", split_axis=0, concat_axis=0, tiled=True)
    w_up_grad = gathered(up_own.transpose(1, 0, 2).reshape(part, columns * ff_share), 0)
    attn_own = scattered(by_plane(jnp.concatenate(attn_terms, axis=1))).reshape(
        columns, part, 3 * share
    )
    attn_own = lax.all_to_all(attn_own, "dp", split_axis=0, concat_axis=0, tiled=True)
    attn_own = attn_own.reshape(columns, part, 3, share).transpose(2, 1, 0, 3)
    w_attn_grad = gathered(attn_own.reshape(3, part, features), 1)

    small_top = jnp.concatenate(
        [
            mix_in_grad * on_root,
            jnp.stack([gain_zero * on_root] + gain_grads).T,
            jnp.zeros((features, 128 - mix_width - 5), jnp.float32),
        ],
        axis=1,
    ).reshape(columns, share, 128)
    small_bottom = jnp.pad(
        mix_out_grad.reshape(columns, mix_rows, mix_width),
        ((0, 0), (0, 16 - mix_rows), (0, 128 - mix_width)),
    )
    small = low(jnp.concatenate([small_top, small_bottom], axis=1))
    small = lax.psum_scatter(small, "dp", scatter_dimension=0, tiled=False)
    small = lax.psum(small, "hist").astype(jnp.float32)
    return (
        block_out,
        history_grad,
        small[:share, mix_width : mix_width + 5].T,
        small[:share, :mix_width],
        small[share : share + mix_rows, :mix_width],
        w_attn_grad,
        w_out_grad,
        w_up_grad,
        w_down_grad,
    )


def splits_by_heads(mesh, micro_count, sequence_length):
    columns, planes = mesh.shape["dp"], mesh.shape["hist"]
    all_rows = micro_count * sequence_length
    rows = all_rows // planes
    return (
        columns == 8
        and HEADS % columns == 0
        and all_rows % planes == 0
        and sequence_length % planes == 0
        and rows % 64 == 0
        and math.gcd(micro_count, planes) == 1
        and all(
            (p * rows) // sequence_length * sequence_length >= (p - 1) * rows
            for p in range(planes)
        )
    )


def solution(mesh):
    placed = (
        P("hist", "dp", None, None),
        P(),
        P("dp"),
        P(None, "dp"),
        P("dp", None),
        P("dp", None),
        P(None, "dp", None),
        P("dp", None),
        P("dp", None),
        P("dp", None),
        P("dp", "hist", None),
    )
    def plan(*arrays):
        micro_count = arrays[2].shape[0]
        if splits_by_heads(mesh, micro_count, arrays[0].shape[2]):
            return shards_split(*arrays)
        return shards(*arrays)

    return jax.shard_map(
        plan,
        mesh=mesh,
        in_specs=placed,
        out_specs=(
            P("dp", "hist", None),
            P("hist", "dp", None, None),
            P(None, "dp"),
            P("dp", None),
            P("dp", None),
            P(None, "dp", None),
            P("dp", None),
            P("dp", None),
            P("dp", None),
        ),
        check_vma=False,
    )
```

```python
import functools
import math

import jax
import jax.numpy as jnp
from jax import lax
from jax.experimental import pallas as pl
from jax.experimental.pallas import tpu as pltpu
from jax.sharding import PartitionSpec as P

MODEL_WIDTH = 2048
HEADS = 16
HEAD_DIM = 128
FF = 8192
STREAM_COUNT = 4


epsilon = 1e-06
masked_out = -1e30
highest = lax.Precision.HIGHEST
contract_rows = (((0,), (0,)), ((), ()))
contract_cols = (((1,), (1,)), ((), ()))


def broadcast(value, axis, source):
    kept = jnp.where(lax.axis_index(axis) == source, value, 0).astype(value.dtype)
    return lax.psum(kept, axis)


def matmul(left_side, right_side):
    return jnp.dot(left_side, right_side, preferred_element_type=jnp.float32)


def precise(left_side, right_side):
    return jnp.dot(left_side, right_side, precision=highest, preferred_element_type=jnp.float32)


def gelu_slope(values):
    return 0.5 * (1.0 + lax.erf(values * (1.0 / math.sqrt(2.0)))) + values * jnp.exp(
        -0.5 * values * values
    ) * (1.0 / math.sqrt(2.0 * math.pi))


def rms_scale(values, gain_row):
    inverse = lax.rsqrt(jnp.mean(values * values, axis=-1, keepdims=True) + epsilon)
    return (values * inverse * gain_row, inverse)


def rms_back(values, inverse, gain_row, grad_in):
    scaled = grad_in * gain_row
    gain_grad = jnp.sum(grad_in * values * inverse, axis=0)
    inner_mean = jnp.mean(scaled * values, axis=-1, keepdims=True)
    return (inverse * scaled - values * (inverse * inverse * inverse) * inner_mean, gain_grad)


def rotate(values, positions, turn_sign):
    half_dim = values.shape[-1] // 2
    frequency = jnp.exp(
        jnp.arange(half_dim, dtype=jnp.float32) * (-2.0 * math.log(10000.0) / values.shape[-1])
    )
    angles = positions.astype(jnp.float32)[:, None] * frequency[None, :]
    cosine = jnp.cos(angles)[:, None, :]
    sine_part = jnp.sin(angles)[:, None, :] * turn_sign
    lower_half = values[..., :half_dim]
    upper_half = values[..., half_dim:]
    return jnp.concatenate(
        [
            lower_half * cosine - upper_half * sine_part,
            upper_half * cosine + lower_half * sine_part,
        ],
        axis=-1,
    )


def first_rows(weights, lefts):

    def add_piece(totals, pieces, start_at):
        return tuple(
            (matmul(left_side, piece_rows) for left_side, piece_rows in zip(lefts, pieces))
        )

    initial = tuple(
        (jnp.zeros((lefts[0].shape[0], weight.shape[1]), jnp.float32) for weight in weights)
    )
    return add_piece(
        initial,
        (
            lax.all_gather(weights[0], "dp", axis=0, tiled=True),
            lax.all_gather(weights[1], "dp", axis=0, tiled=True),
            lax.all_gather(weights[2], "dp", axis=0, tiled=True),
            lax.all_gather(weights[3], "dp", axis=0, tiled=True),
        ),
        jnp.int32(0),
    )


def second_rows(w_out, down_folded, attended_low, hidden, ratio):

    def add_piece(total_sum, pieces, start_at):
        count = pieces[0].shape[0]
        down_rows = pieces[1].reshape(count * ratio, pieces[1].shape[1] // ratio)
        return matmul(attended_low, pieces[0]) + matmul(hidden, down_rows)

    initial = jnp.zeros((attended_low.shape[0], w_out.shape[1]), jnp.float32)
    return add_piece(
        initial,
        (
            lax.all_gather(w_out, "dp", axis=0, tiled=True),
            lax.all_gather(down_folded, "dp", axis=0, tiled=True),
        ),
        jnp.int32(0),
    )


def back_first(w_out, down_folded, grad_low, ratio):

    def add_piece(totals, pieces, start_at):
        count = pieces[0].shape[0]
        out_part = lax.dot_general(
            grad_low, pieces[0], contract_cols, preferred_element_type=jnp.float32
        )
        down_rows = pieces[1].reshape(count * ratio, pieces[1].shape[1] // ratio)
        down_part = lax.dot_general(
            grad_low, down_rows, contract_cols, preferred_element_type=jnp.float32
        )
        return (out_part, down_part)

    features = w_out.shape[1]
    initial = (
        jnp.zeros((grad_low.shape[0], features), jnp.float32),
        jnp.zeros((grad_low.shape[0], features * ratio), jnp.float32),
    )
    return add_piece(
        initial,
        (
            lax.all_gather(w_out, "dp", axis=0, tiled=True),
            lax.all_gather(down_folded, "dp", axis=0, tiled=True),
        ),
        jnp.int32(0),
    )


def back_second(weights, rights):

    def add_piece(totals, pieces, start_at):
        return tuple(
            (
                lax.dot_general(
                    right_side, piece_rows, contract_cols, preferred_element_type=jnp.float32
                )
                for right_side, piece_rows in zip(rights, pieces)
            )
        )

    features = weights[1].shape[1]
    initial = tuple((jnp.zeros((rights[0].shape[0], features), jnp.float32) for weight in weights))
    return add_piece(
        initial,
        (
            lax.all_gather(weights[0], "dp", axis=0, tiled=True),
            lax.all_gather(weights[1], "dp", axis=0, tiled=True),
            lax.all_gather(weights[2], "dp", axis=0, tiled=True),
            lax.all_gather(weights[3], "dp", axis=0, tiled=True),
        ),
        jnp.int32(0),
    )


def mix_forward(values_low, gain_row, mix_in_all, mixer_output_wide):
    values = values_low.astype(jnp.float32)
    scaled, inverse = rms_scale(values, gain_row)
    normed_mix = scaled.astype(jnp.bfloat16)
    mixer_preactivation = matmul(normed_mix, mix_in_all)
    mix_act = jax.nn.gelu(mixer_preactivation, approximate=False)
    return (
        precise(mix_act, mixer_output_wide),
        (values, inverse, normed_mix, mixer_preactivation, mix_act),
    )


def mix_backward(kept_mix, act_grad, gain_row, mix_in_all):
    values, inverse, normed_mix, mixer_preactivation, mix_act = kept_mix
    pre_grad = act_grad * gelu_slope(mixer_preactivation)
    in_grad = precise(normed_mix.astype(jnp.float32).T, pre_grad)
    normed_grad = precise(pre_grad, mix_in_all.astype(jnp.float32).T)
    latest_grad, gain_grad = rms_back(values, inverse, gain_row, normed_grad)
    return (latest_grad, gain_grad, in_grad)


def shards(
    history,
    history_layer_index,
    lengths,
    norm_gains,
    mix_in,
    mix_out,
    w_attn,
    w_out,
    w_up,
    w_down,
    cotangent,
):
    local_slots, micro_count, sequence_length, features = history.shape
    hist_count = lax.axis_size("hist")
    dp_count = lax.axis_size("dp")
    hist_place = lax.axis_index("hist")
    slot_count = local_slots * hist_count
    ratio = FF // MODEL_WIDTH
    gains_all, mix_in_all, mix_out_all = (
        lax.all_gather(norm_gains, "dp", axis=1, tiled=True),
        lax.all_gather(mix_in, "dp", axis=0, tiled=True),
        lax.all_gather(mix_out, "dp", axis=0, tiled=True),
    )
    gains_all = gains_all.astype(jnp.float32)
    mixer_output_wide = mix_out_all.astype(jnp.float32)
    mix_width = mixer_output_wide.shape[0]
    layer_lookup = (
        history_layer_index[:, None] == jnp.arange(slot_count, dtype=jnp.int32)[None, :]
    ).astype(jnp.float32)
    newest_output = jnp.sum(
        jnp.arange(slot_count, dtype=jnp.int32)
        * (history_layer_index == slot_count - 1).astype(jnp.int32)
    )
    down_folded = w_down.reshape(w_down.shape[0] // ratio, ratio * w_down.shape[1])
    quarter = cotangent.shape[1]
    own_rows = micro_count * quarter
    positions = hist_place * quarter + jnp.arange(quarter, dtype=jnp.int32)
    valid_rows = (positions[None, :] < lengths[:, None]).astype(jnp.float32).reshape(own_rows, 1)
    root = newest_output // local_slots
    latest_local = lax.dynamic_index_in_dim(history, newest_output % local_slots, 0, keepdims=False)
    latest_rows = broadcast(latest_local, "hist", root)
    dynamic_weights, kept_mix = mix_forward(
        latest_rows.reshape(micro_count * sequence_length, features),
        gains_all[0],
        mix_in_all,
        mixer_output_wide,
    )
    dynamic_weights = dynamic_weights.reshape(
        micro_count, sequence_length, STREAM_COUNT, slot_count
    )
    own_table = lax.dynamic_slice_in_dim(layer_lookup, hist_place * local_slots, local_slots, 0)
    depth_combination_factors = jnp.einsum(
        "mtcj,sj->scmt", dynamic_weights, own_table, precision=highest
    )
    partial_sums = jnp.zeros((STREAM_COUNT, micro_count, sequence_length, features), jnp.float32)
    for depth_position_number in range(local_slots):
        partial_sums = (
            partial_sums
            + depth_combination_factors[depth_position_number][..., None]
            * history[depth_position_number].astype(jnp.float32)[None]
        )
    blended_residual_inputs = lax.psum_scatter(
        partial_sums, "hist", scatter_dimension=2, tiled=True
    )
    stream_rows = blended_residual_inputs.reshape(STREAM_COUNT, own_rows, features)
    normed = []
    inverses = []
    for stream_idx in range(STREAM_COUNT):
        scaled, inverse = rms_scale(stream_rows[stream_idx], gains_all[stream_idx + 1])
        normed.append(scaled.astype(jnp.bfloat16))
        inverses.append(inverse)
    head_shape = (micro_count, quarter, HEADS, HEAD_DIM)
    query_pre, key_pre, value_pre, up_pre = first_rows(
        (w_attn[0], w_attn[1], w_attn[2], w_up), (normed[0], normed[1], normed[2], normed[3])
    )
    attention_asker_vectors = rotate(query_pre.reshape(head_shape), positions, 1.0).astype(
        jnp.bfloat16
    )
    keys_rot = rotate(key_pre.reshape(head_shape), positions, 1.0).astype(jnp.bfloat16)
    values_low = value_pre.astype(jnp.bfloat16)
    keys_all, values_all = (
        lax.all_gather(
            keys_rot.reshape(micro_count, quarter, features), "hist", axis=1, tiled=True
        ),
        lax.all_gather(
            values_low.reshape(micro_count, quarter, features), "hist", axis=1, tiled=True
        ),
    )
    key_heads = keys_all.reshape(micro_count, sequence_length, HEADS, HEAD_DIM)
    value_wide = values_all.reshape(micro_count, sequence_length, HEADS, HEAD_DIM).astype(
        jnp.float32
    )
    score_scale = 1.0 / math.sqrt(HEAD_DIM)
    scores = (
        jnp.einsum(
            "mqhd,mkhd->mhqk",
            attention_asker_vectors,
            key_heads,
            preferred_element_type=jnp.float32,
        )
        * score_scale
    )
    key_positions = jnp.arange(sequence_length, dtype=jnp.int32)
    allowed = (key_positions[None, None, :] <= positions[None, :, None]) & (
        key_positions[None, None, :] < lengths[:, None, None]
    )
    scores = jnp.where(allowed[:, None], scores, masked_out)
    row_top = jnp.max(scores, axis=-1, keepdims=True)
    raised = jnp.exp(scores - row_top)
    soft_weights = raised / jnp.sum(raised, axis=-1, keepdims=True)
    attended = jnp.einsum("mhqk,mkhd->mqhd", soft_weights, value_wide, precision=highest)
    attended_low = attended.reshape(own_rows, features).astype(jnp.bfloat16)
    hidden = jax.nn.gelu(up_pre, approximate=False).astype(jnp.bfloat16)
    branch = second_rows(w_out, down_folded, attended_low, hidden, ratio)
    block_out = (
        ((stream_rows[3] + branch) * valid_rows)
        .astype(jnp.bfloat16)
        .reshape(micro_count, quarter, features)
    )
    grad_rows = cotangent.reshape(own_rows, features).astype(jnp.float32) * valid_rows
    grad_low = grad_rows.astype(jnp.bfloat16)
    attended_back, hidden_grad = back_first(w_out, down_folded, grad_low, ratio)
    up_grad = (hidden_grad * gelu_slope(up_pre)).astype(jnp.bfloat16)
    attended_grad = attended_back.astype(jnp.bfloat16)
    attended_wide = attended_grad.astype(jnp.float32).reshape(head_shape)
    prob_grad = jnp.einsum("mqhd,mkhd->mhqk", attended_wide, value_wide, precision=highest)
    inner_rows = jnp.sum(attended_wide * attended, axis=-1)
    logit_derivative = (
        soft_weights * (prob_grad - jnp.transpose(inner_rows, (0, 2, 1))[..., None]) * score_scale
    )
    query_grad = jnp.einsum(
        "mhqk,mkhd->mqhd", logit_derivative, key_heads.astype(jnp.float32), precision=highest
    )
    key_grad_all = jnp.einsum(
        "mhqk,mqhd->mkhd",
        logit_derivative,
        attention_asker_vectors.astype(jnp.float32),
        precision=highest,
    )
    value_grad_all = jnp.einsum("mhqk,mqhd->mkhd", soft_weights, attended_wide, precision=highest)
    key_grad, value_grad = (
        lax.psum_scatter(
            key_grad_all.reshape(micro_count, sequence_length, features).astype(jnp.bfloat16),
            "hist",
            scatter_dimension=1,
            tiled=True,
        ).astype(jnp.float32),
        lax.psum_scatter(
            value_grad_all.reshape(micro_count, sequence_length, features).astype(jnp.bfloat16),
            "hist",
            scatter_dimension=1,
            tiled=True,
        ).astype(jnp.float32),
    )
    projection_grads = [
        rotate(query_grad, positions, -1.0).reshape(own_rows, features).astype(jnp.bfloat16),
        rotate(key_grad.reshape(head_shape), positions, -1.0)
        .reshape(own_rows, features)
        .astype(jnp.bfloat16),
        value_grad.reshape(own_rows, features).astype(jnp.bfloat16),
    ]
    resid_normed_grad, query_normed_grad, key_normed_grad, value_normed_grad = back_second(
        (w_up, w_attn[0], w_attn[1], w_attn[2]),
        (up_grad, projection_grads[0], projection_grads[1], projection_grads[2]),
    )
    normed_grads = [query_normed_grad, key_normed_grad, value_normed_grad]
    stream_grads = []
    gain_grads = []
    for stream_idx in range(3):
        stream_grad, gain_grad = rms_back(
            stream_rows[stream_idx],
            inverses[stream_idx],
            gains_all[stream_idx + 1],
            normed_grads[stream_idx],
        )
        stream_grads.append(stream_grad)
        gain_grads.append(gain_grad)
    resid_grad, skip_scaling_derivative = rms_back(
        stream_rows[3], inverses[3], gains_all[4], resid_normed_grad
    )
    stream_grads.append(resid_grad + grad_rows)
    gain_grads.append(skip_scaling_derivative)
    stream_grads_all = jnp.stack(stream_grads).reshape(STREAM_COUNT, micro_count, quarter, features)
    full_grads = lax.all_gather(
        stream_grads_all.astype(jnp.bfloat16), "hist", axis=2, tiled=True
    ).astype(stream_grads_all.dtype)
    slot_grads = []
    dyn_grad = jnp.zeros((micro_count, sequence_length, STREAM_COUNT, slot_count), jnp.float32)
    for depth_position_number in range(local_slots):
        rows_now = history[depth_position_number].astype(jnp.float32)
        slot_grads.append(
            jnp.sum(
                depth_combination_factors[depth_position_number][..., None] * full_grads, axis=0
            )
        )
        inner_now = jnp.sum(full_grads * rows_now[None], axis=-1)
        dyn_grad = dyn_grad + jnp.einsum("cmt,j->mtcj", inner_now, own_table[depth_position_number])
    dyn_grad = dyn_grad.reshape(micro_count * sequence_length, STREAM_COUNT * slot_count)
    act_part = precise(dyn_grad, mixer_output_wide.T)
    mix_out_grad = precise(kept_mix[4].T, dyn_grad)
    act_grad = lax.psum(act_part.astype(jnp.bfloat16), "hist").astype(jnp.float32)
    on_root = (hist_place == root).astype(jnp.float32)
    latest_grad, gain_zero, mix_in_grad = mix_backward(kept_mix, act_grad, gains_all[0], mix_in_all)
    gain_zero = gain_zero * on_root
    mix_in_grad = mix_in_grad * on_root
    latest_grad = latest_grad.reshape(micro_count, sequence_length, features)
    marked = []
    for depth_position_number in range(local_slots):
        is_latest = (hist_place * local_slots + depth_position_number == newest_output).astype(
            jnp.float32
        )
        marked.append(slot_grads[depth_position_number] + latest_grad * is_latest)
    history_grad = jnp.stack(marked).astype(jnp.bfloat16)
    gains_grad_full = jnp.stack(
        [gain_zero, gain_grads[0], gain_grads[1], gain_grads[2], gain_grads[3]]
    )
    share_rows = w_out.shape[0]
    per_device = mix_width // dp_count
    mix_out_padded = jnp.pad(
        mix_out_grad.reshape(dp_count, per_device, mix_width),
        ((0, 0), (0, share_rows - per_device), (0, 0)),
    ).reshape(dp_count * share_rows, mix_width)
    small_wide = jnp.concatenate([mix_in_grad, gains_grad_full.T, mix_out_padded], axis=1)
    attn_lefts = (normed[0], normed[1], normed[2], attended_low)
    attn_rights = (projection_grads[0], projection_grads[1], projection_grads[2], grad_low)
    attn_share = lax.psum_scatter(
        jnp.concatenate(
            [
                lax.dot_general(
                    left_side, right_side, contract_rows, preferred_element_type=jnp.float32
                )
                for left_side, right_side in zip(attn_lefts, attn_rights)
            ],
            axis=1,
        ).astype(jnp.bfloat16),
        "dp",
        scatter_dimension=0,
        tiled=True,
    )
    up_term = lax.dot_general(normed[3], up_grad, contract_rows, preferred_element_type=jnp.float32)
    down_term = lax.dot_general(
        hidden, grad_low, contract_rows, preferred_element_type=jnp.float32
    ).reshape(share_rows * lax.axis_size("dp"), ratio * features)
    ffn_share = lax.psum_scatter(
        jnp.concatenate([up_term, down_term, small_wide], axis=1).astype(jnp.bfloat16),
        "dp",
        scatter_dimension=0,
        tiled=True,
    )
    attn_total, ffn_total = (
        lax.psum(attn_share, "hist").astype(jnp.float32),
        lax.psum(ffn_share, "hist").astype(jnp.float32),
    )
    ff_width = ratio * features
    w_attn_grad = jnp.stack(
        [
            attn_total[:, 0:features],
            attn_total[:, features : 2 * features],
            attn_total[:, 2 * features : 3 * features],
        ]
    )
    w_out_grad = attn_total[:, 3 * features : 4 * features]
    w_up_grad = ffn_total[:, 0:ff_width]
    w_down_grad = ffn_total[:, ff_width : 2 * ff_width].reshape(share_rows * ratio, features)
    mix_in_share = ffn_total[:, 2 * ff_width : 2 * ff_width + mix_width]
    gains_share = ffn_total[:, 2 * ff_width + mix_width : 2 * ff_width + mix_width + 5].T
    mix_out_share = ffn_total[0:per_device, 2 * ff_width + mix_width + 5 :]
    return (
        block_out,
        history_grad,
        gains_share,
        mix_in_share,
        mix_out_share,
        w_attn_grad,
        w_out_grad,
        w_up_grad,
        w_down_grad,
    )


DEVICE_MESH = pl.DeviceIdType.MESH
CORE, ACROSS_X, ACROSS_Y = 1, 2, 4


def partner(column, mask):
    moved = column
    for bit in (1, 2, 4):
        if mask & bit:
            on = lax.rem(lax.div(moved, bit), 2)
            moved = moved + bit - 2 * bit * on
    return moved


def greet(column, masks):
    barrier = pltpu.get_barrier_semaphore()
    for mask in masks:
        pl.semaphore_signal(
            barrier, inc=1, device_id={"dp": partner(column, mask)}, device_id_type=DEVICE_MESH
        )
    pl.semaphore_wait(barrier, len(masks))


def push(source, target, send_sem, recv_sem, place):
    copy = pltpu.make_async_remote_copy(
        src_ref=source,
        dst_ref=target,
        send_sem=send_sem,
        recv_sem=recv_sem,
        device_id={"dp": place},
        device_id_type=DEVICE_MESH,
    )
    copy.start()
    return copy


def z_place(plane):
    return {"hist": plane}


class PlaneGatherSteps:

    def __init__(self, column, own, whole, send_sem, recv_sem, local_sem):
        self.column, self.own, self.whole = column, own, whole
        self.send_sem, self.recv_sem, self.local_sem = send_sem, recv_sem, local_sem
        self.rows = own.shape[0]
        self.half = self.rows // 2
        self.across = partner(column, ACROSS_X)
        self.along = partner(column, ACROSS_Y)
        self.beside = partner(column, CORE)
        self.corner = partner(column, ACROSS_X + ACROSS_Y)
        self.copies = []

    def place(self, owner, part):
        start = owner * self.rows + (self.half if part == 1 else 0)
        count = self.rows if part is None else self.half
        return self.whole.at[pl.ds(pl.multiple_of(start, 16), count)]

    def mine(self, part):
        start = self.half if part == 1 else 0
        return self.own.at[pl.ds(start, self.rows if part is None else self.half)]

    def send(self, source, owner, part, to):
        index = len(self.copies)
        copy = push(
            source, self.place(owner, part), self.send_sem.at[index], self.recv_sem.at[index], to
        )
        self.copies.append(copy)

    def begin(self):
        me = self.column
        self.local = pltpu.make_async_copy(self.mine(None), self.place(me, None), self.local_sem)
        self.local.start()
        self.send(self.mine(1), me, 1, self.across)
        self.send(self.mine(0), me, 0, self.along)
        self.send(self.mine(0), me, 0, self.across)
        self.send(self.mine(1), me, 1, self.along)
        self.send(self.mine(None), me, None, self.beside)

    def corners(self):
        self.copies[1].wait_recv()
        self.send(self.place(self.along, 0), self.along, 0, self.across)
        self.copies[0].wait_recv()
        self.send(self.place(self.across, 1), self.across, 1, self.along)

    def siblings(self):
        self.copies[2].wait_recv()
        self.send(self.place(self.across, None), self.across, None, self.beside)
        self.copies[3].wait_recv()
        self.send(self.place(self.along, None), self.along, None, self.beside)

    def rest(self):
        self.copies[5].wait_recv()
        self.send(self.place(self.corner, 0), self.corner, 0, self.beside)
        self.copies[6].wait_recv()
        self.send(self.place(self.corner, 1), self.corner, 1, self.beside)

    def finish(self):
        for index in (4, 7, 8, 9, 10):
            self.copies[index].wait_recv()
        for copy in self.copies:
            copy.wait_send()
        self.local.wait()


class PlaneScatterSteps:
    def __init__(self, column, product, refs, send_sem, recv_sem):
        self.column, self.product = column, product
        self.out_buf, self.side, self.chip, self.from_x, self.from_y, self.last = refs
        self.send_sem, self.recv_sem = send_sem, recv_sem
        rows = self.chip.shape[1]
        self.first, self.second = pl.ds(0, rows // 2), pl.ds(rows // 2, rows // 2)
        self.across = partner(column, ACROSS_X)
        self.along = partner(column, ACROSS_Y)
        self.beside = partner(column, CORE)
        self.pair, self.sends = [], []

    def block(self, i):
        mask = (6, 2, 4, 0)[i]
        self.product(partner(self.column, mask + CORE), self.out_buf.at[i])
        self.pair.append(
            push(
                self.out_buf.at[i],
                self.side.at[i],
                self.send_sem.at[i],
                self.recv_sem.at[i],
                self.beside,
            )
        )
        self.product(partner(self.column, mask), self.chip.at[i])
        self.pair[i].wait_recv()
        add_into(self.chip.at[i], self.side.at[i])
        if i == 0:
            self.send(self.chip.at[0, self.first], self.from_x.at[0], self.across)
            self.send(self.chip.at[0, self.second], self.from_y.at[0], self.along)
        if i == 1:
            self.send(self.chip.at[1, self.first], self.from_x.at[1], self.across)
        if i == 2:
            self.send(self.chip.at[2, self.second], self.from_y.at[1], self.along)

    def send(self, source, target, to):
        index = 4 + len(self.sends)
        self.sends.append(
            push(source, target, self.send_sem.at[index], self.recv_sem.at[index], to)
        )

    def turn(self):
        self.sends[0].wait_recv()
        add_into(self.chip.at[2, self.first], self.from_x.at[0])
        self.send(self.chip.at[2, self.first], self.last.at[0], self.along)
        self.sends[1].wait_recv()
        add_into(self.chip.at[1, self.second], self.from_y.at[0])
        self.send(self.chip.at[1, self.second], self.last.at[1], self.across)

    def finish(self, out_ref):
        self.sends[2].wait_recv()
        add_into(self.chip.at[3, self.first], self.from_x.at[1])
        self.sends[3].wait_recv()
        add_into(self.chip.at[3, self.second], self.from_y.at[1])
        self.sends[4].wait_recv()
        add_into(self.chip.at[3, self.first], self.last.at[0])
        self.sends[5].wait_recv()
        add_into(self.chip.at[3, self.second], self.last.at[1])
        out_ref[...] = self.chip[3]
        for copy in self.pair + self.sends:
            copy.wait_send()


def add_into(target, other):
    rows = target.shape[0]
    step = 32 if rows % 32 == 0 else 16

    def some_rows(r, carry):
        piece = pl.ds(pl.multiple_of(r * step, step), step)
        target[piece, :] = (
            target[piece, :].astype(jnp.float32) + other[piece, :].astype(jnp.float32)
        ).astype(jnp.bfloat16)
        return carry

    lax.fori_loop(0, rows // step, some_rows, 0)


class LineSums:

    def __init__(self, plane, parts, arrived, own, last, held, send_sem, recv_sem, load_sem):
        self.plane, self.parts, self.arrived = plane, parts, arrived
        self.own, self.last, self.held = own, last, held
        self.send_sem, self.recv_sem, self.load_sem = send_sem, recv_sem, load_sem
        self.rows = own.shape[0]

    def part(self, way, item, b):
        place = b if way == 0 else 3 - b
        return self.parts.at[pl.ds((item * 4 + place) * self.rows, self.rows)]

    def message(self, way, turn, a, source):
        to = a + 1 if way == 0 else 2 - a
        return pltpu.make_async_remote_copy(
            src_ref=source,
            dst_ref=self.arrived.at[way * 12 + turn],
            send_sem=self.send_sem.at[way * 12 + turn],
            recv_sem=self.recv_sem.at[way * 12 + turn],
            device_id=z_place(to),
            device_id_type=DEVICE_MESH,
        )

    def origin(self, way, turn):
        item, t = divmod(turn, 3)
        return self.message(way, turn, 0, self.part(way, item, 3 - t))

    def slot(self, way, a, turn):
        item, t = divmod(turn, 3)
        return way * 2 + (item * (3 - a) + t) % 2

    def relay(self, way, turn, a):
        return self.message(way, turn, a, self.held.at[self.slot(way, a, turn)])

    def start(self):
        for place in (0, 3):

            @pl.when(self.plane == place)
            def _():
                way = 0 if place == 0 else 1
                self.origin(way, 0).start()
                self.origin(way, 1).start()

    def load(self, source, target, index):
        return pltpu.make_async_copy(source, target, self.load_sem.at[index])

    def service(self, sigma):
        for place in range(4):

            @pl.when(self.plane == place)
            def _():
                for way in (0, 1):
                    a = place if way == 0 else 3 - place
                    if a == 0:
                        if sigma < 12:
                            self.origin(way, sigma).wait_send()
                        if sigma + 2 < 12:
                            self.origin(way, sigma + 2).start()
                        continue
                    turn = sigma - a + 1
                    if turn < 0 or turn >= 12:
                        continue
                    item, t = divmod(turn, 3)
                    b = 3 - t
                    if b < a:
                        continue
                    if b > a:
                        slot = self.slot(way, a, turn)
                        sent = [
                            earlier
                            for earlier in range(turn)
                            if 3 - earlier % 3 > a and self.slot(way, a, earlier) == slot
                        ]
                        if sent:
                            self.relay(way, sent[-1], a).wait_send()
                        target = self.held.at[slot]
                        mine = self.load(self.part(way, item, b), self.own, 0)
                        mine.start()
                        self.relay(way, turn, a).wait_recv()
                        came = self.load(self.arrived.at[way * 12 + turn], target, 1)
                        came.start()
                        mine.wait()
                        came.wait()
                        add_into(target, self.own)
                        self.relay(way, turn, a).start()
                    else:
                        self.message(way, turn, a - 1, self.own).wait_recv()
                        came = self.load(self.arrived.at[way * 12 + turn], self.last.at[way], 1)
                        came.start()
                        came.wait()
                if sigma % 3 == 2:
                    item = sigma // 3
                    mine = self.load(self.part(0, item, place), self.own, 0)
                    mine.start()
                    mine.wait()

    def drain(self):
        for place in range(4):

            @pl.when(self.plane == place)
            def _():
                for way in (0, 1):
                    a = place if way == 0 else 3 - place
                    if a == 0 or a == 3:
                        continue
                    for slot in (way * 2, way * 2 + 1):
                        sent = [
                            turn
                            for turn in range(12)
                            if 3 - turn % 3 > a and self.slot(way, a, turn) == slot
                        ]
                        self.relay(way, sent[-1], a).wait_send()


def forward_kernel(
    part_ref,
    grad_ref,
    w_up_ref,
    w_attn_ref,
    w_down_ref,
    gain_ref,
    x_ref,
    normed_ref,
    grad_all_ref,
    hidden_ref,
    up_term_ref,
    down_term_ref,
    back_ref,
    attn_columns_ref,
    arrived_ref,
    normed3,
    grads,
    up_columns,
    up_grad,
    out_buf,
    side,
    chip,
    from_x,
    from_y,
    last,
    own,
    ends,
    held,
    x_buf,
    normed_buf,
    term_buf,
    gather_send,
    gather_recv,
    gather_local,
    scatter_send,
    scatter_recv,
    line_send,
    line_recv,
    line_load,
    swap_send,
    swap_recv,
    swap_local,
    out_sem,
):
    column = lax.axis_index("dp")
    plane = lax.axis_index("hist")
    rows, features = grad_ref.shape
    total = 8 * rows
    share = w_up_ref.shape[0]
    ff_share = w_down_ref.shape[0]
    tile = 256

    barrier = pltpu.get_barrier_semaphore()
    for mask in range(1, 8):
        pl.semaphore_signal(
            barrier, inc=1, device_id={"dp": partner(column, mask)}, device_id_type=DEVICE_MESH
        )
    for place in range(4):

        @pl.when(plane == place)
        def _():
            nearby = [p for p in (place - 1, place + 1) if 0 <= p < 4]
            for p in nearby:
                pl.semaphore_signal(
                    barrier, inc=1, device_id=z_place(p), device_id_type=DEVICE_MESH
                )
            pl.semaphore_wait(barrier, 7 + len(nearby))

    line = LineSums(
        plane, part_ref, arrived_ref, own, ends, held, line_send, line_recv, line_load
    )
    line.start()
    zeros = jnp.zeros((16, features), jnp.bfloat16)

    def clear(r, carry):
        ends[0, pl.ds(pl.multiple_of(r * 16, 16), 16), :] = zeros
        ends[1, pl.ds(pl.multiple_of(r * 16, 16), 16), :] = zeros
        return carry

    lax.fori_loop(0, rows // 16, clear, 0)

    my_rows = pl.ds(pl.multiple_of(column * share, 16), share)

    def up_piece(owner):
        return w_up_ref.at[:, pl.ds(pl.multiple_of(owner * ff_share, 128), ff_share)]

    up_local = pltpu.make_async_copy(up_piece(column), up_columns.at[my_rows], swap_local.at[0])
    up_local.start()
    up_swaps = [
        push(
            up_piece(partner(column, mask)),
            up_columns.at[my_rows],
            swap_send.at[mask],
            swap_recv.at[mask],
            partner(column, mask),
        )
        for mask in (6, 7, 2, 3, 4, 5, 1)
    ]

    def gather(index, own_rows, whole):
        return PlaneGatherSteps(
            column,
            own_rows,
            whole,
            gather_send.at[index],
            gather_recv.at[index],
            gather_local.at[index],
        )

    grad_gather = gather(4, grad_ref, grads)
    grad_gather.begin()

    x_copies = []

    def combine(item):
        if item >= 2:
            x_copies[item - 2].wait()
        x_now = x_buf.at[item % 2]

        def some_rows(r, carry):
            piece = pl.ds(pl.multiple_of(r * 16, 16), 16)
            x = (
                own[piece, :].astype(jnp.float32)
                + ends[0, piece, :].astype(jnp.float32)
                + ends[1, piece, :].astype(jnp.float32)
            )
            x_now[piece, :] = x
            inverse = lax.rsqrt(jnp.mean(x * x, axis=-1, keepdims=True) + epsilon)
            normed_buf[item, piece, :] = (x * inverse * gain_ref[pl.ds(item, 1), :]).astype(
                jnp.bfloat16
            )
            return carry

        lax.fori_loop(0, rows // 16, some_rows, 0)
        copy = pltpu.make_async_copy(x_now, x_ref.at[item], out_sem.at[item % 2])
        copy.start()
        x_copies.append(copy)
        steps = gather(
            item, normed_buf.at[item], normed3 if item == 0 else normed_ref.at[item - 1]
        )
        steps.begin()
        return steps

    line.service(0)
    grad_gather.corners()
    line.service(1)
    grad_gather.siblings()
    line.service(2)
    gather3 = combine(0)
    grad_gather.rest()
    gather3.corners()
    line.service(3)
    grad_gather.finish()
    grads_out = pltpu.make_async_copy(grads, grad_all_ref, out_sem.at[2])
    grads_out.start()
    gather3.siblings()
    gather3.rest()
    line.service(4)
    for copy in up_swaps:
        copy.wait_recv()
    up_local.wait()
    gather3.finish()

    def attn_piece(stream, owner):
        return w_attn_ref.at[stream, :, pl.ds(pl.multiple_of(owner * share, 128), share)]

    def attn_place(stream):
        return attn_columns_ref.at[stream, my_rows]

    attn_swaps, attn_locals = [], []
    for stream in range(3):
        local = pltpu.make_async_copy(
            attn_piece(stream, column), attn_place(stream), swap_local.at[1 + stream]
        )
        local.start()
        attn_locals.append(local)
        for mask in (6, 7, 2, 3, 4, 5, 1):
            attn_swaps.append(
                push(
                    attn_piece(stream, partner(column, mask)),
                    attn_place(stream),
                    swap_send.at[8 * (stream + 1) + mask],
                    swap_recv.at[8 * (stream + 1) + mask],
                    partner(column, mask),
                )
            )

    def feed(first_block, count):
        def one_tile(step, carry):
            piece = pl.ds(pl.multiple_of((step // (ff_share // tile)) * rows, 16), rows)
            lanes = pl.ds(pl.multiple_of((step % (ff_share // tile)) * tile, tile), tile)
            up = jnp.dot(normed3[piece, :], up_columns[:, lanes], preferred_element_type=jnp.float32)
            spread = 0.5 * (1.0 + lax.erf(up * (1.0 / math.sqrt(2.0))))
            hidden_ref[piece, lanes] = (up * spread).astype(jnp.bfloat16)
            slope = spread + up * jnp.exp(-0.5 * up * up) * (1.0 / math.sqrt(2.0 * math.pi))
            hidden_grad = lax.dot_general(
                grads[piece, :],
                w_down_ref[lanes, :],
                contract_cols,
                preferred_element_type=jnp.float32,
            )
            up_grad[piece, lanes] = (hidden_grad * slope).astype(jnp.bfloat16)
            return carry

        per_block = ff_share // tile
        lax.fori_loop(first_block * per_block, (first_block + count) * per_block, one_tile, 0)

    feed(0, 1)
    line.service(5)
    gather0 = combine(1)
    feed(1, 3)
    gather0.corners()
    line.service(6)
    feed(4, 2)
    gather0.siblings()
    gather0.rest()
    line.service(7)
    feed(6, 2)

    def back_product(owner, target):
        left_rows = pl.ds(pl.multiple_of(owner * rows, 16), rows)

        def one_tile(t, carry):
            lanes = pl.ds(pl.multiple_of(t * 2 * tile, 2 * tile), 2 * tile)
            target[:, lanes] = lax.dot_general(
                up_grad[left_rows, :],
                up_columns[lanes, :],
                contract_cols,
                preferred_element_type=jnp.float32,
            ).astype(jnp.bfloat16)
            return carry

        lax.fori_loop(0, features // (2 * tile), one_tile, 0)

    scatter = PlaneScatterSteps(
        column,
        back_product,
        (out_buf, side, chip, from_x, from_y, last),
        scatter_send,
        scatter_recv,
    )
    scatter.block(0)
    line.service(8)
    gather1 = combine(2)
    gather0.finish()
    scatter.block(1)
    scatter.block(2)
    scatter.block(3)
    scatter.turn()
    gather1.corners()
    line.service(9)
    scatter.finish(back_ref)

    term_slots = 2
    part = share // 4

    def term_copies(kind, slot, index):
        if kind == 0:
            return [
                pltpu.make_async_copy(
                    term_buf.at[slot, pl.ds(h * part, part), pl.ds(0, ff_share)],
                    up_term_ref.at[
                        pl.ds(h * 4 * part + index % 4 * part, part),
                        pl.ds(index // 4 * ff_share, ff_share),
                    ],
                    out_sem.at[3 + 4 * slot + h],
                )
                for h in range(4)
            ]
        return [
            pltpu.make_async_copy(
                term_buf.at[slot], down_term_ref.at[pl.ds(index * tile, tile)], out_sem.at[3 + 4 * slot]
            )
        ]

    def terms(kind, first, count):
        width = ff_share if kind == 0 else features
        pending = []
        for index in range(first, first + count):
            slot = index % term_slots
            if len(pending) >= term_slots:
                for copy in pending[-term_slots]:
                    copy.wait()

            def one_tile(t, carry):
                lanes = pl.ds(pl.multiple_of(t * 2 * tile, 2 * tile), 2 * tile)
                if kind == 0:
                    left, right = normed3[:, index * tile : (index + 1) * tile], up_grad[:, lanes]
                else:
                    left, right = hidden_ref[:, index * tile : (index + 1) * tile], grads[:, lanes]
                term_buf[slot, :, lanes] = lax.dot_general(
                    left, right, contract_rows, preferred_element_type=jnp.float32
                ).astype(jnp.bfloat16)
                return carry

            lax.fori_loop(0, width // (2 * tile), one_tile, 0)
            copies = term_copies(kind, slot, index)
            for copy in copies:
                copy.start()
            pending.append(copies)
        for copies in pending[-term_slots:]:
            for copy in copies:
                copy.wait()

    terms(1, 0, 2)
    gather1.siblings()
    gather1.rest()
    terms(1, 2, ff_share // tile - 2)
    line.service(10)
    terms(0, 0, 4)
    gather1.finish()
    line.service(11)
    gather2 = combine(3)
    terms(0, 4, features // tile - 4)
    gather2.corners()
    gather2.siblings()
    gather2.rest()
    line.drain()
    for copy in attn_swaps:
        copy.wait_recv()
    for copy in attn_locals:
        copy.wait()
    for copy in up_swaps + attn_swaps:
        copy.wait_send()
    grads_out.wait()
    for copy in x_copies[-2:]:
        copy.wait()
    gather2.finish()


def forward_and_feed(parts, grad_low, w_up, w_attn, w_down, gains):
    rows, features = grad_low.shape
    total = 8 * rows
    share = w_up.shape[0]
    ff_share = w_down.shape[0]
    block = (rows, features)
    half = (2, rows // 2, features)
    anywhere = pl.BlockSpec(memory_space=pl.ANY)
    near = pl.BlockSpec(memory_space=pltpu.VMEM)
    shape = jax.ShapeDtypeStruct
    low_type = jnp.bfloat16
    return pl.pallas_call(
        forward_kernel,
        in_specs=[anywhere, near, anywhere, anywhere, near, near],
        out_specs=[anywhere, anywhere, anywhere, near, anywhere, anywhere, near]
        + [anywhere, anywhere],
        out_shape=[
            shape((4,) + block, jnp.float32),
            shape((3, total, features), low_type),
            shape((total, features), low_type),
            shape((total, ff_share), low_type),
            shape((features * ff_share // features, features), low_type),
            shape((ff_share, features), low_type),
            shape(block, low_type),
            shape((3, features, share), low_type),
            shape((24,) + block, low_type),
        ],
        scratch_shapes=[
            pltpu.VMEM((total, features), low_type),
            pltpu.VMEM((total, features), low_type),
            pltpu.VMEM((features, ff_share), low_type),
            pltpu.VMEM((total, ff_share), low_type),
            pltpu.VMEM((4,) + block, low_type),
            pltpu.VMEM((4,) + block, low_type),
            pltpu.VMEM((4,) + block, low_type),
            pltpu.VMEM(half, low_type),
            pltpu.VMEM(half, low_type),
            pltpu.VMEM(half, low_type),
            pltpu.VMEM(block, low_type),
            pltpu.VMEM((2,) + block, low_type),
            pltpu.VMEM((4,) + block, low_type),
            pltpu.VMEM((2,) + block, jnp.float32),
            pltpu.VMEM((4,) + block, low_type),
            pltpu.VMEM((2, 256, features), low_type),
            pltpu.SemaphoreType.DMA((5, 11)),
            pltpu.SemaphoreType.DMA((5, 11)),
            pltpu.SemaphoreType.DMA((5,)),
            pltpu.SemaphoreType.DMA((10,)),
            pltpu.SemaphoreType.DMA((10,)),
            pltpu.SemaphoreType.DMA((24,)),
            pltpu.SemaphoreType.DMA((24,)),
            pltpu.SemaphoreType.DMA((2,)),
            pltpu.SemaphoreType.DMA((32,)),
            pltpu.SemaphoreType.DMA((32,)),
            pltpu.SemaphoreType.DMA((4,)),
            pltpu.SemaphoreType.DMA((11,)),
        ],
        compiler_params=pltpu.CompilerParams(
            collective_id=5, has_side_effects=True, vmem_limit_bytes=62 * 1024 * 1024
        ),
        cost_estimate=pl.CostEstimate(
            flops=12 * total * features * ff_share,
            bytes_accessed=400 * 1000 * 1000,
            transcendentals=0,
        ),
    )(parts, grad_low, w_up, w_attn, w_down, gains)


class LineSum:

    def __init__(self, plane, parts, arrived, own, last, held, send_sem, recv_sem, load_sem):
        self.plane, self.parts, self.arrived = plane, parts, arrived
        self.own, self.last, self.held = own, last, held
        self.send_sem, self.recv_sem, self.load_sem = send_sem, recv_sem, load_sem
        self.rows = own.shape[0]

    def part(self, way, b):
        place = b if way == 0 else 3 - b
        return self.parts.at[pl.ds(place * self.rows, self.rows)]

    def message(self, way, t, a, source):
        return pltpu.make_async_remote_copy(
            src_ref=source,
            dst_ref=self.arrived.at[way * 3 + t],
            send_sem=self.send_sem.at[way * 3 + t],
            recv_sem=self.recv_sem.at[way * 3 + t],
            device_id=z_place(a + 1 if way == 0 else 2 - a),
            device_id_type=DEVICE_MESH,
        )

    def origin(self, way, t):
        return self.message(way, t, 0, self.part(way, 3 - t))

    def relay(self, way, t, a):
        return self.message(way, t, a, self.held.at[t if a == 1 else 2])

    def start(self):
        for place in (0, 3):

            @pl.when(self.plane == place)
            def _():
                way = 0 if place == 0 else 1
                self.origin(way, 0).start()
                self.origin(way, 1).start()

    def load(self, source, target, index):
        copy = pltpu.make_async_copy(source, target, self.load_sem.at[index])
        copy.start()
        return copy

    def service(self, sigma):
        for place in range(4):

            @pl.when(self.plane == place)
            def _():
                for way in (0, 1):
                    a = place if way == 0 else 3 - place
                    if a == 0:
                        self.origin(way, sigma).wait_send()
                        if sigma == 0:
                            self.origin(way, 2).start()
                        continue
                    t = sigma - a + 1
                    if t < 0 or 3 - t < a:
                        continue
                    b = 3 - t
                    source = self.arrived.at[way * 3 + t]
                    if b > a:
                        relay = self.relay(way, t, a)
                        target = self.held.at[t if a == 1 else 2]
                        mine = self.load(self.part(way, b), self.own, 0)
                        relay.wait_recv()
                        came = self.load(source, target, 1)
                        mine.wait()
                        came.wait()
                        add_into(target, self.own)
                        relay.start()
                    else:
                        self.message(way, t, a - 1, self.own).wait_recv()
                        self.load(source, self.last.at[way], 1).wait()
                if sigma == 2:
                    self.load(self.part(0, place), self.own, 0).wait()

    def finish(self, target):
        step = 16

        def some_rows(r, carry):
            piece = pl.ds(pl.multiple_of(r * step, step), step)
            total = self.own[piece, :].astype(jnp.float32)
            total = total + self.last[0, piece, :].astype(jnp.float32)
            total = total + self.last[1, piece, :].astype(jnp.float32)
            target[piece, :] = total.astype(jnp.bfloat16)
            return carry

        lax.fori_loop(0, self.rows // step, some_rows, 0)
        for place in (1, 2):

            @pl.when(self.plane == place)
            def _():
                for way in (0, 1):
                    a = place if way == 0 else 3 - place
                    for t in range(3 - a):
                        self.relay(way, t, a).wait_send()


class LineGather:

    def __init__(self, plane, own, slot, send_sem, recv_sem, local_sem):
        self.plane, self.own, self.slot = plane, own, slot
        self.send_sem, self.recv_sem, self.local_sem = send_sem, recv_sem, local_sem

    def message(self, way, a, distance):
        origin = a - distance
        plane_of_origin = origin if way == 0 else 3 - origin
        target = self.slot(plane_of_origin)
        return pltpu.make_async_remote_copy(
            src_ref=self.own if distance == 0 else target,
            dst_ref=target,
            send_sem=self.send_sem.at[way * 3 + distance],
            recv_sem=self.recv_sem.at[way * 3 + distance],
            device_id=z_place(a + 1 if way == 0 else 2 - a),
            device_id_type=DEVICE_MESH,
        )

    def service(self, step):
        for place in range(4):

            @pl.when(self.plane == place)
            def _():
                if step == 0:
                    pltpu.make_async_copy(self.own, self.slot(place), self.local_sem).start()
                for way in (0, 1):
                    a = place if way == 0 else 3 - place
                    if step > a:
                        continue
                    if step > 0:
                        self.message(way, a - 1, step - 1).wait_recv()
                    if a < 3:
                        self.message(way, a, step).start()

    def finish(self):
        for place in range(4):

            @pl.when(self.plane == place)
            def _():
                pltpu.make_async_copy(self.own, self.slot(place), self.local_sem).wait()
                for way in (0, 1):
                    a = place if way == 0 else 3 - place
                    if a < 3:
                        for distance in range(a + 1):
                            self.message(way, a, distance).wait_send()


def attend_column(
    column,
    plane,
    length_ref,
    cosine,
    sine_part,
    q_ref,
    k_ref,
    v_ref,
    kv_before_ref,
    out_grad_ref,
    att_ref,
    q_grad_ref,
    kv_grad_ref,
    kv_before_grad_ref,
    rows,
    micro_count,
    sequence_length,
):
    here = pl.ds(pl.multiple_of(column * rows, 16), rows)
    width = q_ref.shape[1]
    scale = 1.0 / math.sqrt(HEAD_DIM)
    row = plane * rows + lax.broadcasted_iota(jnp.int32, (rows, 1), 0)
    start = jnp.zeros((rows, 1), jnp.int32)
    limit = jnp.zeros((rows, 1), jnp.int32)
    for m in range(micro_count):
        inside = (row >= m * sequence_length) & (row < (m + 1) * sequence_length)
        start = jnp.where(inside, m * sequence_length, start)
        limit = jnp.where(inside, m * sequence_length + length_ref[column * micro_count + m], limit)
    limit = jnp.minimum(limit, row + 1)
    key_row = (plane - 1) * rows + lax.broadcasted_iota(jnp.int32, (1, 2 * rows), 1)
    allowed = (key_row >= start) & (key_row < limit)
    for head in range(width // HEAD_DIM):
        lanes = slice(head * HEAD_DIM, (head + 1) * HEAD_DIM)
        value_lanes = slice(width + head * HEAD_DIM, width + (head + 1) * HEAD_DIM)
        query = q_ref[here, lanes]
        keys = jnp.concatenate([kv_before_ref[here, lanes], k_ref[here, lanes]], axis=0)
        values = jnp.concatenate([kv_before_ref[here, value_lanes], v_ref[here, lanes]], axis=0)
        out_grad = out_grad_ref[here, lanes]
        scores = (
            lax.dot_general(query, keys, contract_cols, preferred_element_type=jnp.float32) * scale
        )
        scores = jnp.where(allowed, scores, masked_out)
        raised = jnp.exp(scores - jnp.max(scores, axis=-1, keepdims=True))
        weights = raised / jnp.sum(raised, axis=-1, keepdims=True)
        weights_low = weights.astype(jnp.bfloat16)
        att_ref[here, lanes] = matmul(weights_low, values).astype(jnp.bfloat16)
        weight_grad = lax.dot_general(
            out_grad, values, contract_cols, preferred_element_type=jnp.float32
        )
        inner = jnp.sum(weights * weight_grad, axis=-1, keepdims=True)
        score_grad = (weights * (weight_grad - inner) * scale).astype(jnp.bfloat16)
        query_grad = matmul(score_grad, keys)
        swapped = jnp.concatenate(
            [query_grad[:, HEAD_DIM // 2 :], query_grad[:, : HEAD_DIM // 2]], axis=1
        )
        q_grad_ref[here, lanes] = (query_grad * cosine - swapped * sine_part).astype(jnp.bfloat16)
        key_grad = lax.dot_general(
            score_grad, query, contract_rows, preferred_element_type=jnp.float32
        )
        value_grad = lax.dot_general(
            weights_low, out_grad, contract_rows, preferred_element_type=jnp.float32
        )
        kv_before_grad_ref[here, lanes] = key_grad[:rows].astype(jnp.bfloat16)
        kv_before_grad_ref[here, value_lanes] = value_grad[:rows].astype(jnp.bfloat16)
        kv_grad_ref[here, lanes] = key_grad[rows:]
        kv_grad_ref[here, value_lanes] = value_grad[rows:]


def backward_kernel(
    length_ref,
    cos_ref,
    sin_ref,
    q_ref,
    k_ref,
    v_ref,
    out_grad_ref,
    normed_ref,
    grad_all_ref,
    hidden_ref,
    w_out_ref,
    w_down_ref,
    attn_columns_ref,
    x_ref,
    gain_ref,
    grad_ref,
    back3_ref,
    down_term_ref,
    up_term_ref,
    full_ref,
    down_all_ref,
    up_all_ref,
    quarter_ref,
    branch_ref,
    gain_grad_ref,
    attn_parts_ref,
    arrived_ref,
    big,
    att,
    q_grad,
    kv_grad,
    kv_before,
    kv_before_grad,
    kv_after,
    out_buf,
    side,
    chip,
    from_x,
    from_y,
    last,
    line_own,
    line_ends,
    line_held,
    down_own,
    up_sum,
    up_own,
    stream_own,
    back_buf,
    x_buf,
    stage,
    scatter_send,
    scatter_recv,
    sum_send,
    sum_recv,
    load_sem,
    spread_send,
    spread_recv,
    spread_local,
    key_send,
    key_recv,
    swap_send,
    swap_recv,
    local_sem,
    *,
    micro_count,
    sequence_length,
):
    column = lax.axis_index("dp")
    plane = lax.axis_index("hist")
    rows, features = grad_ref.shape
    total = 8 * rows
    width = q_ref.shape[1]
    ff_share = w_down_ref.shape[0]
    quarter = features // 8 // 4
    k_grad, v_grad, attn_sum = q_grad, att, up_sum
    tile = 512

    barrier = pltpu.get_barrier_semaphore()
    for mask in range(1, 8):
        pl.semaphore_signal(
            barrier, inc=1, device_id={"dp": partner(column, mask)}, device_id_type=DEVICE_MESH
        )
    for place in range(4):

        @pl.when(plane == place)
        def _():
            nearby = [p for p in (place - 1, place + 1) if 0 <= p < 4]
            for p in nearby:
                pl.semaphore_signal(
                    barrier, inc=1, device_id=z_place(p), device_id_type=DEVICE_MESH
                )
            pl.semaphore_wait(barrier, 7 + len(nearby))

    def key_copies(place):
        return [
            pltpu.make_async_remote_copy(
                src_ref=source,
                dst_ref=kv_before.at[:, pl.ds(i * width, width)],
                send_sem=key_send.at[i],
                recv_sem=key_recv.at[i],
                device_id=z_place(place + 1),
                device_id_type=DEVICE_MESH,
            )
            for i, source in enumerate((k_ref, v_ref))
        ]

    def back_copy(place):
        return pltpu.make_async_remote_copy(
            src_ref=kv_before_grad,
            dst_ref=kv_after,
            send_sem=key_send.at[2],
            recv_sem=key_recv.at[2],
            device_id=z_place(place - 1),
            device_id_type=DEVICE_MESH,
        )

    def clear(target):
        step = 64

        def some_rows(r, carry):
            target[pl.ds(pl.multiple_of(r * step, step), step), :] = jnp.zeros(
                (step, target.shape[1]), jnp.bfloat16
            )
            return carry

        lax.fori_loop(0, target.shape[0] // step, some_rows, 0)

    for place in range(3):

        @pl.when(plane == place)
        def _():
            for copy in key_copies(place):
                copy.start()

    line_sums = [
        LineSum(
            plane,
            parts,
            arrived_ref.at[pl.ds(6 * i, 6)],
            line_own,
            line_ends,
            line_held,
            sum_send.at[i],
            sum_recv.at[i],
            load_sem,
        )
        for i, parts in enumerate((down_term_ref, up_term_ref, attn_parts_ref))
    ]
    down_sum, up_line, attn_line = line_sums

    def spread(index, own, slot):
        return LineGather(
            plane, own, slot, spread_send.at[index], spread_recv.at[index], spread_local.at[index]
        )

    def stream_spread(item):
        return spread(
            item,
            stream_own.at[item],
            lambda p: full_ref.at[pl.ds((item * 4 + p) * rows, rows)],
        )

    def norm_back(item, back):
        load = pltpu.make_async_copy(x_ref.at[item], x_buf, local_sem.at[0])
        load.start()
        load.wait()
        gain = gain_ref[pl.ds(item, 1), :]

        def some_rows(r, gain_sum):
            piece = pl.ds(pl.multiple_of(r * 16, 16), 16)
            x = x_buf[piece, :]
            inverse = lax.rsqrt(jnp.mean(x * x, axis=-1, keepdims=True) + epsilon)
            grad = back[piece, :].astype(jnp.float32)
            scaled = grad * gain
            mean = jnp.mean(scaled * x, axis=-1, keepdims=True)
            result = inverse * scaled - x * (inverse * inverse * inverse) * mean
            if item == 0:
                result = result + grad_ref[piece, :].astype(jnp.float32)
            stream_own[item, piece, :] = result.astype(jnp.bfloat16)
            return gain_sum + jnp.sum(grad * x * inverse, axis=0, keepdims=True)

        gain_grad_ref[pl.ds(item, 1), :] = lax.fori_loop(
            0, rows // 16, some_rows, jnp.zeros((1, features), jnp.float32)
        )

    def scatter_of(product, index):
        return PlaneScatterSteps(
            column,
            product,
            (out_buf, side, chip)
            + tuple(arriving.at[pl.ds(2 * (index % 2), 2)] for arriving in (from_x, from_y, last)),
            scatter_send.at[index],
            scatter_recv.at[index],
        )

    def projection_product(stream, grad):
        def product(owner, target):
            left = pl.ds(pl.multiple_of(owner * rows, 16), rows)

            def one_tile(t, carry):
                lanes = pl.ds(pl.multiple_of(t * tile, tile), tile)
                target[:, lanes] = lax.dot_general(
                    grad[left, :],
                    attn_columns_ref[stream, lanes, :],
                    contract_cols,
                    preferred_element_type=jnp.float32,
                ).astype(jnp.bfloat16)
                return carry

            lax.fori_loop(0, features // tile, one_tile, 0)

        return product

    def branch_product(owner, target):
        left = pl.ds(pl.multiple_of(owner * rows, 16), rows)

        def one_tile(t, carry):
            lanes = pl.ds(pl.multiple_of(t * tile, tile), tile)
            target[:, lanes] = (
                matmul(att[left, :], w_out_ref[:, lanes])
                + matmul(hidden_ref[left, :], w_down_ref[:, lanes])
            ).astype(jnp.bfloat16)
            return carry

        lax.fori_loop(0, features // tile, one_tile, 0)

    def attend(first, count):
        def one_column(m, carry):
            attend_column(
                m,
                plane,
                length_ref,
                cos_ref[...],
                sin_ref[...],
                q_ref,
                k_ref,
                v_ref,
                kv_before,
                out_grad_ref,
                att,
                q_grad,
                kv_grad,
                kv_before_grad,
                rows,
                micro_count,
                sequence_length,
            )
            return carry

        lax.fori_loop(first, first + count, one_column, 0)

    def part_copies(first_row):
        return [
            pltpu.make_async_copy(
                stage.at[pl.ds(p * quarter, quarter)],
                attn_parts_ref.at[pl.ds(p * 4 * quarter + first_row, quarter)],
                local_sem.at[4 + p],
            )
            for p in range(4)
        ]

    def load_big(source):
        copy = pltpu.make_async_copy(source, big, local_sem.at[2])
        copy.start()
        return copy

    def attn_term(stream, grad):
        def one_owner(d, carry):
            lanes = pl.ds(pl.multiple_of(d * width, width), width)
            stage[:, lanes] = lax.dot_general(
                big[:, lanes], grad[...], contract_rows, preferred_element_type=jnp.float32
            ).astype(jnp.bfloat16)
            return carry

        lax.fori_loop(0, 8, one_owner, 0)
        copies = part_copies(stream * quarter)
        for copy in copies:
            copy.start()
        return copies

    def out_term():
        def one_tile(t, carry):
            lanes = pl.ds(pl.multiple_of(t * tile, tile), tile)
            stage[:, lanes] = lax.dot_general(
                att[...], big[:, lanes], contract_rows, preferred_element_type=jnp.float32
            ).astype(jnp.bfloat16)
            return carry

        lax.fori_loop(0, features // tile, one_tile, 0)
        copies = part_copies(3 * quarter)
        for copy in copies:
            copy.start()
        return copies

    def swap(kind):
        copies = []
        for mask in (6, 7, 2, 3, 4, 5, 1):
            owner = partner(column, mask)
            if kind == 0:
                source, target = up_piece(owner), up_target()
            else:
                source, target = attn_piece(owner), attn_target()
            copies.append(
                push(
                    source,
                    target,
                    swap_send.at[8 * kind + mask],
                    swap_recv.at[8 * kind + mask],
                    owner,
                )
            )
        if kind == 0:
            source, target = up_piece(column), up_target()
        else:
            source, target = attn_piece(column), attn_target()
        local = pltpu.make_async_copy(source, target, local_sem.at[3])
        local.start()
        return copies, local

    def up_piece(owner):
        return up_sum.at[
            pl.ds(pl.multiple_of(lax.rem(owner, 4) * quarter, 16), quarter),
            pl.ds(pl.multiple_of(lax.div(owner, 4) * ff_share, 128), ff_share),
        ]

    def up_target():
        return up_own.at[:, pl.ds(pl.multiple_of(column * ff_share, 128), ff_share)]

    def attn_piece(owner):
        return attn_sum.at[
            pl.ds(0, 3 * quarter), pl.ds(pl.multiple_of(owner * width, 128), width)
        ]

    def attn_target():
        return quarter_ref.at[
            pl.ds(0, 3 * quarter), pl.ds(pl.multiple_of(column * width, 128), width)
        ]

    def swapped_in(swapping):
        copies, local = swapping
        for copy in copies:
            copy.wait_recv()
        local.wait()
        for copy in copies:
            copy.wait_send()

    down_sum.start()
    norm_back(0, back3_ref)
    spread3 = stream_spread(0)
    spread3.service(0)

    @pl.when(plane == 0)
    def _():
        clear(kv_before)
        clear(line_ends.at[0])

    @pl.when(plane == 3)
    def _():
        clear(kv_after)
        clear(line_ends.at[1])

    down_sum.service(0)
    spread3.service(1)
    down_sum.service(1)
    for place in range(1, 4):

        @pl.when(plane == place)
        def _():
            for copy in key_copies(place - 1):
                copy.wait_recv()

    attend(0, 4)
    spread3.service(2)
    down_sum.service(2)
    up_line.start()
    down_sum.finish(down_own)
    down_spread = spread(4, down_own, lambda p: down_all_ref.at[pl.ds(p * 4 * quarter, 4 * quarter)])
    down_spread.service(0)
    attend(4, 4)
    for place in range(1, 4):

        @pl.when(plane == place)
        def _():
            back_copy(place).start()

    spread3.service(3)
    loading = load_big(normed_ref.at[0])
    query_scatter = scatter_of(projection_product(0, q_grad), 0)
    query_scatter.block(0)
    query_scatter.block(1)
    up_line.service(0)
    query_scatter.block(2)
    query_scatter.block(3)
    down_spread.service(1)
    query_scatter.turn()
    loading.wait()
    parts_out = attn_term(0, q_grad)
    query_scatter.finish(back_buf)
    up_line.service(1)
    norm_back(1, back_buf)
    query_spread = stream_spread(1)
    query_spread.service(0)
    down_spread.service(2)
    for copy in parts_out:
        copy.wait()
    loading = load_big(grad_all_ref)
    branch_scatter = scatter_of(branch_product, 1)
    branch_scatter.block(0)
    branch_scatter.block(1)
    up_line.service(2)
    up_line.finish(up_sum)
    up_swap = swap(0)
    branch_scatter.block(2)
    down_spread.service(3)
    branch_scatter.block(3)
    query_spread.service(1)
    branch_scatter.turn()
    loading.wait()
    parts_out = out_term()
    branch_scatter.finish(branch_ref)
    swapped_in(up_swap)
    up_spread = spread(5, up_own, lambda p: up_all_ref.at[pl.ds(p * quarter, quarter)])
    up_spread.service(0)
    for copy in parts_out:
        copy.wait()
    loading = load_big(normed_ref.at[1])

    for place in range(3):

        @pl.when(plane == place)
        def _():
            back_copy(place + 1).wait_recv()

    def key_value(m, carry):
        here = pl.ds(pl.multiple_of(m * rows, 16), rows)
        for head in range(width // HEAD_DIM):
            lanes = slice(head * HEAD_DIM, (head + 1) * HEAD_DIM)
            value_lanes = slice(width + head * HEAD_DIM, width + (head + 1) * HEAD_DIM)
            grad = kv_grad[here, lanes] + kv_after[here, lanes].astype(jnp.float32)
            turned_half = jnp.concatenate(
                [grad[:, HEAD_DIM // 2 :], grad[:, : HEAD_DIM // 2]], axis=1
            )
            k_grad[here, lanes] = (grad * cos_ref[...] - turned_half * sin_ref[...]).astype(
                jnp.bfloat16
            )
            v_grad[here, lanes] = (
                kv_grad[here, value_lanes] + kv_after[here, value_lanes].astype(jnp.float32)
            ).astype(jnp.bfloat16)
        return carry

    lax.fori_loop(0, 8, key_value, 0)
    query_spread.service(2)
    key_scatter = scatter_of(projection_product(1, k_grad), 2)
    key_scatter.block(0)
    key_scatter.block(1)
    key_scatter.block(2)
    key_scatter.block(3)
    up_spread.service(1)
    query_spread.service(3)
    key_scatter.turn()
    loading.wait()
    parts_out = attn_term(1, k_grad)
    key_scatter.finish(back_buf)
    norm_back(2, back_buf)
    key_spread = stream_spread(2)
    key_spread.service(0)
    for copy in parts_out:
        copy.wait()
    loading = load_big(normed_ref.at[2])
    up_spread.service(2)
    value_scatter = scatter_of(projection_product(2, v_grad), 3)
    value_scatter.block(0)
    value_scatter.block(1)
    loading.wait()
    parts_out = attn_term(2, v_grad)
    for copy in parts_out:
        copy.wait()
    attn_line.start()
    key_spread.service(1)
    value_scatter.block(2)
    value_scatter.block(3)
    up_spread.service(3)
    attn_line.service(0)
    value_scatter.turn()
    key_spread.service(2)
    value_scatter.finish(back_buf)
    norm_back(3, back_buf)
    value_spread = stream_spread(3)
    value_spread.service(0)
    attn_line.service(1)
    key_spread.service(3)
    value_spread.service(1)
    attn_line.service(2)
    attn_line.finish(attn_sum)
    attn_swap = swap(1)
    quarter_ref[pl.ds(3 * quarter, quarter), :] = attn_sum[pl.ds(3 * quarter, quarter), :]
    value_spread.service(2)
    swapped_in(attn_swap)
    value_spread.service(3)
    for spreading in (
        spread3,
        down_spread,
        query_spread,
        up_spread,
        key_spread,
        value_spread,
    ):
        spreading.finish()
    for place in range(3):

        @pl.when(plane == place)
        def _():
            for copy in key_copies(place):
                copy.wait_send()

    for place in range(1, 4):

        @pl.when(plane == place)
        def _():
            back_copy(place).wait_send()


def attend_and_back(
    lengths_all,
    cosine,
    sine_part,
    q,
    k,
    v,
    out_grad,
    normed_all,
    grad_all,
    hidden,
    w_out,
    w_down,
    attn_columns,
    x_ordered,
    gains,
    grad_low,
    back3,
    down_term,
    up_term,
    micro_count,
    sequence_length,
):
    rows, features = grad_low.shape
    total, width = q.shape
    ff_share = w_down.shape[0]
    quarter = features // 32
    block = (rows, features)
    piece = (4 * quarter, features)
    half = (4, rows // 2, features)
    anywhere = pl.BlockSpec(memory_space=pl.ANY)
    near = pl.BlockSpec(memory_space=pltpu.VMEM)
    shape = jax.ShapeDtypeStruct
    low_type = jnp.bfloat16
    some = lambda *dims: pltpu.VMEM(dims, low_type)
    dma = pltpu.SemaphoreType.DMA
    return pl.pallas_call(
        functools.partial(
            backward_kernel, micro_count=micro_count, sequence_length=sequence_length
        ),
        in_specs=[pl.BlockSpec(memory_space=pltpu.SMEM)]
        + [near] * 6
        + [anywhere, anywhere]
        + [near] * 4
        + [anywhere]
        + [near] * 3
        + [anywhere, anywhere],
        out_specs=[anywhere, anywhere, anywhere, near, near, near, anywhere, anywhere],
        out_shape=[
            shape((16 * rows, features), low_type),
            shape((ff_share, features), low_type),
            shape((4 * quarter, 8 * ff_share), low_type),
            shape(piece, low_type),
            shape(block, low_type),
            shape((8, features), jnp.float32),
            shape((16 * quarter, features), low_type),
            shape((18,) + piece, low_type),
        ],
        scratch_shapes=[
            some(total, features),
            some(total, width),
            some(total, width),
            pltpu.VMEM((total, 2 * width), jnp.float32),
            some(total, 2 * width),
            some(total, 2 * width),
            some(total, 2 * width),
            some(4, *block),
            some(4, *block),
            some(4, *block),
            some(*half),
            some(*half),
            some(*half),
            some(*piece),
            some(2, *piece),
            some(3, *piece),
            some(*piece),
            some(*piece),
            some(quarter, 8 * ff_share),
            some(4, *block),
            some(*block),
            pltpu.VMEM(block, jnp.float32),
            some(*piece),
            dma((4, 10)),
            dma((4, 10)),
            dma((3, 6)),
            dma((3, 6)),
            dma((2,)),
            dma((6, 6)),
            dma((6, 6)),
            dma((6,)),
            dma((3,)),
            dma((3,)),
            dma((16,)),
            dma((16,)),
            dma((8,)),
        ],
        compiler_params=pltpu.CompilerParams(
            collective_id=6, has_side_effects=True, vmem_limit_bytes=63 * 1024 * 1024
        ),
        cost_estimate=pl.CostEstimate(
            flops=20 * total * features * width,
            bytes_accessed=1000 * 1000 * 1000,
            transcendentals=0,
        ),
    )(
        lengths_all,
        cosine,
        sine_part,
        q,
        k,
        v,
        out_grad,
        normed_all,
        grad_all,
        hidden,
        w_out,
        w_down,
        attn_columns,
        x_ordered,
        gains,
        grad_low,
        back3,
        down_term,
        up_term,
    )


def rotary_table(row_positions, head_dim):
    half_dim = head_dim // 2
    frequency = jnp.exp(
        jnp.arange(half_dim, dtype=jnp.float32) * (-2.0 * math.log(10000.0) / head_dim)
    )
    angles = row_positions.astype(jnp.float32)[:, None] * frequency[None, :]
    cosine = jnp.cos(angles)
    sine_part = jnp.sin(angles)
    return (
        jnp.concatenate([cosine, cosine], axis=-1),
        jnp.concatenate([-sine_part, sine_part], axis=-1),
    )


def turned(values, cosine, sine_part, rows, sign):
    total, width = values.shape
    heads = values.reshape(total // rows, rows, width // HEAD_DIM, HEAD_DIM)
    swapped = jnp.concatenate(
        [heads[..., HEAD_DIM // 2 :], heads[..., : HEAD_DIM // 2]], axis=-1
    )
    return (
        heads * cosine[None, :, None, :] + sign * swapped * sine_part[None, :, None, :]
    ).reshape(total, width)


def shards_split(
    history,
    history_layer_index,
    lengths,
    norm_gains,
    mix_in,
    mix_out,
    w_attn,
    w_out,
    w_up,
    w_down,
    cotangent,
):
    local_slots, micro_count, sequence_length, features = history.shape
    planes = lax.axis_size("hist")
    columns = lax.axis_size("dp")
    plane = lax.axis_index("hist")
    slot_count = local_slots * planes
    all_rows = micro_count * sequence_length
    rows = all_rows // planes
    share = features // columns
    mix_width = mix_in.shape[1]
    ff_share = w_down.shape[0]
    low = lambda values: values.astype(jnp.bfloat16)

    top = jnp.concatenate(
        [mix_in, norm_gains.T, jnp.zeros((share, 128 - mix_width - 5), jnp.bfloat16)], axis=1
    )
    mix_rows = mix_out.shape[0]
    bottom = jnp.zeros((16, 128), jnp.bfloat16)
    bottom = bottom.at[:mix_rows, :mix_width].set(mix_out)
    bottom = bottom.at[0, mix_width : mix_width + micro_count].set(low(lengths))
    packed = lax.all_gather(jnp.concatenate([top, bottom], axis=0), "dp", axis=0, tiled=False)
    mix_in_all = packed[:, :share, :mix_width].reshape(features, mix_width)
    gains_all = (
        packed[:, :share, mix_width : mix_width + 5].reshape(features, 5).astype(jnp.float32).T
    )
    mixer_output_wide = (
        packed[:, share : share + mix_rows, :mix_width]
        .reshape(mix_width, mix_width)
        .astype(jnp.float32)
    )
    lengths_all = (
        packed[:, share, mix_width : mix_width + micro_count].reshape(-1).astype(jnp.int32)
    )

    chunk = sequence_length // planes
    inverse_step = pow(micro_count, -1, planes)
    received = []
    for i in range(micro_count):
        target = lax.rem((plane - i + planes * micro_count) * inverse_step, planes)
        which = lax.div(target * micro_count + i, planes)
        piece = lax.dynamic_index_in_dim(cotangent, which, 0, keepdims=False)
        pairs = [(t, ((t - i) * inverse_step) % planes) for t in range(planes)]
        received.append(lax.ppermute(piece, "hist", pairs))
    my_row = plane * rows + jnp.arange(rows, dtype=jnp.int32)
    my_position = lax.rem(my_row, sequence_length)
    my_sequence = lax.div(my_row, sequence_length)
    my_length = jnp.sum(
        jnp.where(
            my_sequence[:, None] == jnp.arange(micro_count, dtype=jnp.int32)[None, :],
            lengths[None, :],
            0,
        ),
        axis=1,
    )
    valid_rows = (my_position < my_length).astype(jnp.float32)[:, None]
    grad_rows = jnp.concatenate(received, axis=0).astype(jnp.float32) * valid_rows

    layer_lookup = (
        history_layer_index[:, None] == jnp.arange(slot_count, dtype=jnp.int32)[None, :]
    ).astype(jnp.float32)
    newest_output = jnp.sum(
        jnp.arange(slot_count, dtype=jnp.int32)
        * (history_layer_index == slot_count - 1).astype(jnp.int32)
    )
    root = newest_output // local_slots
    on_root = (plane == root).astype(jnp.float32)
    latest_local = lax.dynamic_index_in_dim(history, newest_output % local_slots, 0, keepdims=False)
    dyn_local, kept_mix = mix_forward(
        latest_local.reshape(all_rows, features), gains_all[0], mix_in_all, mixer_output_wide
    )
    dyn_every = lax.all_gather(dyn_local, "hist", axis=0, tiled=False)
    dyn = lax.dynamic_index_in_dim(dyn_every, root, 0, keepdims=False)
    own_table = lax.dynamic_slice_in_dim(layer_lookup, plane * local_slots, local_slots, 0)
    factors = jnp.einsum(
        "tcj,sj->sct",
        dyn.reshape(all_rows, STREAM_COUNT, slot_count),
        own_table,
        precision=highest,
    )
    flat_history = history.reshape(local_slots, all_rows, features)

    def mixed(stream):
        total = jnp.zeros((all_rows, features), jnp.float32)
        for slot in range(local_slots):
            total = total + factors[slot, stream][:, None] * flat_history[slot].astype(jnp.float32)
        return low(total)

    order = (3, 0, 1, 2)
    parts = jnp.concatenate([mixed(stream) for stream in order], axis=0)
    gains_ordered = jnp.pad(jnp.stack([gains_all[stream + 1] for stream in order]), ((0, 4), (0, 0)))
    (
        x_ordered,
        normed_all,
        grad_all,
        hidden,
        up_term,
        down_term,
        back3,
        attn_columns,
        _,
    ) = forward_and_feed(parts, low(grad_rows), w_up, w_attn, w_down, gains_ordered)
    normed = [normed_all[0], normed_all[1], normed_all[2]]

    cosine, sine_part = rotary_table(my_position, HEAD_DIM)
    att_grad = low(
        lax.dot_general(grad_all, w_out, contract_cols, preferred_element_type=jnp.float32)
    )
    q = low(turned(matmul(normed[0], attn_columns[0]), cosine, sine_part, rows, 1.0))
    k = low(turned(matmul(normed[1], attn_columns[1]), cosine, sine_part, rows, 1.0))
    v = low(matmul(normed[2], attn_columns[2]))
    full, down_all, up_all, attn_quarter, branch, gain_sums, _, _ = attend_and_back(
        lengths_all,
        cosine,
        sine_part,
        q,
        k,
        v,
        att_grad,
        normed_all,
        grad_all,
        hidden,
        w_out,
        w_down,
        attn_columns,
        x_ordered,
        gains_ordered,
        low(grad_rows),
        back3,
        down_term,
        up_term,
        micro_count,
        sequence_length,
    )
    block_rows = low((x_ordered[0] + branch.astype(jnp.float32)) * valid_rows)
    block_out = jnp.zeros((micro_count, chunk, features), jnp.bfloat16)
    for i in range(micro_count):
        pairs = [(p, (micro_count * p + i) % planes) for p in range(planes)]
        piece = lax.ppermute(block_rows[i * chunk : (i + 1) * chunk], "hist", pairs)
        source = lax.rem((plane - i + planes * micro_count) * inverse_step, planes)
        which = lax.div(source * micro_count + i, planes)
        block_out = lax.dynamic_update_index_in_dim(block_out, piece, which, 0)

    full_ordered = full.reshape(STREAM_COUNT, all_rows, features)
    full_grads = [
        full_ordered[order.index(stream)].astype(jnp.float32) for stream in range(STREAM_COUNT)
    ]
    inner = jnp.stack(
        [
            jnp.stack(
                [
                    jnp.sum(full_grads[stream] * flat_history[slot].astype(jnp.float32), axis=-1)
                    for slot in range(local_slots)
                ],
                axis=-1,
            )
            for stream in range(STREAM_COUNT)
        ],
        axis=1,
    )
    dyn_part = jnp.einsum("tcs,sj->tcj", inner, own_table, precision=highest)
    dyn_grad = jnp.sum(
        lax.all_gather(
            dyn_part.reshape(all_rows, STREAM_COUNT * slot_count), "hist", axis=0, tiled=False
        ),
        axis=0,
    )
    act_grad = precise(dyn_grad, mixer_output_wide.T)
    mix_out_grad = precise(kept_mix[4].T, dyn_grad) * on_root
    latest_grad, gain_zero, mix_in_grad = mix_backward(kept_mix, act_grad, gains_all[0], mix_in_all)
    slot_grads = []
    for slot in range(local_slots):
        is_latest = (plane * local_slots + slot == newest_output).astype(jnp.float32)
        slot_grad = latest_grad * is_latest
        for stream in range(STREAM_COUNT):
            slot_grad = slot_grad + factors[slot, stream][:, None] * full_grads[stream]
        slot_grads.append(low(slot_grad))
    history_grad = jnp.stack(slot_grads).reshape(history.shape)

    attn_every = lax.all_gather(attn_quarter, "hist", axis=0, tiled=False).astype(jnp.float32)
    part = share // planes
    w_attn_grad = (
        attn_every[:, : 3 * part]
        .reshape(planes, 3, part, features)
        .transpose(1, 0, 2, 3)
        .reshape(3, share, features)
    )
    w_out_grad = attn_every[:, 3 * part :].reshape(share, features)
    w_down_grad = down_all.astype(jnp.float32)
    w_up_grad = up_all.astype(jnp.float32)

    small_top = jnp.concatenate(
        [
            mix_in_grad * on_root,
            jnp.stack(
                [gain_zero * on_root]
                + [gain_sums[order.index(stream)] for stream in range(STREAM_COUNT)]
            ).T,
            jnp.zeros((features, 128 - mix_width - 5), jnp.float32),
        ],
        axis=1,
    ).reshape(columns, share, 128)
    small_bottom = jnp.pad(
        mix_out_grad.reshape(columns, mix_rows, mix_width),
        ((0, 0), (0, 16 - mix_rows), (0, 128 - mix_width)),
    )
    small = low(jnp.concatenate([small_top, small_bottom], axis=1))
    small = lax.psum_scatter(small, "dp", scatter_dimension=0, tiled=False)
    small = lax.psum(small, "hist").astype(jnp.float32)
    return (
        block_out,
        history_grad,
        small[:share, mix_width : mix_width + 5].T,
        small[:share, :mix_width],
        small[share : share + mix_rows, :mix_width],
        w_attn_grad,
        w_out_grad,
        w_up_grad,
        w_down_grad,
    )


def splits_by_heads(mesh, micro_count, sequence_length):
    columns, planes = mesh.shape["dp"], mesh.shape["hist"]
    all_rows = micro_count * sequence_length
    rows = all_rows // planes
    return (
        columns == 8
        and planes == 4
        and HEADS % columns == 0
        and all_rows % planes == 0
        and sequence_length % planes == 0
        and rows % 64 == 0
        and math.gcd(micro_count, planes) == 1
        and all(
            (p * rows) // sequence_length * sequence_length >= (p - 1) * rows
            for p in range(planes)
        )
    )


def solution(mesh):
    placed = (
        P("hist", "dp", None, None),
        P(),
        P("dp"),
        P(None, "dp"),
        P("dp", None),
        P("dp", None),
        P(None, "dp", None),
        P("dp", None),
        P("dp", None),
        P("dp", None),
        P("dp", "hist", None),
    )
    def plan(*arrays):
        micro_count = arrays[2].shape[0]
        if splits_by_heads(mesh, micro_count, arrays[0].shape[2]):
            return shards_split(*arrays)
        return shards(*arrays)

    return jax.shard_map(
        plan,
        mesh=mesh,
        in_specs=placed,
        out_specs=(
            P("dp", "hist", None),
            P("hist", "dp", None, None),
            P(None, "dp"),
            P("dp", None),
            P("dp", None),
            P(None, "dp", None),
            P("dp", None),
            P("dp", None),
            P("dp", None),
        ),
        check_vma=False,
    )
```

```python
import functools
import math

import jax
import jax.numpy as jnp
from jax import lax
from jax.experimental import pallas as pl
from jax.experimental.pallas import tpu as pltpu
from jax.sharding import PartitionSpec as P

MODEL_WIDTH = 2048
HEADS = 16
HEAD_DIM = 128
FF = 8192
STREAM_COUNT = 4


epsilon = 1e-06
masked_out = -1e30
highest = lax.Precision.HIGHEST
contract_rows = (((0,), (0,)), ((), ()))
contract_cols = (((1,), (1,)), ((), ()))


def broadcast(value, axis, source):
    kept = jnp.where(lax.axis_index(axis) == source, value, 0).astype(value.dtype)
    return lax.psum(kept, axis)


def matmul(left_side, right_side):
    return jnp.dot(left_side, right_side, preferred_element_type=jnp.float32)


def precise(left_side, right_side):
    return jnp.dot(left_side, right_side, precision=highest, preferred_element_type=jnp.float32)


def gelu_slope(values):
    return 0.5 * (1.0 + lax.erf(values * (1.0 / math.sqrt(2.0)))) + values * jnp.exp(
        -0.5 * values * values
    ) * (1.0 / math.sqrt(2.0 * math.pi))


def rms_scale(values, gain_row):
    inverse = lax.rsqrt(jnp.mean(values * values, axis=-1, keepdims=True) + epsilon)
    return (values * inverse * gain_row, inverse)


def rms_back(values, inverse, gain_row, grad_in):
    scaled = grad_in * gain_row
    gain_grad = jnp.sum(grad_in * values * inverse, axis=0)
    inner_mean = jnp.mean(scaled * values, axis=-1, keepdims=True)
    return (inverse * scaled - values * (inverse * inverse * inverse) * inner_mean, gain_grad)


def rotate(values, positions, turn_sign):
    half_dim = values.shape[-1] // 2
    frequency = jnp.exp(
        jnp.arange(half_dim, dtype=jnp.float32) * (-2.0 * math.log(10000.0) / values.shape[-1])
    )
    angles = positions.astype(jnp.float32)[:, None] * frequency[None, :]
    cosine = jnp.cos(angles)[:, None, :]
    sine_part = jnp.sin(angles)[:, None, :] * turn_sign
    lower_half = values[..., :half_dim]
    upper_half = values[..., half_dim:]
    return jnp.concatenate(
        [
            lower_half * cosine - upper_half * sine_part,
            upper_half * cosine + lower_half * sine_part,
        ],
        axis=-1,
    )


def first_rows(weights, lefts):

    def add_piece(totals, pieces, start_at):
        return tuple(
            (matmul(left_side, piece_rows) for left_side, piece_rows in zip(lefts, pieces))
        )

    initial = tuple(
        (jnp.zeros((lefts[0].shape[0], weight.shape[1]), jnp.float32) for weight in weights)
    )
    return add_piece(
        initial,
        (
            lax.all_gather(weights[0], "dp", axis=0, tiled=True),
            lax.all_gather(weights[1], "dp", axis=0, tiled=True),
            lax.all_gather(weights[2], "dp", axis=0, tiled=True),
            lax.all_gather(weights[3], "dp", axis=0, tiled=True),
        ),
        jnp.int32(0),
    )


def second_rows(w_out, down_folded, attended_low, hidden, ratio):

    def add_piece(total_sum, pieces, start_at):
        count = pieces[0].shape[0]
        down_rows = pieces[1].reshape(count * ratio, pieces[1].shape[1] // ratio)
        return matmul(attended_low, pieces[0]) + matmul(hidden, down_rows)

    initial = jnp.zeros((attended_low.shape[0], w_out.shape[1]), jnp.float32)
    return add_piece(
        initial,
        (
            lax.all_gather(w_out, "dp", axis=0, tiled=True),
            lax.all_gather(down_folded, "dp", axis=0, tiled=True),
        ),
        jnp.int32(0),
    )


def back_first(w_out, down_folded, grad_low, ratio):

    def add_piece(totals, pieces, start_at):
        count = pieces[0].shape[0]
        out_part = lax.dot_general(
            grad_low, pieces[0], contract_cols, preferred_element_type=jnp.float32
        )
        down_rows = pieces[1].reshape(count * ratio, pieces[1].shape[1] // ratio)
        down_part = lax.dot_general(
            grad_low, down_rows, contract_cols, preferred_element_type=jnp.float32
        )
        return (out_part, down_part)

    features = w_out.shape[1]
    initial = (
        jnp.zeros((grad_low.shape[0], features), jnp.float32),
        jnp.zeros((grad_low.shape[0], features * ratio), jnp.float32),
    )
    return add_piece(
        initial,
        (
            lax.all_gather(w_out, "dp", axis=0, tiled=True),
            lax.all_gather(down_folded, "dp", axis=0, tiled=True),
        ),
        jnp.int32(0),
    )


def back_second(weights, rights):

    def add_piece(totals, pieces, start_at):
        return tuple(
            (
                lax.dot_general(
                    right_side, piece_rows, contract_cols, preferred_element_type=jnp.float32
                )
                for right_side, piece_rows in zip(rights, pieces)
            )
        )

    features = weights[1].shape[1]
    initial = tuple((jnp.zeros((rights[0].shape[0], features), jnp.float32) for weight in weights))
    return add_piece(
        initial,
        (
            lax.all_gather(weights[0], "dp", axis=0, tiled=True),
            lax.all_gather(weights[1], "dp", axis=0, tiled=True),
            lax.all_gather(weights[2], "dp", axis=0, tiled=True),
            lax.all_gather(weights[3], "dp", axis=0, tiled=True),
        ),
        jnp.int32(0),
    )


def mix_forward(values_low, gain_row, mix_in_all, mixer_output_wide):
    values = values_low.astype(jnp.float32)
    scaled, inverse = rms_scale(values, gain_row)
    normed_mix = scaled.astype(jnp.bfloat16)
    mixer_preactivation = matmul(normed_mix, mix_in_all)
    mix_act = jax.nn.gelu(mixer_preactivation, approximate=False)
    return (
        precise(mix_act, mixer_output_wide),
        (values, inverse, normed_mix, mixer_preactivation, mix_act),
    )


def mix_backward(kept_mix, act_grad, gain_row, mix_in_all):
    values, inverse, normed_mix, mixer_preactivation, mix_act = kept_mix
    pre_grad = act_grad * gelu_slope(mixer_preactivation)
    in_grad = precise(normed_mix.astype(jnp.float32).T, pre_grad)
    normed_grad = precise(pre_grad, mix_in_all.astype(jnp.float32).T)
    latest_grad, gain_grad = rms_back(values, inverse, gain_row, normed_grad)
    return (latest_grad, gain_grad, in_grad)


def shards(
    history,
    history_layer_index,
    lengths,
    norm_gains,
    mix_in,
    mix_out,
    w_attn,
    w_out,
    w_up,
    w_down,
    cotangent,
):
    local_slots, micro_count, sequence_length, features = history.shape
    hist_count = lax.axis_size("hist")
    dp_count = lax.axis_size("dp")
    hist_place = lax.axis_index("hist")
    slot_count = local_slots * hist_count
    ratio = FF // MODEL_WIDTH
    gains_all, mix_in_all, mix_out_all = (
        lax.all_gather(norm_gains, "dp", axis=1, tiled=True),
        lax.all_gather(mix_in, "dp", axis=0, tiled=True),
        lax.all_gather(mix_out, "dp", axis=0, tiled=True),
    )
    gains_all = gains_all.astype(jnp.float32)
    mixer_output_wide = mix_out_all.astype(jnp.float32)
    mix_width = mixer_output_wide.shape[0]
    layer_lookup = (
        history_layer_index[:, None] == jnp.arange(slot_count, dtype=jnp.int32)[None, :]
    ).astype(jnp.float32)
    newest_output = jnp.sum(
        jnp.arange(slot_count, dtype=jnp.int32)
        * (history_layer_index == slot_count - 1).astype(jnp.int32)
    )
    down_folded = w_down.reshape(w_down.shape[0] // ratio, ratio * w_down.shape[1])
    quarter = cotangent.shape[1]
    own_rows = micro_count * quarter
    positions = hist_place * quarter + jnp.arange(quarter, dtype=jnp.int32)
    valid_rows = (positions[None, :] < lengths[:, None]).astype(jnp.float32).reshape(own_rows, 1)
    root = newest_output // local_slots
    latest_local = lax.dynamic_index_in_dim(history, newest_output % local_slots, 0, keepdims=False)
    latest_rows = broadcast(latest_local, "hist", root)
    dynamic_weights, kept_mix = mix_forward(
        latest_rows.reshape(micro_count * sequence_length, features),
        gains_all[0],
        mix_in_all,
        mixer_output_wide,
    )
    dynamic_weights = dynamic_weights.reshape(
        micro_count, sequence_length, STREAM_COUNT, slot_count
    )
    own_table = lax.dynamic_slice_in_dim(layer_lookup, hist_place * local_slots, local_slots, 0)
    depth_combination_factors = jnp.einsum(
        "mtcj,sj->scmt", dynamic_weights, own_table, precision=highest
    )
    partial_sums = jnp.zeros((STREAM_COUNT, micro_count, sequence_length, features), jnp.float32)
    for depth_position_number in range(local_slots):
        partial_sums = (
            partial_sums
            + depth_combination_factors[depth_position_number][..., None]
            * history[depth_position_number].astype(jnp.float32)[None]
        )
    blended_residual_inputs = lax.psum_scatter(
        partial_sums, "hist", scatter_dimension=2, tiled=True
    )
    stream_rows = blended_residual_inputs.reshape(STREAM_COUNT, own_rows, features)
    normed = []
    inverses = []
    for stream_idx in range(STREAM_COUNT):
        scaled, inverse = rms_scale(stream_rows[stream_idx], gains_all[stream_idx + 1])
        normed.append(scaled.astype(jnp.bfloat16))
        inverses.append(inverse)
    head_shape = (micro_count, quarter, HEADS, HEAD_DIM)
    query_pre, key_pre, value_pre, up_pre = first_rows(
        (w_attn[0], w_attn[1], w_attn[2], w_up), (normed[0], normed[1], normed[2], normed[3])
    )
    attention_asker_vectors = rotate(query_pre.reshape(head_shape), positions, 1.0).astype(
        jnp.bfloat16
    )
    keys_rot = rotate(key_pre.reshape(head_shape), positions, 1.0).astype(jnp.bfloat16)
    values_low = value_pre.astype(jnp.bfloat16)
    keys_all, values_all = (
        lax.all_gather(
            keys_rot.reshape(micro_count, quarter, features), "hist", axis=1, tiled=True
        ),
        lax.all_gather(
            values_low.reshape(micro_count, quarter, features), "hist", axis=1, tiled=True
        ),
    )
    key_heads = keys_all.reshape(micro_count, sequence_length, HEADS, HEAD_DIM)
    value_wide = values_all.reshape(micro_count, sequence_length, HEADS, HEAD_DIM).astype(
        jnp.float32
    )
    score_scale = 1.0 / math.sqrt(HEAD_DIM)
    scores = (
        jnp.einsum(
            "mqhd,mkhd->mhqk",
            attention_asker_vectors,
            key_heads,
            preferred_element_type=jnp.float32,
        )
        * score_scale
    )
    key_positions = jnp.arange(sequence_length, dtype=jnp.int32)
    allowed = (key_positions[None, None, :] <= positions[None, :, None]) & (
        key_positions[None, None, :] < lengths[:, None, None]
    )
    scores = jnp.where(allowed[:, None], scores, masked_out)
    row_top = jnp.max(scores, axis=-1, keepdims=True)
    raised = jnp.exp(scores - row_top)
    soft_weights = raised / jnp.sum(raised, axis=-1, keepdims=True)
    attended = jnp.einsum("mhqk,mkhd->mqhd", soft_weights, value_wide, precision=highest)
    attended_low = attended.reshape(own_rows, features).astype(jnp.bfloat16)
    hidden = jax.nn.gelu(up_pre, approximate=False).astype(jnp.bfloat16)
    branch = second_rows(w_out, down_folded, attended_low, hidden, ratio)
    block_out = (
        ((stream_rows[3] + branch) * valid_rows)
        .astype(jnp.bfloat16)
        .reshape(micro_count, quarter, features)
    )
    grad_rows = cotangent.reshape(own_rows, features).astype(jnp.float32) * valid_rows
    grad_low = grad_rows.astype(jnp.bfloat16)
    attended_back, hidden_grad = back_first(w_out, down_folded, grad_low, ratio)
    up_grad = (hidden_grad * gelu_slope(up_pre)).astype(jnp.bfloat16)
    attended_grad = attended_back.astype(jnp.bfloat16)
    attended_wide = attended_grad.astype(jnp.float32).reshape(head_shape)
    prob_grad = jnp.einsum("mqhd,mkhd->mhqk", attended_wide, value_wide, precision=highest)
    inner_rows = jnp.sum(attended_wide * attended, axis=-1)
    logit_derivative = (
        soft_weights * (prob_grad - jnp.transpose(inner_rows, (0, 2, 1))[..., None]) * score_scale
    )
    query_grad = jnp.einsum(
        "mhqk,mkhd->mqhd", logit_derivative, key_heads.astype(jnp.float32), precision=highest
    )
    key_grad_all = jnp.einsum(
        "mhqk,mqhd->mkhd",
        logit_derivative,
        attention_asker_vectors.astype(jnp.float32),
        precision=highest,
    )
    value_grad_all = jnp.einsum("mhqk,mqhd->mkhd", soft_weights, attended_wide, precision=highest)
    key_grad, value_grad = (
        lax.psum_scatter(
            key_grad_all.reshape(micro_count, sequence_length, features).astype(jnp.bfloat16),
            "hist",
            scatter_dimension=1,
            tiled=True,
        ).astype(jnp.float32),
        lax.psum_scatter(
            value_grad_all.reshape(micro_count, sequence_length, features).astype(jnp.bfloat16),
            "hist",
            scatter_dimension=1,
            tiled=True,
        ).astype(jnp.float32),
    )
    projection_grads = [
        rotate(query_grad, positions, -1.0).reshape(own_rows, features).astype(jnp.bfloat16),
        rotate(key_grad.reshape(head_shape), positions, -1.0)
        .reshape(own_rows, features)
        .astype(jnp.bfloat16),
        value_grad.reshape(own_rows, features).astype(jnp.bfloat16),
    ]
    resid_normed_grad, query_normed_grad, key_normed_grad, value_normed_grad = back_second(
        (w_up, w_attn[0], w_attn[1], w_attn[2]),
        (up_grad, projection_grads[0], projection_grads[1], projection_grads[2]),
    )
    normed_grads = [query_normed_grad, key_normed_grad, value_normed_grad]
    stream_grads = []
    gain_grads = []
    for stream_idx in range(3):
        stream_grad, gain_grad = rms_back(
            stream_rows[stream_idx],
            inverses[stream_idx],
            gains_all[stream_idx + 1],
            normed_grads[stream_idx],
        )
        stream_grads.append(stream_grad)
        gain_grads.append(gain_grad)
    resid_grad, skip_scaling_derivative = rms_back(
        stream_rows[3], inverses[3], gains_all[4], resid_normed_grad
    )
    stream_grads.append(resid_grad + grad_rows)
    gain_grads.append(skip_scaling_derivative)
    stream_grads_all = jnp.stack(stream_grads).reshape(STREAM_COUNT, micro_count, quarter, features)
    full_grads = lax.all_gather(
        stream_grads_all.astype(jnp.bfloat16), "hist", axis=2, tiled=True
    ).astype(stream_grads_all.dtype)
    slot_grads = []
    dyn_grad = jnp.zeros((micro_count, sequence_length, STREAM_COUNT, slot_count), jnp.float32)
    for depth_position_number in range(local_slots):
        rows_now = history[depth_position_number].astype(jnp.float32)
        slot_grads.append(
            jnp.sum(
                depth_combination_factors[depth_position_number][..., None] * full_grads, axis=0
            )
        )
        inner_now = jnp.sum(full_grads * rows_now[None], axis=-1)
        dyn_grad = dyn_grad + jnp.einsum("cmt,j->mtcj", inner_now, own_table[depth_position_number])
    dyn_grad = dyn_grad.reshape(micro_count * sequence_length, STREAM_COUNT * slot_count)
    act_part = precise(dyn_grad, mixer_output_wide.T)
    mix_out_grad = precise(kept_mix[4].T, dyn_grad)
    act_grad = lax.psum(act_part.astype(jnp.bfloat16), "hist").astype(jnp.float32)
    on_root = (hist_place == root).astype(jnp.float32)
    latest_grad, gain_zero, mix_in_grad = mix_backward(kept_mix, act_grad, gains_all[0], mix_in_all)
    gain_zero = gain_zero * on_root
    mix_in_grad = mix_in_grad * on_root
    latest_grad = latest_grad.reshape(micro_count, sequence_length, features)
    marked = []
    for depth_position_number in range(local_slots):
        is_latest = (hist_place * local_slots + depth_position_number == newest_output).astype(
            jnp.float32
        )
        marked.append(slot_grads[depth_position_number] + latest_grad * is_latest)
    history_grad = jnp.stack(marked).astype(jnp.bfloat16)
    gains_grad_full = jnp.stack(
        [gain_zero, gain_grads[0], gain_grads[1], gain_grads[2], gain_grads[3]]
    )
    share_rows = w_out.shape[0]
    per_device = mix_width // dp_count
    mix_out_padded = jnp.pad(
        mix_out_grad.reshape(dp_count, per_device, mix_width),
        ((0, 0), (0, share_rows - per_device), (0, 0)),
    ).reshape(dp_count * share_rows, mix_width)
    small_wide = jnp.concatenate([mix_in_grad, gains_grad_full.T, mix_out_padded], axis=1)
    attn_lefts = (normed[0], normed[1], normed[2], attended_low)
    attn_rights = (projection_grads[0], projection_grads[1], projection_grads[2], grad_low)
    attn_share = lax.psum_scatter(
        jnp.concatenate(
            [
                lax.dot_general(
                    left_side, right_side, contract_rows, preferred_element_type=jnp.float32
                )
                for left_side, right_side in zip(attn_lefts, attn_rights)
            ],
            axis=1,
        ).astype(jnp.bfloat16),
        "dp",
        scatter_dimension=0,
        tiled=True,
    )
    up_term = lax.dot_general(normed[3], up_grad, contract_rows, preferred_element_type=jnp.float32)
    down_term = lax.dot_general(
        hidden, grad_low, contract_rows, preferred_element_type=jnp.float32
    ).reshape(share_rows * lax.axis_size("dp"), ratio * features)
    ffn_share = lax.psum_scatter(
        jnp.concatenate([up_term, down_term, small_wide], axis=1).astype(jnp.bfloat16),
        "dp",
        scatter_dimension=0,
        tiled=True,
    )
    attn_total, ffn_total = (
        lax.psum(attn_share, "hist").astype(jnp.float32),
        lax.psum(ffn_share, "hist").astype(jnp.float32),
    )
    ff_width = ratio * features
    w_attn_grad = jnp.stack(
        [
            attn_total[:, 0:features],
            attn_total[:, features : 2 * features],
            attn_total[:, 2 * features : 3 * features],
        ]
    )
    w_out_grad = attn_total[:, 3 * features : 4 * features]
    w_up_grad = ffn_total[:, 0:ff_width]
    w_down_grad = ffn_total[:, ff_width : 2 * ff_width].reshape(share_rows * ratio, features)
    mix_in_share = ffn_total[:, 2 * ff_width : 2 * ff_width + mix_width]
    gains_share = ffn_total[:, 2 * ff_width + mix_width : 2 * ff_width + mix_width + 5].T
    mix_out_share = ffn_total[0:per_device, 2 * ff_width + mix_width + 5 :]
    return (
        block_out,
        history_grad,
        gains_share,
        mix_in_share,
        mix_out_share,
        w_attn_grad,
        w_out_grad,
        w_up_grad,
        w_down_grad,
    )


DEVICE_MESH = pl.DeviceIdType.MESH
CORE, ACROSS_X, ACROSS_Y = 1, 2, 4


def partner(column, mask):
    moved = column
    for bit in (1, 2, 4):
        if mask & bit:
            on = lax.rem(lax.div(moved, bit), 2)
            moved = moved + bit - 2 * bit * on
    return moved


def push(source, target, send_sem, recv_sem, place):
    copy = pltpu.make_async_remote_copy(
        src_ref=source,
        dst_ref=target,
        send_sem=send_sem,
        recv_sem=recv_sem,
        device_id={"dp": place},
        device_id_type=DEVICE_MESH,
    )
    copy.start()
    return copy


def z_place(plane):
    return {"hist": plane}


class PlaneGatherSteps:

    def __init__(self, column, own, whole, send_sem, recv_sem, local_sem):
        self.column, self.own, self.whole = column, own, whole
        self.send_sem, self.recv_sem, self.local_sem = send_sem, recv_sem, local_sem
        self.rows = own.shape[0]
        self.half = self.rows // 2
        self.across = partner(column, ACROSS_X)
        self.along = partner(column, ACROSS_Y)
        self.beside = partner(column, CORE)
        self.corner = partner(column, ACROSS_X + ACROSS_Y)
        self.copies = []

    def place(self, owner, part):
        start = owner * self.rows + (self.half if part == 1 else 0)
        count = self.rows if part is None else self.half
        return self.whole.at[pl.ds(pl.multiple_of(start, 16), count)]

    def mine(self, part):
        start = self.half if part == 1 else 0
        return self.own.at[pl.ds(start, self.rows if part is None else self.half)]

    def send(self, source, owner, part, to):
        index = len(self.copies)
        copy = push(
            source, self.place(owner, part), self.send_sem.at[index], self.recv_sem.at[index], to
        )
        self.copies.append(copy)

    def begin(self):
        me = self.column
        self.local = pltpu.make_async_copy(self.mine(None), self.place(me, None), self.local_sem)
        self.local.start()
        self.send(self.mine(1), me, 1, self.across)
        self.send(self.mine(0), me, 0, self.along)
        self.send(self.mine(0), me, 0, self.across)
        self.send(self.mine(1), me, 1, self.along)
        self.send(self.mine(None), me, None, self.beside)

    def corners(self):
        self.copies[1].wait_recv()
        self.send(self.place(self.along, 0), self.along, 0, self.across)
        self.copies[0].wait_recv()
        self.send(self.place(self.across, 1), self.across, 1, self.along)

    def siblings(self):
        self.copies[2].wait_recv()
        self.send(self.place(self.across, None), self.across, None, self.beside)
        self.copies[3].wait_recv()
        self.send(self.place(self.along, None), self.along, None, self.beside)

    def rest(self):
        self.copies[5].wait_recv()
        self.send(self.place(self.corner, 0), self.corner, 0, self.beside)
        self.copies[6].wait_recv()
        self.send(self.place(self.corner, 1), self.corner, 1, self.beside)

    def finish(self):
        for index in (4, 7, 8, 9, 10):
            self.copies[index].wait_recv()
        for copy in self.copies:
            copy.wait_send()
        self.local.wait()


class PlaneScatterSteps:
    def __init__(self, column, product, refs, send_sem, recv_sem):
        self.column, self.product = column, product
        self.out_buf, self.side, self.chip, self.from_x, self.from_y, self.last = refs
        self.send_sem, self.recv_sem = send_sem, recv_sem
        rows = self.chip.shape[1]
        self.first, self.second = pl.ds(0, rows // 2), pl.ds(rows // 2, rows // 2)
        self.across = partner(column, ACROSS_X)
        self.along = partner(column, ACROSS_Y)
        self.beside = partner(column, CORE)
        self.pair, self.sends = [], []

    def block(self, i):
        mask = (6, 2, 4, 0)[i]
        if i >= 2:
            self.pair[i - 2].wait_send()
        self.product(partner(self.column, mask + CORE), self.out_buf.at[i % 2])
        self.pair.append(
            push(
                self.out_buf.at[i % 2],
                self.side.at[i],
                self.send_sem.at[i],
                self.recv_sem.at[i],
                self.beside,
            )
        )
        self.product(partner(self.column, mask), self.chip.at[i])
        self.pair[i].wait_recv()
        add_into(self.chip.at[i], self.side.at[i])
        if i == 0:
            self.send(self.chip.at[0, self.first], self.from_x.at[0], self.across)
            self.send(self.chip.at[0, self.second], self.from_y.at[0], self.along)
        if i == 1:
            self.send(self.chip.at[1, self.first], self.from_x.at[1], self.across)
        if i == 2:
            self.send(self.chip.at[2, self.second], self.from_y.at[1], self.along)

    def send(self, source, target, to):
        index = 4 + len(self.sends)
        self.sends.append(
            push(source, target, self.send_sem.at[index], self.recv_sem.at[index], to)
        )

    def turn(self):
        self.sends[0].wait_recv()
        add_into(self.chip.at[2, self.first], self.from_x.at[0])
        self.send(self.chip.at[2, self.first], self.last.at[0], self.along)
        self.sends[1].wait_recv()
        add_into(self.chip.at[1, self.second], self.from_y.at[0])
        self.send(self.chip.at[1, self.second], self.last.at[1], self.across)

    def finish(self, out_ref):
        self.sends[2].wait_recv()
        add_into(self.chip.at[3, self.first], self.from_x.at[1])
        self.sends[3].wait_recv()
        add_into(self.chip.at[3, self.second], self.from_y.at[1])
        self.sends[4].wait_recv()
        add_into(self.chip.at[3, self.first], self.last.at[0])
        self.sends[5].wait_recv()
        add_into(self.chip.at[3, self.second], self.last.at[1])
        if out_ref is not None:
            out_ref[...] = self.chip[3]
        for copy in self.pair[2:] + self.sends:
            copy.wait_send()


def add_into(target, other):
    rows = target.shape[0]
    step = 32 if rows % 32 == 0 else 16

    def some_rows(r, carry):
        piece = pl.ds(pl.multiple_of(r * step, step), step)
        target[piece, :] = (
            target[piece, :].astype(jnp.float32) + other[piece, :].astype(jnp.float32)
        ).astype(jnp.bfloat16)
        return carry

    lax.fori_loop(0, rows // step, some_rows, 0)


class LineSums:

    def __init__(self, plane, parts, arrived, own, last, held, send_sem, recv_sem, load_sem):
        self.plane, self.parts, self.arrived = plane, parts, arrived
        self.own, self.last, self.held = own, last, held
        self.send_sem, self.recv_sem, self.load_sem = send_sem, recv_sem, load_sem
        self.rows = own.shape[0]

    def part(self, way, item, b):
        place = b if way == 0 else 3 - b
        return self.parts.at[pl.ds((item * 4 + place) * self.rows, self.rows)]

    def message(self, way, turn, a, source):
        to = a + 1 if way == 0 else 2 - a
        return pltpu.make_async_remote_copy(
            src_ref=source,
            dst_ref=self.arrived.at[way * 12 + turn],
            send_sem=self.send_sem.at[way * 12 + turn],
            recv_sem=self.recv_sem.at[way * 12 + turn],
            device_id=z_place(to),
            device_id_type=DEVICE_MESH,
        )

    def origin(self, way, turn):
        item, t = divmod(turn, 3)
        return self.message(way, turn, 0, self.part(way, item, 3 - t))

    def slot(self, way, a, turn):
        item, t = divmod(turn, 3)
        return way * 2 + (item * (3 - a) + t) % 2

    def relay(self, way, turn, a):
        return self.message(way, turn, a, self.held.at[self.slot(way, a, turn)])

    def start(self):
        for place in (0, 3):

            @pl.when(self.plane == place)
            def _():
                way = 0 if place == 0 else 1
                self.origin(way, 0).start()
                self.origin(way, 1).start()

    def load(self, source, target, index):
        return pltpu.make_async_copy(source, target, self.load_sem.at[index])

    def service(self, sigma):
        for place in range(4):

            @pl.when(self.plane == place)
            def _():
                for way in (0, 1):
                    a = place if way == 0 else 3 - place
                    if a == 0:
                        if sigma < 12:
                            self.origin(way, sigma).wait_send()
                        if sigma + 2 < 12:
                            self.origin(way, sigma + 2).start()
                        continue
                    turn = sigma - a + 1
                    if turn < 0 or turn >= 12:
                        continue
                    item, t = divmod(turn, 3)
                    b = 3 - t
                    if b < a:
                        continue
                    if b > a:
                        slot = self.slot(way, a, turn)
                        sent = [
                            earlier
                            for earlier in range(turn)
                            if 3 - earlier % 3 > a and self.slot(way, a, earlier) == slot
                        ]
                        if sent:
                            self.relay(way, sent[-1], a).wait_send()
                        target = self.held.at[slot]
                        mine = self.load(self.part(way, item, b), self.own, 0)
                        mine.start()
                        self.relay(way, turn, a).wait_recv()
                        came = self.load(self.arrived.at[way * 12 + turn], target, 1)
                        came.start()
                        mine.wait()
                        came.wait()
                        add_into(target, self.own)
                        self.relay(way, turn, a).start()
                    else:
                        self.message(way, turn, a - 1, self.own).wait_recv()
                        came = self.load(self.arrived.at[way * 12 + turn], self.last.at[way], 1)
                        came.start()
                        came.wait()
                if sigma % 3 == 2:
                    item = sigma // 3
                    mine = self.load(self.part(0, item, place), self.own, 0)
                    mine.start()
                    mine.wait()

    def drain(self):
        for place in range(4):

            @pl.when(self.plane == place)
            def _():
                for way in (0, 1):
                    a = place if way == 0 else 3 - place
                    if a == 0 or a == 3:
                        continue
                    for slot in (way * 2, way * 2 + 1):
                        sent = [
                            turn
                            for turn in range(12)
                            if 3 - turn % 3 > a and self.slot(way, a, turn) == slot
                        ]
                        self.relay(way, sent[-1], a).wait_send()


class LineSum:

    def __init__(self, plane, parts, arrived, own, last, held, send_sem, recv_sem, load_sem):
        self.plane, self.parts, self.arrived = plane, parts, arrived
        self.own, self.last, self.held = own, last, held
        self.send_sem, self.recv_sem, self.load_sem = send_sem, recv_sem, load_sem
        self.rows = own.shape[0]

    def part(self, way, b):
        place = b if way == 0 else 3 - b
        return self.parts.at[pl.ds(place * self.rows, self.rows)]

    def message(self, way, t, a, source):
        return pltpu.make_async_remote_copy(
            src_ref=source,
            dst_ref=self.arrived.at[way * 3 + t],
            send_sem=self.send_sem.at[way * 3 + t],
            recv_sem=self.recv_sem.at[way * 3 + t],
            device_id=z_place(a + 1 if way == 0 else 2 - a),
            device_id_type=DEVICE_MESH,
        )

    def origin(self, way, t):
        return self.message(way, t, 0, self.part(way, 3 - t))

    def relay(self, way, t, a):
        return self.message(way, t, a, self.held.at[t if a == 1 else 2])

    def start(self):
        for place in (0, 3):

            @pl.when(self.plane == place)
            def _():
                way = 0 if place == 0 else 1
                self.origin(way, 0).start()
                self.origin(way, 1).start()

    def load(self, source, target, index):
        copy = pltpu.make_async_copy(source, target, self.load_sem.at[index])
        copy.start()
        return copy

    def service(self, sigma):
        for place in range(4):

            @pl.when(self.plane == place)
            def _():
                for way in (0, 1):
                    a = place if way == 0 else 3 - place
                    if a == 0:
                        self.origin(way, sigma).wait_send()
                        if sigma == 0:
                            self.origin(way, 2).start()
                        continue
                    t = sigma - a + 1
                    if t < 0 or 3 - t < a:
                        continue
                    b = 3 - t
                    source = self.arrived.at[way * 3 + t]
                    if b > a:
                        relay = self.relay(way, t, a)
                        target = self.held.at[t if a == 1 else 2]
                        mine = self.load(self.part(way, b), self.own, 0)
                        relay.wait_recv()
                        came = self.load(source, target, 1)
                        mine.wait()
                        came.wait()
                        add_into(target, self.own)
                        relay.start()
                    else:
                        self.message(way, t, a - 1, self.own).wait_recv()
                        self.load(source, self.last.at[way], 1).wait()
                if sigma == 2:
                    self.load(self.part(0, place), self.own, 0).wait()

    def finish(self, target):
        step = 16

        def some_rows(r, carry):
            piece = pl.ds(pl.multiple_of(r * step, step), step)
            total = self.own[piece, :].astype(jnp.float32)
            total = total + self.last[0, piece, :].astype(jnp.float32)
            total = total + self.last[1, piece, :].astype(jnp.float32)
            target[piece, :] = total.astype(jnp.bfloat16)
            return carry

        lax.fori_loop(0, self.rows // step, some_rows, 0)
        for place in (1, 2):

            @pl.when(self.plane == place)
            def _():
                for way in (0, 1):
                    a = place if way == 0 else 3 - place
                    for t in range(3 - a):
                        self.relay(way, t, a).wait_send()


class LineGather:

    def __init__(self, plane, own, slot, send_sem, recv_sem, local_sem):
        self.plane, self.own, self.slot = plane, own, slot
        self.send_sem, self.recv_sem, self.local_sem = send_sem, recv_sem, local_sem

    def message(self, way, a, distance):
        origin = a - distance
        plane_of_origin = origin if way == 0 else 3 - origin
        target = self.slot(plane_of_origin)
        return pltpu.make_async_remote_copy(
            src_ref=self.own if distance == 0 else target,
            dst_ref=target,
            send_sem=self.send_sem.at[way * 3 + distance],
            recv_sem=self.recv_sem.at[way * 3 + distance],
            device_id=z_place(a + 1 if way == 0 else 2 - a),
            device_id_type=DEVICE_MESH,
        )

    def service(self, step):
        for place in range(4):

            @pl.when(self.plane == place)
            def _():
                if step == 0:
                    pltpu.make_async_copy(self.own, self.slot(place), self.local_sem).start()
                for way in (0, 1):
                    a = place if way == 0 else 3 - place
                    if step > a:
                        continue
                    if step > 0:
                        self.message(way, a - 1, step - 1).wait_recv()
                    if a < 3:
                        self.message(way, a, step).start()

    def finish(self):
        for place in range(4):

            @pl.when(self.plane == place)
            def _():
                pltpu.make_async_copy(self.own, self.slot(place), self.local_sem).wait()
                for way in (0, 1):
                    a = place if way == 0 else 3 - place
                    if a < 3:
                        for distance in range(a + 1):
                            self.message(way, a, distance).wait_send()


GAIN_ROW = (4, 1, 2, 3)


def norm_rows_back(x_buf, back, gain_ref, gain_grad_ref, item, extra, target):
    gain = gain_ref[pl.ds(GAIN_ROW[item], 1), :]
    rows, features = target.shape

    def some_rows(r, gain_sum):
        piece = pl.ds(pl.multiple_of(r * 16, 16), 16)
        x = x_buf[piece, :]
        inverse = lax.rsqrt(jnp.mean(x * x, axis=-1, keepdims=True) + epsilon)
        grad = back[piece, :].astype(jnp.float32)
        scaled = grad * gain
        mean = jnp.mean(scaled * x, axis=-1, keepdims=True)
        result = inverse * scaled - x * (inverse * inverse * inverse) * mean
        if extra is not None:
            result = result + extra[piece, :].astype(jnp.float32)
        target[piece, :] = result.astype(jnp.bfloat16)
        return gain_sum + jnp.sum(grad * x * inverse, axis=0, keepdims=True)

    gain_grad_ref[pl.ds(item, 1), :] = lax.fori_loop(
        0, rows // 16, some_rows, jnp.zeros((1, features), jnp.float32)
    )


def forward_kernel(
    length_ref,
    pack_ref,
    latest_ref,
    history_ref,
    select_ref,
    root_ref,
    cotangent_ref,
    w_up_ref,
    w_attn_ref,
    w_down_ref,
    w_out_ref,
    cos_ref,
    sin_ref,
    packed_ref,
    gain_ref,
    pre_ref,
    factor_ref,
    x_ref,
    normed_ref,
    grad_all_ref,
    hidden_ref,
    up_term_ref,
    down_sum_ref,
    full3_ref,
    gain_grad_ref,
    attn_columns,
    q_ref,
    k_ref,
    v_ref,
    out_grad_ref,
    kv_before_ref,
    part_ref,
    down_term_ref,
    arrived_ref,
    arrived_down_ref,
    normed3,
    grads,
    up_columns,
    up_grad,
    out_buf,
    side,
    chip,
    from_x,
    from_y,
    last,
    own,
    ends,
    held,
    x_buf,
    normed_buf,
    term_buf,
    grad_own,
    stream_own,
    mix_out_buf,
    dyn_got,
    gather_send,
    gather_recv,
    gather_local,
    scatter_send,
    scatter_recv,
    line_send,
    line_recv,
    line_load,
    swap_send,
    swap_recv,
    swap_local,
    out_sem,
    small_send,
    small_recv,
    dyn_send,
    dyn_recv,
    route_send,
    route_recv,
    block_sem,
    spread_send,
    spread_recv,
    sum_send,
    sum_recv,
    key_send,
    key_recv,
    ready_sem,
    *,
    micro_count,
    sequence_length,
):
    column = lax.axis_index("dp")
    plane = lax.axis_index("hist")
    rows, features = grad_own.shape
    total = 8 * rows
    share = w_up_ref.shape[0]
    ff_share = w_down_ref.shape[0]
    width = share
    tile = 256
    mix_rows = pack_ref.shape[0] - share - 32 + 8
    every_mask = (6, 7, 2, 3, 4, 5, 1)

    barrier = pltpu.get_barrier_semaphore()
    for mask in every_mask:
        pl.semaphore_signal(
            barrier, inc=1, device_id={"dp": partner(column, mask)}, device_id_type=DEVICE_MESH
        )
    for place in range(4):

        @pl.when(plane == place)
        def _():
            for p in range(4):
                if p != place:
                    pl.semaphore_signal(
                        barrier, inc=1, device_id=z_place(p), device_id_type=DEVICE_MESH
                    )

    pl.semaphore_wait(barrier, 10)

    def block_load(source, target, index):
        copy = pltpu.make_async_copy(source, target, block_sem.at[index])
        copy.start()
        return copy

    small_copies = [
        push(
            pack_ref,
            packed_ref.at[column],
            small_send.at[mask],
            small_recv.at[mask],
            partner(column, mask),
        )
        for mask in every_mask
    ]
    small_local = pltpu.make_async_copy(pack_ref, packed_ref.at[column], small_send.at[0])
    small_local.start()
    latest_loads = [
        block_load(latest_ref.at[pl.ds(q * rows, rows)], normed_buf.at[q], 8 + q) for q in range(4)
    ]

    my_rows = pl.ds(pl.multiple_of(column * share, 16), share)

    def up_piece(owner):
        return w_up_ref.at[:, pl.ds(pl.multiple_of(owner * ff_share, 128), ff_share)]

    up_local = pltpu.make_async_copy(up_piece(column), up_columns.at[my_rows], swap_local.at[0])
    up_local.start()
    up_swaps = [
        push(
            up_piece(partner(column, mask)),
            up_columns.at[my_rows],
            swap_send.at[mask],
            swap_recv.at[mask],
            partner(column, mask),
        )
        for mask in every_mask
    ]

    chunk = rows // micro_count

    def route_source(place, s):
        return cotangent_ref.at[pl.ds(s * chunk, chunk)]

    def route_copy(place, s, target_place, slot):
        return pltpu.make_async_remote_copy(
            src_ref=route_source(place, s),
            dst_ref=grad_own.at[pl.ds(slot * chunk, chunk)],
            send_sem=route_send.at[s],
            recv_sem=route_recv.at[slot],
            device_id=z_place(target_place),
            device_id_type=DEVICE_MESH,
        )

    def route_local(place, s, slot):
        return pltpu.make_async_copy(
            route_source(place, s), grad_own.at[pl.ds(slot * chunk, chunk)], route_recv.at[slot]
        )

    for place in range(4):

        @pl.when(plane == place)
        def _():
            for s in range(micro_count):
                target_place, slot = divmod(s * 4 + place, micro_count)
                if target_place == place:
                    route_local(place, s, slot).start()
                else:
                    route_copy(place, s, target_place, slot).start()

    block_order = (3, 0, 2, 1)

    def history_loads(i):
        p, h = block_order[i], i % 2
        return [
            block_load(
                history_ref.at[pl.ds((slot * 4 + p) * rows, rows)],
                normed3.at[pl.ds((h * 4 + slot) * rows, rows)],
                h * 4 + slot,
            )
            for slot in range(4)
        ]

    loads = [history_loads(0), history_loads(1)]
    zeros = jnp.zeros((16, features), jnp.bfloat16)

    def clear(r, carry):
        ends[0, pl.ds(pl.multiple_of(r * 16, 16), 16), :] = zeros
        ends[1, pl.ds(pl.multiple_of(r * 16, 16), 16), :] = zeros
        return carry

    lax.fori_loop(0, ends.shape[1] // 16, clear, 0)

    small_local.wait()
    for copy in small_copies:
        copy.wait_recv()
    for d in range(8):
        gains = packed_ref[d, pl.ds(share + 16, 16), :].astype(jnp.float32)
        gain_ref[:, pl.ds(d * share, share // 2)] = gains[:8]
        gain_ref[:, pl.ds(d * share + share // 2, share // 2)] = gains[8:]
        mix_out_buf[pl.ds(d * mix_rows, mix_rows), :] = packed_ref[
            d, pl.ds(share, 16), :
        ].astype(jnp.float32)[:mix_rows]
    for copy in latest_loads:
        copy.wait()
    for q in range(4):

        def norm_rows(r, carry):
            piece = pl.ds(pl.multiple_of(r * 16, 16), 16)
            x = normed_buf[q, piece, :].astype(jnp.float32)
            inverse = lax.rsqrt(jnp.mean(x * x, axis=-1, keepdims=True) + epsilon)
            normed_buf[q, piece, :] = (x * inverse * gain_ref[pl.ds(0, 1), :]).astype(jnp.bfloat16)
            return carry

        lax.fori_loop(0, rows // 16, norm_rows, 0)
        pre = None
        for d in range(8):
            term = matmul(normed_buf[q, :, d * share : (d + 1) * share], packed_ref[d, :share, :])
            pre = term if pre is None else pre + term
        pre_ref[pl.ds(q * rows, rows), :] = pre
    pre = pre_ref[...]
    act = 0.5 * pre * (1.0 + lax.erf(pre * (1.0 / math.sqrt(2.0))))
    dyn = precise(act[:, : 8 * mix_rows], mix_out_buf[...])
    dyn_columns = (jnp.transpose(dyn)[: 8 * mix_rows] * root_ref[pl.ds(0, 1), :]).astype(jnp.bfloat16)

    def dyn_copy(source_place, target_place):
        return pltpu.make_async_remote_copy(
            src_ref=dyn_got.at[source_place],
            dst_ref=dyn_got.at[source_place],
            send_sem=dyn_send.at[target_place],
            recv_sem=dyn_recv.at[source_place],
            device_id=z_place(target_place),
            device_id_type=DEVICE_MESH,
        )

    for place in range(4):

        @pl.when(plane == place)
        def _():
            dyn_got[place] = dyn_columns
            for p in range(4):
                if p != place:
                    dyn_copy(place, p).start()
            for p in range(4):
                if p != place:
                    dyn_copy(p, place).wait_recv()

    dyn_sum = dyn_got[0] + dyn_got[1] + dyn_got[2] + dyn_got[3]
    factor_ref[...] = lax.dot_general(
        dyn_sum, select_ref[...], contract_rows, preferred_element_type=jnp.float32
    )

    stores = [None, None]
    for i, p in enumerate(block_order):
        h = i % 2
        for copy in loads[i]:
            copy.wait()
        if stores[h] is not None:
            for copy in stores[h]:
                copy.wait()

        def mix_rows_of(r, carry):
            factors = factor_ref[pl.ds(pl.multiple_of(p * rows + r * 16, 16), 16), :]
            for lane in range(0, features, 512):
                slots = [
                    normed3[
                        pl.ds(pl.multiple_of((h * 4 + slot) * rows + r * 16, 16), 16),
                        lane : lane + 512,
                    ].astype(jnp.float32)
                    for slot in range(4)
                ]
                for item in range(4):
                    mixed = None
                    for slot in range(4):
                        one = item * 4 + slot
                        term = factors[:, one : one + 1] * slots[slot]
                        mixed = term if mixed is None else mixed + term
                    grads[
                        pl.ds(pl.multiple_of((h * 4 + item) * rows + r * 16, 16), 16),
                        lane : lane + 512,
                    ] = mixed.astype(jnp.bfloat16)
            return carry

        lax.fori_loop(0, rows // 16, mix_rows_of, 0)
        stores[h] = [
            pltpu.make_async_copy(
                grads.at[pl.ds((h * 4 + item) * rows, rows)],
                part_ref.at[pl.ds((item * 4 + p) * rows, rows)],
                block_sem.at[12 + h * 4 + item],
            )
            for item in range(4)
        ]
        for copy in stores[h]:
            copy.start()
        if i + 2 < 4:
            loads.append(history_loads(i + 2))
    for copies in stores:
        for copy in copies:
            copy.wait()

    block = pl.ds(0, rows)
    line = LineSums(
        plane,
        part_ref,
        arrived_ref,
        own.at[block],
        ends.at[:, block],
        held.at[:, block],
        line_send,
        line_recv,
        line_load,
    )
    line.start()
    for mask in (CORE, ACROSS_X, ACROSS_Y):
        pl.semaphore_signal(
            ready_sem, inc=1, device_id={"dp": partner(column, mask)}, device_id_type=DEVICE_MESH
        )

    def attn_piece(stream, owner):
        return w_attn_ref.at[stream, :, pl.ds(pl.multiple_of(owner * share, 128), share)]

    attn_swaps, attn_locals = [], []
    for stream in range(3):
        local = pltpu.make_async_copy(
            attn_piece(stream, column),
            attn_columns.at[stream, my_rows],
            swap_local.at[1 + stream],
        )
        local.start()
        attn_locals.append(local)
        for mask in every_mask:
            attn_swaps.append(
                push(
                    attn_piece(stream, partner(column, mask)),
                    attn_columns.at[stream, my_rows],
                    swap_send.at[8 * (stream + 1) + mask],
                    swap_recv.at[8 * (stream + 1) + mask],
                    partner(column, mask),
                )
            )

    def gather(index, own_rows, whole):
        return PlaneGatherSteps(
            column,
            own_rows,
            whole,
            gather_send.at[index],
            gather_recv.at[index],
            gather_local.at[index],
        )

    for place in range(4):

        @pl.when(plane == place)
        def _():
            for slot in range(micro_count):
                s, source_place = divmod(place * micro_count + slot, 4)
                if source_place == place:
                    route_local(place, s, slot).wait()
                else:
                    route_copy(source_place, s, place, slot).wait_recv()

    def mask_rows(r, carry):
        piece = pl.ds(pl.multiple_of(r * 16, 16), 16)
        row = plane * rows + r * 16 + lax.broadcasted_iota(jnp.int32, (16, 1), 0)
        limit = jnp.zeros((16, 1), jnp.int32)
        for m in range(micro_count):
            inside = (row >= m * sequence_length) & (row < (m + 1) * sequence_length)
            limit = jnp.where(inside, m * sequence_length + length_ref[m], limit)
        kept = jnp.where(row < limit, grad_own[piece, :].astype(jnp.float32), 0.0)
        grad_own[piece, :] = kept.astype(jnp.bfloat16)
        return carry

    lax.fori_loop(0, rows // 16, mask_rows, 0)
    pl.semaphore_wait(ready_sem, 3)
    grad_gather = gather(4, grad_own, grads)
    grad_gather.begin()

    x_copies = []

    def combine(item):
        if x_copies:
            x_copies[-1].wait()

        def some_rows(r, carry):
            piece = pl.ds(pl.multiple_of(r * 16, 16), 16)
            x = (
                own[piece, :].astype(jnp.float32)
                + ends[0, piece, :].astype(jnp.float32)
                + ends[1, piece, :].astype(jnp.float32)
            )
            x_buf[piece, :] = x
            inverse = lax.rsqrt(jnp.mean(x * x, axis=-1, keepdims=True) + epsilon)
            normed_buf[item, piece, :] = (
                x * inverse * gain_ref[pl.ds(GAIN_ROW[item], 1), :]
            ).astype(jnp.bfloat16)
            return carry

        lax.fori_loop(0, rows // 16, some_rows, 0)
        copy = pltpu.make_async_copy(x_buf, x_ref.at[item], out_sem.at[0])
        copy.start()
        x_copies.append(copy)
        steps = gather(
            item, normed_buf.at[item], normed3 if item == 0 else normed_ref.at[item - 1]
        )
        steps.begin()
        return steps

    line.service(0)
    line.service(1)
    line.service(2)
    gather3 = combine(0)
    grad_gather.corners()
    grad_gather.siblings()
    line.service(3)
    grad_gather.rest()
    gather3.corners()
    line.service(4)
    grad_gather.finish()
    grads_out = pltpu.make_async_copy(grads, grad_all_ref, out_sem.at[2])
    grads_out.start()
    gather3.siblings()
    gather3.rest()
    for copy in up_swaps:
        copy.wait_recv()
    up_local.wait()
    gather3.finish()

    def feed(first_block, count):
        def one_tile(step, carry):
            piece = pl.ds(pl.multiple_of((step // (ff_share // tile)) * rows, 16), rows)
            lanes = pl.ds(pl.multiple_of((step % (ff_share // tile)) * tile, tile), tile)
            up = jnp.dot(normed3[piece, :], up_columns[:, lanes], preferred_element_type=jnp.float32)
            spread = 0.5 * (1.0 + lax.erf(up * (1.0 / math.sqrt(2.0))))
            hidden_ref[piece, lanes] = (up * spread).astype(jnp.bfloat16)
            slope = spread + up * jnp.exp(-0.5 * up * up) * (1.0 / math.sqrt(2.0 * math.pi))
            hidden_grad = lax.dot_general(
                grads[piece, :],
                w_down_ref[lanes, :],
                contract_cols,
                preferred_element_type=jnp.float32,
            )
            up_grad[piece, lanes] = (hidden_grad * slope).astype(jnp.bfloat16)
            return carry

        per_block = ff_share // tile
        lax.fori_loop(first_block * per_block, (first_block + count) * per_block, one_tile, 0)

    def back_product(owner, target):
        left_rows = pl.ds(pl.multiple_of(owner * rows, 16), rows)

        def one_tile(t, carry):
            lanes = pl.ds(pl.multiple_of(t * 2 * tile, 2 * tile), 2 * tile)
            target[:, lanes] = lax.dot_general(
                up_grad[left_rows, :],
                up_columns[lanes, :],
                contract_cols,
                preferred_element_type=jnp.float32,
            ).astype(jnp.bfloat16)
            return carry

        lax.fori_loop(0, features // (2 * tile), one_tile, 0)

    term_slots = 2
    part = share // 4

    def term_copies(kind, slot, index):
        if kind == 0:
            return [
                pltpu.make_async_copy(
                    term_buf.at[slot, pl.ds(h * part, part), pl.ds(0, ff_share)],
                    up_term_ref.at[
                        pl.ds(h * 4 * part + index % 4 * part, part),
                        pl.ds(index // 4 * ff_share, ff_share),
                    ],
                    out_sem.at[3 + 4 * slot + h],
                )
                for h in range(4)
            ]
        return [
            pltpu.make_async_copy(
                term_buf.at[slot],
                down_term_ref.at[pl.ds(index * tile, tile)],
                out_sem.at[3 + 4 * slot],
            )
        ]

    def terms(kind, first, count):
        term_width = ff_share if kind == 0 else features
        pending = []
        for index in range(first, first + count):
            slot = index % term_slots
            if len(pending) >= term_slots:
                for copy in pending[-term_slots]:
                    copy.wait()

            def one_tile(t, carry):
                lanes = pl.ds(pl.multiple_of(t * 2 * tile, 2 * tile), 2 * tile)
                if kind == 0:
                    left, right = normed3[:, index * tile : (index + 1) * tile], up_grad[:, lanes]
                else:
                    left, right = hidden_ref[:, index * tile : (index + 1) * tile], grads[:, lanes]
                term_buf[slot, :, lanes] = lax.dot_general(
                    left, right, contract_rows, preferred_element_type=jnp.float32
                ).astype(jnp.bfloat16)
                return carry

            lax.fori_loop(0, term_width // (2 * tile), one_tile, 0)
            copies = term_copies(kind, slot, index)
            for copy in copies:
                copy.start()
            pending.append(copies)
        for copies in pending[-term_slots:]:
            for copy in copies:
                copy.wait()

    def project(stream, target):
        def one_block(b, carry):
            piece = pl.ds(pl.multiple_of(b * rows, 16), rows)
            value = matmul(normed3[piece, :], attn_columns[stream])
            if stream < 2:
                parts = []
                for head in range(width // HEAD_DIM):
                    one = value[:, head * HEAD_DIM : (head + 1) * HEAD_DIM]
                    swapped = jnp.concatenate(
                        [one[:, HEAD_DIM // 2 :], one[:, : HEAD_DIM // 2]], axis=1
                    )
                    parts.append(one * cos_ref[...] + swapped * sin_ref[...])
                value = jnp.concatenate(parts, axis=1)
            target[piece, :] = value.astype(jnp.bfloat16)
            return carry

        lax.fori_loop(0, 8, one_block, 0)

    def out_grads(b, carry):
        piece = pl.ds(pl.multiple_of(b * rows, 16), rows)
        out_grad_ref[piece, :] = lax.dot_general(
            grads[piece, :], w_out_ref[...], contract_cols, preferred_element_type=jnp.float32
        ).astype(jnp.bfloat16)
        return carry

    def key_copy(i, place):
        return pltpu.make_async_remote_copy(
            src_ref=(k_ref, v_ref)[i],
            dst_ref=kv_before_ref.at[:, pl.ds(i * width, width)],
            send_sem=key_send.at[i],
            recv_sem=key_recv.at[i],
            device_id=z_place(place + 1),
            device_id_type=DEVICE_MESH,
        )

    def send_keys(i):
        for place in range(3):

            @pl.when(plane == place)
            def _():
                key_copy(i, place).start()

    feed(0, 2)
    line.service(5)
    gather0 = combine(1)
    feed(2, 3)
    gather0.corners()
    line.service(6)
    feed(5, 2)
    gather0.siblings()
    line.service(7)
    feed(7, 1)
    gather0.rest()
    scatter = PlaneScatterSteps(
        column,
        back_product,
        (out_buf, side, chip, from_x, from_y, last),
        scatter_send,
        scatter_recv,
    )
    scatter.block(0)
    scatter.block(1)
    line.service(8)
    gather1 = combine(2)
    scatter.block(2)
    scatter.block(3)
    gather0.finish()
    scatter.turn()
    terms(1, 0, 2)
    gather1.corners()
    line.service(9)
    scatter.finish(None)
    x_copies[-1].wait()
    x_load = pltpu.make_async_copy(x_ref.at[0], x_buf, out_sem.at[1])
    x_load.start()
    x_load.wait()
    norm_rows_back(x_buf, chip.at[3], gain_ref, gain_grad_ref, 0, grad_own, stream_own)
    x_copies.clear()
    spread3 = LineGather(
        plane,
        stream_own,
        lambda p: full3_ref.at[pl.ds(p * rows, rows)],
        spread_send,
        spread_recv,
        out_sem.at[11],
    )
    spread3.service(0)
    gather1.siblings()
    terms(1, 2, ff_share // tile - 2)
    gather1.rest()
    down_line = LineSum(
        plane, down_term_ref, arrived_down_ref, own, ends, held, sum_send, sum_recv, line_load
    )
    line.service(10)
    spread3.service(1)
    down_line.start()
    terms(0, 0, 2)
    spread3.service(2)
    line.service(11)
    gather2 = combine(3)
    terms(0, 2, features // tile - 2)
    spread3.service(3)
    line.drain()
    gather1.finish()
    for copy in attn_swaps:
        copy.wait_recv()
    for copy in attn_locals:
        copy.wait()
    load = block_load(normed_ref.at[1], normed3, 0)
    gather2.corners()
    load.wait()
    project(1, k_ref)
    send_keys(0)
    down_line.service(0)
    load = block_load(normed_ref.at[0], normed3, 0)
    gather2.siblings()
    gather2.rest()
    load.wait()
    project(0, q_ref)
    gather2.finish()
    load = block_load(normed_ref.at[2], normed3, 0)
    lax.fori_loop(0, 8, out_grads, 0)
    load.wait()
    project(2, v_ref)
    send_keys(1)
    down_line.service(1)
    for copy in small_copies + up_swaps + attn_swaps:
        copy.wait_send()
    grads_out.wait()
    x_copies[-1].wait()
    for place in range(4):

        @pl.when(plane == place)
        def _():
            for p in range(4):
                if p != place:
                    dyn_copy(place, p).wait_send()
            for s in range(micro_count):
                target_place, slot = divmod(s * 4 + place, micro_count)
                if target_place != place:
                    route_copy(place, s, target_place, slot).wait_send()

    down_line.service(2)
    down_line.finish(down_sum_ref)
    spread3.finish()
    for place in range(4):

        @pl.when(plane == place)
        def _():
            for i in range(2):
                if place > 0:
                    key_copy(i, place - 1).wait_recv()
                if place < 3:
                    key_copy(i, place).wait_send()


def forward_and_feed(
    lengths,
    pack,
    latest,
    history,
    select,
    root,
    cotangent,
    w_up,
    w_attn,
    w_down,
    w_out,
    cosine,
    sine_part,
    sequence_length,
):
    rows, features = cotangent.shape
    micro_count = lengths.shape[0]
    total = 8 * rows
    share = w_up.shape[0]
    ff_share = w_down.shape[0]
    mix_width = select.shape[0]
    block = (rows, features)
    piece = (4 * (share // 4), features)
    half = (2, rows // 2, features)
    anywhere = pl.BlockSpec(memory_space=pl.ANY)
    near = pl.BlockSpec(memory_space=pltpu.VMEM)
    shape = jax.ShapeDtypeStruct
    low_type = jnp.bfloat16
    some = lambda *dims: pltpu.VMEM(dims, low_type)
    wide = lambda *dims: pltpu.VMEM(dims, jnp.float32)
    dma = pltpu.SemaphoreType.DMA
    outputs = [
        (near, shape((8,) + pack.shape, low_type)),
        (near, shape((8, features), jnp.float32)),
        (near, shape((4 * rows, 128), jnp.float32)),
        (near, shape((4 * rows, 128), jnp.float32)),
        (anywhere, shape((4,) + block, jnp.float32)),
        (anywhere, shape((3, total, features), low_type)),
        (anywhere, shape((total, features), low_type)),
        (near, shape((total, ff_share), low_type)),
        (anywhere, shape((ff_share, features), low_type)),
        (near, shape(piece, low_type)),
        (anywhere, shape((4 * rows, features), low_type)),
        (near, shape((8, features), jnp.float32)),
        (near, shape((3, features, share), low_type)),
        (near, shape((total, share), low_type)),
        (near, shape((total, share), low_type)),
        (near, shape((total, share), low_type)),
        (near, shape((total, share), low_type)),
        (anywhere, shape((total, 2 * share), low_type)),
        (anywhere, shape((16 * rows, features), low_type)),
        (anywhere, shape((ff_share, features), low_type)),
        (anywhere, shape((24,) + block, low_type)),
        (anywhere, shape((6,) + piece, low_type)),
    ]
    return pl.pallas_call(
        functools.partial(
            forward_kernel, micro_count=micro_count, sequence_length=sequence_length
        ),
        in_specs=[pl.BlockSpec(memory_space=pltpu.SMEM), near, anywhere, anywhere]
        + [near, near, anywhere, anywhere, anywhere]
        + [near] * 4,
        out_specs=[spec for spec, _ in outputs],
        out_shape=[out for _, out in outputs],
        scratch_shapes=[
            some(total, features),
            some(total, features),
            some(features, ff_share),
            some(total, ff_share),
            some(2, *block),
            some(4, *block),
            some(4, *block),
            some(*half),
            some(*half),
            some(*half),
            some(*piece),
            some(2, *piece),
            some(4, *piece),
            wide(*block),
            some(4, *block),
            some(2, 256, features),
            some(*block),
            some(*block),
            wide(mix_width, 128),
            some(4, mix_width, 4 * rows),
            dma((5, 11)),
            dma((5, 11)),
            dma((5,)),
            dma((10,)),
            dma((10,)),
            dma((24,)),
            dma((24,)),
            dma((2,)),
            dma((32,)),
            dma((32,)),
            dma((4,)),
            dma((12,)),
            dma((8,)),
            dma((8,)),
            dma((4,)),
            dma((4,)),
            dma((micro_count,)),
            dma((micro_count,)),
            dma((20,)),
            dma((6,)),
            dma((6,)),
            dma((6,)),
            dma((6,)),
            dma((2,)),
            dma((2,)),
            pltpu.SemaphoreType.REGULAR,
        ],
        compiler_params=pltpu.CompilerParams(
            collective_id=5, has_side_effects=True, vmem_limit_bytes=63 * 1024 * 1024
        ),
        cost_estimate=pl.CostEstimate(
            flops=12 * total * features * ff_share,
            bytes_accessed=600 * 1000 * 1000,
            transcendentals=0,
        ),
    )(
        lengths,
        pack,
        latest,
        history,
        select,
        root,
        cotangent,
        w_up,
        w_attn,
        w_down,
        w_out,
        cosine,
        sine_part,
    )


def small_sum_kernel(parts_ref, out_ref, got, sums, send_sem, recv_sem, z_send, z_recv):
    column = lax.axis_index("dp")
    plane = lax.axis_index("hist")
    every_mask = (6, 7, 2, 3, 4, 5, 1)
    barrier = pltpu.get_barrier_semaphore()
    for mask in every_mask:
        pl.semaphore_signal(
            barrier, inc=1, device_id={"dp": partner(column, mask)}, device_id_type=DEVICE_MESH
        )
    for place in range(4):

        @pl.when(plane == place)
        def _():
            for p in range(4):
                if p != place:
                    pl.semaphore_signal(
                        barrier, inc=1, device_id=z_place(p), device_id_type=DEVICE_MESH
                    )

    pl.semaphore_wait(barrier, 10)
    copies = [
        push(
            parts_ref.at[partner(column, mask)],
            got.at[mask],
            send_sem.at[mask],
            recv_sem.at[mask],
            partner(column, mask),
        )
        for mask in every_mask
    ]
    total = parts_ref[column].astype(jnp.float32)
    for mask, copy in zip(every_mask, copies):
        copy.wait_recv()
        total = total + got[mask].astype(jnp.float32)

    def line_copy(source_place, target_place):
        return pltpu.make_async_remote_copy(
            src_ref=sums.at[source_place],
            dst_ref=sums.at[source_place],
            send_sem=z_send.at[target_place],
            recv_sem=z_recv.at[source_place],
            device_id=z_place(target_place),
            device_id_type=DEVICE_MESH,
        )

    for place in range(4):

        @pl.when(plane == place)
        def _():
            others = [p for p in range(4) if p != place]
            sums[place] = total.astype(jnp.bfloat16)
            for p in others:
                line_copy(place, p).start()
            for p in others:
                line_copy(p, place).wait_recv()
            for p in others:
                line_copy(place, p).wait_send()

    out_ref[...] = (sums[0].astype(jnp.float32) + sums[1].astype(jnp.float32)) + (
        sums[2].astype(jnp.float32) + sums[3].astype(jnp.float32)
    )
    for copy in copies:
        copy.wait_send()


def small_sums(parts):
    dims = parts.shape[1:]
    dma = pltpu.SemaphoreType.DMA
    return pl.pallas_call(
        small_sum_kernel,
        out_shape=jax.ShapeDtypeStruct(dims, jnp.float32),
        in_specs=[pl.BlockSpec(memory_space=pltpu.VMEM)],
        out_specs=pl.BlockSpec(memory_space=pltpu.VMEM),
        scratch_shapes=[
            pltpu.VMEM((8,) + dims, jnp.bfloat16),
            pltpu.VMEM((4,) + dims, jnp.bfloat16),
            dma((8,)),
            dma((8,)),
            dma((4,)),
            dma((4,)),
        ],
        compiler_params=pltpu.CompilerParams(collective_id=7, has_side_effects=True),
        cost_estimate=pl.CostEstimate(
            flops=0, bytes_accessed=40 * 1000 * 1000, transcendentals=0
        ),
    )(parts)


def line_share_kernel(own_ref, all_ref, send_sem, recv_sem):
    plane = lax.axis_index("hist")
    barrier = pltpu.get_barrier_semaphore()
    for place in range(4):

        @pl.when(plane == place)
        def _():
            for p in range(4):
                if p != place:
                    pl.semaphore_signal(
                        barrier, inc=1, device_id=z_place(p), device_id_type=DEVICE_MESH
                    )

    pl.semaphore_wait(barrier, 3)

    def line_copy(source_place, target_place):
        return pltpu.make_async_remote_copy(
            src_ref=own_ref,
            dst_ref=all_ref.at[source_place],
            send_sem=send_sem.at[target_place],
            recv_sem=recv_sem.at[source_place],
            device_id=z_place(target_place),
            device_id_type=DEVICE_MESH,
        )

    for place in range(4):

        @pl.when(plane == place)
        def _():
            others = [p for p in range(4) if p != place]
            for p in others:
                line_copy(place, p).start()
            all_ref[place] = own_ref[...]
            for p in others:
                line_copy(p, place).wait_recv()
            for p in others:
                line_copy(place, p).wait_send()


def line_share(own):
    dma = pltpu.SemaphoreType.DMA
    return pl.pallas_call(
        line_share_kernel,
        out_shape=jax.ShapeDtypeStruct((4,) + own.shape, own.dtype),
        in_specs=[pl.BlockSpec(memory_space=pltpu.VMEM)],
        out_specs=pl.BlockSpec(memory_space=pltpu.VMEM),
        scratch_shapes=[dma((4,)), dma((4,))],
        compiler_params=pltpu.CompilerParams(collective_id=8, has_side_effects=True),
        cost_estimate=pl.CostEstimate(
            flops=0, bytes_accessed=20 * 1000 * 1000, transcendentals=0
        ),
    )(own)


def attend_column(
    column,
    plane,
    length_ref,
    cosine,
    sine_part,
    q_ref,
    k_ref,
    v_ref,
    kv_before_ref,
    out_grad_ref,
    att_ref,
    q_grad_ref,
    kv_grad_ref,
    kv_before_grad_ref,
    rows,
    micro_count,
    sequence_length,
):
    here = pl.ds(pl.multiple_of(column * rows, 16), rows)
    width = q_ref.shape[1]
    scale = 1.0 / math.sqrt(HEAD_DIM)
    row = plane * rows + lax.broadcasted_iota(jnp.int32, (rows, 1), 0)
    start = jnp.zeros((rows, 1), jnp.int32)
    limit = jnp.zeros((rows, 1), jnp.int32)
    for m in range(micro_count):
        inside = (row >= m * sequence_length) & (row < (m + 1) * sequence_length)
        start = jnp.where(inside, m * sequence_length, start)
        limit = jnp.where(inside, m * sequence_length + length_ref[column * micro_count + m], limit)
    limit = jnp.minimum(limit, row + 1)
    key_row = (plane - 1) * rows + lax.broadcasted_iota(jnp.int32, (1, 2 * rows), 1)
    allowed = (key_row >= start) & (key_row < limit)
    for head in range(width // HEAD_DIM):
        lanes = slice(head * HEAD_DIM, (head + 1) * HEAD_DIM)
        value_lanes = slice(width + head * HEAD_DIM, width + (head + 1) * HEAD_DIM)
        query = q_ref[here, lanes]
        keys = jnp.concatenate([kv_before_ref[here, lanes], k_ref[here, lanes]], axis=0)
        values = jnp.concatenate([kv_before_ref[here, value_lanes], v_ref[here, lanes]], axis=0)
        out_grad = out_grad_ref[here, lanes]
        scores = (
            lax.dot_general(query, keys, contract_cols, preferred_element_type=jnp.float32) * scale
        )
        scores = jnp.where(allowed, scores, masked_out)
        raised = jnp.exp(scores - jnp.max(scores, axis=-1, keepdims=True))
        weights = raised / jnp.sum(raised, axis=-1, keepdims=True)
        weights_low = weights.astype(jnp.bfloat16)
        att_ref[here, lanes] = matmul(weights_low, values).astype(jnp.bfloat16)
        weight_grad = lax.dot_general(
            out_grad, values, contract_cols, preferred_element_type=jnp.float32
        )
        inner = jnp.sum(weights * weight_grad, axis=-1, keepdims=True)
        score_grad = (weights * (weight_grad - inner) * scale).astype(jnp.bfloat16)
        query_grad = matmul(score_grad, keys)
        swapped = jnp.concatenate(
            [query_grad[:, HEAD_DIM // 2 :], query_grad[:, : HEAD_DIM // 2]], axis=1
        )
        q_grad_ref[here, lanes] = (query_grad * cosine - swapped * sine_part).astype(jnp.bfloat16)
        key_grad = lax.dot_general(
            score_grad, query, contract_rows, preferred_element_type=jnp.float32
        )
        value_grad = lax.dot_general(
            weights_low, out_grad, contract_rows, preferred_element_type=jnp.float32
        )
        kv_before_grad_ref[here, lanes] = key_grad[:rows].astype(jnp.bfloat16)
        kv_before_grad_ref[here, value_lanes] = value_grad[:rows].astype(jnp.bfloat16)
        kv_grad_ref[here, lanes] = key_grad[rows:]
        kv_grad_ref[here, value_lanes] = value_grad[rows:]


def backward_kernel(
    length_ref,
    cos_ref,
    sin_ref,
    q_ref,
    k_ref,
    v_ref,
    out_grad_ref,
    normed_ref,
    grad_all_ref,
    hidden_ref,
    w_out_ref,
    w_down_ref,
    attn_columns_ref,
    x_ref,
    gain_ref,
    down_own,
    up_term_ref,
    kv_ref,
    full_ref,
    down_all_ref,
    up_all_ref,
    quarter_ref,
    branch_ref,
    gain_grad_ref,
    attn_parts_ref,
    arrived_ref,
    big,
    att,
    q_grad,
    kv_grad,
    kv_before,
    kv_before_grad,
    kv_after,
    out_buf,
    side,
    chip,
    from_x,
    from_y,
    last,
    line_own,
    line_ends,
    line_held,
    up_sum,
    up_own,
    stream_own,
    back_buf,
    x_buf,
    stage,
    scatter_send,
    scatter_recv,
    sum_send,
    sum_recv,
    load_sem,
    spread_send,
    spread_recv,
    spread_local,
    key_send,
    key_recv,
    swap_send,
    swap_recv,
    local_sem,
    *,
    micro_count,
    sequence_length,
):
    column = lax.axis_index("dp")
    plane = lax.axis_index("hist")
    total, width = q_ref.shape
    rows, features = total // 8, w_down_ref.shape[1]
    ff_share = w_down_ref.shape[0]
    quarter = features // 8 // 4
    k_grad, v_grad, attn_sum = q_grad, att, up_sum
    tile = 512

    barrier = pltpu.get_barrier_semaphore()
    for mask in range(1, 8):
        pl.semaphore_signal(
            barrier, inc=1, device_id={"dp": partner(column, mask)}, device_id_type=DEVICE_MESH
        )
    for place in range(4):

        @pl.when(plane == place)
        def _():
            nearby = [p for p in (place - 1, place + 1) if 0 <= p < 4]
            for p in nearby:
                pl.semaphore_signal(
                    barrier, inc=1, device_id=z_place(p), device_id_type=DEVICE_MESH
                )
            pl.semaphore_wait(barrier, 7 + len(nearby))

    def back_copy(place):
        return pltpu.make_async_remote_copy(
            src_ref=kv_before_grad,
            dst_ref=kv_after,
            send_sem=key_send.at[0],
            recv_sem=key_recv.at[0],
            device_id=z_place(place - 1),
            device_id_type=DEVICE_MESH,
        )

    def clear(target):
        step = 64

        def some_rows(r, carry):
            target[pl.ds(pl.multiple_of(r * step, step), step), :] = jnp.zeros(
                (step, target.shape[1]), jnp.bfloat16
            )
            return carry

        lax.fori_loop(0, target.shape[0] // step, some_rows, 0)

    line_sums = [
        LineSum(
            plane,
            parts,
            arrived_ref.at[pl.ds(6 * i, 6)],
            line_own,
            line_ends,
            line_held,
            sum_send.at[i],
            sum_recv.at[i],
            load_sem,
        )
        for i, parts in enumerate((up_term_ref, attn_parts_ref))
    ]
    up_line, attn_line = line_sums

    def spread(index, own, slot):
        return LineGather(
            plane, own, slot, spread_send.at[index], spread_recv.at[index], spread_local.at[index]
        )

    def stream_spread(item):
        return spread(
            item,
            stream_own.at[item - 1],
            lambda p: full_ref.at[pl.ds(((item - 1) * 4 + p) * rows, rows)],
        )

    def norm_back(item, back):
        load = pltpu.make_async_copy(x_ref.at[item], x_buf, local_sem.at[0])
        load.start()
        load.wait()
        norm_rows_back(
            x_buf, back, gain_ref, gain_grad_ref, item, None, stream_own.at[item - 1]
        )

    def scatter_of(product, index):
        return PlaneScatterSteps(
            column,
            product,
            (out_buf, side, chip)
            + tuple(arriving.at[pl.ds(2 * (index % 2), 2)] for arriving in (from_x, from_y, last)),
            scatter_send.at[index],
            scatter_recv.at[index],
        )

    def projection_product(stream, grad):
        def product(owner, target):
            left = pl.ds(pl.multiple_of(owner * rows, 16), rows)

            def one_tile(t, carry):
                lanes = pl.ds(pl.multiple_of(t * tile, tile), tile)
                target[:, lanes] = lax.dot_general(
                    grad[left, :],
                    attn_columns_ref[stream, lanes, :],
                    contract_cols,
                    preferred_element_type=jnp.float32,
                ).astype(jnp.bfloat16)
                return carry

            lax.fori_loop(0, features // tile, one_tile, 0)

        return product

    def branch_product(owner, target):
        left = pl.ds(pl.multiple_of(owner * rows, 16), rows)

        def one_tile(t, carry):
            lanes = pl.ds(pl.multiple_of(t * tile, tile), tile)
            target[:, lanes] = (
                matmul(att[left, :], w_out_ref[:, lanes])
                + matmul(hidden_ref[left, :], w_down_ref[:, lanes])
            ).astype(jnp.bfloat16)
            return carry

        lax.fori_loop(0, features // tile, one_tile, 0)

    def attend(first, count):
        def one_column(m, carry):
            attend_column(
                m,
                plane,
                length_ref,
                cos_ref[...],
                sin_ref[...],
                q_ref,
                k_ref,
                v_ref,
                kv_before,
                out_grad_ref,
                att,
                q_grad,
                kv_grad,
                kv_before_grad,
                rows,
                micro_count,
                sequence_length,
            )
            return carry

        lax.fori_loop(first, first + count, one_column, 0)

    def part_copies(first_row):
        return [
            pltpu.make_async_copy(
                stage.at[pl.ds(p * quarter, quarter)],
                attn_parts_ref.at[pl.ds(p * 4 * quarter + first_row, quarter)],
                local_sem.at[4 + p],
            )
            for p in range(4)
        ]

    def load_big(source):
        copy = pltpu.make_async_copy(source, big, local_sem.at[2])
        copy.start()
        return copy

    def attn_term(stream, grad):
        def one_owner(d, carry):
            lanes = pl.ds(pl.multiple_of(d * width, width), width)
            stage[:, lanes] = lax.dot_general(
                big[:, lanes], grad[...], contract_rows, preferred_element_type=jnp.float32
            ).astype(jnp.bfloat16)
            return carry

        lax.fori_loop(0, 8, one_owner, 0)
        copies = part_copies(stream * quarter)
        for copy in copies:
            copy.start()
        return copies

    def out_term():
        def one_tile(t, carry):
            lanes = pl.ds(pl.multiple_of(t * tile, tile), tile)
            stage[:, lanes] = lax.dot_general(
                att[...], big[:, lanes], contract_rows, preferred_element_type=jnp.float32
            ).astype(jnp.bfloat16)
            return carry

        lax.fori_loop(0, features // tile, one_tile, 0)
        copies = part_copies(3 * quarter)
        for copy in copies:
            copy.start()
        return copies

    def swap(kind):
        copies = []
        for mask in (6, 7, 2, 3, 4, 5, 1):
            owner = partner(column, mask)
            if kind == 0:
                source, target = up_piece(owner), up_target()
            else:
                source, target = attn_piece(owner), attn_target()
            copies.append(
                push(
                    source,
                    target,
                    swap_send.at[8 * kind + mask],
                    swap_recv.at[8 * kind + mask],
                    owner,
                )
            )
        if kind == 0:
            source, target = up_piece(column), up_target()
        else:
            source, target = attn_piece(column), attn_target()
        local = pltpu.make_async_copy(source, target, local_sem.at[3])
        local.start()
        return copies, local

    def up_piece(owner):
        return up_sum.at[
            pl.ds(pl.multiple_of(lax.rem(owner, 4) * quarter, 16), quarter),
            pl.ds(pl.multiple_of(lax.div(owner, 4) * ff_share, 128), ff_share),
        ]

    def up_target():
        return up_own.at[:, pl.ds(pl.multiple_of(column * ff_share, 128), ff_share)]

    def attn_piece(owner):
        return attn_sum.at[
            pl.ds(0, 3 * quarter), pl.ds(pl.multiple_of(owner * width, 128), width)
        ]

    def attn_target():
        return quarter_ref.at[
            pl.ds(0, 3 * quarter), pl.ds(pl.multiple_of(column * width, 128), width)
        ]

    def swapped_in(swapping):
        copies, local = swapping
        for copy in copies:
            copy.wait_recv()
        local.wait()
        for copy in copies:
            copy.wait_send()

    up_line.start()
    down_spread = spread(4, down_own, lambda p: down_all_ref.at[pl.ds(p * 4 * quarter, 4 * quarter)])
    down_spread.service(0)
    kv_load = pltpu.make_async_copy(kv_ref, kv_before, local_sem.at[0])

    @pl.when(plane == 0)
    def _():
        clear(kv_before)
        clear(line_ends.at[0])

    @pl.when(plane > 0)
    def _():
        kv_load.start()
        kv_load.wait()

    @pl.when(plane == 3)
    def _():
        clear(kv_after)
        clear(line_ends.at[1])

    attend(0, 8)
    for place in range(1, 4):

        @pl.when(plane == place)
        def _():
            back_copy(place).start()

    loading = load_big(normed_ref.at[0])
    query_scatter = scatter_of(projection_product(0, q_grad), 0)
    query_scatter.block(0)
    query_scatter.block(1)
    up_line.service(0)
    query_scatter.block(2)
    query_scatter.block(3)
    down_spread.service(1)
    query_scatter.turn()
    loading.wait()
    parts_out = attn_term(0, q_grad)
    query_scatter.finish(back_buf)
    up_line.service(1)
    norm_back(1, back_buf)
    query_spread = stream_spread(1)
    query_spread.service(0)
    down_spread.service(2)
    for copy in parts_out:
        copy.wait()
    loading = load_big(grad_all_ref)
    branch_scatter = scatter_of(branch_product, 1)
    branch_scatter.block(0)
    branch_scatter.block(1)
    up_line.service(2)
    up_line.finish(up_sum)
    up_swap = swap(0)
    branch_scatter.block(2)
    down_spread.service(3)
    branch_scatter.block(3)
    query_spread.service(1)
    branch_scatter.turn()
    loading.wait()
    parts_out = out_term()
    branch_scatter.finish(branch_ref)
    swapped_in(up_swap)
    up_spread = spread(5, up_own, lambda p: up_all_ref.at[pl.ds(p * quarter, quarter)])
    up_spread.service(0)
    for copy in parts_out:
        copy.wait()
    loading = load_big(normed_ref.at[1])

    for place in range(3):

        @pl.when(plane == place)
        def _():
            back_copy(place + 1).wait_recv()

    def key_value(m, carry):
        here = pl.ds(pl.multiple_of(m * rows, 16), rows)
        for head in range(width // HEAD_DIM):
            lanes = slice(head * HEAD_DIM, (head + 1) * HEAD_DIM)
            value_lanes = slice(width + head * HEAD_DIM, width + (head + 1) * HEAD_DIM)
            grad = kv_grad[here, lanes] + kv_after[here, lanes].astype(jnp.float32)
            turned_half = jnp.concatenate(
                [grad[:, HEAD_DIM // 2 :], grad[:, : HEAD_DIM // 2]], axis=1
            )
            k_grad[here, lanes] = (grad * cos_ref[...] - turned_half * sin_ref[...]).astype(
                jnp.bfloat16
            )
            v_grad[here, lanes] = (
                kv_grad[here, value_lanes] + kv_after[here, value_lanes].astype(jnp.float32)
            ).astype(jnp.bfloat16)
        return carry

    lax.fori_loop(0, 8, key_value, 0)
    query_spread.service(2)
    key_scatter = scatter_of(projection_product(1, k_grad), 2)
    key_scatter.block(0)
    key_scatter.block(1)
    key_scatter.block(2)
    key_scatter.block(3)
    up_spread.service(1)
    query_spread.service(3)
    key_scatter.turn()
    loading.wait()
    parts_out = attn_term(1, k_grad)
    key_scatter.finish(back_buf)
    norm_back(2, back_buf)
    key_spread = stream_spread(2)
    key_spread.service(0)
    for copy in parts_out:
        copy.wait()
    loading = load_big(normed_ref.at[2])
    up_spread.service(2)
    value_scatter = scatter_of(projection_product(2, v_grad), 3)
    value_scatter.block(0)
    value_scatter.block(1)
    loading.wait()
    parts_out = attn_term(2, v_grad)
    for copy in parts_out:
        copy.wait()
    attn_line.start()
    key_spread.service(1)
    value_scatter.block(2)
    value_scatter.block(3)
    up_spread.service(3)
    attn_line.service(0)
    value_scatter.turn()
    key_spread.service(2)
    value_scatter.finish(back_buf)
    norm_back(3, back_buf)
    value_spread = stream_spread(3)
    value_spread.service(0)
    attn_line.service(1)
    key_spread.service(3)
    value_spread.service(1)
    attn_line.service(2)
    attn_line.finish(attn_sum)
    attn_swap = swap(1)
    quarter_ref[pl.ds(3 * quarter, quarter), :] = attn_sum[pl.ds(3 * quarter, quarter), :]
    value_spread.service(2)
    swapped_in(attn_swap)
    value_spread.service(3)
    for spreading in (
        down_spread,
        query_spread,
        up_spread,
        key_spread,
        value_spread,
    ):
        spreading.finish()
    for place in range(1, 4):

        @pl.when(plane == place)
        def _():
            back_copy(place).wait_send()


def attend_and_back(
    lengths_all,
    cosine,
    sine_part,
    q,
    k,
    v,
    out_grad,
    normed_all,
    grad_all,
    hidden,
    w_out,
    w_down,
    attn_columns,
    x_ordered,
    gains,
    down_own,
    up_term,
    kv_before,
    micro_count,
    sequence_length,
):
    total, width = q.shape
    rows, features = total // 8, w_down.shape[1]
    ff_share = w_down.shape[0]
    quarter = features // 32
    block = (rows, features)
    piece = (4 * quarter, features)
    half = (4, rows // 2, features)
    anywhere = pl.BlockSpec(memory_space=pl.ANY)
    near = pl.BlockSpec(memory_space=pltpu.VMEM)
    shape = jax.ShapeDtypeStruct
    low_type = jnp.bfloat16
    some = lambda *dims: pltpu.VMEM(dims, low_type)
    dma = pltpu.SemaphoreType.DMA
    return pl.pallas_call(
        functools.partial(
            backward_kernel, micro_count=micro_count, sequence_length=sequence_length
        ),
        in_specs=[pl.BlockSpec(memory_space=pltpu.SMEM)]
        + [near] * 6
        + [anywhere, anywhere]
        + [near] * 4
        + [anywhere]
        + [near] * 2
        + [anywhere, anywhere],
        out_specs=[anywhere, anywhere, anywhere, near, near, near, anywhere, anywhere],
        out_shape=[
            shape((12 * rows, features), low_type),
            shape((ff_share, features), low_type),
            shape((4 * quarter, 8 * ff_share), low_type),
            shape(piece, low_type),
            shape(block, low_type),
            shape((8, features), jnp.float32),
            shape((16 * quarter, features), low_type),
            shape((12,) + piece, low_type),
        ],
        scratch_shapes=[
            some(total, features),
            some(total, width),
            some(total, width),
            pltpu.VMEM((total, 2 * width), jnp.float32),
            some(total, 2 * width),
            some(total, 2 * width),
            some(total, 2 * width),
            some(2, *block),
            some(4, *block),
            some(4, *block),
            some(*half),
            some(*half),
            some(*half),
            some(*piece),
            some(2, *piece),
            some(3, *piece),
            some(*piece),
            some(quarter, 8 * ff_share),
            some(3, *block),
            some(*block),
            pltpu.VMEM(block, jnp.float32),
            some(*piece),
            dma((4, 10)),
            dma((4, 10)),
            dma((3, 6)),
            dma((3, 6)),
            dma((2,)),
            dma((6, 6)),
            dma((6, 6)),
            dma((6,)),
            dma((3,)),
            dma((3,)),
            dma((16,)),
            dma((16,)),
            dma((8,)),
        ],
        compiler_params=pltpu.CompilerParams(
            collective_id=6, has_side_effects=True, vmem_limit_bytes=63 * 1024 * 1024
        ),
        cost_estimate=pl.CostEstimate(
            flops=20 * total * features * width,
            bytes_accessed=1000 * 1000 * 1000,
            transcendentals=0,
        ),
    )(
        lengths_all,
        cosine,
        sine_part,
        q,
        k,
        v,
        out_grad,
        normed_all,
        grad_all,
        hidden,
        w_out,
        w_down,
        attn_columns,
        x_ordered,
        gains,
        down_own,
        up_term,
        kv_before,
    )


def rotary_table(row_positions, head_dim):
    half_dim = head_dim // 2
    frequency = jnp.exp(
        jnp.arange(half_dim, dtype=jnp.float32) * (-2.0 * math.log(10000.0) / head_dim)
    )
    angles = row_positions.astype(jnp.float32)[:, None] * frequency[None, :]
    cosine = jnp.cos(angles)
    sine_part = jnp.sin(angles)
    return (
        jnp.concatenate([cosine, cosine], axis=-1),
        jnp.concatenate([-sine_part, sine_part], axis=-1),
    )


def shards_split(
    history,
    history_layer_index,
    lengths,
    norm_gains,
    mix_in,
    mix_out,
    w_attn,
    w_out,
    w_up,
    w_down,
    cotangent,
):
    local_slots, micro_count, sequence_length, features = history.shape
    planes = lax.axis_size("hist")
    columns = lax.axis_size("dp")
    plane = lax.axis_index("hist")
    slot_count = local_slots * planes
    all_rows = micro_count * sequence_length
    rows = all_rows // planes
    share = features // columns
    mix_width = mix_in.shape[1]
    mix_rows = mix_out.shape[0]
    low = lambda values: values.astype(jnp.bfloat16)
    order = (3, 0, 1, 2)

    spare = 128 - mix_width
    middle = jnp.concatenate(
        [
            jnp.pad(mix_out, ((0, 8 - mix_rows), (0, spare))),
            jnp.pad(low(lengths)[None, :], ((0, 7), (0, 128 - micro_count))),
        ],
        axis=0,
    )
    gain_rows = jnp.pad(norm_gains, ((0, 3), (0, 0))).reshape(8, 2, share // 2)
    pack = jnp.concatenate(
        [
            jnp.pad(mix_in, ((0, 0), (0, spare))),
            middle,
            gain_rows.transpose(1, 0, 2).reshape(16, share // 2),
        ],
        axis=0,
    )

    layer_lookup = (
        history_layer_index[:, None] == jnp.arange(slot_count, dtype=jnp.int32)[None, :]
    ).astype(jnp.float32)
    newest_output = jnp.sum(
        jnp.arange(slot_count, dtype=jnp.int32)
        * (history_layer_index == slot_count - 1).astype(jnp.int32)
    )
    root = newest_output // local_slots
    on_root = (plane == root).astype(jnp.float32)
    latest_rows = lax.dynamic_index_in_dim(
        history, newest_output % local_slots, 0, keepdims=False
    ).reshape(all_rows, features)
    own_table = lax.dynamic_slice_in_dim(layer_lookup, plane * local_slots, local_slots, 0)
    ordered = jnp.eye(STREAM_COUNT, dtype=jnp.float32)[:, jnp.array(order)]
    select = jnp.einsum("ci,sj->cjis", ordered, own_table).reshape(
        STREAM_COUNT * slot_count, STREAM_COUNT * local_slots
    )
    select = low(jnp.pad(select, ((0, 0), (0, 128 - STREAM_COUNT * local_slots))))

    my_row = plane * rows + jnp.arange(rows, dtype=jnp.int32)
    my_position = lax.rem(my_row, sequence_length)
    my_sequence = lax.div(my_row, sequence_length)
    my_length = jnp.sum(
        jnp.where(
            my_sequence[:, None] == jnp.arange(micro_count, dtype=jnp.int32)[None, :],
            lengths[None, :],
            0,
        ),
        axis=1,
    )
    valid_rows = (my_position < my_length).astype(jnp.float32)[:, None]
    cosine, sine_part = rotary_table(my_position, HEAD_DIM)

    (
        packed,
        gains,
        pre,
        factors,
        x_ordered,
        normed_all,
        grad_all,
        hidden,
        up_term,
        down_own,
        full3,
        gain_sum3,
        attn_columns,
        q,
        k,
        v,
        out_grad,
        kv_before,
        _,
        _,
        _,
        _,
    ) = forward_and_feed(
        lengths,
        pack,
        latest_rows,
        history.reshape(local_slots * all_rows, features),
        select,
        jnp.broadcast_to(on_root, (8, all_rows)),
        cotangent.reshape(rows, features),
        w_up,
        w_attn,
        w_down,
        w_out,
        cosine,
        sine_part,
        sequence_length,
    )
    lengths_all = packed[:, share + 8, :micro_count].reshape(-1).astype(jnp.int32)
    full, down_all, up_all, attn_quarter, branch, gain_sums, _, _ = attend_and_back(
        lengths_all,
        cosine,
        sine_part,
        q,
        k,
        v,
        out_grad,
        normed_all,
        grad_all,
        hidden,
        w_out,
        w_down,
        attn_columns,
        x_ordered,
        gains,
        down_own,
        up_term,
        kv_before,
        micro_count,
        sequence_length,
    )
    attn_every = lax.all_gather(attn_quarter, "hist", axis=0, tiled=False)

    chunk = sequence_length // planes
    inverse_step = pow(micro_count, -1, planes)
    block_rows = low((x_ordered[0] + branch.astype(jnp.float32)) * valid_rows)
    block_out = jnp.zeros((micro_count, chunk, features), jnp.bfloat16)
    for i in range(micro_count):
        pairs = [(p, (micro_count * p + i) % planes) for p in range(planes)]
        piece = lax.ppermute(block_rows[i * chunk : (i + 1) * chunk], "hist", pairs)
        source = lax.rem((plane - i + planes * micro_count) * inverse_step, planes)
        which = lax.div(source * micro_count + i, planes)
        block_out = lax.dynamic_update_index_in_dim(block_out, piece, which, 0)

    flat_history = history.reshape(local_slots, all_rows, features)
    full_rest = full.reshape(3, all_rows, features)
    item_grads = [full3.astype(jnp.float32)] + [
        full_rest[i].astype(jnp.float32) for i in range(3)
    ]
    inner = jnp.stack(
        [
            jnp.sum(item_grads[item] * flat_history[slot].astype(jnp.float32), axis=-1)
            for item in range(STREAM_COUNT)
            for slot in range(local_slots)
        ],
        axis=0,
    )
    inner_all = line_share(inner)
    mixer_output_wide = (
        packed[:, share : share + mix_rows, :mix_width]
        .reshape(mix_width, mix_width)
        .astype(jnp.float32)
    )
    mix_in_all = packed[:, :share, :mix_width].reshape(features, mix_width)
    tables = layer_lookup.reshape(planes, local_slots, slot_count)
    dyn_grad = jnp.einsum(
        "pist,ic,psj->tcj",
        inner_all.reshape(planes, STREAM_COUNT, local_slots, all_rows),
        ordered.T,
        tables,
        precision=highest,
    ).reshape(all_rows, STREAM_COUNT * slot_count)
    mixer_preactivation = pre[:, :mix_width]
    mix_act = jax.nn.gelu(mixer_preactivation, approximate=False)
    latest_values = latest_rows.astype(jnp.float32)
    latest_scaled, latest_inverse = rms_scale(latest_values, gains[0])
    kept_mix = (latest_values, latest_inverse, low(latest_scaled), mixer_preactivation, mix_act)
    act_grad = precise(dyn_grad, mixer_output_wide.T)
    mix_out_grad = precise(mix_act.T, dyn_grad) * on_root
    latest_grad, gain_zero, mix_in_grad = mix_backward(kept_mix, act_grad, gains[0], mix_in_all)
    slot_grads = []
    for slot in range(local_slots):
        is_latest = (plane * local_slots + slot == newest_output).astype(jnp.float32)
        slot_grad = latest_grad * is_latest
        for item in range(STREAM_COUNT):
            one = item * local_slots + slot
            slot_grad = slot_grad + factors[:, one : one + 1] * item_grads[item]
        slot_grads.append(low(slot_grad))
    history_grad = jnp.stack(slot_grads).reshape(history.shape)

    small_top = jnp.concatenate(
        [
            mix_in_grad * on_root,
            jnp.stack(
                [gain_zero * on_root, gain_sums[1], gain_sums[2], gain_sums[3], gain_sum3[0]]
            ).T,
            jnp.zeros((features, 128 - mix_width - 5), jnp.float32),
        ],
        axis=1,
    ).reshape(columns, share, 128)
    small_bottom = jnp.pad(
        mix_out_grad.reshape(columns, mix_rows, mix_width),
        ((0, 0), (0, 16 - mix_rows), (0, 128 - mix_width)),
    )
    small = small_sums(low(jnp.concatenate([small_top, small_bottom], axis=1)))

    part = share // planes
    w_attn_grad = (
        attn_every[:, : 3 * part]
        .astype(jnp.float32)
        .reshape(planes, 3, part, features)
        .transpose(1, 0, 2, 3)
        .reshape(3, share, features)
    )
    w_out_grad = attn_every[:, 3 * part :].astype(jnp.float32).reshape(share, features)
    return (
        block_out,
        history_grad,
        small[:share, mix_width : mix_width + 5].T,
        small[:share, :mix_width],
        small[share : share + mix_rows, :mix_width],
        w_attn_grad,
        w_out_grad,
        up_all.astype(jnp.float32),
        down_all.astype(jnp.float32),
    )


def splits_by_heads(mesh, micro_count, sequence_length):
    columns, planes = mesh.shape["dp"], mesh.shape["hist"]
    all_rows = micro_count * sequence_length
    rows = all_rows // planes
    return (
        columns == 8
        and planes == 4
        and HEADS % columns == 0
        and all_rows % planes == 0
        and sequence_length % planes == 0
        and rows % 64 == 0
        and math.gcd(micro_count, planes) == 1
        and all(
            (p * rows) // sequence_length * sequence_length >= (p - 1) * rows
            for p in range(planes)
        )
    )


def solution(mesh):
    placed = (
        P("hist", "dp", None, None),
        P(),
        P("dp"),
        P(None, "dp"),
        P("dp", None),
        P("dp", None),
        P(None, "dp", None),
        P("dp", None),
        P("dp", None),
        P("dp", None),
        P("dp", "hist", None),
    )
    def plan(*arrays):
        micro_count = arrays[2].shape[0]
        if splits_by_heads(mesh, micro_count, arrays[0].shape[2]):
            return shards_split(*arrays)
        return shards(*arrays)

    return jax.shard_map(
        plan,
        mesh=mesh,
        in_specs=placed,
        out_specs=(
            P("dp", "hist", None),
            P("hist", "dp", None, None),
            P(None, "dp"),
            P("dp", None),
            P("dp", None),
            P(None, "dp", None),
            P("dp", None),
            P("dp", None),
            P("dp", None),
        ),
        check_vma=False,
    )
```

```python
import functools
import math

import jax
import jax.numpy as jnp
from jax import lax
from jax.experimental import pallas as pl
from jax.experimental.pallas import tpu as pltpu
from jax.sharding import PartitionSpec as P

MODEL_WIDTH = 2048
HEADS = 16
HEAD_DIM = 128
FF = 8192
STREAM_COUNT = 4


epsilon = 1e-06
masked_out = -1e30
highest = lax.Precision.HIGHEST
contract_rows = (((0,), (0,)), ((), ()))
contract_cols = (((1,), (1,)), ((), ()))


def broadcast(value, axis, source):
    kept = jnp.where(lax.axis_index(axis) == source, value, 0).astype(value.dtype)
    return lax.psum(kept, axis)


def matmul(left_side, right_side):
    return jnp.dot(left_side, right_side, preferred_element_type=jnp.float32)


def precise(left_side, right_side):
    return jnp.dot(left_side, right_side, precision=highest, preferred_element_type=jnp.float32)


def gelu_slope(values):
    return 0.5 * (1.0 + lax.erf(values * (1.0 / math.sqrt(2.0)))) + values * jnp.exp(
        -0.5 * values * values
    ) * (1.0 / math.sqrt(2.0 * math.pi))


def rms_scale(values, gain_row):
    inverse = lax.rsqrt(jnp.mean(values * values, axis=-1, keepdims=True) + epsilon)
    return (values * inverse * gain_row, inverse)


def rms_back(values, inverse, gain_row, grad_in):
    scaled = grad_in * gain_row
    gain_grad = jnp.sum(grad_in * values * inverse, axis=0)
    inner_mean = jnp.mean(scaled * values, axis=-1, keepdims=True)
    return (inverse * scaled - values * (inverse * inverse * inverse) * inner_mean, gain_grad)


def rotate(values, positions, turn_sign):
    half_dim = values.shape[-1] // 2
    frequency = jnp.exp(
        jnp.arange(half_dim, dtype=jnp.float32) * (-2.0 * math.log(10000.0) / values.shape[-1])
    )
    angles = positions.astype(jnp.float32)[:, None] * frequency[None, :]
    cosine = jnp.cos(angles)[:, None, :]
    sine_part = jnp.sin(angles)[:, None, :] * turn_sign
    lower_half = values[..., :half_dim]
    upper_half = values[..., half_dim:]
    return jnp.concatenate(
        [
            lower_half * cosine - upper_half * sine_part,
            upper_half * cosine + lower_half * sine_part,
        ],
        axis=-1,
    )


def first_rows(weights, lefts):

    def add_piece(totals, pieces, start_at):
        return tuple(
            (matmul(left_side, piece_rows) for left_side, piece_rows in zip(lefts, pieces))
        )

    initial = tuple(
        (jnp.zeros((lefts[0].shape[0], weight.shape[1]), jnp.float32) for weight in weights)
    )
    return add_piece(
        initial,
        (
            lax.all_gather(weights[0], "dp", axis=0, tiled=True),
            lax.all_gather(weights[1], "dp", axis=0, tiled=True),
            lax.all_gather(weights[2], "dp", axis=0, tiled=True),
            lax.all_gather(weights[3], "dp", axis=0, tiled=True),
        ),
        jnp.int32(0),
    )


def second_rows(w_out, down_folded, attended_low, hidden, ratio):

    def add_piece(total_sum, pieces, start_at):
        count = pieces[0].shape[0]
        down_rows = pieces[1].reshape(count * ratio, pieces[1].shape[1] // ratio)
        return matmul(attended_low, pieces[0]) + matmul(hidden, down_rows)

    initial = jnp.zeros((attended_low.shape[0], w_out.shape[1]), jnp.float32)
    return add_piece(
        initial,
        (
            lax.all_gather(w_out, "dp", axis=0, tiled=True),
            lax.all_gather(down_folded, "dp", axis=0, tiled=True),
        ),
        jnp.int32(0),
    )


def back_first(w_out, down_folded, grad_low, ratio):

    def add_piece(totals, pieces, start_at):
        count = pieces[0].shape[0]
        out_part = lax.dot_general(
            grad_low, pieces[0], contract_cols, preferred_element_type=jnp.float32
        )
        down_rows = pieces[1].reshape(count * ratio, pieces[1].shape[1] // ratio)
        down_part = lax.dot_general(
            grad_low, down_rows, contract_cols, preferred_element_type=jnp.float32
        )
        return (out_part, down_part)

    features = w_out.shape[1]
    initial = (
        jnp.zeros((grad_low.shape[0], features), jnp.float32),
        jnp.zeros((grad_low.shape[0], features * ratio), jnp.float32),
    )
    return add_piece(
        initial,
        (
            lax.all_gather(w_out, "dp", axis=0, tiled=True),
            lax.all_gather(down_folded, "dp", axis=0, tiled=True),
        ),
        jnp.int32(0),
    )


def back_second(weights, rights):

    def add_piece(totals, pieces, start_at):
        return tuple(
            (
                lax.dot_general(
                    right_side, piece_rows, contract_cols, preferred_element_type=jnp.float32
                )
                for right_side, piece_rows in zip(rights, pieces)
            )
        )

    features = weights[1].shape[1]
    initial = tuple((jnp.zeros((rights[0].shape[0], features), jnp.float32) for weight in weights))
    return add_piece(
        initial,
        (
            lax.all_gather(weights[0], "dp", axis=0, tiled=True),
            lax.all_gather(weights[1], "dp", axis=0, tiled=True),
            lax.all_gather(weights[2], "dp", axis=0, tiled=True),
            lax.all_gather(weights[3], "dp", axis=0, tiled=True),
        ),
        jnp.int32(0),
    )


def mix_forward(values_low, gain_row, mix_in_all, mixer_output_wide):
    values = values_low.astype(jnp.float32)
    scaled, inverse = rms_scale(values, gain_row)
    normed_mix = scaled.astype(jnp.bfloat16)
    mixer_preactivation = matmul(normed_mix, mix_in_all)
    mix_act = jax.nn.gelu(mixer_preactivation, approximate=False)
    return (
        precise(mix_act, mixer_output_wide),
        (values, inverse, normed_mix, mixer_preactivation, mix_act),
    )


def mix_backward(kept_mix, act_grad, gain_row, mix_in_all):
    values, inverse, normed_mix, mixer_preactivation, mix_act = kept_mix
    pre_grad = act_grad * gelu_slope(mixer_preactivation)
    in_grad = precise(normed_mix.astype(jnp.float32).T, pre_grad)
    normed_grad = precise(pre_grad, mix_in_all.astype(jnp.float32).T)
    latest_grad, gain_grad = rms_back(values, inverse, gain_row, normed_grad)
    return (latest_grad, gain_grad, in_grad)


def shards(
    history,
    history_layer_index,
    lengths,
    norm_gains,
    mix_in,
    mix_out,
    w_attn,
    w_out,
    w_up,
    w_down,
    cotangent,
):
    local_slots, micro_count, sequence_length, features = history.shape
    hist_count = lax.axis_size("hist")
    dp_count = lax.axis_size("dp")
    hist_place = lax.axis_index("hist")
    slot_count = local_slots * hist_count
    ratio = FF // MODEL_WIDTH
    gains_all, mix_in_all, mix_out_all = (
        lax.all_gather(norm_gains, "dp", axis=1, tiled=True),
        lax.all_gather(mix_in, "dp", axis=0, tiled=True),
        lax.all_gather(mix_out, "dp", axis=0, tiled=True),
    )
    gains_all = gains_all.astype(jnp.float32)
    mixer_output_wide = mix_out_all.astype(jnp.float32)
    mix_width = mixer_output_wide.shape[0]
    layer_lookup = (
        history_layer_index[:, None] == jnp.arange(slot_count, dtype=jnp.int32)[None, :]
    ).astype(jnp.float32)
    newest_output = jnp.sum(
        jnp.arange(slot_count, dtype=jnp.int32)
        * (history_layer_index == slot_count - 1).astype(jnp.int32)
    )
    down_folded = w_down.reshape(w_down.shape[0] // ratio, ratio * w_down.shape[1])
    quarter = cotangent.shape[1]
    own_rows = micro_count * quarter
    positions = hist_place * quarter + jnp.arange(quarter, dtype=jnp.int32)
    valid_rows = (positions[None, :] < lengths[:, None]).astype(jnp.float32).reshape(own_rows, 1)
    root = newest_output // local_slots
    latest_local = lax.dynamic_index_in_dim(history, newest_output % local_slots, 0, keepdims=False)
    latest_rows = broadcast(latest_local, "hist", root)
    dynamic_weights, kept_mix = mix_forward(
        latest_rows.reshape(micro_count * sequence_length, features),
        gains_all[0],
        mix_in_all,
        mixer_output_wide,
    )
    dynamic_weights = dynamic_weights.reshape(
        micro_count, sequence_length, STREAM_COUNT, slot_count
    )
    own_table = lax.dynamic_slice_in_dim(layer_lookup, hist_place * local_slots, local_slots, 0)
    depth_combination_factors = jnp.einsum(
        "mtcj,sj->scmt", dynamic_weights, own_table, precision=highest
    )
    partial_sums = jnp.zeros((STREAM_COUNT, micro_count, sequence_length, features), jnp.float32)
    for depth_position_number in range(local_slots):
        partial_sums = (
            partial_sums
            + depth_combination_factors[depth_position_number][..., None]
            * history[depth_position_number].astype(jnp.float32)[None]
        )
    blended_residual_inputs = lax.psum_scatter(
        partial_sums, "hist", scatter_dimension=2, tiled=True
    )
    stream_rows = blended_residual_inputs.reshape(STREAM_COUNT, own_rows, features)
    normed = []
    inverses = []
    for stream_idx in range(STREAM_COUNT):
        scaled, inverse = rms_scale(stream_rows[stream_idx], gains_all[stream_idx + 1])
        normed.append(scaled.astype(jnp.bfloat16))
        inverses.append(inverse)
    head_shape = (micro_count, quarter, HEADS, HEAD_DIM)
    query_pre, key_pre, value_pre, up_pre = first_rows(
        (w_attn[0], w_attn[1], w_attn[2], w_up), (normed[0], normed[1], normed[2], normed[3])
    )
    attention_asker_vectors = rotate(query_pre.reshape(head_shape), positions, 1.0).astype(
        jnp.bfloat16
    )
    keys_rot = rotate(key_pre.reshape(head_shape), positions, 1.0).astype(jnp.bfloat16)
    values_low = value_pre.astype(jnp.bfloat16)
    keys_all, values_all = (
        lax.all_gather(
            keys_rot.reshape(micro_count, quarter, features), "hist", axis=1, tiled=True
        ),
        lax.all_gather(
            values_low.reshape(micro_count, quarter, features), "hist", axis=1, tiled=True
        ),
    )
    key_heads = keys_all.reshape(micro_count, sequence_length, HEADS, HEAD_DIM)
    value_wide = values_all.reshape(micro_count, sequence_length, HEADS, HEAD_DIM).astype(
        jnp.float32
    )
    score_scale = 1.0 / math.sqrt(HEAD_DIM)
    scores = (
        jnp.einsum(
            "mqhd,mkhd->mhqk",
            attention_asker_vectors,
            key_heads,
            preferred_element_type=jnp.float32,
        )
        * score_scale
    )
    key_positions = jnp.arange(sequence_length, dtype=jnp.int32)
    allowed = (key_positions[None, None, :] <= positions[None, :, None]) & (
        key_positions[None, None, :] < lengths[:, None, None]
    )
    scores = jnp.where(allowed[:, None], scores, masked_out)
    row_top = jnp.max(scores, axis=-1, keepdims=True)
    raised = jnp.exp(scores - row_top)
    soft_weights = raised / jnp.sum(raised, axis=-1, keepdims=True)
    attended = jnp.einsum("mhqk,mkhd->mqhd", soft_weights, value_wide, precision=highest)
    attended_low = attended.reshape(own_rows, features).astype(jnp.bfloat16)
    hidden = jax.nn.gelu(up_pre, approximate=False).astype(jnp.bfloat16)
    branch = second_rows(w_out, down_folded, attended_low, hidden, ratio)
    block_out = (
        ((stream_rows[3] + branch) * valid_rows)
        .astype(jnp.bfloat16)
        .reshape(micro_count, quarter, features)
    )
    grad_rows = cotangent.reshape(own_rows, features).astype(jnp.float32) * valid_rows
    grad_low = grad_rows.astype(jnp.bfloat16)
    attended_back, hidden_grad = back_first(w_out, down_folded, grad_low, ratio)
    up_grad = (hidden_grad * gelu_slope(up_pre)).astype(jnp.bfloat16)
    attended_grad = attended_back.astype(jnp.bfloat16)
    attended_wide = attended_grad.astype(jnp.float32).reshape(head_shape)
    prob_grad = jnp.einsum("mqhd,mkhd->mhqk", attended_wide, value_wide, precision=highest)
    inner_rows = jnp.sum(attended_wide * attended, axis=-1)
    logit_derivative = (
        soft_weights * (prob_grad - jnp.transpose(inner_rows, (0, 2, 1))[..., None]) * score_scale
    )
    query_grad = jnp.einsum(
        "mhqk,mkhd->mqhd", logit_derivative, key_heads.astype(jnp.float32), precision=highest
    )
    key_grad_all = jnp.einsum(
        "mhqk,mqhd->mkhd",
        logit_derivative,
        attention_asker_vectors.astype(jnp.float32),
        precision=highest,
    )
    value_grad_all = jnp.einsum("mhqk,mqhd->mkhd", soft_weights, attended_wide, precision=highest)
    key_grad, value_grad = (
        lax.psum_scatter(
            key_grad_all.reshape(micro_count, sequence_length, features).astype(jnp.bfloat16),
            "hist",
            scatter_dimension=1,
            tiled=True,
        ).astype(jnp.float32),
        lax.psum_scatter(
            value_grad_all.reshape(micro_count, sequence_length, features).astype(jnp.bfloat16),
            "hist",
            scatter_dimension=1,
            tiled=True,
        ).astype(jnp.float32),
    )
    projection_grads = [
        rotate(query_grad, positions, -1.0).reshape(own_rows, features).astype(jnp.bfloat16),
        rotate(key_grad.reshape(head_shape), positions, -1.0)
        .reshape(own_rows, features)
        .astype(jnp.bfloat16),
        value_grad.reshape(own_rows, features).astype(jnp.bfloat16),
    ]
    resid_normed_grad, query_normed_grad, key_normed_grad, value_normed_grad = back_second(
        (w_up, w_attn[0], w_attn[1], w_attn[2]),
        (up_grad, projection_grads[0], projection_grads[1], projection_grads[2]),
    )
    normed_grads = [query_normed_grad, key_normed_grad, value_normed_grad]
    stream_grads = []
    gain_grads = []
    for stream_idx in range(3):
        stream_grad, gain_grad = rms_back(
            stream_rows[stream_idx],
            inverses[stream_idx],
            gains_all[stream_idx + 1],
            normed_grads[stream_idx],
        )
        stream_grads.append(stream_grad)
        gain_grads.append(gain_grad)
    resid_grad, skip_scaling_derivative = rms_back(
        stream_rows[3], inverses[3], gains_all[4], resid_normed_grad
    )
    stream_grads.append(resid_grad + grad_rows)
    gain_grads.append(skip_scaling_derivative)
    stream_grads_all = jnp.stack(stream_grads).reshape(STREAM_COUNT, micro_count, quarter, features)
    full_grads = lax.all_gather(
        stream_grads_all.astype(jnp.bfloat16), "hist", axis=2, tiled=True
    ).astype(stream_grads_all.dtype)
    slot_grads = []
    dyn_grad = jnp.zeros((micro_count, sequence_length, STREAM_COUNT, slot_count), jnp.float32)
    for depth_position_number in range(local_slots):
        rows_now = history[depth_position_number].astype(jnp.float32)
        slot_grads.append(
            jnp.sum(
                depth_combination_factors[depth_position_number][..., None] * full_grads, axis=0
            )
        )
        inner_now = jnp.sum(full_grads * rows_now[None], axis=-1)
        dyn_grad = dyn_grad + jnp.einsum("cmt,j->mtcj", inner_now, own_table[depth_position_number])
    dyn_grad = dyn_grad.reshape(micro_count * sequence_length, STREAM_COUNT * slot_count)
    act_part = precise(dyn_grad, mixer_output_wide.T)
    mix_out_grad = precise(kept_mix[4].T, dyn_grad)
    act_grad = lax.psum(act_part.astype(jnp.bfloat16), "hist").astype(jnp.float32)
    on_root = (hist_place == root).astype(jnp.float32)
    latest_grad, gain_zero, mix_in_grad = mix_backward(kept_mix, act_grad, gains_all[0], mix_in_all)
    gain_zero = gain_zero * on_root
    mix_in_grad = mix_in_grad * on_root
    latest_grad = latest_grad.reshape(micro_count, sequence_length, features)
    marked = []
    for depth_position_number in range(local_slots):
        is_latest = (hist_place * local_slots + depth_position_number == newest_output).astype(
            jnp.float32
        )
        marked.append(slot_grads[depth_position_number] + latest_grad * is_latest)
    history_grad = jnp.stack(marked).astype(jnp.bfloat16)
    gains_grad_full = jnp.stack(
        [gain_zero, gain_grads[0], gain_grads[1], gain_grads[2], gain_grads[3]]
    )
    share_rows = w_out.shape[0]
    per_device = mix_width // dp_count
    mix_out_padded = jnp.pad(
        mix_out_grad.reshape(dp_count, per_device, mix_width),
        ((0, 0), (0, share_rows - per_device), (0, 0)),
    ).reshape(dp_count * share_rows, mix_width)
    small_wide = jnp.concatenate([mix_in_grad, gains_grad_full.T, mix_out_padded], axis=1)
    attn_lefts = (normed[0], normed[1], normed[2], attended_low)
    attn_rights = (projection_grads[0], projection_grads[1], projection_grads[2], grad_low)
    attn_share = lax.psum_scatter(
        jnp.concatenate(
            [
                lax.dot_general(
                    left_side, right_side, contract_rows, preferred_element_type=jnp.float32
                )
                for left_side, right_side in zip(attn_lefts, attn_rights)
            ],
            axis=1,
        ).astype(jnp.bfloat16),
        "dp",
        scatter_dimension=0,
        tiled=True,
    )
    up_term = lax.dot_general(normed[3], up_grad, contract_rows, preferred_element_type=jnp.float32)
    down_term = lax.dot_general(
        hidden, grad_low, contract_rows, preferred_element_type=jnp.float32
    ).reshape(share_rows * lax.axis_size("dp"), ratio * features)
    ffn_share = lax.psum_scatter(
        jnp.concatenate([up_term, down_term, small_wide], axis=1).astype(jnp.bfloat16),
        "dp",
        scatter_dimension=0,
        tiled=True,
    )
    attn_total, ffn_total = (
        lax.psum(attn_share, "hist").astype(jnp.float32),
        lax.psum(ffn_share, "hist").astype(jnp.float32),
    )
    ff_width = ratio * features
    w_attn_grad = jnp.stack(
        [
            attn_total[:, 0:features],
            attn_total[:, features : 2 * features],
            attn_total[:, 2 * features : 3 * features],
        ]
    )
    w_out_grad = attn_total[:, 3 * features : 4 * features]
    w_up_grad = ffn_total[:, 0:ff_width]
    w_down_grad = ffn_total[:, ff_width : 2 * ff_width].reshape(share_rows * ratio, features)
    mix_in_share = ffn_total[:, 2 * ff_width : 2 * ff_width + mix_width]
    gains_share = ffn_total[:, 2 * ff_width + mix_width : 2 * ff_width + mix_width + 5].T
    mix_out_share = ffn_total[0:per_device, 2 * ff_width + mix_width + 5 :]
    return (
        block_out,
        history_grad,
        gains_share,
        mix_in_share,
        mix_out_share,
        w_attn_grad,
        w_out_grad,
        w_up_grad,
        w_down_grad,
    )


DEVICE_MESH = pl.DeviceIdType.MESH
CORE, ACROSS_X, ACROSS_Y = 1, 2, 4


def partner(column, mask):
    moved = column
    for bit in (1, 2, 4):
        if mask & bit:
            on = lax.rem(lax.div(moved, bit), 2)
            moved = moved + bit - 2 * bit * on
    return moved


def push(source, target, send_sem, recv_sem, place):
    copy = pltpu.make_async_remote_copy(
        src_ref=source,
        dst_ref=target,
        send_sem=send_sem,
        recv_sem=recv_sem,
        device_id={"dp": place},
        device_id_type=DEVICE_MESH,
    )
    copy.start()
    return copy


def z_place(plane):
    return {"hist": plane}


class PlaneGatherSteps:

    def __init__(self, column, own, whole, send_sem, recv_sem, local_sem):
        self.column, self.own, self.whole = column, own, whole
        self.send_sem, self.recv_sem, self.local_sem = send_sem, recv_sem, local_sem
        self.rows = own.shape[0]
        self.half = self.rows // 2
        self.across = partner(column, ACROSS_X)
        self.along = partner(column, ACROSS_Y)
        self.beside = partner(column, CORE)
        self.corner = partner(column, ACROSS_X + ACROSS_Y)
        self.copies = []

    def place(self, owner, part):
        start = owner * self.rows + (self.half if part == 1 else 0)
        count = self.rows if part is None else self.half
        return self.whole.at[pl.ds(pl.multiple_of(start, 16), count)]

    def mine(self, part):
        start = self.half if part == 1 else 0
        return self.own.at[pl.ds(start, self.rows if part is None else self.half)]

    def send(self, source, owner, part, to):
        index = len(self.copies)
        copy = push(
            source, self.place(owner, part), self.send_sem.at[index], self.recv_sem.at[index], to
        )
        self.copies.append(copy)

    def begin(self):
        me = self.column
        self.local = pltpu.make_async_copy(self.mine(None), self.place(me, None), self.local_sem)
        self.local.start()
        self.send(self.mine(1), me, 1, self.across)
        self.send(self.mine(0), me, 0, self.along)
        self.send(self.mine(0), me, 0, self.across)
        self.send(self.mine(1), me, 1, self.along)
        self.send(self.mine(None), me, None, self.beside)

    def corners(self):
        self.copies[1].wait_recv()
        self.send(self.place(self.along, 0), self.along, 0, self.across)
        self.copies[0].wait_recv()
        self.send(self.place(self.across, 1), self.across, 1, self.along)

    def siblings(self):
        self.copies[2].wait_recv()
        self.send(self.place(self.across, None), self.across, None, self.beside)
        self.copies[3].wait_recv()
        self.send(self.place(self.along, None), self.along, None, self.beside)

    def rest(self):
        self.copies[5].wait_recv()
        self.send(self.place(self.corner, 0), self.corner, 0, self.beside)
        self.copies[6].wait_recv()
        self.send(self.place(self.corner, 1), self.corner, 1, self.beside)

    def finish(self):
        for index in (4, 7, 8, 9, 10):
            self.copies[index].wait_recv()
        for copy in self.copies:
            copy.wait_send()
        self.local.wait()


class PlaneScatterSteps:
    def __init__(self, column, product, refs, send_sem, recv_sem):
        self.column, self.product = column, product
        self.out_buf, self.side, self.chip, self.from_x, self.from_y, self.last = refs
        self.send_sem, self.recv_sem = send_sem, recv_sem
        rows = self.chip.shape[1]
        self.first, self.second = pl.ds(0, rows // 2), pl.ds(rows // 2, rows // 2)
        self.across = partner(column, ACROSS_X)
        self.along = partner(column, ACROSS_Y)
        self.beside = partner(column, CORE)
        self.pair, self.sends = [], []

    def block(self, i):
        mask = (6, 2, 4, 0)[i]
        if i >= 2:
            self.pair[i - 2].wait_send()
        self.product(partner(self.column, mask + CORE), self.out_buf.at[i % 2])
        self.pair.append(
            push(
                self.out_buf.at[i % 2],
                self.side.at[i],
                self.send_sem.at[i],
                self.recv_sem.at[i],
                self.beside,
            )
        )
        self.product(partner(self.column, mask), self.chip.at[i])
        self.pair[i].wait_recv()
        add_into(self.chip.at[i], self.side.at[i])
        if i == 0:
            self.send(self.chip.at[0, self.first], self.from_x.at[0], self.across)
            self.send(self.chip.at[0, self.second], self.from_y.at[0], self.along)
        if i == 1:
            self.send(self.chip.at[1, self.first], self.from_x.at[1], self.across)
        if i == 2:
            self.send(self.chip.at[2, self.second], self.from_y.at[1], self.along)

    def send(self, source, target, to):
        index = 4 + len(self.sends)
        self.sends.append(
            push(source, target, self.send_sem.at[index], self.recv_sem.at[index], to)
        )

    def turn(self):
        self.sends[0].wait_recv()
        add_into(self.chip.at[2, self.first], self.from_x.at[0])
        self.send(self.chip.at[2, self.first], self.last.at[0], self.along)
        self.sends[1].wait_recv()
        add_into(self.chip.at[1, self.second], self.from_y.at[0])
        self.send(self.chip.at[1, self.second], self.last.at[1], self.across)

    def finish(self, out_ref):
        self.sends[2].wait_recv()
        add_into(self.chip.at[3, self.first], self.from_x.at[1])
        self.sends[3].wait_recv()
        add_into(self.chip.at[3, self.second], self.from_y.at[1])
        self.sends[4].wait_recv()
        add_into(self.chip.at[3, self.first], self.last.at[0])
        self.sends[5].wait_recv()
        add_into(self.chip.at[3, self.second], self.last.at[1])
        if out_ref is not None:
            out_ref[...] = self.chip[3]
        for copy in self.pair[2:] + self.sends:
            copy.wait_send()


def add_into(target, other):
    rows = target.shape[0]
    step = 32 if rows % 32 == 0 else 16

    def some_rows(r, carry):
        piece = pl.ds(pl.multiple_of(r * step, step), step)
        target[piece, :] = (
            target[piece, :].astype(jnp.float32) + other[piece, :].astype(jnp.float32)
        ).astype(jnp.bfloat16)
        return carry

    lax.fori_loop(0, rows // step, some_rows, 0)


class LineSums:

    def __init__(self, plane, parts, arrived, own, last, held, send_sem, recv_sem, load_sem):
        self.plane, self.parts, self.arrived = plane, parts, arrived
        self.own, self.last, self.held = own, last, held
        self.send_sem, self.recv_sem, self.load_sem = send_sem, recv_sem, load_sem
        self.rows = own.shape[0]

    def part(self, way, item, b):
        place = b if way == 0 else 3 - b
        return self.parts.at[pl.ds((item * 4 + place) * self.rows, self.rows)]

    def message(self, way, turn, a, source):
        to = a + 1 if way == 0 else 2 - a
        return pltpu.make_async_remote_copy(
            src_ref=source,
            dst_ref=self.arrived.at[way * 12 + turn],
            send_sem=self.send_sem.at[way * 12 + turn],
            recv_sem=self.recv_sem.at[way * 12 + turn],
            device_id=z_place(to),
            device_id_type=DEVICE_MESH,
        )

    def origin(self, way, turn):
        item, t = divmod(turn, 3)
        return self.message(way, turn, 0, self.part(way, item, 3 - t))

    def slot(self, way, a, turn):
        item, t = divmod(turn, 3)
        return way * 2 + (item * (3 - a) + t) % 2

    def relay(self, way, turn, a):
        return self.message(way, turn, a, self.held.at[self.slot(way, a, turn)])

    def start(self, turn):
        for place in (0, 3):

            @pl.when(self.plane == place)
            def _():
                self.origin(0 if place == 0 else 1, turn).start()

    def load(self, source, target, index):
        return pltpu.make_async_copy(source, target, self.load_sem.at[index])

    def service(self, sigma):
        for place in range(4):

            @pl.when(self.plane == place)
            def _():
                for way in (0, 1):
                    a = place if way == 0 else 3 - place
                    if a == 0:
                        if sigma < 12:
                            self.origin(way, sigma).wait_send()
                        if sigma + 2 < 12:
                            self.origin(way, sigma + 2).start()
                        continue
                    turn = sigma - a + 1
                    if turn < 0 or turn >= 12:
                        continue
                    item, t = divmod(turn, 3)
                    b = 3 - t
                    if b < a:
                        continue
                    if b > a:
                        slot = self.slot(way, a, turn)
                        sent = [
                            earlier
                            for earlier in range(turn)
                            if 3 - earlier % 3 > a and self.slot(way, a, earlier) == slot
                        ]
                        if sent:
                            self.relay(way, sent[-1], a).wait_send()
                        target = self.held.at[slot]
                        mine = self.load(self.part(way, item, b), self.own, 0)
                        mine.start()
                        self.relay(way, turn, a).wait_recv()
                        came = self.load(self.arrived.at[way * 12 + turn], target, 1)
                        came.start()
                        mine.wait()
                        came.wait()
                        add_into(target, self.own)
                        self.relay(way, turn, a).start()
                    else:
                        self.message(way, turn, a - 1, self.own).wait_recv()
                        came = self.load(self.arrived.at[way * 12 + turn], self.last.at[way], 1)
                        came.start()
                        came.wait()
                if sigma % 3 == 2:
                    item = sigma // 3
                    mine = self.load(self.part(0, item, place), self.own, 0)
                    mine.start()
                    mine.wait()

    def drain(self):
        for place in range(4):

            @pl.when(self.plane == place)
            def _():
                for way in (0, 1):
                    a = place if way == 0 else 3 - place
                    if a == 0 or a == 3:
                        continue
                    for slot in (way * 2, way * 2 + 1):
                        sent = [
                            turn
                            for turn in range(12)
                            if 3 - turn % 3 > a and self.slot(way, a, turn) == slot
                        ]
                        self.relay(way, sent[-1], a).wait_send()


class LineSum:

    def __init__(
        self, plane, parts, arrived, own, last, held, send_sem, recv_sem, load_sem, stride, first
    ):
        self.plane, self.parts, self.arrived = plane, parts, arrived
        self.own, self.last, self.held = own, last, held
        self.send_sem, self.recv_sem, self.load_sem = send_sem, recv_sem, load_sem
        self.rows, self.stride, self.first = own.shape[0], stride, first

    def part(self, way, b):
        place = b if way == 0 else 3 - b
        return self.parts.at[pl.ds(place * self.stride + self.first, self.rows)]

    def message(self, way, t, a, source):
        return pltpu.make_async_remote_copy(
            src_ref=source,
            dst_ref=self.arrived.at[way * 3 + t],
            send_sem=self.send_sem.at[way * 3 + t],
            recv_sem=self.recv_sem.at[way * 3 + t],
            device_id=z_place(a + 1 if way == 0 else 2 - a),
            device_id_type=DEVICE_MESH,
        )

    def origin(self, way, t):
        return self.message(way, t, 0, self.part(way, 3 - t))

    def relay(self, way, t, a):
        return self.message(way, t, a, self.held.at[t if a == 1 else 2])

    def start(self):
        for place in (0, 3):

            @pl.when(self.plane == place)
            def _():
                way = 0 if place == 0 else 1
                self.origin(way, 0).start()
                self.origin(way, 1).start()

    def load(self, source, target, index):
        copy = pltpu.make_async_copy(source, target, self.load_sem.at[index])
        copy.start()
        return copy

    def service(self, sigma):
        for place in range(4):

            @pl.when(self.plane == place)
            def _():
                for way in (0, 1):
                    a = place if way == 0 else 3 - place
                    if a == 0:
                        self.origin(way, sigma).wait_send()
                        if sigma == 0:
                            self.origin(way, 2).start()
                        continue
                    t = sigma - a + 1
                    if t < 0 or 3 - t < a:
                        continue
                    b = 3 - t
                    source = self.arrived.at[way * 3 + t]
                    if b > a:
                        relay = self.relay(way, t, a)
                        target = self.held.at[t if a == 1 else 2]
                        mine = self.load(self.part(way, b), self.own, 0)
                        relay.wait_recv()
                        came = self.load(source, target, 1)
                        mine.wait()
                        came.wait()
                        add_into(target, self.own)
                        relay.start()
                    else:
                        self.message(way, t, a - 1, self.own).wait_recv()
                        self.load(source, self.last.at[way], 1).wait()
                if sigma == 2:
                    self.load(self.part(0, place), self.own, 0).wait()

    def finish(self, target):
        step = 16

        def some_rows(r, carry):
            piece = pl.ds(pl.multiple_of(r * step, step), step)
            total = self.own[piece, :].astype(jnp.float32)
            total = total + self.last[0, piece, :].astype(jnp.float32)
            total = total + self.last[1, piece, :].astype(jnp.float32)
            target[piece, :] = total.astype(jnp.bfloat16)
            return carry

        lax.fori_loop(0, self.rows // step, some_rows, 0)
        for place in (1, 2):

            @pl.when(self.plane == place)
            def _():
                for way in (0, 1):
                    a = place if way == 0 else 3 - place
                    for t in range(3 - a):
                        self.relay(way, t, a).wait_send()


class LineGather:

    def __init__(self, plane, own, slot, send_sem, recv_sem, local_sem):
        self.plane, self.own, self.slot = plane, own, slot
        self.send_sem, self.recv_sem, self.local_sem = send_sem, recv_sem, local_sem

    def message(self, way, a, distance):
        origin = a - distance
        plane_of_origin = origin if way == 0 else 3 - origin
        target = self.slot(plane_of_origin)
        return pltpu.make_async_remote_copy(
            src_ref=self.own if distance == 0 else target,
            dst_ref=target,
            send_sem=self.send_sem.at[way * 3 + distance],
            recv_sem=self.recv_sem.at[way * 3 + distance],
            device_id=z_place(a + 1 if way == 0 else 2 - a),
            device_id_type=DEVICE_MESH,
        )

    def service(self, step):
        for place in range(4):

            @pl.when(self.plane == place)
            def _():
                if step == 0:
                    pltpu.make_async_copy(self.own, self.slot(place), self.local_sem).start()
                for way in (0, 1):
                    a = place if way == 0 else 3 - place
                    if step > a:
                        continue
                    if step > 0:
                        self.message(way, a - 1, step - 1).wait_recv()
                    if a < 3:
                        self.message(way, a, step).start()

    def placed(self):
        for place in range(4):

            @pl.when(self.plane == place)
            def _():
                pltpu.make_async_copy(self.own, self.slot(place), self.local_sem).wait()

    def finish(self):
        for place in range(4):

            @pl.when(self.plane == place)
            def _():
                for way in (0, 1):
                    a = place if way == 0 else 3 - place
                    if a < 3:
                        for distance in range(a + 1):
                            self.message(way, a, distance).wait_send()


GAIN_ROW = (4, 1, 2, 3)


def norm_rows_back(x_buf, back, gain_ref, gain_grad_ref, item, extra, target):
    gain = gain_ref[pl.ds(GAIN_ROW[item], 1), :]
    rows, features = target.shape

    def some_rows(r, gain_sum):
        piece = pl.ds(pl.multiple_of(r * 16, 16), 16)
        x = x_buf[piece, :]
        inverse = lax.rsqrt(jnp.mean(x * x, axis=-1, keepdims=True) + epsilon)
        grad = back[piece, :].astype(jnp.float32)
        scaled = grad * gain
        mean = jnp.mean(scaled * x, axis=-1, keepdims=True)
        result = inverse * scaled - x * (inverse * inverse * inverse) * mean
        if extra is not None:
            result = result + extra[piece, :].astype(jnp.float32)
        target[piece, :] = result.astype(jnp.bfloat16)
        return gain_sum + jnp.sum(grad * x * inverse, axis=0, keepdims=True)

    gain_grad_ref[pl.ds(item, 1), :] = lax.fori_loop(
        0, rows // 16, some_rows, jnp.zeros((1, features), jnp.float32)
    )


def forward_kernel(
    length_ref,
    pack_ref,
    latest_ref,
    history_ref,
    select_ref,
    root_ref,
    cotangent_ref,
    w_up_ref,
    w_attn_ref,
    w_down_ref,
    w_out_ref,
    cos_ref,
    sin_ref,
    packed_ref,
    gain_ref,
    pre_ref,
    factor_ref,
    x_ref,
    normed_ref,
    grad_all_ref,
    hidden_ref,
    up_term_ref,
    down_sum_ref,
    full3_ref,
    gain_grad_ref,
    attn_columns,
    q_ref,
    k_ref,
    v_ref,
    out_grad_ref,
    key_before_ref,
    part_ref,
    down_term_ref,
    arrived_ref,
    arrived_down_ref,
    normed3,
    grads,
    up_columns,
    up_grad,
    out_buf,
    side,
    chip,
    from_x,
    from_y,
    last,
    own,
    ends,
    held,
    x_buf,
    normed_buf,
    term_buf,
    grad_own,
    stream_own,
    mix_out_buf,
    dyn_got,
    gather_send,
    gather_recv,
    gather_local,
    scatter_send,
    scatter_recv,
    line_send,
    line_recv,
    line_load,
    swap_send,
    swap_recv,
    swap_local,
    out_sem,
    small_send,
    small_recv,
    dyn_send,
    dyn_recv,
    route_send,
    route_recv,
    block_sem,
    spread_send,
    spread_recv,
    sum_send,
    sum_recv,
    key_send,
    key_recv,
    ready_sem,
    *,
    micro_count,
    sequence_length,
):
    column = lax.axis_index("dp")
    plane = lax.axis_index("hist")
    rows, features = grad_own.shape
    total = 8 * rows
    share = w_up_ref.shape[0]
    ff_share = w_down_ref.shape[0]
    width = share
    tile = 256
    mix_rows = pack_ref.shape[0] - share - 32 + 8
    every_mask = (6, 7, 2, 3, 4, 5, 1)

    barrier = pltpu.get_barrier_semaphore()
    for mask in every_mask:
        pl.semaphore_signal(
            barrier, inc=1, device_id={"dp": partner(column, mask)}, device_id_type=DEVICE_MESH
        )
    for place in range(4):

        @pl.when(plane == place)
        def _():
            for p in range(4):
                if p != place:
                    pl.semaphore_signal(
                        barrier, inc=1, device_id=z_place(p), device_id_type=DEVICE_MESH
                    )

    pl.semaphore_wait(barrier, 10)

    def block_load(source, target, index):
        copy = pltpu.make_async_copy(source, target, block_sem.at[index])
        copy.start()
        return copy

    small_copies = [
        push(
            pack_ref,
            packed_ref.at[column],
            small_send.at[mask],
            small_recv.at[mask],
            partner(column, mask),
        )
        for mask in every_mask
    ]
    small_local = pltpu.make_async_copy(pack_ref, packed_ref.at[column], small_send.at[0])
    small_local.start()
    latest_loads = [
        block_load(latest_ref.at[pl.ds(q * rows, rows)], normed_buf.at[q], 8 + q) for q in range(4)
    ]

    my_rows = pl.ds(pl.multiple_of(column * share, 16), share)

    def up_piece(owner):
        return w_up_ref.at[:, pl.ds(pl.multiple_of(owner * ff_share, 128), ff_share)]

    up_local = pltpu.make_async_copy(up_piece(column), up_columns.at[my_rows], swap_local.at[0])
    up_local.start()
    up_swaps = [
        push(
            up_piece(partner(column, mask)),
            up_columns.at[my_rows],
            swap_send.at[mask],
            swap_recv.at[mask],
            partner(column, mask),
        )
        for mask in every_mask
    ]

    chunk = rows // micro_count

    def route_source(place, s):
        return cotangent_ref.at[pl.ds(s * chunk, chunk)]

    def route_copy(place, s, target_place, slot):
        return pltpu.make_async_remote_copy(
            src_ref=route_source(place, s),
            dst_ref=grad_own.at[pl.ds(slot * chunk, chunk)],
            send_sem=route_send.at[s],
            recv_sem=route_recv.at[slot],
            device_id=z_place(target_place),
            device_id_type=DEVICE_MESH,
        )

    def route_local(place, s, slot):
        return pltpu.make_async_copy(
            route_source(place, s), grad_own.at[pl.ds(slot * chunk, chunk)], route_recv.at[slot]
        )

    for place in range(4):

        @pl.when(plane == place)
        def _():
            for s in range(micro_count):
                target_place, slot = divmod(s * 4 + place, micro_count)
                if target_place == place:
                    route_local(place, s, slot).start()
                else:
                    route_copy(place, s, target_place, slot).start()

    block_order = (3, 0, 2, 1)

    def history_loads(i):
        p, h = block_order[i], i % 2
        return [
            block_load(
                history_ref.at[pl.ds((slot * 4 + p) * rows, rows)],
                normed3.at[pl.ds((h * 4 + slot) * rows, rows)],
                h * 4 + slot,
            )
            for slot in range(4)
        ]

    loads = [history_loads(0), history_loads(1)]
    zeros = jnp.zeros((16, features), jnp.bfloat16)

    def clear(r, carry):
        ends[0, pl.ds(pl.multiple_of(r * 16, 16), 16), :] = zeros
        ends[1, pl.ds(pl.multiple_of(r * 16, 16), 16), :] = zeros
        return carry

    lax.fori_loop(0, ends.shape[1] // 16, clear, 0)

    small_local.wait()
    for copy in small_copies:
        copy.wait_recv()
    for d in range(8):
        gains = packed_ref[d, pl.ds(share + 16, 16), :].astype(jnp.float32)
        gain_ref[:, pl.ds(d * share, share // 2)] = gains[:8]
        gain_ref[:, pl.ds(d * share + share // 2, share // 2)] = gains[8:]
        mix_out_buf[pl.ds(d * mix_rows, mix_rows), :] = packed_ref[
            d, pl.ds(share, 16), :
        ].astype(jnp.float32)[:mix_rows]
    for copy in latest_loads:
        copy.wait()
    for q in range(4):

        def norm_rows(r, carry):
            piece = pl.ds(pl.multiple_of(r * 16, 16), 16)
            x = normed_buf[q, piece, :].astype(jnp.float32)
            inverse = lax.rsqrt(jnp.mean(x * x, axis=-1, keepdims=True) + epsilon)
            normed_buf[q, piece, :] = (x * inverse * gain_ref[pl.ds(0, 1), :]).astype(jnp.bfloat16)
            return carry

        lax.fori_loop(0, rows // 16, norm_rows, 0)
        pre = None
        for d in range(8):
            term = matmul(normed_buf[q, :, d * share : (d + 1) * share], packed_ref[d, :share, :])
            pre = term if pre is None else pre + term
        pre_ref[pl.ds(q * rows, rows), :] = pre
    pre = pre_ref[...]
    act = 0.5 * pre * (1.0 + lax.erf(pre * (1.0 / math.sqrt(2.0))))
    dyn = precise(act[:, : 8 * mix_rows], mix_out_buf[...])
    dyn_columns = (jnp.transpose(dyn)[: 8 * mix_rows] * root_ref[pl.ds(0, 1), :]).astype(jnp.bfloat16)

    def dyn_copy(source_place, target_place):
        return pltpu.make_async_remote_copy(
            src_ref=dyn_got.at[source_place],
            dst_ref=dyn_got.at[source_place],
            send_sem=dyn_send.at[target_place],
            recv_sem=dyn_recv.at[source_place],
            device_id=z_place(target_place),
            device_id_type=DEVICE_MESH,
        )

    for place in range(4):

        @pl.when(plane == place)
        def _():
            dyn_got[place] = dyn_columns
            for p in range(4):
                if p != place:
                    dyn_copy(place, p).start()
            for p in range(4):
                if p != place:
                    dyn_copy(p, place).wait_recv()

    dyn_sum = dyn_got[0] + dyn_got[1] + dyn_got[2] + dyn_got[3]
    factor_ref[...] = lax.dot_general(
        dyn_sum, select_ref[...], contract_rows, preferred_element_type=jnp.float32
    )

    block = pl.ds(0, rows)
    line = LineSums(
        plane,
        part_ref,
        arrived_ref,
        own.at[block],
        ends.at[:, block],
        held.at[:, block],
        line_send,
        line_recv,
        line_load,
    )
    stores = [None, None]
    for i, p in enumerate(block_order):
        h = i % 2
        for copy in loads[i]:
            copy.wait()
        if stores[h] is not None:
            for copy in stores[h]:
                copy.wait()

        def mix_rows_of(r, carry):
            factors = factor_ref[pl.ds(pl.multiple_of(p * rows + r * 16, 16), 16), :]
            for lane in range(0, features, 512):
                slots = [
                    normed3[
                        pl.ds(pl.multiple_of((h * 4 + slot) * rows + r * 16, 16), 16),
                        lane : lane + 512,
                    ].astype(jnp.float32)
                    for slot in range(4)
                ]
                for item in range(4):
                    mixed = None
                    for slot in range(4):
                        one = item * 4 + slot
                        term = factors[:, one : one + 1] * slots[slot]
                        mixed = term if mixed is None else mixed + term
                    grads[
                        pl.ds(pl.multiple_of((h * 4 + item) * rows + r * 16, 16), 16),
                        lane : lane + 512,
                    ] = mixed.astype(jnp.bfloat16)
            return carry

        lax.fori_loop(0, rows // 16, mix_rows_of, 0)
        stores[h] = [
            pltpu.make_async_copy(
                grads.at[pl.ds((h * 4 + item) * rows, rows)],
                part_ref.at[pl.ds((item * 4 + p) * rows, rows)],
                block_sem.at[12 + h * 4 + item],
            )
            for item in range(4)
        ]
        for copy in stores[h]:
            copy.start()
        if i + 2 < 4:
            loads.append(history_loads(i + 2))
        if i % 2 == 1:
            for copies in stores:
                for copy in copies:
                    copy.wait()
            stores = [None, None]
        if i == 1:
            line.start(0)

    line.start(1)
    for mask in (CORE, ACROSS_X, ACROSS_Y):
        pl.semaphore_signal(
            ready_sem, inc=1, device_id={"dp": partner(column, mask)}, device_id_type=DEVICE_MESH
        )

    def attn_piece(stream, owner):
        return w_attn_ref.at[stream, :, pl.ds(pl.multiple_of(owner * share, 128), share)]

    def gather(index, own_rows, whole):
        return PlaneGatherSteps(
            column,
            own_rows,
            whole,
            gather_send.at[index],
            gather_recv.at[index],
            gather_local.at[index],
        )

    for place in range(4):

        @pl.when(plane == place)
        def _():
            for slot in range(micro_count):
                s, source_place = divmod(place * micro_count + slot, 4)
                if source_place == place:
                    route_local(place, s, slot).wait()
                else:
                    route_copy(source_place, s, place, slot).wait_recv()

    def mask_rows(r, carry):
        piece = pl.ds(pl.multiple_of(r * 16, 16), 16)
        row = plane * rows + r * 16 + lax.broadcasted_iota(jnp.int32, (16, 1), 0)
        limit = jnp.zeros((16, 1), jnp.int32)
        for m in range(micro_count):
            inside = (row >= m * sequence_length) & (row < (m + 1) * sequence_length)
            limit = jnp.where(inside, m * sequence_length + length_ref[m], limit)
        kept = jnp.where(row < limit, grad_own[piece, :].astype(jnp.float32), 0.0)
        grad_own[piece, :] = kept.astype(jnp.bfloat16)
        return carry

    lax.fori_loop(0, rows // 16, mask_rows, 0)
    pl.semaphore_wait(ready_sem, 3)
    grad_gather = gather(4, grad_own, grads)
    grad_gather.begin()

    x_copies = []

    def combine(item):
        if x_copies:
            x_copies[-1].wait()

        def some_rows(r, carry):
            piece = pl.ds(pl.multiple_of(r * 16, 16), 16)
            x = (
                own[piece, :].astype(jnp.float32)
                + ends[0, piece, :].astype(jnp.float32)
                + ends[1, piece, :].astype(jnp.float32)
            )
            x_buf[piece, :] = x
            inverse = lax.rsqrt(jnp.mean(x * x, axis=-1, keepdims=True) + epsilon)
            normed_buf[item, piece, :] = (
                x * inverse * gain_ref[pl.ds(GAIN_ROW[item], 1), :]
            ).astype(jnp.bfloat16)
            return carry

        lax.fori_loop(0, rows // 16, some_rows, 0)
        copy = pltpu.make_async_copy(x_buf, x_ref.at[item], out_sem.at[0])
        copy.start()
        x_copies.append(copy)
        steps = gather(
            item, normed_buf.at[item], normed3 if item == 0 else normed_ref.at[item - 1]
        )
        steps.begin()
        return steps

    line.service(0)
    line.service(1)
    grad_gather.corners()
    grad_gather.siblings()
    line.service(2)
    gather3 = combine(0)
    grad_gather.rest()
    grad_gather.finish()
    grads_out = pltpu.make_async_copy(grads, grad_all_ref, out_sem.at[2])
    grads_out.start()
    gather3.corners()
    line.service(3)
    gather3.siblings()
    gather3.rest()
    line.service(4)
    for copy in up_swaps:
        copy.wait_recv()
    up_local.wait()
    gather3.finish()
    attn_swaps, attn_locals = [], []
    for stream in range(3):
        local = pltpu.make_async_copy(
            attn_piece(stream, column),
            attn_columns.at[stream, my_rows],
            swap_local.at[1 + stream],
        )
        local.start()
        attn_locals.append(local)
        for mask in every_mask:
            attn_swaps.append(
                push(
                    attn_piece(stream, partner(column, mask)),
                    attn_columns.at[stream, my_rows],
                    swap_send.at[8 * (stream + 1) + mask],
                    swap_recv.at[8 * (stream + 1) + mask],
                    partner(column, mask),
                )
            )

    def feed(first_block, count):
        def one_tile(step, carry):
            piece = pl.ds(pl.multiple_of((step // (ff_share // tile)) * rows, 16), rows)
            lanes = pl.ds(pl.multiple_of((step % (ff_share // tile)) * tile, tile), tile)
            up = jnp.dot(normed3[piece, :], up_columns[:, lanes], preferred_element_type=jnp.float32)
            spread = 0.5 * (1.0 + lax.erf(up * (1.0 / math.sqrt(2.0))))
            hidden_ref[piece, lanes] = (up * spread).astype(jnp.bfloat16)
            slope = spread + up * jnp.exp(-0.5 * up * up) * (1.0 / math.sqrt(2.0 * math.pi))
            hidden_grad = lax.dot_general(
                grads[piece, :],
                w_down_ref[lanes, :],
                contract_cols,
                preferred_element_type=jnp.float32,
            )
            up_grad[piece, lanes] = (hidden_grad * slope).astype(jnp.bfloat16)
            return carry

        per_block = ff_share // tile
        lax.fori_loop(first_block * per_block, (first_block + count) * per_block, one_tile, 0)

    def back_product(owner, target):
        left_rows = pl.ds(pl.multiple_of(owner * rows, 16), rows)

        def one_tile(t, carry):
            lanes = pl.ds(pl.multiple_of(t * 2 * tile, 2 * tile), 2 * tile)
            target[:, lanes] = lax.dot_general(
                up_grad[left_rows, :],
                up_columns[lanes, :],
                contract_cols,
                preferred_element_type=jnp.float32,
            ).astype(jnp.bfloat16)
            return carry

        lax.fori_loop(0, features // (2 * tile), one_tile, 0)

    term_slots = 2
    part = share // 4

    def term_copies(kind, slot, index):
        if kind == 0:
            return [
                pltpu.make_async_copy(
                    term_buf.at[slot, pl.ds(h * part, part), pl.ds(0, ff_share)],
                    up_term_ref.at[
                        pl.ds(h * 4 * part + index % 4 * part, part),
                        pl.ds(index // 4 * ff_share, ff_share),
                    ],
                    out_sem.at[3 + 4 * slot + h],
                )
                for h in range(4)
            ]
        return [
            pltpu.make_async_copy(
                term_buf.at[slot],
                down_term_ref.at[pl.ds(index * tile, tile)],
                out_sem.at[3 + 4 * slot],
            )
        ]

    def terms(kind, first, count):
        term_width = ff_share if kind == 0 else features
        pending = []
        for index in range(first, first + count):
            slot = index % term_slots
            if len(pending) >= term_slots:
                for copy in pending[-term_slots]:
                    copy.wait()

            def one_tile(t, carry):
                lanes = pl.ds(pl.multiple_of(t * 2 * tile, 2 * tile), 2 * tile)
                if kind == 0:
                    left, right = normed3[:, index * tile : (index + 1) * tile], up_grad[:, lanes]
                else:
                    left, right = hidden_ref[:, index * tile : (index + 1) * tile], grads[:, lanes]
                term_buf[slot, :, lanes] = lax.dot_general(
                    left, right, contract_rows, preferred_element_type=jnp.float32
                ).astype(jnp.bfloat16)
                return carry

            lax.fori_loop(0, term_width // (2 * tile), one_tile, 0)
            copies = term_copies(kind, slot, index)
            for copy in copies:
                copy.start()
            pending.append(copies)
        for copies in pending[-term_slots:]:
            for copy in copies:
                copy.wait()

    def project(stream, target):
        def one_block(b, carry):
            piece = pl.ds(pl.multiple_of(b * rows, 16), rows)
            value = matmul(normed3[piece, :], attn_columns[stream])
            if stream < 2:
                parts = []
                for head in range(width // HEAD_DIM):
                    one = value[:, head * HEAD_DIM : (head + 1) * HEAD_DIM]
                    swapped = jnp.concatenate(
                        [one[:, HEAD_DIM // 2 :], one[:, : HEAD_DIM // 2]], axis=1
                    )
                    parts.append(one * cos_ref[...] + swapped * sin_ref[...])
                value = jnp.concatenate(parts, axis=1)
            target[piece, :] = value.astype(jnp.bfloat16)
            return carry

        lax.fori_loop(0, 8, one_block, 0)

    def out_grads(b, carry):
        piece = pl.ds(pl.multiple_of(b * rows, 16), rows)
        out_grad_ref[piece, :] = lax.dot_general(
            grads[piece, :], w_out_ref[...], contract_cols, preferred_element_type=jnp.float32
        ).astype(jnp.bfloat16)
        return carry

    def key_copy(place):
        return pltpu.make_async_remote_copy(
            src_ref=k_ref,
            dst_ref=key_before_ref,
            send_sem=key_send.at[0],
            recv_sem=key_recv.at[0],
            device_id=z_place(place + 1),
            device_id_type=DEVICE_MESH,
        )

    feed(0, 2)
    line.service(5)
    gather0 = combine(1)
    feed(2, 2)
    line.service(6)
    gather0.corners()
    feed(4, 2)
    line.service(7)
    gather0.siblings()
    feed(6, 2)
    gather0.rest()
    scatter = PlaneScatterSteps(
        column,
        back_product,
        (out_buf, side, chip, from_x, from_y, last),
        scatter_send,
        scatter_recv,
    )
    scatter.block(0)
    line.service(8)
    gather1 = combine(2)
    scatter.block(1)
    scatter.block(2)
    scatter.block(3)
    gather0.finish()
    terms(1, 0, 2)
    line.service(9)
    scatter.turn()
    gather1.corners()
    terms(1, 2, ff_share // tile - 2)
    line.service(10)
    scatter.finish(None)
    x_copies[-1].wait()
    x_load = pltpu.make_async_copy(x_ref.at[0], x_buf, out_sem.at[1])
    x_load.start()
    x_load.wait()
    norm_rows_back(x_buf, chip.at[3], gain_ref, gain_grad_ref, 0, grad_own, stream_own)
    x_copies.clear()
    spread3 = LineGather(
        plane,
        stream_own,
        lambda p: full3_ref.at[pl.ds(p * rows, rows)],
        spread_send,
        spread_recv,
        out_sem.at[11],
    )
    spread3.service(0)
    gather1.siblings()
    down_line = LineSum(
        plane,
        down_term_ref,
        arrived_down_ref,
        own,
        ends,
        held,
        sum_send,
        sum_recv,
        line_load,
        share,
        0,
    )
    line.service(11)
    gather2 = combine(3)
    down_line.start()
    gather1.rest()
    terms(0, 0, features // tile)
    line.drain()
    gather1.finish()
    load = block_load(normed_ref.at[1], normed3, 0)
    gather2.corners()
    for copy in attn_swaps:
        copy.wait_recv()
    for copy in attn_locals:
        copy.wait()
    spread3.service(1)
    load.wait()
    project(1, k_ref)
    for place in range(3):

        @pl.when(plane == place)
        def _():
            key_copy(place).start()

    load = block_load(normed_ref.at[0], normed3, 0)
    down_line.service(0)
    gather2.siblings()
    gather2.rest()
    load.wait()
    project(0, q_ref)
    spread3.service(2)
    lax.fori_loop(0, 8, out_grads, 0)
    gather2.finish()
    load = block_load(normed_ref.at[2], normed3, 0)
    down_line.service(1)
    load.wait()
    project(2, v_ref)
    spread3.service(3)
    for copy in small_copies + up_swaps + attn_swaps:
        copy.wait_send()
    grads_out.wait()
    x_copies[-1].wait()
    for place in range(4):

        @pl.when(plane == place)
        def _():
            for p in range(4):
                if p != place:
                    dyn_copy(place, p).wait_send()
            for s in range(micro_count):
                target_place, slot = divmod(s * 4 + place, micro_count)
                if target_place != place:
                    route_copy(place, s, target_place, slot).wait_send()

    down_line.service(2)
    down_line.finish(down_sum_ref)
    spread3.placed()
    spread3.finish()
    for place in range(4):

        @pl.when(plane == place)
        def _():
            if place > 0:
                key_copy(place - 1).wait_recv()
            if place < 3:
                key_copy(place).wait_send()


def forward_and_feed(
    lengths,
    pack,
    latest,
    history,
    select,
    root,
    cotangent,
    w_up,
    w_attn,
    w_down,
    w_out,
    cosine,
    sine_part,
    sequence_length,
):
    rows, features = cotangent.shape
    micro_count = lengths.shape[0]
    total = 8 * rows
    share = w_up.shape[0]
    ff_share = w_down.shape[0]
    mix_width = select.shape[0]
    block = (rows, features)
    piece = (share, features)
    half = (2, rows // 2, features)
    anywhere = pl.BlockSpec(memory_space=pl.ANY)
    near = pl.BlockSpec(memory_space=pltpu.VMEM)
    shape = jax.ShapeDtypeStruct
    low_type = jnp.bfloat16
    some = lambda *dims: pltpu.VMEM(dims, low_type)
    wide = lambda *dims: pltpu.VMEM(dims, jnp.float32)
    dma = pltpu.SemaphoreType.DMA
    outputs = [
        (near, shape((8,) + pack.shape, low_type)),
        (near, shape((8, features), jnp.float32)),
        (near, shape((4 * rows, 128), jnp.float32)),
        (near, shape((4 * rows, 128), jnp.float32)),
        (anywhere, shape((4,) + block, jnp.float32)),
        (anywhere, shape((3, total, features), low_type)),
        (anywhere, shape((total, features), low_type)),
        (near, shape((total, ff_share), low_type)),
        (anywhere, shape((ff_share, features), low_type)),
        (near, shape(piece, low_type)),
        (anywhere, shape((4 * rows, features), low_type)),
        (near, shape((8, features), jnp.float32)),
        (near, shape((3, features, share), low_type)),
        (near, shape((total, share), low_type)),
        (near, shape((total, share), low_type)),
        (near, shape((total, share), low_type)),
        (near, shape((total, share), low_type)),
        (anywhere, shape((total, share), low_type)),
        (anywhere, shape((16 * rows, features), low_type)),
        (anywhere, shape((ff_share, features), low_type)),
        (anywhere, shape((24,) + block, low_type)),
        (anywhere, shape((6,) + piece, low_type)),
    ]
    return pl.pallas_call(
        functools.partial(
            forward_kernel, micro_count=micro_count, sequence_length=sequence_length
        ),
        in_specs=[pl.BlockSpec(memory_space=pltpu.SMEM), near, anywhere, anywhere]
        + [near, near, anywhere, anywhere, anywhere]
        + [near] * 4,
        out_specs=[spec for spec, _ in outputs],
        out_shape=[out for _, out in outputs],
        scratch_shapes=[
            some(total, features),
            some(total, features),
            some(features, ff_share),
            some(total, ff_share),
            some(2, *block),
            some(4, *block),
            some(4, *block),
            some(*half),
            some(*half),
            some(*half),
            some(*piece),
            some(2, *piece),
            some(4, *piece),
            wide(*block),
            some(4, *block),
            some(2, 256, features),
            some(*block),
            some(*block),
            wide(mix_width, 128),
            some(4, mix_width, 4 * rows),
            dma((5, 11)),
            dma((5, 11)),
            dma((5,)),
            dma((10,)),
            dma((10,)),
            dma((24,)),
            dma((24,)),
            dma((2,)),
            dma((32,)),
            dma((32,)),
            dma((4,)),
            dma((12,)),
            dma((8,)),
            dma((8,)),
            dma((4,)),
            dma((4,)),
            dma((micro_count,)),
            dma((micro_count,)),
            dma((20,)),
            dma((6,)),
            dma((6,)),
            dma((6,)),
            dma((6,)),
            dma((1,)),
            dma((1,)),
            pltpu.SemaphoreType.REGULAR,
        ],
        compiler_params=pltpu.CompilerParams(
            collective_id=5, has_side_effects=True, vmem_limit_bytes=63 * 1024 * 1024
        ),
        cost_estimate=pl.CostEstimate(
            flops=12 * total * features * ff_share,
            bytes_accessed=600 * 1000 * 1000,
            transcendentals=0,
        ),
    )(
        lengths,
        pack,
        latest,
        history,
        select,
        root,
        cotangent,
        w_up,
        w_attn,
        w_down,
        w_out,
        cosine,
        sine_part,
    )


def small_sum_kernel(parts_ref, out_ref, got, sums, send_sem, recv_sem, z_send, z_recv):
    column = lax.axis_index("dp")
    plane = lax.axis_index("hist")
    every_mask = (6, 7, 2, 3, 4, 5, 1)
    barrier = pltpu.get_barrier_semaphore()
    for mask in every_mask:
        pl.semaphore_signal(
            barrier, inc=1, device_id={"dp": partner(column, mask)}, device_id_type=DEVICE_MESH
        )
    for place in range(4):

        @pl.when(plane == place)
        def _():
            for p in range(4):
                if p != place:
                    pl.semaphore_signal(
                        barrier, inc=1, device_id=z_place(p), device_id_type=DEVICE_MESH
                    )

    pl.semaphore_wait(barrier, 10)
    copies = [
        push(
            parts_ref.at[partner(column, mask)],
            got.at[mask],
            send_sem.at[mask],
            recv_sem.at[mask],
            partner(column, mask),
        )
        for mask in every_mask
    ]
    total = parts_ref[column].astype(jnp.float32)
    for mask, copy in zip(every_mask, copies):
        copy.wait_recv()
        total = total + got[mask].astype(jnp.float32)

    def line_copy(source_place, target_place):
        return pltpu.make_async_remote_copy(
            src_ref=sums.at[source_place],
            dst_ref=sums.at[source_place],
            send_sem=z_send.at[target_place],
            recv_sem=z_recv.at[source_place],
            device_id=z_place(target_place),
            device_id_type=DEVICE_MESH,
        )

    for place in range(4):

        @pl.when(plane == place)
        def _():
            others = [p for p in range(4) if p != place]
            sums[place] = total.astype(jnp.bfloat16)
            for p in others:
                line_copy(place, p).start()
            for p in others:
                line_copy(p, place).wait_recv()
            for p in others:
                line_copy(place, p).wait_send()

    out_ref[...] = (sums[0].astype(jnp.float32) + sums[1].astype(jnp.float32)) + (
        sums[2].astype(jnp.float32) + sums[3].astype(jnp.float32)
    )
    for copy in copies:
        copy.wait_send()


def small_sums(parts):
    dims = parts.shape[1:]
    dma = pltpu.SemaphoreType.DMA
    return pl.pallas_call(
        small_sum_kernel,
        out_shape=jax.ShapeDtypeStruct(dims, jnp.float32),
        in_specs=[pl.BlockSpec(memory_space=pltpu.VMEM)],
        out_specs=pl.BlockSpec(memory_space=pltpu.VMEM),
        scratch_shapes=[
            pltpu.VMEM((8,) + dims, jnp.bfloat16),
            pltpu.VMEM((4,) + dims, jnp.bfloat16),
            dma((8,)),
            dma((8,)),
            dma((4,)),
            dma((4,)),
        ],
        compiler_params=pltpu.CompilerParams(collective_id=7, has_side_effects=True),
        cost_estimate=pl.CostEstimate(
            flops=0, bytes_accessed=40 * 1000 * 1000, transcendentals=0
        ),
    )(parts)


def slot_grad_kernel(
    latest_ref, factor_ref, first_ref, rest_ref, latest_grad_ref, out_ref
):
    grads = [first_ref[...].astype(jnp.float32)] + [
        rest_ref[i].astype(jnp.float32) for i in range(3)
    ]
    latest_grad = latest_grad_ref[...]
    factors = factor_ref[...]
    for slot in range(4):
        total = latest_grad * latest_ref[slot]
        for item in range(4):
            one = item * 4 + slot
            total = total + factors[:, one : one + 1] * grads[item]
        out_ref[slot] = total.astype(jnp.bfloat16)


def slot_grads_of(latest_here, factors, first, rest, latest_grad):
    total, features = first.shape
    step = 32
    rows_of = lambda *lead: pl.BlockSpec(
        lead + (step, features), lambda r: (0,) * len(lead) + (r, 0)
    )
    return pl.pallas_call(
        slot_grad_kernel,
        grid=(total // step,),
        in_specs=[
            pl.BlockSpec(memory_space=pltpu.SMEM),
            pl.BlockSpec((step, 128), lambda r: (r, 0)),
            rows_of(),
            rows_of(3),
            rows_of(),
        ],
        out_specs=rows_of(4),
        out_shape=jax.ShapeDtypeStruct((4, total, features), jnp.bfloat16),
        compiler_params=pltpu.CompilerParams(vmem_limit_bytes=24 * 1024 * 1024),
        cost_estimate=pl.CostEstimate(
            flops=40 * total * features, bytes_accessed=20 * total * features, transcendentals=0
        ),
    )(latest_here, factors, first, rest, latest_grad)


def lay_out_kernel(part_ref, attn_ref, out_ref):
    quarter = out_ref.shape[0]
    for stream in range(3):
        attn_ref[stream] = part_ref[stream * quarter : (stream + 1) * quarter, :].astype(
            jnp.float32
        )
    out_ref[...] = part_ref[3 * quarter :, :].astype(jnp.float32)


def lay_out(parts):
    total, features = parts.shape
    step = total // 4
    quarter = step // 4
    return pl.pallas_call(
        lay_out_kernel,
        grid=(4,),
        in_specs=[pl.BlockSpec((step, features), lambda p: (p, 0))],
        out_specs=[
            pl.BlockSpec((3, quarter, features), lambda p: (0, p, 0)),
            pl.BlockSpec((quarter, features), lambda p: (p, 0)),
        ],
        out_shape=[
            jax.ShapeDtypeStruct((3, step, features), jnp.float32),
            jax.ShapeDtypeStruct((step, features), jnp.float32),
        ],
        compiler_params=pltpu.CompilerParams(vmem_limit_bytes=16 * 1024 * 1024),
        cost_estimate=pl.CostEstimate(
            flops=0, bytes_accessed=6 * total * features, transcendentals=0
        ),
    )(parts)


def attend_column(
    column,
    plane,
    length_ref,
    cosine,
    sine_part,
    q_ref,
    k_ref,
    v_ref,
    kv_before_ref,
    out_grad_ref,
    att_ref,
    q_grad_ref,
    kv_grad_ref,
    kv_before_grad_ref,
    rows,
    micro_count,
    sequence_length,
):
    here = pl.ds(pl.multiple_of(column * rows, 16), rows)
    width = q_ref.shape[1]
    scale = 1.0 / math.sqrt(HEAD_DIM)
    row = plane * rows + lax.broadcasted_iota(jnp.int32, (rows, 1), 0)
    start = jnp.zeros((rows, 1), jnp.int32)
    limit = jnp.zeros((rows, 1), jnp.int32)
    for m in range(micro_count):
        inside = (row >= m * sequence_length) & (row < (m + 1) * sequence_length)
        start = jnp.where(inside, m * sequence_length, start)
        limit = jnp.where(inside, m * sequence_length + length_ref[column * micro_count + m], limit)
    limit = jnp.minimum(limit, row + 1)
    key_row = (plane - 1) * rows + lax.broadcasted_iota(jnp.int32, (1, 2 * rows), 1)
    allowed = (key_row >= start) & (key_row < limit)
    for head in range(width // HEAD_DIM):
        lanes = slice(head * HEAD_DIM, (head + 1) * HEAD_DIM)
        value_lanes = slice(width + head * HEAD_DIM, width + (head + 1) * HEAD_DIM)
        query = q_ref[here, lanes]
        keys = jnp.concatenate([kv_before_ref[here, lanes], k_ref[here, lanes]], axis=0)
        values = jnp.concatenate([kv_before_ref[here, value_lanes], v_ref[here, lanes]], axis=0)
        out_grad = out_grad_ref[here, lanes]
        scores = (
            lax.dot_general(query, keys, contract_cols, preferred_element_type=jnp.float32) * scale
        )
        scores = jnp.where(allowed, scores, masked_out)
        raised = jnp.exp(scores - jnp.max(scores, axis=-1, keepdims=True))
        weights = raised / jnp.sum(raised, axis=-1, keepdims=True)
        weights_low = weights.astype(jnp.bfloat16)
        att_ref[here, lanes] = matmul(weights_low, values).astype(jnp.bfloat16)
        weight_grad = lax.dot_general(
            out_grad, values, contract_cols, preferred_element_type=jnp.float32
        )
        inner = jnp.sum(weights * weight_grad, axis=-1, keepdims=True)
        score_grad = (weights * (weight_grad - inner) * scale).astype(jnp.bfloat16)
        query_grad = matmul(score_grad, keys)
        swapped = jnp.concatenate(
            [query_grad[:, HEAD_DIM // 2 :], query_grad[:, : HEAD_DIM // 2]], axis=1
        )
        q_grad_ref[here, lanes] = (query_grad * cosine - swapped * sine_part).astype(jnp.bfloat16)
        key_grad = lax.dot_general(
            score_grad, query, contract_rows, preferred_element_type=jnp.float32
        )
        value_grad = lax.dot_general(
            weights_low, out_grad, contract_rows, preferred_element_type=jnp.float32
        )
        kv_before_grad_ref[here, lanes] = key_grad[:rows].astype(jnp.bfloat16)
        kv_before_grad_ref[here, value_lanes] = value_grad[:rows].astype(jnp.bfloat16)
        kv_grad_ref[here, lanes] = key_grad[rows:]
        kv_grad_ref[here, value_lanes] = value_grad[rows:]


def backward_kernel(
    length_ref,
    cos_ref,
    sin_ref,
    q_ref,
    k_ref,
    v_ref,
    out_grad_ref,
    normed_ref,
    grad_all_ref,
    hidden_ref,
    w_out_ref,
    w_down_ref,
    attn_columns_ref,
    x_ref,
    gain_ref,
    down_own,
    up_term_ref,
    full3_ref,
    history_ref,
    key_before_ref,
    full_ref,
    down_all_ref,
    up_all_ref,
    inner_ref,
    quarter_ref,
    branch_ref,
    gain_grad_ref,
    attn_parts_ref,
    arrived_ref,
    big,
    att,
    q_grad,
    kv_grad,
    kv_before,
    kv_before_grad,
    kv_after,
    out_buf,
    side,
    chip,
    from_x,
    from_y,
    last,
    line_own,
    line_ends,
    line_held,
    up_sum,
    up_own,
    stream_own,
    back_buf,
    x_buf,
    stage,
    inner_columns,
    scatter_send,
    scatter_recv,
    sum_send,
    sum_recv,
    load_sem,
    spread_send,
    spread_recv,
    spread_local,
    key_send,
    key_recv,
    swap_send,
    swap_recv,
    local_sem,
    inner_sem,
    share_send,
    share_recv,
    *,
    micro_count,
    sequence_length,
):
    column = lax.axis_index("dp")
    plane = lax.axis_index("hist")
    total, width = q_ref.shape
    rows, features = total // 8, w_down_ref.shape[1]
    ff_share = w_down_ref.shape[0]
    quarter = features // 8 // 4
    v_grad = kv_before.at[:, pl.ds(0, width)]
    k_grad = kv_before.at[:, pl.ds(width, width)]
    attn_sum = up_sum
    tile = 512

    barrier = pltpu.get_barrier_semaphore()
    for mask in range(1, 8):
        pl.semaphore_signal(
            barrier, inc=1, device_id={"dp": partner(column, mask)}, device_id_type=DEVICE_MESH
        )
    for place in range(4):

        @pl.when(plane == place)
        def _():
            for p in range(4):
                if p != place:
                    pl.semaphore_signal(
                        barrier, inc=1, device_id=z_place(p), device_id_type=DEVICE_MESH
                    )

    pl.semaphore_wait(barrier, 10)

    def value_copy(place):
        return pltpu.make_async_remote_copy(
            src_ref=v_ref,
            dst_ref=kv_before.at[:, pl.ds(width, width)],
            send_sem=key_send.at[1],
            recv_sem=key_recv.at[1],
            device_id=z_place(place + 1),
            device_id_type=DEVICE_MESH,
        )

    for place in range(3):

        @pl.when(plane == place)
        def _():
            value_copy(place).start()

    def back_copy(place):
        return pltpu.make_async_remote_copy(
            src_ref=kv_before_grad,
            dst_ref=kv_after,
            send_sem=key_send.at[0],
            recv_sem=key_recv.at[0],
            device_id=z_place(place - 1),
            device_id_type=DEVICE_MESH,
        )

    def clear(target):
        step = 64

        def some_rows(r, carry):
            target[pl.ds(pl.multiple_of(r * step, step), step), :] = jnp.zeros(
                (step, target.shape[1]), jnp.bfloat16
            )
            return carry

        lax.fori_loop(0, target.shape[0] // step, some_rows, 0)

    line_sums = [
        LineSum(
            plane,
            parts,
            arrived_ref.at[pl.ds(6 * i, 6)],
            line_own,
            line_ends,
            line_held,
            sum_send.at[i],
            sum_recv.at[i],
            load_sem,
            4 * quarter,
            0,
        )
        for i, parts in enumerate((up_term_ref, attn_parts_ref))
    ]
    up_line, attn_line = line_sums

    def spread(index, own, slot):
        return LineGather(
            plane, own, slot, spread_send.at[index], spread_recv.at[index], spread_local.at[index]
        )

    def stream_spread(item):
        return spread(
            item,
            stream_own.at[item - 1],
            lambda p: full_ref.at[pl.ds(((item - 1) * 4 + p) * rows, rows)],
        )

    def norm_back(item, back):
        load = pltpu.make_async_copy(x_ref.at[item], x_buf, local_sem.at[0])
        load.start()
        load.wait()
        norm_rows_back(
            x_buf, back, gain_ref, gain_grad_ref, item, None, stream_own.at[item - 1]
        )

    def scatter_of(product, index):
        return PlaneScatterSteps(
            column,
            product,
            (out_buf, side, chip)
            + tuple(arriving.at[pl.ds(2 * (index % 2), 2)] for arriving in (from_x, from_y, last)),
            scatter_send.at[index],
            scatter_recv.at[index],
        )

    def projection_product(stream, grad):
        def product(owner, target):
            left = pl.ds(pl.multiple_of(owner * rows, 16), rows)

            def one_tile(t, carry):
                lanes = pl.ds(pl.multiple_of(t * tile, tile), tile)
                target[:, lanes] = lax.dot_general(
                    grad[left, :],
                    attn_columns_ref[stream, lanes, :],
                    contract_cols,
                    preferred_element_type=jnp.float32,
                ).astype(jnp.bfloat16)
                return carry

            lax.fori_loop(0, features // tile, one_tile, 0)

        return product

    def branch_product(owner, target):
        left = pl.ds(pl.multiple_of(owner * rows, 16), rows)

        def one_tile(t, carry):
            lanes = pl.ds(pl.multiple_of(t * tile, tile), tile)
            target[:, lanes] = (
                matmul(att[left, :], w_out_ref[:, lanes])
                + matmul(hidden_ref[left, :], w_down_ref[:, lanes])
            ).astype(jnp.bfloat16)
            return carry

        lax.fori_loop(0, features // tile, one_tile, 0)

    def attend(first, count):
        def one_column(m, carry):
            attend_column(
                m,
                plane,
                length_ref,
                cos_ref[...],
                sin_ref[...],
                q_ref,
                k_ref,
                v_ref,
                kv_before,
                out_grad_ref,
                att,
                q_grad,
                kv_grad,
                kv_before_grad,
                rows,
                micro_count,
                sequence_length,
            )
            return carry

        lax.fori_loop(first, first + count, one_column, 0)

    step_rows = rows // 2

    def inner_loads(item, i):
        source = full3_ref if item == 0 else full_ref
        first = 0 if item == 0 else (item - 1) * 4 * rows
        base = (i % 2) * 5 * step_rows
        copies = [
            pltpu.make_async_copy(
                source.at[pl.ds(first + i * step_rows, step_rows)],
                big.at[pl.ds(base + 4 * step_rows, step_rows)],
                inner_sem.at[(i % 2) * 5 + 4],
            )
        ] + [
            pltpu.make_async_copy(
                history_ref.at[pl.ds(slot * 4 * rows + i * step_rows, step_rows)],
                big.at[pl.ds(base + slot * step_rows, step_rows)],
                inner_sem.at[(i % 2) * 5 + slot],
            )
            for slot in range(4)
        ]
        for copy in copies:
            copy.start()
        return copies

    def inner_products(item):
        loads = [inner_loads(item, 0)]
        for i in range(8):
            if i + 1 < 8:
                loads.append(inner_loads(item, i + 1))
            for copy in loads[i]:
                copy.wait()
            base = (i % 2) * 5 * step_rows

            def some_rows(r, carry):
                grad = big[
                    pl.ds(pl.multiple_of(base + 4 * step_rows + r * 16, 16), 16), :
                ].astype(jnp.float32)
                for slot in range(4):
                    values = big[
                        pl.ds(pl.multiple_of(base + slot * step_rows + r * 16, 16), 16), :
                    ].astype(jnp.float32)
                    one = item * 4 + slot
                    inner_columns[
                        pl.ds(pl.multiple_of(i * step_rows + r * 16, 16), 16), one : one + 1
                    ] = jnp.sum(grad * values, axis=-1, keepdims=True)
                return carry

            lax.fori_loop(0, step_rows // 16, some_rows, 0)

    def part_copies(first_row):
        return [
            pltpu.make_async_copy(
                stage.at[pl.ds(p * quarter, quarter)],
                attn_parts_ref.at[pl.ds(p * 4 * quarter + first_row, quarter)],
                local_sem.at[4 + p],
            )
            for p in range(4)
        ]

    def load_big(source):
        copy = pltpu.make_async_copy(source, big, local_sem.at[2])
        copy.start()
        return copy

    def attn_term(stream, grad):
        def one_owner(d, carry):
            lanes = pl.ds(pl.multiple_of(d * width, width), width)
            stage[:, lanes] = lax.dot_general(
                big[:, lanes], grad[...], contract_rows, preferred_element_type=jnp.float32
            ).astype(jnp.bfloat16)
            return carry

        lax.fori_loop(0, 8, one_owner, 0)
        copies = part_copies(stream * quarter)
        for copy in copies:
            copy.start()
        return copies

    def out_term():
        def one_tile(t, carry):
            lanes = pl.ds(pl.multiple_of(t * tile, tile), tile)
            stage[:, lanes] = lax.dot_general(
                att[...], big[:, lanes], contract_rows, preferred_element_type=jnp.float32
            ).astype(jnp.bfloat16)
            return carry

        lax.fori_loop(0, features // tile, one_tile, 0)
        copies = part_copies(3 * quarter)
        for copy in copies:
            copy.start()
        return copies

    def swap(kind):
        copies = []
        for mask in (6, 7, 2, 3, 4, 5, 1):
            owner = partner(column, mask)
            if kind == 0:
                source, target = up_piece(owner), up_target()
            else:
                source, target = attn_piece(owner), attn_target()
            copies.append(
                push(
                    source,
                    target,
                    swap_send.at[8 * kind + mask],
                    swap_recv.at[8 * kind + mask],
                    owner,
                )
            )
        if kind == 0:
            source, target = up_piece(column), up_target()
        else:
            source, target = attn_piece(column), attn_target()
        local = pltpu.make_async_copy(source, target, local_sem.at[3])
        local.start()
        return copies, local

    def up_piece(owner):
        return up_sum.at[
            pl.ds(pl.multiple_of(lax.rem(owner, 4) * quarter, 16), quarter),
            pl.ds(pl.multiple_of(lax.div(owner, 4) * ff_share, 128), ff_share),
        ]

    def up_target():
        return up_own.at[:, pl.ds(pl.multiple_of(column * ff_share, 128), ff_share)]

    def attn_piece(owner):
        return attn_sum.at[
            pl.ds(0, 3 * quarter), pl.ds(pl.multiple_of(owner * width, 128), width)
        ]

    def attn_target():
        return quarter_ref.at[
            pl.ds(0, 3 * quarter), pl.ds(pl.multiple_of(column * width, 128), width)
        ]

    def swapped_in(swapping):
        copies, local = swapping
        for copy in copies:
            copy.wait_recv()
        local.wait()
        for copy in copies:
            copy.wait_send()

    up_line.start()
    down_spread = spread(4, down_own, lambda p: down_all_ref.at[pl.ds(p * 4 * quarter, 4 * quarter)])
    down_spread.service(0)

    @pl.when(plane == 0)
    def _():
        clear(kv_before)
        clear(line_ends.at[0])

    @pl.when(plane > 0)
    def _():
        load = pltpu.make_async_copy(
            key_before_ref, kv_before.at[:, pl.ds(0, width)], local_sem.at[0]
        )
        load.start()
        load.wait()

    @pl.when(plane == 3)
    def _():
        clear(kv_after)
        clear(line_ends.at[1])

    def key_value(m, carry):
        here = pl.ds(pl.multiple_of(m * rows, 16), rows)
        for head in range(width // HEAD_DIM):
            lanes = slice(head * HEAD_DIM, (head + 1) * HEAD_DIM)
            value_lanes = slice(width + head * HEAD_DIM, width + (head + 1) * HEAD_DIM)
            grad = kv_grad[here, lanes] + kv_after[here, lanes].astype(jnp.float32)
            turned_half = jnp.concatenate(
                [grad[:, HEAD_DIM // 2 :], grad[:, : HEAD_DIM // 2]], axis=1
            )
            k_grad[here, lanes] = (grad * cos_ref[...] - turned_half * sin_ref[...]).astype(
                jnp.bfloat16
            )
            v_grad[here, lanes] = (
                kv_grad[here, value_lanes] + kv_after[here, value_lanes].astype(jnp.float32)
            ).astype(jnp.bfloat16)
        return carry

    for place in range(1, 4):

        @pl.when(plane == place)
        def _():
            value_copy(place - 1).wait_recv()

    attend(0, 8)
    for place in range(1, 4):

        @pl.when(plane == place)
        def _():
            back_copy(place).start()

    loading = load_big(grad_all_ref)
    query_scatter = scatter_of(projection_product(0, q_grad), 0)
    query_scatter.block(0)
    query_scatter.block(1)
    query_scatter.block(2)
    query_scatter.block(3)
    up_line.service(0)
    query_scatter.turn()
    loading.wait()
    parts_out = out_term()
    query_scatter.finish(back_buf)
    norm_back(1, back_buf)
    query_spread = stream_spread(1)
    query_spread.service(0)
    down_spread.service(1)
    up_line.service(1)
    for copy in parts_out:
        copy.wait()
    loading = load_big(normed_ref.at[0])

    for place in range(3):

        @pl.when(plane == place)
        def _():
            back_copy(place + 1).wait_recv()

    lax.fori_loop(0, 8, key_value, 0)
    key_scatter = scatter_of(projection_product(1, k_grad), 1)
    key_scatter.block(0)
    key_scatter.block(1)
    key_scatter.block(2)
    key_scatter.block(3)
    down_spread.service(2)
    loading.wait()
    parts_out = attn_term(0, q_grad)
    key_scatter.turn()
    key_scatter.finish(back_buf)
    norm_back(2, back_buf)
    key_spread = stream_spread(2)
    key_spread.service(0)
    up_line.service(2)
    up_line.finish(up_sum)
    up_swap = swap(0)
    for copy in parts_out:
        copy.wait()
    loading = load_big(normed_ref.at[1])
    value_scatter = scatter_of(projection_product(2, v_grad), 2)
    value_scatter.block(0)
    value_scatter.block(1)
    value_scatter.block(2)
    value_scatter.block(3)
    down_spread.service(3)
    query_spread.service(1)
    loading.wait()
    parts_out = attn_term(1, k_grad)
    value_scatter.turn()
    swapped_in(up_swap)
    up_spread = spread(5, up_own, lambda p: up_all_ref.at[pl.ds(p * quarter, quarter)])
    up_spread.service(0)
    value_scatter.finish(back_buf)
    norm_back(3, back_buf)
    value_spread = stream_spread(3)
    for copy in parts_out:
        copy.wait()
    loading = load_big(normed_ref.at[2])
    loading.wait()
    parts_out = attn_term(2, v_grad)
    for copy in parts_out:
        copy.wait()
    attn_line.start()
    value_spread.service(0)
    query_spread.service(2)
    branch_scatter = scatter_of(branch_product, 3)
    branch_scatter.block(0)
    branch_scatter.block(1)
    key_spread.service(1)
    branch_scatter.block(2)
    branch_scatter.block(3)
    up_spread.service(1)
    query_spread.service(3)
    branch_scatter.turn()
    branch_scatter.finish(branch_ref)
    attn_line.service(0)
    key_spread.service(2)
    up_spread.service(2)
    value_spread.service(1)
    attn_line.service(1)
    key_spread.service(3)
    query_spread.placed()
    inner_products(0)
    inner_products(1)
    up_spread.service(3)
    attn_line.service(2)
    attn_line.finish(attn_sum)
    attn_swap = swap(1)
    quarter_ref[pl.ds(3 * quarter, quarter), :] = attn_sum[pl.ds(3 * quarter, quarter), :]
    value_spread.service(2)
    key_spread.placed()
    inner_products(2)
    down_spread.placed()
    up_spread.placed()
    swapped_in(attn_swap)
    value_spread.service(3)
    value_spread.placed()
    inner_products(3)

    def share_copy(source_place, target_place):
        return pltpu.make_async_remote_copy(
            src_ref=inner_ref.at[source_place],
            dst_ref=inner_ref.at[source_place],
            send_sem=share_send.at[target_place],
            recv_sem=share_recv.at[source_place],
            device_id=z_place(target_place),
            device_id_type=DEVICE_MESH,
        )

    for place in range(4):

        @pl.when(plane == place)
        def _():
            others = [p for p in range(4) if p != place]
            inner_ref[place] = jnp.transpose(inner_columns[...])[:16]
            for p in others:
                share_copy(place, p).start()
            for p in others:
                share_copy(p, place).wait_recv()
            for p in others:
                share_copy(place, p).wait_send()

    for spreading in (
        down_spread,
        query_spread,
        up_spread,
        key_spread,
        value_spread,
    ):
        spreading.finish()
    for place in range(3):

        @pl.when(plane == place)
        def _():
            value_copy(place).wait_send()

    for place in range(1, 4):

        @pl.when(plane == place)
        def _():
            back_copy(place).wait_send()


def attend_and_back(
    lengths_all,
    cosine,
    sine_part,
    q,
    k,
    v,
    out_grad,
    normed_all,
    grad_all,
    hidden,
    w_out,
    w_down,
    attn_columns,
    x_ordered,
    gains,
    down_own,
    up_term,
    full3,
    history,
    key_before,
    micro_count,
    sequence_length,
):
    total, width = q.shape
    rows, features = total // 8, w_down.shape[1]
    ff_share = w_down.shape[0]
    quarter = features // 32
    block = (rows, features)
    piece = (4 * quarter, features)
    half = (4, rows // 2, features)
    anywhere = pl.BlockSpec(memory_space=pl.ANY)
    near = pl.BlockSpec(memory_space=pltpu.VMEM)
    shape = jax.ShapeDtypeStruct
    low_type = jnp.bfloat16
    some = lambda *dims: pltpu.VMEM(dims, low_type)
    dma = pltpu.SemaphoreType.DMA
    return pl.pallas_call(
        functools.partial(
            backward_kernel, micro_count=micro_count, sequence_length=sequence_length
        ),
        in_specs=[pl.BlockSpec(memory_space=pltpu.SMEM)]
        + [near] * 6
        + [anywhere, anywhere]
        + [near] * 4
        + [anywhere]
        + [near] * 2
        + [anywhere] * 4,
        out_specs=[anywhere] * 3 + [near, near, near, near, anywhere, anywhere],
        out_shape=[
            shape((12 * rows, features), low_type),
            shape((ff_share, features), low_type),
            shape((4 * quarter, 8 * ff_share), low_type),
            shape((4, 16, 4 * rows), jnp.float32),
            shape(piece, low_type),
            shape(block, low_type),
            shape((8, features), jnp.float32),
            shape((16 * quarter, features), low_type),
            shape((12,) + piece, low_type),
        ],
        scratch_shapes=[
            some(total, features),
            some(total, width),
            some(total, width),
            pltpu.VMEM((total, 2 * width), jnp.float32),
            some(total, 2 * width),
            some(total, 2 * width),
            some(total, 2 * width),
            some(2, *block),
            some(4, *block),
            some(4, *block),
            some(*half),
            some(*half),
            some(*half),
            some(*piece),
            some(2, *piece),
            some(3, *piece),
            some(*piece),
            some(quarter, 8 * ff_share),
            some(3, *block),
            some(*block),
            pltpu.VMEM(block, jnp.float32),
            some(*piece),
            pltpu.VMEM((4 * rows, 128), jnp.float32),
            dma((4, 10)),
            dma((4, 10)),
            dma((3, 6)),
            dma((3, 6)),
            dma((2,)),
            dma((6, 6)),
            dma((6, 6)),
            dma((6,)),
            dma((3,)),
            dma((3,)),
            dma((16,)),
            dma((16,)),
            dma((8,)),
            dma((10,)),
            dma((4,)),
            dma((4,)),
        ],
        compiler_params=pltpu.CompilerParams(
            collective_id=6, has_side_effects=True, vmem_limit_bytes=63 * 1024 * 1024
        ),
        cost_estimate=pl.CostEstimate(
            flops=20 * total * features * width,
            bytes_accessed=1000 * 1000 * 1000,
            transcendentals=0,
        ),
    )(
        lengths_all,
        cosine,
        sine_part,
        q,
        k,
        v,
        out_grad,
        normed_all,
        grad_all,
        hidden,
        w_out,
        w_down,
        attn_columns,
        x_ordered,
        gains,
        down_own,
        up_term,
        full3,
        history,
        key_before,
    )


def rotary_table(row_positions, head_dim):
    half_dim = head_dim // 2
    frequency = jnp.exp(
        jnp.arange(half_dim, dtype=jnp.float32) * (-2.0 * math.log(10000.0) / head_dim)
    )
    angles = row_positions.astype(jnp.float32)[:, None] * frequency[None, :]
    cosine = jnp.cos(angles)
    sine_part = jnp.sin(angles)
    return (
        jnp.concatenate([cosine, cosine], axis=-1),
        jnp.concatenate([-sine_part, sine_part], axis=-1),
    )


def shards_split(
    history,
    history_layer_index,
    lengths,
    norm_gains,
    mix_in,
    mix_out,
    w_attn,
    w_out,
    w_up,
    w_down,
    cotangent,
):
    local_slots, micro_count, sequence_length, features = history.shape
    planes = lax.axis_size("hist")
    columns = lax.axis_size("dp")
    plane = lax.axis_index("hist")
    slot_count = local_slots * planes
    all_rows = micro_count * sequence_length
    rows = all_rows // planes
    share = features // columns
    mix_width = mix_in.shape[1]
    mix_rows = mix_out.shape[0]
    low = lambda values: values.astype(jnp.bfloat16)
    order = (3, 0, 1, 2)

    spare = 128 - mix_width
    middle = jnp.concatenate(
        [
            jnp.pad(mix_out, ((0, 8 - mix_rows), (0, spare))),
            jnp.pad(low(lengths)[None, :], ((0, 7), (0, 128 - micro_count))),
        ],
        axis=0,
    )
    gain_rows = jnp.pad(norm_gains, ((0, 3), (0, 0))).reshape(8, 2, share // 2)
    pack = jnp.concatenate(
        [
            jnp.pad(mix_in, ((0, 0), (0, spare))),
            middle,
            gain_rows.transpose(1, 0, 2).reshape(16, share // 2),
        ],
        axis=0,
    )

    layer_lookup = (
        history_layer_index[:, None] == jnp.arange(slot_count, dtype=jnp.int32)[None, :]
    ).astype(jnp.float32)
    newest_output = jnp.sum(
        jnp.arange(slot_count, dtype=jnp.int32)
        * (history_layer_index == slot_count - 1).astype(jnp.int32)
    )
    root = newest_output // local_slots
    on_root = (plane == root).astype(jnp.float32)
    latest_rows = lax.dynamic_index_in_dim(
        history, newest_output % local_slots, 0, keepdims=False
    ).reshape(all_rows, features)
    own_table = lax.dynamic_slice_in_dim(layer_lookup, plane * local_slots, local_slots, 0)
    ordered = jnp.eye(STREAM_COUNT, dtype=jnp.float32)[:, jnp.array(order)]
    select = jnp.einsum("ci,sj->cjis", ordered, own_table).reshape(
        STREAM_COUNT * slot_count, STREAM_COUNT * local_slots
    )
    select = low(jnp.pad(select, ((0, 0), (0, 128 - STREAM_COUNT * local_slots))))

    my_row = plane * rows + jnp.arange(rows, dtype=jnp.int32)
    my_position = lax.rem(my_row, sequence_length)
    my_sequence = lax.div(my_row, sequence_length)
    my_length = jnp.sum(
        jnp.where(
            my_sequence[:, None] == jnp.arange(micro_count, dtype=jnp.int32)[None, :],
            lengths[None, :],
            0,
        ),
        axis=1,
    )
    valid_rows = (my_position < my_length).astype(jnp.float32)[:, None]
    cosine, sine_part = rotary_table(my_position, HEAD_DIM)

    (
        packed,
        gains,
        pre,
        factors,
        x_ordered,
        normed_all,
        grad_all,
        hidden,
        up_term,
        down_own,
        full3,
        gain_sum3,
        attn_columns,
        q,
        k,
        v,
        out_grad,
        key_before,
        _,
        _,
        _,
        _,
    ) = forward_and_feed(
        lengths,
        pack,
        latest_rows,
        history.reshape(local_slots * all_rows, features),
        select,
        jnp.broadcast_to(on_root, (8, all_rows)),
        cotangent.reshape(rows, features),
        w_up,
        w_attn,
        w_down,
        w_out,
        cosine,
        sine_part,
        sequence_length,
    )
    lengths_all = packed[:, share + 8, :micro_count].reshape(-1).astype(jnp.int32)
    (
        full,
        down_all,
        up_all,
        inner_all,
        attn_quarter,
        branch,
        gain_sums,
        _,
        _,
    ) = attend_and_back(
        lengths_all,
        cosine,
        sine_part,
        q,
        k,
        v,
        out_grad,
        normed_all,
        grad_all,
        hidden,
        w_out,
        w_down,
        attn_columns,
        x_ordered,
        gains,
        down_own,
        up_term,
        full3,
        history.reshape(local_slots * all_rows, features),
        key_before,
        micro_count,
        sequence_length,
    )
    attn_every = lax.all_gather(attn_quarter, "hist", axis=0, tiled=True)

    chunk = sequence_length // planes
    inverse_step = pow(micro_count, -1, planes)
    block_rows = low((x_ordered[0] + branch.astype(jnp.float32)) * valid_rows)
    block_out = jnp.zeros((micro_count, chunk, features), jnp.bfloat16)
    for i in range(micro_count):
        pairs = [(p, (micro_count * p + i) % planes) for p in range(planes)]
        piece = lax.ppermute(block_rows[i * chunk : (i + 1) * chunk], "hist", pairs)
        source = lax.rem((plane - i + planes * micro_count) * inverse_step, planes)
        which = lax.div(source * micro_count + i, planes)
        block_out = lax.dynamic_update_index_in_dim(block_out, piece, which, 0)

    mixer_output_wide = (
        packed[:, share : share + mix_rows, :mix_width]
        .reshape(mix_width, mix_width)
        .astype(jnp.float32)
    )
    mix_in_all = packed[:, :share, :mix_width].reshape(features, mix_width)
    tables = layer_lookup.reshape(planes, local_slots, slot_count)
    dyn_grad = jnp.einsum(
        "pist,ic,psj->tcj",
        inner_all.reshape(planes, STREAM_COUNT, local_slots, all_rows),
        ordered.T,
        tables,
        precision=highest,
    ).reshape(all_rows, STREAM_COUNT * slot_count)
    mixer_preactivation = pre[:, :mix_width]
    mix_act = jax.nn.gelu(mixer_preactivation, approximate=False)
    latest_values = latest_rows.astype(jnp.float32)
    latest_scaled, latest_inverse = rms_scale(latest_values, gains[0])
    kept_mix = (latest_values, latest_inverse, low(latest_scaled), mixer_preactivation, mix_act)
    act_grad = precise(dyn_grad, mixer_output_wide.T)
    mix_out_grad = precise(mix_act.T, dyn_grad) * on_root
    latest_grad, gain_zero, mix_in_grad = mix_backward(kept_mix, act_grad, gains[0], mix_in_all)
    latest_here = (plane * local_slots + jnp.arange(local_slots) == newest_output).astype(
        jnp.float32
    )
    history_grad = slot_grads_of(
        latest_here, factors, full3, full.reshape(3, all_rows, features), latest_grad
    ).reshape(history.shape)

    small_top = jnp.concatenate(
        [
            mix_in_grad * on_root,
            jnp.stack(
                [gain_zero * on_root, gain_sums[1], gain_sums[2], gain_sums[3], gain_sum3[0]]
            ).T,
            jnp.zeros((features, 128 - mix_width - 5), jnp.float32),
        ],
        axis=1,
    ).reshape(columns, share, 128)
    small_bottom = jnp.pad(
        mix_out_grad.reshape(columns, mix_rows, mix_width),
        ((0, 0), (0, 16 - mix_rows), (0, 128 - mix_width)),
    )
    small = small_sums(low(jnp.concatenate([small_top, small_bottom], axis=1)))

    w_attn_grad, w_out_grad = lay_out(attn_every)
    return (
        block_out,
        history_grad,
        small[:share, mix_width : mix_width + 5].T,
        small[:share, :mix_width],
        small[share : share + mix_rows, :mix_width],
        w_attn_grad,
        w_out_grad,
        up_all.astype(jnp.float32),
        down_all.astype(jnp.float32),
    )


def splits_by_heads(mesh, micro_count, sequence_length):
    columns, planes = mesh.shape["dp"], mesh.shape["hist"]
    all_rows = micro_count * sequence_length
    rows = all_rows // planes
    return (
        columns == 8
        and planes == 4
        and HEADS % columns == 0
        and all_rows % planes == 0
        and sequence_length % planes == 0
        and rows % 64 == 0
        and math.gcd(micro_count, planes) == 1
        and all(
            (p * rows) // sequence_length * sequence_length >= (p - 1) * rows
            for p in range(planes)
        )
    )


def solution(mesh):
    placed = (
        P("hist", "dp", None, None),
        P(),
        P("dp"),
        P(None, "dp"),
        P("dp", None),
        P("dp", None),
        P(None, "dp", None),
        P("dp", None),
        P("dp", None),
        P("dp", None),
        P("dp", "hist", None),
    )
    def plan(*arrays):
        micro_count = arrays[2].shape[0]
        if splits_by_heads(mesh, micro_count, arrays[0].shape[2]):
            return shards_split(*arrays)
        return shards(*arrays)

    return jax.shard_map(
        plan,
        mesh=mesh,
        in_specs=placed,
        out_specs=(
            P("dp", "hist", None),
            P("hist", "dp", None, None),
            P(None, "dp"),
            P("dp", None),
            P("dp", None),
            P(None, "dp", None),
            P("dp", None),
            P("dp", None),
            P("dp", None),
        ),
        check_vma=False,
    )
```

```python
import functools
import math

import jax
import jax.numpy as jnp
from jax import lax
from jax.experimental import pallas as pl
from jax.experimental.pallas import tpu as pltpu
from jax.sharding import PartitionSpec as P

MODEL_WIDTH = 2048
HEADS = 16
HEAD_DIM = 128
FF = 8192
STREAM_COUNT = 4


epsilon = 1e-06
masked_out = -1e30
highest = lax.Precision.HIGHEST
contract_rows = (((0,), (0,)), ((), ()))
contract_cols = (((1,), (1,)), ((), ()))


def broadcast(value, axis, source):
    kept = jnp.where(lax.axis_index(axis) == source, value, 0).astype(value.dtype)
    return lax.psum(kept, axis)


def matmul(left_side, right_side):
    return jnp.dot(left_side, right_side, preferred_element_type=jnp.float32)


def precise(left_side, right_side):
    return jnp.dot(left_side, right_side, precision=highest, preferred_element_type=jnp.float32)


def gelu_slope(values):
    return 0.5 * (1.0 + lax.erf(values * (1.0 / math.sqrt(2.0)))) + values * jnp.exp(
        -0.5 * values * values
    ) * (1.0 / math.sqrt(2.0 * math.pi))


def rms_scale(values, gain_row):
    inverse = lax.rsqrt(jnp.mean(values * values, axis=-1, keepdims=True) + epsilon)
    return (values * inverse * gain_row, inverse)


def rms_back(values, inverse, gain_row, grad_in):
    scaled = grad_in * gain_row
    gain_grad = jnp.sum(grad_in * values * inverse, axis=0)
    inner_mean = jnp.mean(scaled * values, axis=-1, keepdims=True)
    return (inverse * scaled - values * (inverse * inverse * inverse) * inner_mean, gain_grad)


def rotate(values, positions, turn_sign):
    half_dim = values.shape[-1] // 2
    frequency = jnp.exp(
        jnp.arange(half_dim, dtype=jnp.float32) * (-2.0 * math.log(10000.0) / values.shape[-1])
    )
    angles = positions.astype(jnp.float32)[:, None] * frequency[None, :]
    cosine = jnp.cos(angles)[:, None, :]
    sine_part = jnp.sin(angles)[:, None, :] * turn_sign
    lower_half = values[..., :half_dim]
    upper_half = values[..., half_dim:]
    return jnp.concatenate(
        [
            lower_half * cosine - upper_half * sine_part,
            upper_half * cosine + lower_half * sine_part,
        ],
        axis=-1,
    )


def first_rows(weights, lefts):

    def add_piece(totals, pieces, start_at):
        return tuple(
            (matmul(left_side, piece_rows) for left_side, piece_rows in zip(lefts, pieces))
        )

    initial = tuple(
        (jnp.zeros((lefts[0].shape[0], weight.shape[1]), jnp.float32) for weight in weights)
    )
    return add_piece(
        initial,
        (
            lax.all_gather(weights[0], "dp", axis=0, tiled=True),
            lax.all_gather(weights[1], "dp", axis=0, tiled=True),
            lax.all_gather(weights[2], "dp", axis=0, tiled=True),
            lax.all_gather(weights[3], "dp", axis=0, tiled=True),
        ),
        jnp.int32(0),
    )


def second_rows(w_out, down_folded, attended_low, hidden, ratio):

    def add_piece(total_sum, pieces, start_at):
        count = pieces[0].shape[0]
        down_rows = pieces[1].reshape(count * ratio, pieces[1].shape[1] // ratio)
        return matmul(attended_low, pieces[0]) + matmul(hidden, down_rows)

    initial = jnp.zeros((attended_low.shape[0], w_out.shape[1]), jnp.float32)
    return add_piece(
        initial,
        (
            lax.all_gather(w_out, "dp", axis=0, tiled=True),
            lax.all_gather(down_folded, "dp", axis=0, tiled=True),
        ),
        jnp.int32(0),
    )


def back_first(w_out, down_folded, grad_low, ratio):

    def add_piece(totals, pieces, start_at):
        count = pieces[0].shape[0]
        out_part = lax.dot_general(
            grad_low, pieces[0], contract_cols, preferred_element_type=jnp.float32
        )
        down_rows = pieces[1].reshape(count * ratio, pieces[1].shape[1] // ratio)
        down_part = lax.dot_general(
            grad_low, down_rows, contract_cols, preferred_element_type=jnp.float32
        )
        return (out_part, down_part)

    features = w_out.shape[1]
    initial = (
        jnp.zeros((grad_low.shape[0], features), jnp.float32),
        jnp.zeros((grad_low.shape[0], features * ratio), jnp.float32),
    )
    return add_piece(
        initial,
        (
            lax.all_gather(w_out, "dp", axis=0, tiled=True),
            lax.all_gather(down_folded, "dp", axis=0, tiled=True),
        ),
        jnp.int32(0),
    )


def back_second(weights, rights):

    def add_piece(totals, pieces, start_at):
        return tuple(
            (
                lax.dot_general(
                    right_side, piece_rows, contract_cols, preferred_element_type=jnp.float32
                )
                for right_side, piece_rows in zip(rights, pieces)
            )
        )

    features = weights[1].shape[1]
    initial = tuple((jnp.zeros((rights[0].shape[0], features), jnp.float32) for weight in weights))
    return add_piece(
        initial,
        (
            lax.all_gather(weights[0], "dp", axis=0, tiled=True),
            lax.all_gather(weights[1], "dp", axis=0, tiled=True),
            lax.all_gather(weights[2], "dp", axis=0, tiled=True),
            lax.all_gather(weights[3], "dp", axis=0, tiled=True),
        ),
        jnp.int32(0),
    )


def mix_forward(values_low, gain_row, mix_in_all, mixer_output_wide):
    values = values_low.astype(jnp.float32)
    scaled, inverse = rms_scale(values, gain_row)
    normed_mix = scaled.astype(jnp.bfloat16)
    mixer_preactivation = matmul(normed_mix, mix_in_all)
    mix_act = jax.nn.gelu(mixer_preactivation, approximate=False)
    return (
        precise(mix_act, mixer_output_wide),
        (values, inverse, normed_mix, mixer_preactivation, mix_act),
    )


def mix_backward(kept_mix, act_grad, gain_row, mix_in_all):
    values, inverse, normed_mix, mixer_preactivation, mix_act = kept_mix
    pre_grad = act_grad * gelu_slope(mixer_preactivation)
    in_grad = precise(normed_mix.astype(jnp.float32).T, pre_grad)
    normed_grad = precise(pre_grad, mix_in_all.astype(jnp.float32).T)
    latest_grad, gain_grad = rms_back(values, inverse, gain_row, normed_grad)
    return (latest_grad, gain_grad, in_grad)


def shards(
    history,
    history_layer_index,
    lengths,
    norm_gains,
    mix_in,
    mix_out,
    w_attn,
    w_out,
    w_up,
    w_down,
    cotangent,
):
    local_slots, micro_count, sequence_length, features = history.shape
    hist_count = lax.axis_size("hist")
    dp_count = lax.axis_size("dp")
    hist_place = lax.axis_index("hist")
    slot_count = local_slots * hist_count
    ratio = FF // MODEL_WIDTH
    gains_all, mix_in_all, mix_out_all = (
        lax.all_gather(norm_gains, "dp", axis=1, tiled=True),
        lax.all_gather(mix_in, "dp", axis=0, tiled=True),
        lax.all_gather(mix_out, "dp", axis=0, tiled=True),
    )
    gains_all = gains_all.astype(jnp.float32)
    mixer_output_wide = mix_out_all.astype(jnp.float32)
    mix_width = mixer_output_wide.shape[0]
    layer_lookup = (
        history_layer_index[:, None] == jnp.arange(slot_count, dtype=jnp.int32)[None, :]
    ).astype(jnp.float32)
    newest_output = jnp.sum(
        jnp.arange(slot_count, dtype=jnp.int32)
        * (history_layer_index == slot_count - 1).astype(jnp.int32)
    )
    down_folded = w_down.reshape(w_down.shape[0] // ratio, ratio * w_down.shape[1])
    quarter = cotangent.shape[1]
    own_rows = micro_count * quarter
    positions = hist_place * quarter + jnp.arange(quarter, dtype=jnp.int32)
    valid_rows = (positions[None, :] < lengths[:, None]).astype(jnp.float32).reshape(own_rows, 1)
    root = newest_output // local_slots
    latest_local = lax.dynamic_index_in_dim(history, newest_output % local_slots, 0, keepdims=False)
    latest_rows = broadcast(latest_local, "hist", root)
    dynamic_weights, kept_mix = mix_forward(
        latest_rows.reshape(micro_count * sequence_length, features),
        gains_all[0],
        mix_in_all,
        mixer_output_wide,
    )
    dynamic_weights = dynamic_weights.reshape(
        micro_count, sequence_length, STREAM_COUNT, slot_count
    )
    own_table = lax.dynamic_slice_in_dim(layer_lookup, hist_place * local_slots, local_slots, 0)
    depth_combination_factors = jnp.einsum(
        "mtcj,sj->scmt", dynamic_weights, own_table, precision=highest
    )
    partial_sums = jnp.zeros((STREAM_COUNT, micro_count, sequence_length, features), jnp.float32)
    for depth_position_number in range(local_slots):
        partial_sums = (
            partial_sums
            + depth_combination_factors[depth_position_number][..., None]
            * history[depth_position_number].astype(jnp.float32)[None]
        )
    blended_residual_inputs = lax.psum_scatter(
        partial_sums, "hist", scatter_dimension=2, tiled=True
    )
    stream_rows = blended_residual_inputs.reshape(STREAM_COUNT, own_rows, features)
    normed = []
    inverses = []
    for stream_idx in range(STREAM_COUNT):
        scaled, inverse = rms_scale(stream_rows[stream_idx], gains_all[stream_idx + 1])
        normed.append(scaled.astype(jnp.bfloat16))
        inverses.append(inverse)
    head_shape = (micro_count, quarter, HEADS, HEAD_DIM)
    query_pre, key_pre, value_pre, up_pre = first_rows(
        (w_attn[0], w_attn[1], w_attn[2], w_up), (normed[0], normed[1], normed[2], normed[3])
    )
    attention_asker_vectors = rotate(query_pre.reshape(head_shape), positions, 1.0).astype(
        jnp.bfloat16
    )
    keys_rot = rotate(key_pre.reshape(head_shape), positions, 1.0).astype(jnp.bfloat16)
    values_low = value_pre.astype(jnp.bfloat16)
    keys_all, values_all = (
        lax.all_gather(
            keys_rot.reshape(micro_count, quarter, features), "hist", axis=1, tiled=True
        ),
        lax.all_gather(
            values_low.reshape(micro_count, quarter, features), "hist", axis=1, tiled=True
        ),
    )
    key_heads = keys_all.reshape(micro_count, sequence_length, HEADS, HEAD_DIM)
    value_wide = values_all.reshape(micro_count, sequence_length, HEADS, HEAD_DIM).astype(
        jnp.float32
    )
    score_scale = 1.0 / math.sqrt(HEAD_DIM)
    scores = (
        jnp.einsum(
            "mqhd,mkhd->mhqk",
            attention_asker_vectors,
            key_heads,
            preferred_element_type=jnp.float32,
        )
        * score_scale
    )
    key_positions = jnp.arange(sequence_length, dtype=jnp.int32)
    allowed = (key_positions[None, None, :] <= positions[None, :, None]) & (
        key_positions[None, None, :] < lengths[:, None, None]
    )
    scores = jnp.where(allowed[:, None], scores, masked_out)
    row_top = jnp.max(scores, axis=-1, keepdims=True)
    raised = jnp.exp(scores - row_top)
    soft_weights = raised / jnp.sum(raised, axis=-1, keepdims=True)
    attended = jnp.einsum("mhqk,mkhd->mqhd", soft_weights, value_wide, precision=highest)
    attended_low = attended.reshape(own_rows, features).astype(jnp.bfloat16)
    hidden = jax.nn.gelu(up_pre, approximate=False).astype(jnp.bfloat16)
    branch = second_rows(w_out, down_folded, attended_low, hidden, ratio)
    block_out = (
        ((stream_rows[3] + branch) * valid_rows)
        .astype(jnp.bfloat16)
        .reshape(micro_count, quarter, features)
    )
    grad_rows = cotangent.reshape(own_rows, features).astype(jnp.float32) * valid_rows
    grad_low = grad_rows.astype(jnp.bfloat16)
    attended_back, hidden_grad = back_first(w_out, down_folded, grad_low, ratio)
    up_grad = (hidden_grad * gelu_slope(up_pre)).astype(jnp.bfloat16)
    attended_grad = attended_back.astype(jnp.bfloat16)
    attended_wide = attended_grad.astype(jnp.float32).reshape(head_shape)
    prob_grad = jnp.einsum("mqhd,mkhd->mhqk", attended_wide, value_wide, precision=highest)
    inner_rows = jnp.sum(attended_wide * attended, axis=-1)
    logit_derivative = (
        soft_weights * (prob_grad - jnp.transpose(inner_rows, (0, 2, 1))[..., None]) * score_scale
    )
    query_grad = jnp.einsum(
        "mhqk,mkhd->mqhd", logit_derivative, key_heads.astype(jnp.float32), precision=highest
    )
    key_grad_all = jnp.einsum(
        "mhqk,mqhd->mkhd",
        logit_derivative,
        attention_asker_vectors.astype(jnp.float32),
        precision=highest,
    )
    value_grad_all = jnp.einsum("mhqk,mqhd->mkhd", soft_weights, attended_wide, precision=highest)
    key_grad, value_grad = (
        lax.psum_scatter(
            key_grad_all.reshape(micro_count, sequence_length, features).astype(jnp.bfloat16),
            "hist",
            scatter_dimension=1,
            tiled=True,
        ).astype(jnp.float32),
        lax.psum_scatter(
            value_grad_all.reshape(micro_count, sequence_length, features).astype(jnp.bfloat16),
            "hist",
            scatter_dimension=1,
            tiled=True,
        ).astype(jnp.float32),
    )
    projection_grads = [
        rotate(query_grad, positions, -1.0).reshape(own_rows, features).astype(jnp.bfloat16),
        rotate(key_grad.reshape(head_shape), positions, -1.0)
        .reshape(own_rows, features)
        .astype(jnp.bfloat16),
        value_grad.reshape(own_rows, features).astype(jnp.bfloat16),
    ]
    resid_normed_grad, query_normed_grad, key_normed_grad, value_normed_grad = back_second(
        (w_up, w_attn[0], w_attn[1], w_attn[2]),
        (up_grad, projection_grads[0], projection_grads[1], projection_grads[2]),
    )
    normed_grads = [query_normed_grad, key_normed_grad, value_normed_grad]
    stream_grads = []
    gain_grads = []
    for stream_idx in range(3):
        stream_grad, gain_grad = rms_back(
            stream_rows[stream_idx],
            inverses[stream_idx],
            gains_all[stream_idx + 1],
            normed_grads[stream_idx],
        )
        stream_grads.append(stream_grad)
        gain_grads.append(gain_grad)
    resid_grad, skip_scaling_derivative = rms_back(
        stream_rows[3], inverses[3], gains_all[4], resid_normed_grad
    )
    stream_grads.append(resid_grad + grad_rows)
    gain_grads.append(skip_scaling_derivative)
    stream_grads_all = jnp.stack(stream_grads).reshape(STREAM_COUNT, micro_count, quarter, features)
    full_grads = lax.all_gather(
        stream_grads_all.astype(jnp.bfloat16), "hist", axis=2, tiled=True
    ).astype(stream_grads_all.dtype)
    slot_grads = []
    dyn_grad = jnp.zeros((micro_count, sequence_length, STREAM_COUNT, slot_count), jnp.float32)
    for depth_position_number in range(local_slots):
        rows_now = history[depth_position_number].astype(jnp.float32)
        slot_grads.append(
            jnp.sum(
                depth_combination_factors[depth_position_number][..., None] * full_grads, axis=0
            )
        )
        inner_now = jnp.sum(full_grads * rows_now[None], axis=-1)
        dyn_grad = dyn_grad + jnp.einsum("cmt,j->mtcj", inner_now, own_table[depth_position_number])
    dyn_grad = dyn_grad.reshape(micro_count * sequence_length, STREAM_COUNT * slot_count)
    act_part = precise(dyn_grad, mixer_output_wide.T)
    mix_out_grad = precise(kept_mix[4].T, dyn_grad)
    act_grad = lax.psum(act_part.astype(jnp.bfloat16), "hist").astype(jnp.float32)
    on_root = (hist_place == root).astype(jnp.float32)
    latest_grad, gain_zero, mix_in_grad = mix_backward(kept_mix, act_grad, gains_all[0], mix_in_all)
    gain_zero = gain_zero * on_root
    mix_in_grad = mix_in_grad * on_root
    latest_grad = latest_grad.reshape(micro_count, sequence_length, features)
    marked = []
    for depth_position_number in range(local_slots):
        is_latest = (hist_place * local_slots + depth_position_number == newest_output).astype(
            jnp.float32
        )
        marked.append(slot_grads[depth_position_number] + latest_grad * is_latest)
    history_grad = jnp.stack(marked).astype(jnp.bfloat16)
    gains_grad_full = jnp.stack(
        [gain_zero, gain_grads[0], gain_grads[1], gain_grads[2], gain_grads[3]]
    )
    share_rows = w_out.shape[0]
    per_device = mix_width // dp_count
    mix_out_padded = jnp.pad(
        mix_out_grad.reshape(dp_count, per_device, mix_width),
        ((0, 0), (0, share_rows - per_device), (0, 0)),
    ).reshape(dp_count * share_rows, mix_width)
    small_wide = jnp.concatenate([mix_in_grad, gains_grad_full.T, mix_out_padded], axis=1)
    attn_lefts = (normed[0], normed[1], normed[2], attended_low)
    attn_rights = (projection_grads[0], projection_grads[1], projection_grads[2], grad_low)
    attn_share = lax.psum_scatter(
        jnp.concatenate(
            [
                lax.dot_general(
                    left_side, right_side, contract_rows, preferred_element_type=jnp.float32
                )
                for left_side, right_side in zip(attn_lefts, attn_rights)
            ],
            axis=1,
        ).astype(jnp.bfloat16),
        "dp",
        scatter_dimension=0,
        tiled=True,
    )
    up_term = lax.dot_general(normed[3], up_grad, contract_rows, preferred_element_type=jnp.float32)
    down_term = lax.dot_general(
        hidden, grad_low, contract_rows, preferred_element_type=jnp.float32
    ).reshape(share_rows * lax.axis_size("dp"), ratio * features)
    ffn_share = lax.psum_scatter(
        jnp.concatenate([up_term, down_term, small_wide], axis=1).astype(jnp.bfloat16),
        "dp",
        scatter_dimension=0,
        tiled=True,
    )
    attn_total, ffn_total = (
        lax.psum(attn_share, "hist").astype(jnp.float32),
        lax.psum(ffn_share, "hist").astype(jnp.float32),
    )
    ff_width = ratio * features
    w_attn_grad = jnp.stack(
        [
            attn_total[:, 0:features],
            attn_total[:, features : 2 * features],
            attn_total[:, 2 * features : 3 * features],
        ]
    )
    w_out_grad = attn_total[:, 3 * features : 4 * features]
    w_up_grad = ffn_total[:, 0:ff_width]
    w_down_grad = ffn_total[:, ff_width : 2 * ff_width].reshape(share_rows * ratio, features)
    mix_in_share = ffn_total[:, 2 * ff_width : 2 * ff_width + mix_width]
    gains_share = ffn_total[:, 2 * ff_width + mix_width : 2 * ff_width + mix_width + 5].T
    mix_out_share = ffn_total[0:per_device, 2 * ff_width + mix_width + 5 :]
    return (
        block_out,
        history_grad,
        gains_share,
        mix_in_share,
        mix_out_share,
        w_attn_grad,
        w_out_grad,
        w_up_grad,
        w_down_grad,
    )


DEVICE_MESH = pl.DeviceIdType.MESH
CORE, ACROSS_X, ACROSS_Y = 1, 2, 4


def partner(column, mask):
    moved = column
    for bit in (1, 2, 4):
        if mask & bit:
            on = lax.rem(lax.div(moved, bit), 2)
            moved = moved + bit - 2 * bit * on
    return moved


def push(source, target, send_sem, recv_sem, place):
    copy = pltpu.make_async_remote_copy(
        src_ref=source,
        dst_ref=target,
        send_sem=send_sem,
        recv_sem=recv_sem,
        device_id={"dp": place},
        device_id_type=DEVICE_MESH,
    )
    copy.start()
    return copy


def z_place(plane):
    return {"hist": plane}


class PlaneGatherSteps:

    def __init__(self, column, own, whole, send_sem, recv_sem, local_sem):
        self.column, self.own, self.whole = column, own, whole
        self.send_sem, self.recv_sem, self.local_sem = send_sem, recv_sem, local_sem
        self.rows = own.shape[0]
        self.half = self.rows // 2
        self.across = partner(column, ACROSS_X)
        self.along = partner(column, ACROSS_Y)
        self.beside = partner(column, CORE)
        self.corner = partner(column, ACROSS_X + ACROSS_Y)
        self.copies = []

    def place(self, owner, part):
        start = owner * self.rows + (self.half if part == 1 else 0)
        count = self.rows if part is None else self.half
        return self.whole.at[pl.ds(pl.multiple_of(start, 16), count)]

    def mine(self, part):
        start = self.half if part == 1 else 0
        return self.own.at[pl.ds(start, self.rows if part is None else self.half)]

    def send(self, source, owner, part, to):
        index = len(self.copies)
        copy = push(
            source, self.place(owner, part), self.send_sem.at[index], self.recv_sem.at[index], to
        )
        self.copies.append(copy)

    def begin(self):
        me = self.column
        self.local = pltpu.make_async_copy(self.mine(None), self.place(me, None), self.local_sem)
        self.local.start()
        self.send(self.mine(1), me, 1, self.across)
        self.send(self.mine(0), me, 0, self.along)
        self.send(self.mine(0), me, 0, self.across)
        self.send(self.mine(1), me, 1, self.along)
        self.send(self.mine(None), me, None, self.beside)

    def corners(self):
        self.copies[1].wait_recv()
        self.send(self.place(self.along, 0), self.along, 0, self.across)
        self.copies[0].wait_recv()
        self.send(self.place(self.across, 1), self.across, 1, self.along)

    def siblings(self):
        self.copies[2].wait_recv()
        self.send(self.place(self.across, None), self.across, None, self.beside)
        self.copies[3].wait_recv()
        self.send(self.place(self.along, None), self.along, None, self.beside)

    def rest(self):
        self.copies[5].wait_recv()
        self.send(self.place(self.corner, 0), self.corner, 0, self.beside)
        self.copies[6].wait_recv()
        self.send(self.place(self.corner, 1), self.corner, 1, self.beside)

    def finish(self):
        for index in (4, 7, 8, 9, 10):
            self.copies[index].wait_recv()
        for copy in self.copies:
            copy.wait_send()
        self.local.wait()


class PlaneScatterSteps:
    def __init__(self, column, product, refs, send_sem, recv_sem):
        self.column, self.product = column, product
        self.out_buf, self.side, self.chip, self.from_x, self.from_y, self.last = refs
        self.send_sem, self.recv_sem = send_sem, recv_sem
        rows = self.chip.shape[1]
        self.first, self.second = pl.ds(0, rows // 2), pl.ds(rows // 2, rows // 2)
        self.across = partner(column, ACROSS_X)
        self.along = partner(column, ACROSS_Y)
        self.beside = partner(column, CORE)
        self.pair, self.sends = [], []

    def block(self, i):
        mask = (6, 2, 4, 0)[i]
        if i >= 2:
            self.pair[i - 2].wait_send()
        self.product(partner(self.column, mask + CORE), self.out_buf.at[i % 2])
        self.pair.append(
            push(
                self.out_buf.at[i % 2],
                self.side.at[i],
                self.send_sem.at[i],
                self.recv_sem.at[i],
                self.beside,
            )
        )
        self.product(partner(self.column, mask), self.chip.at[i])
        self.pair[i].wait_recv()
        add_into(self.chip.at[i], self.side.at[i])
        if i == 0:
            self.send(self.chip.at[0, self.first], self.from_x.at[0], self.across)
            self.send(self.chip.at[0, self.second], self.from_y.at[0], self.along)
        if i == 1:
            self.send(self.chip.at[1, self.first], self.from_x.at[1], self.across)
        if i == 2:
            self.send(self.chip.at[2, self.second], self.from_y.at[1], self.along)

    def send(self, source, target, to):
        index = 4 + len(self.sends)
        self.sends.append(
            push(source, target, self.send_sem.at[index], self.recv_sem.at[index], to)
        )

    def turn(self):
        self.sends[0].wait_recv()
        add_into(self.chip.at[2, self.first], self.from_x.at[0])
        self.send(self.chip.at[2, self.first], self.last.at[0], self.along)
        self.sends[1].wait_recv()
        add_into(self.chip.at[1, self.second], self.from_y.at[0])
        self.send(self.chip.at[1, self.second], self.last.at[1], self.across)

    def finish(self, out_ref):
        self.sends[2].wait_recv()
        add_into(self.chip.at[3, self.first], self.from_x.at[1])
        self.sends[3].wait_recv()
        add_into(self.chip.at[3, self.second], self.from_y.at[1])
        self.sends[4].wait_recv()
        add_into(self.chip.at[3, self.first], self.last.at[0])
        self.sends[5].wait_recv()
        add_into(self.chip.at[3, self.second], self.last.at[1])
        if out_ref is not None:
            out_ref[...] = self.chip[3]
        for copy in self.pair[2:] + self.sends:
            copy.wait_send()


def add_into(target, other):
    rows = target.shape[0]
    step = 32 if rows % 32 == 0 else 16

    def some_rows(r, carry):
        piece = pl.ds(pl.multiple_of(r * step, step), step)
        target[piece, :] = (
            target[piece, :].astype(jnp.float32) + other[piece, :].astype(jnp.float32)
        ).astype(jnp.bfloat16)
        return carry

    lax.fori_loop(0, rows // step, some_rows, 0)


class LineSums:

    def __init__(self, plane, parts, arrived, own, last, held, send_sem, recv_sem, load_sem):
        self.plane, self.parts, self.arrived = plane, parts, arrived
        self.own, self.last, self.held = own, last, held
        self.send_sem, self.recv_sem, self.load_sem = send_sem, recv_sem, load_sem
        self.rows = own.shape[0]

    def part(self, way, item, b):
        place = b if way == 0 else 3 - b
        return self.parts.at[pl.ds((item * 4 + place) * self.rows, self.rows)]

    def message(self, way, turn, a, source):
        to = a + 1 if way == 0 else 2 - a
        return pltpu.make_async_remote_copy(
            src_ref=source,
            dst_ref=self.arrived.at[way * 12 + turn],
            send_sem=self.send_sem.at[way * 12 + turn],
            recv_sem=self.recv_sem.at[way * 12 + turn],
            device_id=z_place(to),
            device_id_type=DEVICE_MESH,
        )

    def origin(self, way, turn):
        item, t = divmod(turn, 3)
        return self.message(way, turn, 0, self.part(way, item, 3 - t))

    def slot(self, way, a, turn):
        item, t = divmod(turn, 3)
        return way * 2 + (item * (3 - a) + t) % 2

    def relay(self, way, turn, a):
        return self.message(way, turn, a, self.held.at[self.slot(way, a, turn)])

    def start(self, turn):
        for place in (0, 3):

            @pl.when(self.plane == place)
            def _():
                self.origin(0 if place == 0 else 1, turn).start()

    def load(self, source, target, index):
        return pltpu.make_async_copy(source, target, self.load_sem.at[index])

    def service(self, sigma):
        for place in range(4):

            @pl.when(self.plane == place)
            def _():
                for way in (0, 1):
                    a = place if way == 0 else 3 - place
                    if a == 0:
                        if sigma < 12:
                            self.origin(way, sigma).wait_send()
                        if sigma + 2 < 12:
                            self.origin(way, sigma + 2).start()
                        continue
                    turn = sigma - a + 1
                    if turn < 0 or turn >= 12:
                        continue
                    item, t = divmod(turn, 3)
                    b = 3 - t
                    if b < a:
                        continue
                    if b > a:
                        slot = self.slot(way, a, turn)
                        sent = [
                            earlier
                            for earlier in range(turn)
                            if 3 - earlier % 3 > a and self.slot(way, a, earlier) == slot
                        ]
                        if sent:
                            self.relay(way, sent[-1], a).wait_send()
                        target = self.held.at[slot]
                        mine = self.load(self.part(way, item, b), self.own, 0)
                        mine.start()
                        self.relay(way, turn, a).wait_recv()
                        came = self.load(self.arrived.at[way * 12 + turn], target, 1)
                        came.start()
                        mine.wait()
                        came.wait()
                        add_into(target, self.own)
                        self.relay(way, turn, a).start()
                    else:
                        self.message(way, turn, a - 1, self.own).wait_recv()
                        came = self.load(self.arrived.at[way * 12 + turn], self.last.at[way], 1)
                        came.start()
                        came.wait()
                if sigma % 3 == 2:
                    item = sigma // 3
                    mine = self.load(self.part(0, item, place), self.own, 0)
                    mine.start()
                    mine.wait()

    def drain(self):
        for place in range(4):

            @pl.when(self.plane == place)
            def _():
                for way in (0, 1):
                    a = place if way == 0 else 3 - place
                    if a == 0 or a == 3:
                        continue
                    for slot in (way * 2, way * 2 + 1):
                        sent = [
                            turn
                            for turn in range(12)
                            if 3 - turn % 3 > a and self.slot(way, a, turn) == slot
                        ]
                        self.relay(way, sent[-1], a).wait_send()


class LineSum:

    def __init__(
        self, plane, parts, arrived, own, last, held, send_sem, recv_sem, load_sem, stride, first
    ):
        self.plane, self.parts, self.arrived = plane, parts, arrived
        self.own, self.last, self.held = own, last, held
        self.send_sem, self.recv_sem, self.load_sem = send_sem, recv_sem, load_sem
        self.rows, self.stride, self.first = own.shape[0], stride, first

    def part(self, way, b):
        place = b if way == 0 else 3 - b
        return self.parts.at[pl.ds(place * self.stride + self.first, self.rows)]

    def message(self, way, t, a, source):
        return pltpu.make_async_remote_copy(
            src_ref=source,
            dst_ref=self.arrived.at[way * 3 + t],
            send_sem=self.send_sem.at[way * 3 + t],
            recv_sem=self.recv_sem.at[way * 3 + t],
            device_id=z_place(a + 1 if way == 0 else 2 - a),
            device_id_type=DEVICE_MESH,
        )

    def origin(self, way, t):
        return self.message(way, t, 0, self.part(way, 3 - t))

    def relay(self, way, t, a):
        return self.message(way, t, a, self.held.at[t if a == 1 else 2])

    def start(self):
        for place in (0, 3):

            @pl.when(self.plane == place)
            def _():
                way = 0 if place == 0 else 1
                self.origin(way, 0).start()
                self.origin(way, 1).start()

    def load(self, source, target, index):
        copy = pltpu.make_async_copy(source, target, self.load_sem.at[index])
        copy.start()
        return copy

    def service(self, sigma):
        for place in range(4):

            @pl.when(self.plane == place)
            def _():
                for way in (0, 1):
                    a = place if way == 0 else 3 - place
                    if a == 0:
                        self.origin(way, sigma).wait_send()
                        if sigma == 0:
                            self.origin(way, 2).start()
                        continue
                    t = sigma - a + 1
                    if t < 0 or 3 - t < a:
                        continue
                    b = 3 - t
                    source = self.arrived.at[way * 3 + t]
                    if b > a:
                        relay = self.relay(way, t, a)
                        target = self.held.at[t if a == 1 else 2]
                        mine = self.load(self.part(way, b), self.own, 0)
                        relay.wait_recv()
                        came = self.load(source, target, 1)
                        mine.wait()
                        came.wait()
                        add_into(target, self.own)
                        relay.start()
                    else:
                        self.message(way, t, a - 1, self.own).wait_recv()
                        self.load(source, self.last.at[way], 1).wait()
                if sigma == 2:
                    self.load(self.part(0, place), self.own, 0).wait()

    def finish(self, target):
        step = 16

        def some_rows(r, carry):
            piece = pl.ds(pl.multiple_of(r * step, step), step)
            total = self.own[piece, :].astype(jnp.float32)
            total = total + self.last[0, piece, :].astype(jnp.float32)
            total = total + self.last[1, piece, :].astype(jnp.float32)
            target[piece, :] = total.astype(jnp.bfloat16)
            return carry

        lax.fori_loop(0, self.rows // step, some_rows, 0)
        for place in (1, 2):

            @pl.when(self.plane == place)
            def _():
                for way in (0, 1):
                    a = place if way == 0 else 3 - place
                    for t in range(3 - a):
                        self.relay(way, t, a).wait_send()


class LineGather:

    def __init__(self, plane, own, slot, send_sem, recv_sem, local_sem):
        self.plane, self.own, self.slot = plane, own, slot
        self.send_sem, self.recv_sem, self.local_sem = send_sem, recv_sem, local_sem

    def message(self, way, a, distance):
        origin = a - distance
        plane_of_origin = origin if way == 0 else 3 - origin
        target = self.slot(plane_of_origin)
        return pltpu.make_async_remote_copy(
            src_ref=self.own if distance == 0 else target,
            dst_ref=target,
            send_sem=self.send_sem.at[way * 3 + distance],
            recv_sem=self.recv_sem.at[way * 3 + distance],
            device_id=z_place(a + 1 if way == 0 else 2 - a),
            device_id_type=DEVICE_MESH,
        )

    def service(self, step):
        for place in range(4):

            @pl.when(self.plane == place)
            def _():
                if step == 0:
                    pltpu.make_async_copy(self.own, self.slot(place), self.local_sem).start()
                for way in (0, 1):
                    a = place if way == 0 else 3 - place
                    if step > a:
                        continue
                    if step > 0:
                        self.message(way, a - 1, step - 1).wait_recv()
                    if a < 3:
                        self.message(way, a, step).start()

    def placed(self):
        for place in range(4):

            @pl.when(self.plane == place)
            def _():
                pltpu.make_async_copy(self.own, self.slot(place), self.local_sem).wait()

    def finish(self):
        for place in range(4):

            @pl.when(self.plane == place)
            def _():
                for way in (0, 1):
                    a = place if way == 0 else 3 - place
                    if a < 3:
                        for distance in range(a + 1):
                            self.message(way, a, distance).wait_send()


GAIN_ROW = (4, 1, 2, 3)


def norm_rows_back(x_buf, back, gain_ref, gain_grad_ref, item, extra, target):
    gain = gain_ref[pl.ds(GAIN_ROW[item], 1), :]
    rows, features = target.shape

    def some_rows(r, gain_sum):
        piece = pl.ds(pl.multiple_of(r * 16, 16), 16)
        x = x_buf[piece, :]
        inverse = lax.rsqrt(jnp.mean(x * x, axis=-1, keepdims=True) + epsilon)
        grad = back[piece, :].astype(jnp.float32)
        scaled = grad * gain
        mean = jnp.mean(scaled * x, axis=-1, keepdims=True)
        result = inverse * scaled - x * (inverse * inverse * inverse) * mean
        if extra is not None:
            result = result + extra[piece, :].astype(jnp.float32)
        target[piece, :] = result.astype(jnp.bfloat16)
        return gain_sum + jnp.sum(grad * x * inverse, axis=0, keepdims=True)

    gain_grad_ref[pl.ds(item, 1), :] = lax.fori_loop(
        0, rows // 16, some_rows, jnp.zeros((1, features), jnp.float32)
    )


def forward_kernel(
    length_ref,
    pack_ref,
    latest_ref,
    history_ref,
    select_ref,
    root_ref,
    cotangent_ref,
    w_up_ref,
    w_attn_ref,
    w_down_ref,
    w_out_ref,
    cos_ref,
    sin_ref,
    packed_ref,
    gain_ref,
    pre_ref,
    factor_ref,
    x_ref,
    normed_ref,
    grad_all_ref,
    hidden_ref,
    up_term_ref,
    down_sum_ref,
    full3_ref,
    gain_grad_ref,
    attn_columns,
    q_ref,
    k_ref,
    v_ref,
    out_grad_ref,
    key_before_ref,
    part_ref,
    down_term_ref,
    arrived_ref,
    arrived_down_ref,
    normed3,
    grads,
    up_columns,
    up_grad,
    out_buf,
    side,
    chip,
    from_x,
    from_y,
    last,
    own,
    ends,
    held,
    x_buf,
    normed_buf,
    term_buf,
    grad_own,
    stream_own,
    mix_out_buf,
    dyn_got,
    gather_send,
    gather_recv,
    gather_local,
    scatter_send,
    scatter_recv,
    line_send,
    line_recv,
    line_load,
    swap_send,
    swap_recv,
    swap_local,
    out_sem,
    small_send,
    small_recv,
    dyn_send,
    dyn_recv,
    route_send,
    route_recv,
    block_sem,
    spread_send,
    spread_recv,
    sum_send,
    sum_recv,
    key_send,
    key_recv,
    ready_sem,
    *,
    micro_count,
    sequence_length,
):
    column = lax.axis_index("dp")
    plane = lax.axis_index("hist")
    rows, features = grad_own.shape
    total = 8 * rows
    share = w_up_ref.shape[0]
    ff_share = w_down_ref.shape[0]
    width = share
    tile = 256
    mix_rows = pack_ref.shape[0] - share - 32 + 8
    every_mask = (6, 7, 2, 3, 4, 5, 1)

    barrier = pltpu.get_barrier_semaphore()
    for mask in every_mask:
        pl.semaphore_signal(
            barrier, inc=1, device_id={"dp": partner(column, mask)}, device_id_type=DEVICE_MESH
        )
    for place in range(4):

        @pl.when(plane == place)
        def _():
            for p in range(4):
                if p != place:
                    pl.semaphore_signal(
                        barrier, inc=1, device_id=z_place(p), device_id_type=DEVICE_MESH
                    )

    pl.semaphore_wait(barrier, 10)

    def block_load(source, target, index):
        copy = pltpu.make_async_copy(source, target, block_sem.at[index])
        copy.start()
        return copy

    small_copies = [
        push(
            pack_ref,
            packed_ref.at[column],
            small_send.at[mask],
            small_recv.at[mask],
            partner(column, mask),
        )
        for mask in every_mask
    ]
    small_local = pltpu.make_async_copy(pack_ref, packed_ref.at[column], small_send.at[0])
    small_local.start()
    latest_loads = [
        block_load(latest_ref.at[pl.ds(q * rows, rows)], normed_buf.at[q], 8 + q) for q in range(4)
    ]

    my_rows = pl.ds(pl.multiple_of(column * share, 16), share)

    def up_piece(owner):
        return w_up_ref.at[:, pl.ds(pl.multiple_of(owner * ff_share, 128), ff_share)]

    up_local = pltpu.make_async_copy(up_piece(column), up_columns.at[my_rows], swap_local.at[0])
    up_local.start()
    up_swaps = [
        push(
            up_piece(partner(column, mask)),
            up_columns.at[my_rows],
            swap_send.at[mask],
            swap_recv.at[mask],
            partner(column, mask),
        )
        for mask in every_mask
    ]

    chunk = rows // micro_count

    def route_source(place, s):
        return cotangent_ref.at[pl.ds(s * chunk, chunk)]

    def route_copy(place, s, target_place, slot):
        return pltpu.make_async_remote_copy(
            src_ref=route_source(place, s),
            dst_ref=grad_own.at[pl.ds(slot * chunk, chunk)],
            send_sem=route_send.at[s],
            recv_sem=route_recv.at[slot],
            device_id=z_place(target_place),
            device_id_type=DEVICE_MESH,
        )

    def route_local(place, s, slot):
        return pltpu.make_async_copy(
            route_source(place, s), grad_own.at[pl.ds(slot * chunk, chunk)], route_recv.at[slot]
        )

    for place in range(4):

        @pl.when(plane == place)
        def _():
            for s in range(micro_count):
                target_place, slot = divmod(s * 4 + place, micro_count)
                if target_place == place:
                    route_local(place, s, slot).start()
                else:
                    route_copy(place, s, target_place, slot).start()

    block_order = (3, 0, 2, 1)

    def history_loads(i):
        p, h = block_order[i], i % 2
        return [
            block_load(
                history_ref.at[pl.ds((slot * 4 + p) * rows, rows)],
                normed3.at[pl.ds((h * 4 + slot) * rows, rows)],
                h * 4 + slot,
            )
            for slot in range(4)
        ]

    loads = [history_loads(0), history_loads(1)]
    zeros = jnp.zeros((16, features), jnp.bfloat16)

    def clear(r, carry):
        ends[0, pl.ds(pl.multiple_of(r * 16, 16), 16), :] = zeros
        ends[1, pl.ds(pl.multiple_of(r * 16, 16), 16), :] = zeros
        return carry

    lax.fori_loop(0, ends.shape[1] // 16, clear, 0)

    small_local.wait()
    for copy in small_copies:
        copy.wait_recv()
    for d in range(8):
        gains = packed_ref[d, pl.ds(share + 16, 16), :].astype(jnp.float32)
        gain_ref[:, pl.ds(d * share, share // 2)] = gains[:8]
        gain_ref[:, pl.ds(d * share + share // 2, share // 2)] = gains[8:]
        mix_out_buf[pl.ds(d * mix_rows, mix_rows), :] = packed_ref[
            d, pl.ds(share, 16), :
        ].astype(jnp.float32)[:mix_rows]
    for copy in latest_loads:
        copy.wait()
    for q in range(4):

        def norm_rows(r, carry):
            piece = pl.ds(pl.multiple_of(r * 16, 16), 16)
            x = normed_buf[q, piece, :].astype(jnp.float32)
            inverse = lax.rsqrt(jnp.mean(x * x, axis=-1, keepdims=True) + epsilon)
            normed_buf[q, piece, :] = (x * inverse * gain_ref[pl.ds(0, 1), :]).astype(jnp.bfloat16)
            return carry

        lax.fori_loop(0, rows // 16, norm_rows, 0)
        pre = None
        for d in range(8):
            term = matmul(normed_buf[q, :, d * share : (d + 1) * share], packed_ref[d, :share, :])
            pre = term if pre is None else pre + term
        pre_ref[pl.ds(q * rows, rows), :] = pre
    pre = pre_ref[...]
    act = 0.5 * pre * (1.0 + lax.erf(pre * (1.0 / math.sqrt(2.0))))
    dyn = precise(act[:, : 8 * mix_rows], mix_out_buf[...])
    dyn_columns = (jnp.transpose(dyn)[: 8 * mix_rows] * root_ref[pl.ds(0, 1), :]).astype(jnp.bfloat16)

    def dyn_copy(source_place, target_place):
        return pltpu.make_async_remote_copy(
            src_ref=dyn_got.at[source_place],
            dst_ref=dyn_got.at[source_place],
            send_sem=dyn_send.at[target_place],
            recv_sem=dyn_recv.at[source_place],
            device_id=z_place(target_place),
            device_id_type=DEVICE_MESH,
        )

    for place in range(4):

        @pl.when(plane == place)
        def _():
            dyn_got[place] = dyn_columns
            for p in range(4):
                if p != place:
                    dyn_copy(place, p).start()
            for p in range(4):
                if p != place:
                    dyn_copy(p, place).wait_recv()

    dyn_sum = dyn_got[0] + dyn_got[1] + dyn_got[2] + dyn_got[3]
    factor_ref[...] = lax.dot_general(
        dyn_sum, select_ref[...], contract_rows, preferred_element_type=jnp.float32
    )

    block = pl.ds(0, rows)
    line = LineSums(
        plane,
        part_ref,
        arrived_ref,
        own.at[block],
        ends.at[:, block],
        held.at[:, block],
        line_send,
        line_recv,
        line_load,
    )
    stores = [None, None]
    for i, p in enumerate(block_order):
        h = i % 2
        for copy in loads[i]:
            copy.wait()
        if stores[h] is not None:
            for copy in stores[h]:
                copy.wait()

        def mix_rows_of(r, carry):
            factors = factor_ref[pl.ds(pl.multiple_of(p * rows + r * 16, 16), 16), :]
            for lane in range(0, features, 512):
                slots = [
                    normed3[
                        pl.ds(pl.multiple_of((h * 4 + slot) * rows + r * 16, 16), 16),
                        lane : lane + 512,
                    ].astype(jnp.float32)
                    for slot in range(4)
                ]
                for item in range(4):
                    mixed = None
                    for slot in range(4):
                        one = item * 4 + slot
                        term = factors[:, one : one + 1] * slots[slot]
                        mixed = term if mixed is None else mixed + term
                    grads[
                        pl.ds(pl.multiple_of((h * 4 + item) * rows + r * 16, 16), 16),
                        lane : lane + 512,
                    ] = mixed.astype(jnp.bfloat16)
            return carry

        lax.fori_loop(0, rows // 16, mix_rows_of, 0)
        stores[h] = [
            pltpu.make_async_copy(
                grads.at[pl.ds((h * 4 + item) * rows, rows)],
                part_ref.at[pl.ds((item * 4 + p) * rows, rows)],
                block_sem.at[12 + h * 4 + item],
            )
            for item in range(4)
        ]
        for copy in stores[h]:
            copy.start()
        if i + 2 < 4:
            loads.append(history_loads(i + 2))
        if i % 2 == 1:
            for copies in stores:
                for copy in copies:
                    copy.wait()
            stores = [None, None]
        if i == 1:
            line.start(0)

    line.start(1)
    for mask in (CORE, ACROSS_X, ACROSS_Y):
        pl.semaphore_signal(
            ready_sem, inc=1, device_id={"dp": partner(column, mask)}, device_id_type=DEVICE_MESH
        )

    def attn_piece(stream, owner):
        return w_attn_ref.at[stream, :, pl.ds(pl.multiple_of(owner * share, 128), share)]

    def gather(index, own_rows, whole):
        return PlaneGatherSteps(
            column,
            own_rows,
            whole,
            gather_send.at[index],
            gather_recv.at[index],
            gather_local.at[index],
        )

    for place in range(4):

        @pl.when(plane == place)
        def _():
            for slot in range(micro_count):
                s, source_place = divmod(place * micro_count + slot, 4)
                if source_place == place:
                    route_local(place, s, slot).wait()
                else:
                    route_copy(source_place, s, place, slot).wait_recv()

    def mask_rows(r, carry):
        piece = pl.ds(pl.multiple_of(r * 16, 16), 16)
        row = plane * rows + r * 16 + lax.broadcasted_iota(jnp.int32, (16, 1), 0)
        limit = jnp.zeros((16, 1), jnp.int32)
        for m in range(micro_count):
            inside = (row >= m * sequence_length) & (row < (m + 1) * sequence_length)
            limit = jnp.where(inside, m * sequence_length + length_ref[m], limit)
        kept = jnp.where(row < limit, grad_own[piece, :].astype(jnp.float32), 0.0)
        grad_own[piece, :] = kept.astype(jnp.bfloat16)
        return carry

    lax.fori_loop(0, rows // 16, mask_rows, 0)
    pl.semaphore_wait(ready_sem, 3)
    grad_gather = gather(4, grad_own, grads)
    grad_gather.begin()

    x_copies = []

    def combine(item):
        if x_copies:
            x_copies[-1].wait()

        def some_rows(r, carry):
            piece = pl.ds(pl.multiple_of(r * 16, 16), 16)
            x = (
                own[piece, :].astype(jnp.float32)
                + ends[0, piece, :].astype(jnp.float32)
                + ends[1, piece, :].astype(jnp.float32)
            )
            x_buf[piece, :] = x
            inverse = lax.rsqrt(jnp.mean(x * x, axis=-1, keepdims=True) + epsilon)
            normed_buf[item, piece, :] = (
                x * inverse * gain_ref[pl.ds(GAIN_ROW[item], 1), :]
            ).astype(jnp.bfloat16)
            return carry

        lax.fori_loop(0, rows // 16, some_rows, 0)
        copy = pltpu.make_async_copy(x_buf, x_ref.at[item], out_sem.at[0])
        copy.start()
        x_copies.append(copy)
        steps = gather(
            item, normed_buf.at[item], normed3 if item == 0 else normed_ref.at[item - 1]
        )
        steps.begin()
        return steps

    line.service(0)
    line.service(1)
    grad_gather.corners()
    grad_gather.siblings()
    line.service(2)
    gather3 = combine(0)
    grad_gather.rest()
    grad_gather.finish()
    grads_out = pltpu.make_async_copy(grads, grad_all_ref, out_sem.at[2])
    grads_out.start()
    gather3.corners()
    line.service(3)
    gather3.siblings()
    gather3.rest()
    line.service(4)
    for copy in up_swaps:
        copy.wait_recv()
    up_local.wait()
    gather3.finish()
    attn_swaps, attn_locals = [], []
    for stream in range(3):
        local = pltpu.make_async_copy(
            attn_piece(stream, column),
            attn_columns.at[stream, my_rows],
            swap_local.at[1 + stream],
        )
        local.start()
        attn_locals.append(local)
        for mask in every_mask:
            attn_swaps.append(
                push(
                    attn_piece(stream, partner(column, mask)),
                    attn_columns.at[stream, my_rows],
                    swap_send.at[8 * (stream + 1) + mask],
                    swap_recv.at[8 * (stream + 1) + mask],
                    partner(column, mask),
                )
            )

    def feed(first_block, count):
        def one_tile(step, carry):
            piece = pl.ds(pl.multiple_of((step // (ff_share // tile)) * rows, 16), rows)
            lanes = pl.ds(pl.multiple_of((step % (ff_share // tile)) * tile, tile), tile)
            up = jnp.dot(normed3[piece, :], up_columns[:, lanes], preferred_element_type=jnp.float32)
            spread = 0.5 * (1.0 + lax.erf(up * (1.0 / math.sqrt(2.0))))
            hidden_ref[piece, lanes] = (up * spread).astype(jnp.bfloat16)
            slope = spread + up * jnp.exp(-0.5 * up * up) * (1.0 / math.sqrt(2.0 * math.pi))
            hidden_grad = lax.dot_general(
                grads[piece, :],
                w_down_ref[lanes, :],
                contract_cols,
                preferred_element_type=jnp.float32,
            )
            up_grad[piece, lanes] = (hidden_grad * slope).astype(jnp.bfloat16)
            return carry

        per_block = ff_share // tile
        lax.fori_loop(first_block * per_block, (first_block + count) * per_block, one_tile, 0)

    def back_product(owner, target):
        left_rows = pl.ds(pl.multiple_of(owner * rows, 16), rows)

        def one_tile(t, carry):
            lanes = pl.ds(pl.multiple_of(t * 2 * tile, 2 * tile), 2 * tile)
            target[:, lanes] = lax.dot_general(
                up_grad[left_rows, :],
                up_columns[lanes, :],
                contract_cols,
                preferred_element_type=jnp.float32,
            ).astype(jnp.bfloat16)
            return carry

        lax.fori_loop(0, features // (2 * tile), one_tile, 0)

    term_slots = 2
    part = share // 4

    def term_copies(kind, slot, index):
        if kind == 0:
            return [
                pltpu.make_async_copy(
                    term_buf.at[slot, pl.ds(h * part, part), pl.ds(0, ff_share)],
                    up_term_ref.at[
                        pl.ds(h * 4 * part + index % 4 * part, part),
                        pl.ds(index // 4 * ff_share, ff_share),
                    ],
                    out_sem.at[3 + 4 * slot + h],
                )
                for h in range(4)
            ]
        return [
            pltpu.make_async_copy(
                term_buf.at[slot],
                down_term_ref.at[pl.ds(index * tile, tile)],
                out_sem.at[3 + 4 * slot],
            )
        ]

    def terms(kind, first, count):
        term_width = ff_share if kind == 0 else features
        pending = []
        for index in range(first, first + count):
            slot = index % term_slots
            if len(pending) >= term_slots:
                for copy in pending[-term_slots]:
                    copy.wait()

            def one_tile(t, carry):
                lanes = pl.ds(pl.multiple_of(t * 2 * tile, 2 * tile), 2 * tile)
                if kind == 0:
                    left, right = normed3[:, index * tile : (index + 1) * tile], up_grad[:, lanes]
                else:
                    left, right = hidden_ref[:, index * tile : (index + 1) * tile], grads[:, lanes]
                term_buf[slot, :, lanes] = lax.dot_general(
                    left, right, contract_rows, preferred_element_type=jnp.float32
                ).astype(jnp.bfloat16)
                return carry

            lax.fori_loop(0, term_width // (2 * tile), one_tile, 0)
            copies = term_copies(kind, slot, index)
            for copy in copies:
                copy.start()
            pending.append(copies)
        for copies in pending[-term_slots:]:
            for copy in copies:
                copy.wait()

    def project(stream, target):
        def one_block(b, carry):
            piece = pl.ds(pl.multiple_of(b * rows, 16), rows)
            value = matmul(normed3[piece, :], attn_columns[stream])
            if stream < 2:
                parts = []
                for head in range(width // HEAD_DIM):
                    one = value[:, head * HEAD_DIM : (head + 1) * HEAD_DIM]
                    swapped = jnp.concatenate(
                        [one[:, HEAD_DIM // 2 :], one[:, : HEAD_DIM // 2]], axis=1
                    )
                    parts.append(one * cos_ref[...] + swapped * sin_ref[...])
                value = jnp.concatenate(parts, axis=1)
            target[piece, :] = value.astype(jnp.bfloat16)
            return carry

        lax.fori_loop(0, 8, one_block, 0)

    def out_grads(b, carry):
        piece = pl.ds(pl.multiple_of(b * rows, 16), rows)
        out_grad_ref[piece, :] = lax.dot_general(
            grads[piece, :], w_out_ref[...], contract_cols, preferred_element_type=jnp.float32
        ).astype(jnp.bfloat16)
        return carry

    def key_copy(place):
        return pltpu.make_async_remote_copy(
            src_ref=k_ref,
            dst_ref=key_before_ref,
            send_sem=key_send.at[0],
            recv_sem=key_recv.at[0],
            device_id=z_place(place + 1),
            device_id_type=DEVICE_MESH,
        )

    feed(0, 2)
    line.service(5)
    gather0 = combine(1)
    feed(2, 2)
    line.service(6)
    gather0.corners()
    feed(4, 2)
    line.service(7)
    gather0.siblings()
    feed(6, 2)
    gather0.rest()
    scatter = PlaneScatterSteps(
        column,
        back_product,
        (out_buf, side, chip, from_x, from_y, last),
        scatter_send,
        scatter_recv,
    )
    scatter.block(0)
    line.service(8)
    gather1 = combine(2)
    scatter.block(1)
    scatter.block(2)
    scatter.block(3)
    gather0.finish()
    terms(1, 0, 2)
    line.service(9)
    scatter.turn()
    gather1.corners()
    terms(1, 2, ff_share // tile - 2)
    line.service(10)
    scatter.finish(None)
    x_copies[-1].wait()
    x_load = pltpu.make_async_copy(x_ref.at[0], x_buf, out_sem.at[1])
    x_load.start()
    x_load.wait()
    norm_rows_back(x_buf, chip.at[3], gain_ref, gain_grad_ref, 0, grad_own, stream_own)
    x_copies.clear()
    spread3 = LineGather(
        plane,
        stream_own,
        lambda p: full3_ref.at[pl.ds(p * rows, rows)],
        spread_send,
        spread_recv,
        out_sem.at[11],
    )
    spread3.service(0)
    gather1.siblings()
    down_line = LineSum(
        plane,
        down_term_ref,
        arrived_down_ref,
        own,
        ends,
        held,
        sum_send,
        sum_recv,
        line_load,
        share,
        0,
    )
    line.service(11)
    gather2 = combine(3)
    down_line.start()
    gather1.rest()
    terms(0, 0, features // tile)
    line.drain()
    gather1.finish()
    load = block_load(normed_ref.at[1], normed3, 0)
    gather2.corners()
    for copy in attn_swaps:
        copy.wait_recv()
    for copy in attn_locals:
        copy.wait()
    spread3.service(1)
    load.wait()
    project(1, k_ref)
    for place in range(3):

        @pl.when(plane == place)
        def _():
            key_copy(place).start()

    load = block_load(normed_ref.at[0], normed3, 0)
    down_line.service(0)
    gather2.siblings()
    gather2.rest()
    load.wait()
    project(0, q_ref)
    spread3.service(2)
    lax.fori_loop(0, 8, out_grads, 0)
    gather2.finish()
    load = block_load(normed_ref.at[2], normed3, 0)
    down_line.service(1)
    load.wait()
    project(2, v_ref)
    spread3.service(3)
    for copy in small_copies + up_swaps + attn_swaps:
        copy.wait_send()
    grads_out.wait()
    x_copies[-1].wait()
    for place in range(4):

        @pl.when(plane == place)
        def _():
            for p in range(4):
                if p != place:
                    dyn_copy(place, p).wait_send()
            for s in range(micro_count):
                target_place, slot = divmod(s * 4 + place, micro_count)
                if target_place != place:
                    route_copy(place, s, target_place, slot).wait_send()

    down_line.service(2)
    down_line.finish(down_sum_ref)
    spread3.placed()
    spread3.finish()
    for place in range(4):

        @pl.when(plane == place)
        def _():
            if place > 0:
                key_copy(place - 1).wait_recv()
            if place < 3:
                key_copy(place).wait_send()


def forward_and_feed(
    lengths,
    pack,
    latest,
    history,
    select,
    root,
    cotangent,
    w_up,
    w_attn,
    w_down,
    w_out,
    cosine,
    sine_part,
    sequence_length,
):
    rows, features = cotangent.shape
    micro_count = lengths.shape[0]
    total = 8 * rows
    share = w_up.shape[0]
    ff_share = w_down.shape[0]
    mix_width = select.shape[0]
    block = (rows, features)
    piece = (share, features)
    half = (2, rows // 2, features)
    anywhere = pl.BlockSpec(memory_space=pl.ANY)
    near = pl.BlockSpec(memory_space=pltpu.VMEM)
    shape = jax.ShapeDtypeStruct
    low_type = jnp.bfloat16
    some = lambda *dims: pltpu.VMEM(dims, low_type)
    wide = lambda *dims: pltpu.VMEM(dims, jnp.float32)
    dma = pltpu.SemaphoreType.DMA
    outputs = [
        (near, shape((8,) + pack.shape, low_type)),
        (near, shape((8, features), jnp.float32)),
        (near, shape((4 * rows, 128), jnp.float32)),
        (near, shape((4 * rows, 128), jnp.float32)),
        (anywhere, shape((4,) + block, jnp.float32)),
        (anywhere, shape((3, total, features), low_type)),
        (anywhere, shape((total, features), low_type)),
        (near, shape((total, ff_share), low_type)),
        (anywhere, shape((ff_share, features), low_type)),
        (near, shape(piece, low_type)),
        (anywhere, shape((4 * rows, features), low_type)),
        (near, shape((8, features), jnp.float32)),
        (near, shape((3, features, share), low_type)),
        (near, shape((total, share), low_type)),
        (near, shape((total, share), low_type)),
        (near, shape((total, share), low_type)),
        (near, shape((total, share), low_type)),
        (anywhere, shape((total, share), low_type)),
        (anywhere, shape((16 * rows, features), low_type)),
        (anywhere, shape((ff_share, features), low_type)),
        (anywhere, shape((24,) + block, low_type)),
        (anywhere, shape((6,) + piece, low_type)),
    ]
    return pl.pallas_call(
        functools.partial(
            forward_kernel, micro_count=micro_count, sequence_length=sequence_length
        ),
        in_specs=[pl.BlockSpec(memory_space=pltpu.SMEM), near, anywhere, anywhere]
        + [near, near, anywhere, anywhere, anywhere]
        + [near] * 4,
        out_specs=[spec for spec, _ in outputs],
        out_shape=[out for _, out in outputs],
        scratch_shapes=[
            some(total, features),
            some(total, features),
            some(features, ff_share),
            some(total, ff_share),
            some(2, *block),
            some(4, *block),
            some(4, *block),
            some(*half),
            some(*half),
            some(*half),
            some(*piece),
            some(2, *piece),
            some(4, *piece),
            wide(*block),
            some(4, *block),
            some(2, 256, features),
            some(*block),
            some(*block),
            wide(mix_width, 128),
            some(4, mix_width, 4 * rows),
            dma((5, 11)),
            dma((5, 11)),
            dma((5,)),
            dma((10,)),
            dma((10,)),
            dma((24,)),
            dma((24,)),
            dma((2,)),
            dma((32,)),
            dma((32,)),
            dma((4,)),
            dma((12,)),
            dma((8,)),
            dma((8,)),
            dma((4,)),
            dma((4,)),
            dma((micro_count,)),
            dma((micro_count,)),
            dma((20,)),
            dma((6,)),
            dma((6,)),
            dma((6,)),
            dma((6,)),
            dma((1,)),
            dma((1,)),
            pltpu.SemaphoreType.REGULAR,
        ],
        compiler_params=pltpu.CompilerParams(
            collective_id=5, has_side_effects=True, vmem_limit_bytes=63 * 1024 * 1024
        ),
        cost_estimate=pl.CostEstimate(
            flops=12 * total * features * ff_share,
            bytes_accessed=600 * 1000 * 1000,
            transcendentals=0,
        ),
    )(
        lengths,
        pack,
        latest,
        history,
        select,
        root,
        cotangent,
        w_up,
        w_attn,
        w_down,
        w_out,
        cosine,
        sine_part,
    )


def small_sum_kernel(parts_ref, out_ref, got, sums, send_sem, recv_sem, z_send, z_recv):
    column = lax.axis_index("dp")
    plane = lax.axis_index("hist")
    every_mask = (6, 7, 2, 3, 4, 5, 1)
    barrier = pltpu.get_barrier_semaphore()
    for mask in every_mask:
        pl.semaphore_signal(
            barrier, inc=1, device_id={"dp": partner(column, mask)}, device_id_type=DEVICE_MESH
        )
    for place in range(4):

        @pl.when(plane == place)
        def _():
            for p in range(4):
                if p != place:
                    pl.semaphore_signal(
                        barrier, inc=1, device_id=z_place(p), device_id_type=DEVICE_MESH
                    )

    pl.semaphore_wait(barrier, 10)
    copies = [
        push(
            parts_ref.at[partner(column, mask)],
            got.at[mask],
            send_sem.at[mask],
            recv_sem.at[mask],
            partner(column, mask),
        )
        for mask in every_mask
    ]
    total = parts_ref[column].astype(jnp.float32)
    for mask, copy in zip(every_mask, copies):
        copy.wait_recv()
        total = total + got[mask].astype(jnp.float32)

    def line_copy(source_place, target_place):
        return pltpu.make_async_remote_copy(
            src_ref=sums.at[source_place],
            dst_ref=sums.at[source_place],
            send_sem=z_send.at[target_place],
            recv_sem=z_recv.at[source_place],
            device_id=z_place(target_place),
            device_id_type=DEVICE_MESH,
        )

    for place in range(4):

        @pl.when(plane == place)
        def _():
            others = [p for p in range(4) if p != place]
            sums[place] = total.astype(jnp.bfloat16)
            for p in others:
                line_copy(place, p).start()
            for p in others:
                line_copy(p, place).wait_recv()
            for p in others:
                line_copy(place, p).wait_send()

    out_ref[...] = (sums[0].astype(jnp.float32) + sums[1].astype(jnp.float32)) + (
        sums[2].astype(jnp.float32) + sums[3].astype(jnp.float32)
    )
    for copy in copies:
        copy.wait_send()


def small_sums(parts):
    dims = parts.shape[1:]
    dma = pltpu.SemaphoreType.DMA
    return pl.pallas_call(
        small_sum_kernel,
        out_shape=jax.ShapeDtypeStruct(dims, jnp.float32),
        in_specs=[pl.BlockSpec(memory_space=pltpu.VMEM)],
        out_specs=pl.BlockSpec(memory_space=pltpu.VMEM),
        scratch_shapes=[
            pltpu.VMEM((8,) + dims, jnp.bfloat16),
            pltpu.VMEM((4,) + dims, jnp.bfloat16),
            dma((8,)),
            dma((8,)),
            dma((4,)),
            dma((4,)),
        ],
        compiler_params=pltpu.CompilerParams(collective_id=7, has_side_effects=True),
        cost_estimate=pl.CostEstimate(
            flops=0, bytes_accessed=40 * 1000 * 1000, transcendentals=0
        ),
    )(parts)


def slot_grad_kernel(
    flag_ref,
    factor_ref,
    first_ref,
    rest_ref,
    latest_ref,
    pre_grad_ref,
    mix_in_ref,
    gain_ref,
    out_ref,
    gain_grad_ref,
):
    x = latest_ref[...].astype(jnp.float32)
    inverse = lax.rsqrt(jnp.mean(x * x, axis=-1, keepdims=True) + epsilon)
    grad = precise(pre_grad_ref[...], mix_in_ref[...])
    scaled = grad * gain_ref[pl.ds(0, 1), :]
    mean = jnp.mean(scaled * x, axis=-1, keepdims=True)
    latest_grad = inverse * scaled - x * (inverse * inverse * inverse) * mean
    gain_sum = jnp.sum(grad * x * inverse, axis=0, keepdims=True)

    @pl.when(pl.program_id(0) == 0)
    def _():
        gain_grad_ref[...] = jnp.zeros_like(gain_grad_ref)

    gain_grad_ref[pl.ds(0, 1), :] += gain_sum
    grads = [first_ref[...].astype(jnp.float32)] + [
        rest_ref[i].astype(jnp.float32) for i in range(3)
    ]
    factors = factor_ref[...]
    for slot in range(4):
        total = latest_grad * flag_ref[slot]
        for item in range(4):
            one = item * 4 + slot
            total = total + factors[:, one : one + 1] * grads[item]
        out_ref[slot] = total.astype(jnp.bfloat16)


def slot_grads_of(latest_here, factors, first, rest, latest, pre_grad, mix_in_columns, gains):
    total, features = first.shape
    step = 64
    mix_width = pre_grad.shape[1]
    rows_of = lambda *lead: pl.BlockSpec(
        lead + (step, features), lambda r: (0,) * len(lead) + (r, 0)
    )
    whole = lambda *dims: pl.BlockSpec(dims, lambda r: (0, 0))
    return pl.pallas_call(
        slot_grad_kernel,
        grid=(total // step,),
        in_specs=[
            pl.BlockSpec(memory_space=pltpu.SMEM),
            pl.BlockSpec((step, 128), lambda r: (r, 0)),
            rows_of(),
            rows_of(3),
            rows_of(),
            pl.BlockSpec((step, mix_width), lambda r: (r, 0)),
            whole(mix_width, features),
            whole(8, features),
        ],
        out_specs=[rows_of(4), whole(8, features)],
        out_shape=[
            jax.ShapeDtypeStruct((4, total, features), jnp.bfloat16),
            jax.ShapeDtypeStruct((8, features), jnp.float32),
        ],
        compiler_params=pltpu.CompilerParams(vmem_limit_bytes=56 * 1024 * 1024),
        cost_estimate=pl.CostEstimate(
            flops=40 * total * features, bytes_accessed=20 * total * features, transcendentals=0
        ),
    )(latest_here, factors, first, rest, latest, pre_grad, mix_in_columns, gains)


def lay_out_kernel(part_ref, attn_ref, out_ref):
    quarter = out_ref.shape[0]
    for stream in range(3):
        attn_ref[stream] = part_ref[stream * quarter : (stream + 1) * quarter, :].astype(
            jnp.float32
        )
    out_ref[...] = part_ref[3 * quarter :, :].astype(jnp.float32)


def lay_out(parts):
    total, features = parts.shape
    step = total // 4
    quarter = step // 4
    return pl.pallas_call(
        lay_out_kernel,
        grid=(4,),
        in_specs=[pl.BlockSpec((step, features), lambda p: (p, 0))],
        out_specs=[
            pl.BlockSpec((3, quarter, features), lambda p: (0, p, 0)),
            pl.BlockSpec((quarter, features), lambda p: (p, 0)),
        ],
        out_shape=[
            jax.ShapeDtypeStruct((3, step, features), jnp.float32),
            jax.ShapeDtypeStruct((step, features), jnp.float32),
        ],
        compiler_params=pltpu.CompilerParams(vmem_limit_bytes=56 * 1024 * 1024),
        cost_estimate=pl.CostEstimate(
            flops=0, bytes_accessed=6 * total * features, transcendentals=0
        ),
    )(parts)


def attend_column(
    column,
    plane,
    length_ref,
    cosine,
    sine_part,
    q_ref,
    k_ref,
    v_ref,
    kv_before_ref,
    out_grad_ref,
    att_ref,
    q_grad_ref,
    kv_grad_ref,
    kv_before_grad_ref,
    rows,
    micro_count,
    sequence_length,
):
    here = pl.ds(pl.multiple_of(column * rows, 16), rows)
    width = q_ref.shape[1]
    scale = 1.0 / math.sqrt(HEAD_DIM)
    row = plane * rows + lax.broadcasted_iota(jnp.int32, (rows, 1), 0)
    start = jnp.zeros((rows, 1), jnp.int32)
    limit = jnp.zeros((rows, 1), jnp.int32)
    for m in range(micro_count):
        inside = (row >= m * sequence_length) & (row < (m + 1) * sequence_length)
        start = jnp.where(inside, m * sequence_length, start)
        limit = jnp.where(inside, m * sequence_length + length_ref[column * micro_count + m], limit)
    limit = jnp.minimum(limit, row + 1)
    key_row = (plane - 1) * rows + lax.broadcasted_iota(jnp.int32, (1, 2 * rows), 1)
    allowed = (key_row >= start) & (key_row < limit)
    for head in range(width // HEAD_DIM):
        lanes = slice(head * HEAD_DIM, (head + 1) * HEAD_DIM)
        value_lanes = slice(width + head * HEAD_DIM, width + (head + 1) * HEAD_DIM)
        query = q_ref[here, lanes]
        keys = jnp.concatenate([kv_before_ref[here, lanes], k_ref[here, lanes]], axis=0)
        values = jnp.concatenate([kv_before_ref[here, value_lanes], v_ref[here, lanes]], axis=0)
        out_grad = out_grad_ref[here, lanes]
        scores = (
            lax.dot_general(query, keys, contract_cols, preferred_element_type=jnp.float32) * scale
        )
        scores = jnp.where(allowed, scores, masked_out)
        raised = jnp.exp(scores - jnp.max(scores, axis=-1, keepdims=True))
        weights = raised / jnp.sum(raised, axis=-1, keepdims=True)
        weights_low = weights.astype(jnp.bfloat16)
        att_ref[here, lanes] = matmul(weights_low, values).astype(jnp.bfloat16)
        weight_grad = lax.dot_general(
            out_grad, values, contract_cols, preferred_element_type=jnp.float32
        )
        inner = jnp.sum(weights * weight_grad, axis=-1, keepdims=True)
        score_grad = (weights * (weight_grad - inner) * scale).astype(jnp.bfloat16)
        query_grad = matmul(score_grad, keys)
        swapped = jnp.concatenate(
            [query_grad[:, HEAD_DIM // 2 :], query_grad[:, : HEAD_DIM // 2]], axis=1
        )
        q_grad_ref[here, lanes] = (query_grad * cosine - swapped * sine_part).astype(jnp.bfloat16)
        key_grad = lax.dot_general(
            score_grad, query, contract_rows, preferred_element_type=jnp.float32
        )
        value_grad = lax.dot_general(
            weights_low, out_grad, contract_rows, preferred_element_type=jnp.float32
        )
        kv_before_grad_ref[here, lanes] = key_grad[:rows].astype(jnp.bfloat16)
        kv_before_grad_ref[here, value_lanes] = value_grad[:rows].astype(jnp.bfloat16)
        kv_grad_ref[here, lanes] = key_grad[rows:]
        kv_grad_ref[here, value_lanes] = value_grad[rows:]


def backward_kernel(
    length_ref,
    cos_ref,
    sin_ref,
    q_ref,
    k_ref,
    v_ref,
    out_grad_ref,
    normed_ref,
    grad_all_ref,
    hidden_ref,
    w_out_ref,
    w_down_ref,
    attn_columns_ref,
    x_ref,
    gain_ref,
    down_own,
    up_term_ref,
    full3_ref,
    history_ref,
    key_before_ref,
    full_ref,
    down_all_ref,
    up_all_ref,
    inner_ref,
    quarter_ref,
    branch_ref,
    gain_grad_ref,
    attn_parts_ref,
    arrived_ref,
    big,
    att,
    q_grad,
    kv_grad,
    kv_before,
    kv_before_grad,
    kv_after,
    out_buf,
    side,
    chip,
    from_x,
    from_y,
    last,
    line_own,
    line_ends,
    line_held,
    up_sum,
    up_own,
    stream_own,
    back_buf,
    x_buf,
    stage,
    inner_columns,
    scatter_send,
    scatter_recv,
    sum_send,
    sum_recv,
    load_sem,
    spread_send,
    spread_recv,
    spread_local,
    key_send,
    key_recv,
    swap_send,
    swap_recv,
    local_sem,
    inner_sem,
    share_send,
    share_recv,
    *,
    micro_count,
    sequence_length,
):
    column = lax.axis_index("dp")
    plane = lax.axis_index("hist")
    total, width = q_ref.shape
    rows, features = total // 8, w_down_ref.shape[1]
    ff_share = w_down_ref.shape[0]
    quarter = features // 8 // 4
    v_grad = kv_before.at[:, pl.ds(0, width)]
    k_grad = kv_before.at[:, pl.ds(width, width)]
    attn_sum = up_sum
    tile = 512

    barrier = pltpu.get_barrier_semaphore()
    for mask in range(1, 8):
        pl.semaphore_signal(
            barrier, inc=1, device_id={"dp": partner(column, mask)}, device_id_type=DEVICE_MESH
        )
    for place in range(4):

        @pl.when(plane == place)
        def _():
            for p in range(4):
                if p != place:
                    pl.semaphore_signal(
                        barrier, inc=1, device_id=z_place(p), device_id_type=DEVICE_MESH
                    )

    pl.semaphore_wait(barrier, 10)

    def value_copy(place):
        return pltpu.make_async_remote_copy(
            src_ref=v_ref,
            dst_ref=kv_before.at[:, pl.ds(width, width)],
            send_sem=key_send.at[1],
            recv_sem=key_recv.at[1],
            device_id=z_place(place + 1),
            device_id_type=DEVICE_MESH,
        )

    for place in range(3):

        @pl.when(plane == place)
        def _():
            value_copy(place).start()

    def back_copy(place):
        return pltpu.make_async_remote_copy(
            src_ref=kv_before_grad,
            dst_ref=kv_after,
            send_sem=key_send.at[0],
            recv_sem=key_recv.at[0],
            device_id=z_place(place - 1),
            device_id_type=DEVICE_MESH,
        )

    def clear(target):
        step = 64

        def some_rows(r, carry):
            target[pl.ds(pl.multiple_of(r * step, step), step), :] = jnp.zeros(
                (step, target.shape[1]), jnp.bfloat16
            )
            return carry

        lax.fori_loop(0, target.shape[0] // step, some_rows, 0)

    line_sums = [
        LineSum(
            plane,
            parts,
            arrived_ref.at[pl.ds(6 * i, 6)],
            line_own,
            line_ends,
            line_held,
            sum_send.at[i],
            sum_recv.at[i],
            load_sem,
            4 * quarter,
            0,
        )
        for i, parts in enumerate((up_term_ref, attn_parts_ref))
    ]
    up_line, attn_line = line_sums

    def spread(index, own, slot):
        return LineGather(
            plane, own, slot, spread_send.at[index], spread_recv.at[index], spread_local.at[index]
        )

    def stream_spread(item):
        return spread(
            item,
            stream_own.at[item - 1],
            lambda p: full_ref.at[pl.ds(((item - 1) * 4 + p) * rows, rows)],
        )

    def norm_back(item, back):
        load = pltpu.make_async_copy(x_ref.at[item], x_buf, local_sem.at[0])
        load.start()
        load.wait()
        norm_rows_back(
            x_buf, back, gain_ref, gain_grad_ref, item, None, stream_own.at[item - 1]
        )

    def scatter_of(product, index):
        return PlaneScatterSteps(
            column,
            product,
            (out_buf, side, chip)
            + tuple(arriving.at[pl.ds(2 * (index % 2), 2)] for arriving in (from_x, from_y, last)),
            scatter_send.at[index],
            scatter_recv.at[index],
        )

    def projection_product(stream, grad):
        def product(owner, target):
            left = pl.ds(pl.multiple_of(owner * rows, 16), rows)

            def one_tile(t, carry):
                lanes = pl.ds(pl.multiple_of(t * tile, tile), tile)
                target[:, lanes] = lax.dot_general(
                    grad[left, :],
                    attn_columns_ref[stream, lanes, :],
                    contract_cols,
                    preferred_element_type=jnp.float32,
                ).astype(jnp.bfloat16)
                return carry

            lax.fori_loop(0, features // tile, one_tile, 0)

        return product

    def branch_product(owner, target):
        left = pl.ds(pl.multiple_of(owner * rows, 16), rows)

        def one_tile(t, carry):
            lanes = pl.ds(pl.multiple_of(t * tile, tile), tile)
            target[:, lanes] = (
                matmul(att[left, :], w_out_ref[:, lanes])
                + matmul(hidden_ref[left, :], w_down_ref[:, lanes])
            ).astype(jnp.bfloat16)
            return carry

        lax.fori_loop(0, features // tile, one_tile, 0)

    def attend(first, count):
        def one_column(m, carry):
            attend_column(
                m,
                plane,
                length_ref,
                cos_ref[...],
                sin_ref[...],
                q_ref,
                k_ref,
                v_ref,
                kv_before,
                out_grad_ref,
                att,
                q_grad,
                kv_grad,
                kv_before_grad,
                rows,
                micro_count,
                sequence_length,
            )
            return carry

        lax.fori_loop(first, first + count, one_column, 0)

    step_rows = rows // 2

    def inner_loads(item, i):
        source = full3_ref if item == 0 else full_ref
        first = 0 if item == 0 else (item - 1) * 4 * rows
        base = (i % 2) * 5 * step_rows
        copies = [
            pltpu.make_async_copy(
                source.at[pl.ds(first + i * step_rows, step_rows)],
                big.at[pl.ds(base + 4 * step_rows, step_rows)],
                inner_sem.at[(i % 2) * 5 + 4],
            )
        ] + [
            pltpu.make_async_copy(
                history_ref.at[pl.ds(slot * 4 * rows + i * step_rows, step_rows)],
                big.at[pl.ds(base + slot * step_rows, step_rows)],
                inner_sem.at[(i % 2) * 5 + slot],
            )
            for slot in range(4)
        ]
        for copy in copies:
            copy.start()
        return copies

    def inner_products(item):
        loads = [inner_loads(item, 0)]
        for i in range(8):
            if i + 1 < 8:
                loads.append(inner_loads(item, i + 1))
            for copy in loads[i]:
                copy.wait()
            base = (i % 2) * 5 * step_rows

            def some_rows(r, carry):
                grad = big[
                    pl.ds(pl.multiple_of(base + 4 * step_rows + r * 16, 16), 16), :
                ].astype(jnp.float32)
                for slot in range(4):
                    values = big[
                        pl.ds(pl.multiple_of(base + slot * step_rows + r * 16, 16), 16), :
                    ].astype(jnp.float32)
                    one = item * 4 + slot
                    inner_columns[
                        pl.ds(pl.multiple_of(i * step_rows + r * 16, 16), 16), one : one + 1
                    ] = jnp.sum(grad * values, axis=-1, keepdims=True)
                return carry

            lax.fori_loop(0, step_rows // 16, some_rows, 0)

    def part_copies(first_row):
        return [
            pltpu.make_async_copy(
                stage.at[pl.ds(p * quarter, quarter)],
                attn_parts_ref.at[pl.ds(p * 4 * quarter + first_row, quarter)],
                local_sem.at[4 + p],
            )
            for p in range(4)
        ]

    def load_big(source):
        copy = pltpu.make_async_copy(source, big, local_sem.at[2])
        copy.start()
        return copy

    def attn_term(stream, grad):
        def one_owner(d, carry):
            lanes = pl.ds(pl.multiple_of(d * width, width), width)
            stage[:, lanes] = lax.dot_general(
                big[:, lanes], grad[...], contract_rows, preferred_element_type=jnp.float32
            ).astype(jnp.bfloat16)
            return carry

        lax.fori_loop(0, 8, one_owner, 0)
        copies = part_copies(stream * quarter)
        for copy in copies:
            copy.start()
        return copies

    def out_term():
        def one_tile(t, carry):
            lanes = pl.ds(pl.multiple_of(t * tile, tile), tile)
            stage[:, lanes] = lax.dot_general(
                att[...], big[:, lanes], contract_rows, preferred_element_type=jnp.float32
            ).astype(jnp.bfloat16)
            return carry

        lax.fori_loop(0, features // tile, one_tile, 0)
        copies = part_copies(3 * quarter)
        for copy in copies:
            copy.start()
        return copies

    def swap(kind):
        copies = []
        for mask in (6, 7, 2, 3, 4, 5, 1):
            owner = partner(column, mask)
            if kind == 0:
                source, target = up_piece(owner), up_target()
            else:
                source, target = attn_piece(owner), attn_target()
            copies.append(
                push(
                    source,
                    target,
                    swap_send.at[8 * kind + mask],
                    swap_recv.at[8 * kind + mask],
                    owner,
                )
            )
        if kind == 0:
            source, target = up_piece(column), up_target()
        else:
            source, target = attn_piece(column), attn_target()
        local = pltpu.make_async_copy(source, target, local_sem.at[3])
        local.start()
        return copies, local

    def up_piece(owner):
        return up_sum.at[
            pl.ds(pl.multiple_of(lax.rem(owner, 4) * quarter, 16), quarter),
            pl.ds(pl.multiple_of(lax.div(owner, 4) * ff_share, 128), ff_share),
        ]

    def up_target():
        return up_own.at[:, pl.ds(pl.multiple_of(column * ff_share, 128), ff_share)]

    def attn_piece(owner):
        return attn_sum.at[
            pl.ds(0, 3 * quarter), pl.ds(pl.multiple_of(owner * width, 128), width)
        ]

    def attn_target():
        return quarter_ref.at[
            pl.ds(0, 3 * quarter), pl.ds(pl.multiple_of(column * width, 128), width)
        ]

    def swapped_in(swapping):
        copies, local = swapping
        for copy in copies:
            copy.wait_recv()
        local.wait()
        for copy in copies:
            copy.wait_send()

    up_line.start()
    down_spread = spread(4, down_own, lambda p: down_all_ref.at[pl.ds(p * 4 * quarter, 4 * quarter)])
    down_spread.service(0)

    @pl.when(plane == 0)
    def _():
        clear(kv_before)
        clear(line_ends.at[0])

    @pl.when(plane > 0)
    def _():
        load = pltpu.make_async_copy(
            key_before_ref, kv_before.at[:, pl.ds(0, width)], local_sem.at[0]
        )
        load.start()
        load.wait()

    @pl.when(plane == 3)
    def _():
        clear(kv_after)
        clear(line_ends.at[1])

    def key_value(m, carry):
        here = pl.ds(pl.multiple_of(m * rows, 16), rows)
        for head in range(width // HEAD_DIM):
            lanes = slice(head * HEAD_DIM, (head + 1) * HEAD_DIM)
            value_lanes = slice(width + head * HEAD_DIM, width + (head + 1) * HEAD_DIM)
            grad = kv_grad[here, lanes] + kv_after[here, lanes].astype(jnp.float32)
            turned_half = jnp.concatenate(
                [grad[:, HEAD_DIM // 2 :], grad[:, : HEAD_DIM // 2]], axis=1
            )
            k_grad[here, lanes] = (grad * cos_ref[...] - turned_half * sin_ref[...]).astype(
                jnp.bfloat16
            )
            v_grad[here, lanes] = (
                kv_grad[here, value_lanes] + kv_after[here, value_lanes].astype(jnp.float32)
            ).astype(jnp.bfloat16)
        return carry

    for place in range(1, 4):

        @pl.when(plane == place)
        def _():
            value_copy(place - 1).wait_recv()

    attend(0, 8)
    for place in range(1, 4):

        @pl.when(plane == place)
        def _():
            back_copy(place).start()

    loading = load_big(grad_all_ref)
    query_scatter = scatter_of(projection_product(0, q_grad), 0)
    query_scatter.block(0)
    query_scatter.block(1)
    query_scatter.block(2)
    query_scatter.block(3)
    up_line.service(0)
    query_scatter.turn()
    loading.wait()
    parts_out = out_term()
    query_scatter.finish(back_buf)
    norm_back(1, back_buf)
    query_spread = stream_spread(1)
    query_spread.service(0)
    down_spread.service(1)
    up_line.service(1)
    for copy in parts_out:
        copy.wait()
    loading = load_big(normed_ref.at[0])

    for place in range(3):

        @pl.when(plane == place)
        def _():
            back_copy(place + 1).wait_recv()

    lax.fori_loop(0, 8, key_value, 0)
    key_scatter = scatter_of(projection_product(1, k_grad), 1)
    key_scatter.block(0)
    key_scatter.block(1)
    key_scatter.block(2)
    key_scatter.block(3)
    down_spread.service(2)
    loading.wait()
    parts_out = attn_term(0, q_grad)
    key_scatter.turn()
    key_scatter.finish(back_buf)
    norm_back(2, back_buf)
    key_spread = stream_spread(2)
    key_spread.service(0)
    up_line.service(2)
    up_line.finish(up_sum)
    up_swap = swap(0)
    for copy in parts_out:
        copy.wait()
    loading = load_big(normed_ref.at[1])
    value_scatter = scatter_of(projection_product(2, v_grad), 2)
    value_scatter.block(0)
    value_scatter.block(1)
    value_scatter.block(2)
    value_scatter.block(3)
    down_spread.service(3)
    query_spread.service(1)
    loading.wait()
    parts_out = attn_term(1, k_grad)
    value_scatter.turn()
    swapped_in(up_swap)
    up_spread = spread(5, up_own, lambda p: up_all_ref.at[pl.ds(p * quarter, quarter)])
    up_spread.service(0)
    value_scatter.finish(back_buf)
    norm_back(3, back_buf)
    value_spread = stream_spread(3)
    for copy in parts_out:
        copy.wait()
    loading = load_big(normed_ref.at[2])
    loading.wait()
    parts_out = attn_term(2, v_grad)
    for copy in parts_out:
        copy.wait()
    attn_line.start()
    value_spread.service(0)
    query_spread.service(2)
    branch_scatter = scatter_of(branch_product, 3)
    branch_scatter.block(0)
    branch_scatter.block(1)
    key_spread.service(1)
    branch_scatter.block(2)
    branch_scatter.block(3)
    up_spread.service(1)
    query_spread.service(3)
    branch_scatter.turn()
    branch_scatter.finish(branch_ref)
    attn_line.service(0)
    key_spread.service(2)
    up_spread.service(2)
    value_spread.service(1)
    attn_line.service(1)
    key_spread.service(3)
    query_spread.placed()
    inner_products(0)
    inner_products(1)
    up_spread.service(3)
    attn_line.service(2)
    attn_line.finish(attn_sum)
    attn_swap = swap(1)
    quarter_ref[pl.ds(3 * quarter, quarter), :] = attn_sum[pl.ds(3 * quarter, quarter), :]
    value_spread.service(2)
    key_spread.placed()
    inner_products(2)
    down_spread.placed()
    up_spread.placed()
    swapped_in(attn_swap)
    value_spread.service(3)
    value_spread.placed()
    inner_products(3)

    def share_copy(source_place, target_place):
        return pltpu.make_async_remote_copy(
            src_ref=inner_ref.at[source_place],
            dst_ref=inner_ref.at[source_place],
            send_sem=share_send.at[target_place],
            recv_sem=share_recv.at[source_place],
            device_id=z_place(target_place),
            device_id_type=DEVICE_MESH,
        )

    for place in range(4):

        @pl.when(plane == place)
        def _():
            others = [p for p in range(4) if p != place]
            inner_ref[place] = jnp.transpose(inner_columns[...])[:16]
            for p in others:
                share_copy(place, p).start()
            for p in others:
                share_copy(p, place).wait_recv()
            for p in others:
                share_copy(place, p).wait_send()

    for spreading in (
        down_spread,
        query_spread,
        up_spread,
        key_spread,
        value_spread,
    ):
        spreading.finish()
    for place in range(3):

        @pl.when(plane == place)
        def _():
            value_copy(place).wait_send()

    for place in range(1, 4):

        @pl.when(plane == place)
        def _():
            back_copy(place).wait_send()


def attend_and_back(
    lengths_all,
    cosine,
    sine_part,
    q,
    k,
    v,
    out_grad,
    normed_all,
    grad_all,
    hidden,
    w_out,
    w_down,
    attn_columns,
    x_ordered,
    gains,
    down_own,
    up_term,
    full3,
    history,
    key_before,
    micro_count,
    sequence_length,
):
    total, width = q.shape
    rows, features = total // 8, w_down.shape[1]
    ff_share = w_down.shape[0]
    quarter = features // 32
    block = (rows, features)
    piece = (4 * quarter, features)
    half = (4, rows // 2, features)
    anywhere = pl.BlockSpec(memory_space=pl.ANY)
    near = pl.BlockSpec(memory_space=pltpu.VMEM)
    shape = jax.ShapeDtypeStruct
    low_type = jnp.bfloat16
    some = lambda *dims: pltpu.VMEM(dims, low_type)
    dma = pltpu.SemaphoreType.DMA
    return pl.pallas_call(
        functools.partial(
            backward_kernel, micro_count=micro_count, sequence_length=sequence_length
        ),
        in_specs=[pl.BlockSpec(memory_space=pltpu.SMEM)]
        + [near] * 6
        + [anywhere, anywhere]
        + [near] * 4
        + [anywhere]
        + [near] * 2
        + [anywhere] * 4,
        out_specs=[anywhere] * 3 + [near, near, near, near, anywhere, anywhere],
        out_shape=[
            shape((12 * rows, features), low_type),
            shape((ff_share, features), low_type),
            shape((4 * quarter, 8 * ff_share), low_type),
            shape((4, 16, 4 * rows), jnp.float32),
            shape(piece, low_type),
            shape(block, low_type),
            shape((8, features), jnp.float32),
            shape((16 * quarter, features), low_type),
            shape((12,) + piece, low_type),
        ],
        scratch_shapes=[
            some(total, features),
            some(total, width),
            some(total, width),
            pltpu.VMEM((total, 2 * width), jnp.float32),
            some(total, 2 * width),
            some(total, 2 * width),
            some(total, 2 * width),
            some(2, *block),
            some(4, *block),
            some(4, *block),
            some(*half),
            some(*half),
            some(*half),
            some(*piece),
            some(2, *piece),
            some(3, *piece),
            some(*piece),
            some(quarter, 8 * ff_share),
            some(3, *block),
            some(*block),
            pltpu.VMEM(block, jnp.float32),
            some(*piece),
            pltpu.VMEM((4 * rows, 128), jnp.float32),
            dma((4, 10)),
            dma((4, 10)),
            dma((3, 6)),
            dma((3, 6)),
            dma((2,)),
            dma((6, 6)),
            dma((6, 6)),
            dma((6,)),
            dma((3,)),
            dma((3,)),
            dma((16,)),
            dma((16,)),
            dma((8,)),
            dma((10,)),
            dma((4,)),
            dma((4,)),
        ],
        compiler_params=pltpu.CompilerParams(
            collective_id=6, has_side_effects=True, vmem_limit_bytes=63 * 1024 * 1024
        ),
        cost_estimate=pl.CostEstimate(
            flops=20 * total * features * width,
            bytes_accessed=1000 * 1000 * 1000,
            transcendentals=0,
        ),
    )(
        lengths_all,
        cosine,
        sine_part,
        q,
        k,
        v,
        out_grad,
        normed_all,
        grad_all,
        hidden,
        w_out,
        w_down,
        attn_columns,
        x_ordered,
        gains,
        down_own,
        up_term,
        full3,
        history,
        key_before,
    )


def rotary_table(row_positions, head_dim):
    half_dim = head_dim // 2
    frequency = jnp.exp(
        jnp.arange(half_dim, dtype=jnp.float32) * (-2.0 * math.log(10000.0) / head_dim)
    )
    angles = row_positions.astype(jnp.float32)[:, None] * frequency[None, :]
    cosine = jnp.cos(angles)
    sine_part = jnp.sin(angles)
    return (
        jnp.concatenate([cosine, cosine], axis=-1),
        jnp.concatenate([-sine_part, sine_part], axis=-1),
    )


def shards_split(
    history,
    history_layer_index,
    lengths,
    norm_gains,
    mix_in,
    mix_out,
    w_attn,
    w_out,
    w_up,
    w_down,
    cotangent,
):
    local_slots, micro_count, sequence_length, features = history.shape
    planes = lax.axis_size("hist")
    columns = lax.axis_size("dp")
    plane = lax.axis_index("hist")
    slot_count = local_slots * planes
    all_rows = micro_count * sequence_length
    rows = all_rows // planes
    share = features // columns
    mix_width = mix_in.shape[1]
    mix_rows = mix_out.shape[0]
    low = lambda values: values.astype(jnp.bfloat16)
    order = (3, 0, 1, 2)

    spare = 128 - mix_width
    middle = jnp.concatenate(
        [
            jnp.pad(mix_out, ((0, 8 - mix_rows), (0, spare))),
            jnp.pad(low(lengths)[None, :], ((0, 7), (0, 128 - micro_count))),
        ],
        axis=0,
    )
    gain_rows = jnp.pad(norm_gains, ((0, 3), (0, 0))).reshape(8, 2, share // 2)
    pack = jnp.concatenate(
        [
            jnp.pad(mix_in, ((0, 0), (0, spare))),
            middle,
            gain_rows.transpose(1, 0, 2).reshape(16, share // 2),
        ],
        axis=0,
    )

    layer_lookup = (
        history_layer_index[:, None] == jnp.arange(slot_count, dtype=jnp.int32)[None, :]
    ).astype(jnp.float32)
    newest_output = jnp.sum(
        jnp.arange(slot_count, dtype=jnp.int32)
        * (history_layer_index == slot_count - 1).astype(jnp.int32)
    )
    root = newest_output // local_slots
    on_root = (plane == root).astype(jnp.float32)
    latest_rows = lax.dynamic_index_in_dim(
        history, newest_output % local_slots, 0, keepdims=False
    ).reshape(all_rows, features)
    own_table = lax.dynamic_slice_in_dim(layer_lookup, plane * local_slots, local_slots, 0)
    ordered = jnp.eye(STREAM_COUNT, dtype=jnp.float32)[:, jnp.array(order)]
    select = jnp.einsum("ci,sj->cjis", ordered, own_table).reshape(
        STREAM_COUNT * slot_count, STREAM_COUNT * local_slots
    )
    select = low(jnp.pad(select, ((0, 0), (0, 128 - STREAM_COUNT * local_slots))))

    my_row = plane * rows + jnp.arange(rows, dtype=jnp.int32)
    my_position = lax.rem(my_row, sequence_length)
    my_sequence = lax.div(my_row, sequence_length)
    my_length = jnp.sum(
        jnp.where(
            my_sequence[:, None] == jnp.arange(micro_count, dtype=jnp.int32)[None, :],
            lengths[None, :],
            0,
        ),
        axis=1,
    )
    valid_rows = (my_position < my_length).astype(jnp.float32)[:, None]
    cosine, sine_part = rotary_table(my_position, HEAD_DIM)

    (
        packed,
        gains,
        pre,
        factors,
        x_ordered,
        normed_all,
        grad_all,
        hidden,
        up_term,
        down_own,
        full3,
        gain_sum3,
        attn_columns,
        q,
        k,
        v,
        out_grad,
        key_before,
        _,
        _,
        _,
        _,
    ) = forward_and_feed(
        lengths,
        pack,
        latest_rows,
        history.reshape(local_slots * all_rows, features),
        select,
        jnp.broadcast_to(on_root, (8, all_rows)),
        cotangent.reshape(rows, features),
        w_up,
        w_attn,
        w_down,
        w_out,
        cosine,
        sine_part,
        sequence_length,
    )
    lengths_all = packed[:, share + 8, :micro_count].reshape(-1).astype(jnp.int32)
    (
        full,
        down_all,
        up_all,
        inner_all,
        attn_quarter,
        branch,
        gain_sums,
        _,
        _,
    ) = attend_and_back(
        lengths_all,
        cosine,
        sine_part,
        q,
        k,
        v,
        out_grad,
        normed_all,
        grad_all,
        hidden,
        w_out,
        w_down,
        attn_columns,
        x_ordered,
        gains,
        down_own,
        up_term,
        full3,
        history.reshape(local_slots * all_rows, features),
        key_before,
        micro_count,
        sequence_length,
    )
    attn_every = lax.all_gather(attn_quarter, "hist", axis=0, tiled=True)

    chunk = sequence_length // planes
    inverse_step = pow(micro_count, -1, planes)
    block_rows = low((x_ordered[0] + branch.astype(jnp.float32)) * valid_rows)
    block_out = jnp.zeros((micro_count, chunk, features), jnp.bfloat16)
    for i in range(micro_count):
        pairs = [(p, (micro_count * p + i) % planes) for p in range(planes)]
        piece = lax.ppermute(block_rows[i * chunk : (i + 1) * chunk], "hist", pairs)
        source = lax.rem((plane - i + planes * micro_count) * inverse_step, planes)
        which = lax.div(source * micro_count + i, planes)
        block_out = lax.dynamic_update_index_in_dim(block_out, piece, which, 0)

    mixer_output_wide = (
        packed[:, share : share + mix_rows, :mix_width]
        .reshape(mix_width, mix_width)
        .astype(jnp.float32)
    )
    mix_in_all = packed[:, :share, :mix_width].reshape(features, mix_width)
    tables = layer_lookup.reshape(planes, local_slots, slot_count)
    dyn_grad = jnp.einsum(
        "pist,ic,psj->tcj",
        inner_all.reshape(planes, STREAM_COUNT, local_slots, all_rows),
        ordered.T,
        tables,
        precision=highest,
    ).reshape(all_rows, STREAM_COUNT * slot_count)
    mixer_preactivation = pre[:, :mix_width]
    mix_act = jax.nn.gelu(mixer_preactivation, approximate=False)
    act_grad = precise(dyn_grad, mixer_output_wide.T)
    mix_out_grad = precise(mix_act.T, dyn_grad) * on_root
    pre_grad = act_grad * gelu_slope(mixer_preactivation)
    latest_scaled, _ = rms_scale(latest_rows.astype(jnp.float32), gains[0])
    mix_in_grad = precise(low(latest_scaled).astype(jnp.float32).T, pre_grad)
    latest_here = (plane * local_slots + jnp.arange(local_slots) == newest_output).astype(
        jnp.float32
    )
    history_grad, gain_zero = slot_grads_of(
        latest_here,
        factors,
        full3,
        full.reshape(3, all_rows, features),
        latest_rows,
        pre_grad,
        mix_in_all.astype(jnp.float32).T,
        gains,
    )
    history_grad = history_grad.reshape(history.shape)

    small_top = jnp.concatenate(
        [
            mix_in_grad * on_root,
            jnp.stack(
                [gain_zero[0] * on_root, gain_sums[1], gain_sums[2], gain_sums[3], gain_sum3[0]]
            ).T,
            jnp.zeros((features, 128 - mix_width - 5), jnp.float32),
        ],
        axis=1,
    ).reshape(columns, share, 128)
    small_bottom = jnp.pad(
        mix_out_grad.reshape(columns, mix_rows, mix_width),
        ((0, 0), (0, 16 - mix_rows), (0, 128 - mix_width)),
    )
    small = small_sums(low(jnp.concatenate([small_top, small_bottom], axis=1)))

    w_attn_grad, w_out_grad = lay_out(attn_every)
    return (
        block_out,
        history_grad,
        small[:share, mix_width : mix_width + 5].T,
        small[:share, :mix_width],
        small[share : share + mix_rows, :mix_width],
        w_attn_grad,
        w_out_grad,
        up_all.astype(jnp.float32),
        down_all.astype(jnp.float32),
    )


def splits_by_heads(mesh, micro_count, sequence_length):
    columns, planes = mesh.shape["dp"], mesh.shape["hist"]
    all_rows = micro_count * sequence_length
    rows = all_rows // planes
    return (
        columns == 8
        and planes == 4
        and HEADS % columns == 0
        and all_rows % planes == 0
        and sequence_length % planes == 0
        and rows % 64 == 0
        and math.gcd(micro_count, planes) == 1
        and all(
            (p * rows) // sequence_length * sequence_length >= (p - 1) * rows
            for p in range(planes)
        )
    )


def solution(mesh):
    placed = (
        P("hist", "dp", None, None),
        P(),
        P("dp"),
        P(None, "dp"),
        P("dp", None),
        P("dp", None),
        P(None, "dp", None),
        P("dp", None),
        P("dp", None),
        P("dp", None),
        P("dp", "hist", None),
    )
    def plan(*arrays):
        micro_count = arrays[2].shape[0]
        if splits_by_heads(mesh, micro_count, arrays[0].shape[2]):
            return shards_split(*arrays)
        return shards(*arrays)

    return jax.shard_map(
        plan,
        mesh=mesh,
        in_specs=placed,
        out_specs=(
            P("dp", "hist", None),
            P("hist", "dp", None, None),
            P(None, "dp"),
            P("dp", None),
            P("dp", None),
            P(None, "dp", None),
            P("dp", None),
            P("dp", None),
            P("dp", None),
        ),
        check_vma=False,
    )
```

```python
import functools
import math

import jax
import jax.numpy as jnp
from jax import lax
from jax.experimental import pallas as pl
from jax.experimental.pallas import tpu as pltpu
from jax.sharding import PartitionSpec as P

MODEL_WIDTH = 2048
HEADS = 16
HEAD_DIM = 128
FF = 8192
STREAM_COUNT = 4


epsilon = 1e-06
masked_out = -1e30
highest = lax.Precision.HIGHEST
contract_rows = (((0,), (0,)), ((), ()))
contract_cols = (((1,), (1,)), ((), ()))


def broadcast(value, axis, source):
    kept = jnp.where(lax.axis_index(axis) == source, value, 0).astype(value.dtype)
    return lax.psum(kept, axis)


def matmul(left_side, right_side):
    return jnp.dot(left_side, right_side, preferred_element_type=jnp.float32)


def precise(left_side, right_side):
    return jnp.dot(left_side, right_side, precision=highest, preferred_element_type=jnp.float32)


def gelu_slope(values):
    return 0.5 * (1.0 + lax.erf(values * (1.0 / math.sqrt(2.0)))) + values * jnp.exp(
        -0.5 * values * values
    ) * (1.0 / math.sqrt(2.0 * math.pi))


def rms_scale(values, gain_row):
    inverse = lax.rsqrt(jnp.mean(values * values, axis=-1, keepdims=True) + epsilon)
    return (values * inverse * gain_row, inverse)


def rms_back(values, inverse, gain_row, grad_in):
    scaled = grad_in * gain_row
    gain_grad = jnp.sum(grad_in * values * inverse, axis=0)
    inner_mean = jnp.mean(scaled * values, axis=-1, keepdims=True)
    return (inverse * scaled - values * (inverse * inverse * inverse) * inner_mean, gain_grad)


def rotate(values, positions, turn_sign):
    half_dim = values.shape[-1] // 2
    frequency = jnp.exp(
        jnp.arange(half_dim, dtype=jnp.float32) * (-2.0 * math.log(10000.0) / values.shape[-1])
    )
    angles = positions.astype(jnp.float32)[:, None] * frequency[None, :]
    cosine = jnp.cos(angles)[:, None, :]
    sine_part = jnp.sin(angles)[:, None, :] * turn_sign
    lower_half = values[..., :half_dim]
    upper_half = values[..., half_dim:]
    return jnp.concatenate(
        [
            lower_half * cosine - upper_half * sine_part,
            upper_half * cosine + lower_half * sine_part,
        ],
        axis=-1,
    )


def first_rows(weights, lefts):

    def add_piece(totals, pieces, start_at):
        return tuple(
            (matmul(left_side, piece_rows) for left_side, piece_rows in zip(lefts, pieces))
        )

    initial = tuple(
        (jnp.zeros((lefts[0].shape[0], weight.shape[1]), jnp.float32) for weight in weights)
    )
    return add_piece(
        initial,
        (
            lax.all_gather(weights[0], "dp", axis=0, tiled=True),
            lax.all_gather(weights[1], "dp", axis=0, tiled=True),
            lax.all_gather(weights[2], "dp", axis=0, tiled=True),
            lax.all_gather(weights[3], "dp", axis=0, tiled=True),
        ),
        jnp.int32(0),
    )


def second_rows(w_out, down_folded, attended_low, hidden, ratio):

    def add_piece(total_sum, pieces, start_at):
        count = pieces[0].shape[0]
        down_rows = pieces[1].reshape(count * ratio, pieces[1].shape[1] // ratio)
        return matmul(attended_low, pieces[0]) + matmul(hidden, down_rows)

    initial = jnp.zeros((attended_low.shape[0], w_out.shape[1]), jnp.float32)
    return add_piece(
        initial,
        (
            lax.all_gather(w_out, "dp", axis=0, tiled=True),
            lax.all_gather(down_folded, "dp", axis=0, tiled=True),
        ),
        jnp.int32(0),
    )


def back_first(w_out, down_folded, grad_low, ratio):

    def add_piece(totals, pieces, start_at):
        count = pieces[0].shape[0]
        out_part = lax.dot_general(
            grad_low, pieces[0], contract_cols, preferred_element_type=jnp.float32
        )
        down_rows = pieces[1].reshape(count * ratio, pieces[1].shape[1] // ratio)
        down_part = lax.dot_general(
            grad_low, down_rows, contract_cols, preferred_element_type=jnp.float32
        )
        return (out_part, down_part)

    features = w_out.shape[1]
    initial = (
        jnp.zeros((grad_low.shape[0], features), jnp.float32),
        jnp.zeros((grad_low.shape[0], features * ratio), jnp.float32),
    )
    return add_piece(
        initial,
        (
            lax.all_gather(w_out, "dp", axis=0, tiled=True),
            lax.all_gather(down_folded, "dp", axis=0, tiled=True),
        ),
        jnp.int32(0),
    )


def back_second(weights, rights):

    def add_piece(totals, pieces, start_at):
        return tuple(
            (
                lax.dot_general(
                    right_side, piece_rows, contract_cols, preferred_element_type=jnp.float32
                )
                for right_side, piece_rows in zip(rights, pieces)
            )
        )

    features = weights[1].shape[1]
    initial = tuple((jnp.zeros((rights[0].shape[0], features), jnp.float32) for weight in weights))
    return add_piece(
        initial,
        (
            lax.all_gather(weights[0], "dp", axis=0, tiled=True),
            lax.all_gather(weights[1], "dp", axis=0, tiled=True),
            lax.all_gather(weights[2], "dp", axis=0, tiled=True),
            lax.all_gather(weights[3], "dp", axis=0, tiled=True),
        ),
        jnp.int32(0),
    )


def mix_forward(values_low, gain_row, mix_in_all, mixer_output_wide):
    values = values_low.astype(jnp.float32)
    scaled, inverse = rms_scale(values, gain_row)
    normed_mix = scaled.astype(jnp.bfloat16)
    mixer_preactivation = matmul(normed_mix, mix_in_all)
    mix_act = jax.nn.gelu(mixer_preactivation, approximate=False)
    return (
        precise(mix_act, mixer_output_wide),
        (values, inverse, normed_mix, mixer_preactivation, mix_act),
    )


def mix_backward(kept_mix, act_grad, gain_row, mix_in_all):
    values, inverse, normed_mix, mixer_preactivation, mix_act = kept_mix
    pre_grad = act_grad * gelu_slope(mixer_preactivation)
    in_grad = precise(normed_mix.astype(jnp.float32).T, pre_grad)
    normed_grad = precise(pre_grad, mix_in_all.astype(jnp.float32).T)
    latest_grad, gain_grad = rms_back(values, inverse, gain_row, normed_grad)
    return (latest_grad, gain_grad, in_grad)


def shards(
    history,
    history_layer_index,
    lengths,
    norm_gains,
    mix_in,
    mix_out,
    w_attn,
    w_out,
    w_up,
    w_down,
    cotangent,
):
    local_slots, micro_count, sequence_length, features = history.shape
    hist_count = lax.axis_size("hist")
    dp_count = lax.axis_size("dp")
    hist_place = lax.axis_index("hist")
    slot_count = local_slots * hist_count
    ratio = FF // MODEL_WIDTH
    gains_all, mix_in_all, mix_out_all = (
        lax.all_gather(norm_gains, "dp", axis=1, tiled=True),
        lax.all_gather(mix_in, "dp", axis=0, tiled=True),
        lax.all_gather(mix_out, "dp", axis=0, tiled=True),
    )
    gains_all = gains_all.astype(jnp.float32)
    mixer_output_wide = mix_out_all.astype(jnp.float32)
    mix_width = mixer_output_wide.shape[0]
    layer_lookup = (
        history_layer_index[:, None] == jnp.arange(slot_count, dtype=jnp.int32)[None, :]
    ).astype(jnp.float32)
    newest_output = jnp.sum(
        jnp.arange(slot_count, dtype=jnp.int32)
        * (history_layer_index == slot_count - 1).astype(jnp.int32)
    )
    down_folded = w_down.reshape(w_down.shape[0] // ratio, ratio * w_down.shape[1])
    quarter = cotangent.shape[1]
    own_rows = micro_count * quarter
    positions = hist_place * quarter + jnp.arange(quarter, dtype=jnp.int32)
    valid_rows = (positions[None, :] < lengths[:, None]).astype(jnp.float32).reshape(own_rows, 1)
    root = newest_output // local_slots
    latest_local = lax.dynamic_index_in_dim(history, newest_output % local_slots, 0, keepdims=False)
    latest_rows = broadcast(latest_local, "hist", root)
    dynamic_weights, kept_mix = mix_forward(
        latest_rows.reshape(micro_count * sequence_length, features),
        gains_all[0],
        mix_in_all,
        mixer_output_wide,
    )
    dynamic_weights = dynamic_weights.reshape(
        micro_count, sequence_length, STREAM_COUNT, slot_count
    )
    own_table = lax.dynamic_slice_in_dim(layer_lookup, hist_place * local_slots, local_slots, 0)
    depth_combination_factors = jnp.einsum(
        "mtcj,sj->scmt", dynamic_weights, own_table, precision=highest
    )
    partial_sums = jnp.zeros((STREAM_COUNT, micro_count, sequence_length, features), jnp.float32)
    for depth_position_number in range(local_slots):
        partial_sums = (
            partial_sums
            + depth_combination_factors[depth_position_number][..., None]
            * history[depth_position_number].astype(jnp.float32)[None]
        )
    blended_residual_inputs = lax.psum_scatter(
        partial_sums, "hist", scatter_dimension=2, tiled=True
    )
    stream_rows = blended_residual_inputs.reshape(STREAM_COUNT, own_rows, features)
    normed = []
    inverses = []
    for stream_idx in range(STREAM_COUNT):
        scaled, inverse = rms_scale(stream_rows[stream_idx], gains_all[stream_idx + 1])
        normed.append(scaled.astype(jnp.bfloat16))
        inverses.append(inverse)
    head_shape = (micro_count, quarter, HEADS, HEAD_DIM)
    query_pre, key_pre, value_pre, up_pre = first_rows(
        (w_attn[0], w_attn[1], w_attn[2], w_up), (normed[0], normed[1], normed[2], normed[3])
    )
    attention_asker_vectors = rotate(query_pre.reshape(head_shape), positions, 1.0).astype(
        jnp.bfloat16
    )
    keys_rot = rotate(key_pre.reshape(head_shape), positions, 1.0).astype(jnp.bfloat16)
    values_low = value_pre.astype(jnp.bfloat16)
    keys_all, values_all = (
        lax.all_gather(
            keys_rot.reshape(micro_count, quarter, features), "hist", axis=1, tiled=True
        ),
        lax.all_gather(
            values_low.reshape(micro_count, quarter, features), "hist", axis=1, tiled=True
        ),
    )
    key_heads = keys_all.reshape(micro_count, sequence_length, HEADS, HEAD_DIM)
    value_wide = values_all.reshape(micro_count, sequence_length, HEADS, HEAD_DIM).astype(
        jnp.float32
    )
    score_scale = 1.0 / math.sqrt(HEAD_DIM)
    scores = (
        jnp.einsum(
            "mqhd,mkhd->mhqk",
            attention_asker_vectors,
            key_heads,
            preferred_element_type=jnp.float32,
        )
        * score_scale
    )
    key_positions = jnp.arange(sequence_length, dtype=jnp.int32)
    allowed = (key_positions[None, None, :] <= positions[None, :, None]) & (
        key_positions[None, None, :] < lengths[:, None, None]
    )
    scores = jnp.where(allowed[:, None], scores, masked_out)
    row_top = jnp.max(scores, axis=-1, keepdims=True)
    raised = jnp.exp(scores - row_top)
    soft_weights = raised / jnp.sum(raised, axis=-1, keepdims=True)
    attended = jnp.einsum("mhqk,mkhd->mqhd", soft_weights, value_wide, precision=highest)
    attended_low = attended.reshape(own_rows, features).astype(jnp.bfloat16)
    hidden = jax.nn.gelu(up_pre, approximate=False).astype(jnp.bfloat16)
    branch = second_rows(w_out, down_folded, attended_low, hidden, ratio)
    block_out = (
        ((stream_rows[3] + branch) * valid_rows)
        .astype(jnp.bfloat16)
        .reshape(micro_count, quarter, features)
    )
    grad_rows = cotangent.reshape(own_rows, features).astype(jnp.float32) * valid_rows
    grad_low = grad_rows.astype(jnp.bfloat16)
    attended_back, hidden_grad = back_first(w_out, down_folded, grad_low, ratio)
    up_grad = (hidden_grad * gelu_slope(up_pre)).astype(jnp.bfloat16)
    attended_grad = attended_back.astype(jnp.bfloat16)
    attended_wide = attended_grad.astype(jnp.float32).reshape(head_shape)
    prob_grad = jnp.einsum("mqhd,mkhd->mhqk", attended_wide, value_wide, precision=highest)
    inner_rows = jnp.sum(attended_wide * attended, axis=-1)
    logit_derivative = (
        soft_weights * (prob_grad - jnp.transpose(inner_rows, (0, 2, 1))[..., None]) * score_scale
    )
    query_grad = jnp.einsum(
        "mhqk,mkhd->mqhd", logit_derivative, key_heads.astype(jnp.float32), precision=highest
    )
    key_grad_all = jnp.einsum(
        "mhqk,mqhd->mkhd",
        logit_derivative,
        attention_asker_vectors.astype(jnp.float32),
        precision=highest,
    )
    value_grad_all = jnp.einsum("mhqk,mqhd->mkhd", soft_weights, attended_wide, precision=highest)
    key_grad, value_grad = (
        lax.psum_scatter(
            key_grad_all.reshape(micro_count, sequence_length, features).astype(jnp.bfloat16),
            "hist",
            scatter_dimension=1,
            tiled=True,
        ).astype(jnp.float32),
        lax.psum_scatter(
            value_grad_all.reshape(micro_count, sequence_length, features).astype(jnp.bfloat16),
            "hist",
            scatter_dimension=1,
            tiled=True,
        ).astype(jnp.float32),
    )
    projection_grads = [
        rotate(query_grad, positions, -1.0).reshape(own_rows, features).astype(jnp.bfloat16),
        rotate(key_grad.reshape(head_shape), positions, -1.0)
        .reshape(own_rows, features)
        .astype(jnp.bfloat16),
        value_grad.reshape(own_rows, features).astype(jnp.bfloat16),
    ]
    resid_normed_grad, query_normed_grad, key_normed_grad, value_normed_grad = back_second(
        (w_up, w_attn[0], w_attn[1], w_attn[2]),
        (up_grad, projection_grads[0], projection_grads[1], projection_grads[2]),
    )
    normed_grads = [query_normed_grad, key_normed_grad, value_normed_grad]
    stream_grads = []
    gain_grads = []
    for stream_idx in range(3):
        stream_grad, gain_grad = rms_back(
            stream_rows[stream_idx],
            inverses[stream_idx],
            gains_all[stream_idx + 1],
            normed_grads[stream_idx],
        )
        stream_grads.append(stream_grad)
        gain_grads.append(gain_grad)
    resid_grad, skip_scaling_derivative = rms_back(
        stream_rows[3], inverses[3], gains_all[4], resid_normed_grad
    )
    stream_grads.append(resid_grad + grad_rows)
    gain_grads.append(skip_scaling_derivative)
    stream_grads_all = jnp.stack(stream_grads).reshape(STREAM_COUNT, micro_count, quarter, features)
    full_grads = lax.all_gather(
        stream_grads_all.astype(jnp.bfloat16), "hist", axis=2, tiled=True
    ).astype(stream_grads_all.dtype)
    slot_grads = []
    dyn_grad = jnp.zeros((micro_count, sequence_length, STREAM_COUNT, slot_count), jnp.float32)
    for depth_position_number in range(local_slots):
        rows_now = history[depth_position_number].astype(jnp.float32)
        slot_grads.append(
            jnp.sum(
                depth_combination_factors[depth_position_number][..., None] * full_grads, axis=0
            )
        )
        inner_now = jnp.sum(full_grads * rows_now[None], axis=-1)
        dyn_grad = dyn_grad + jnp.einsum("cmt,j->mtcj", inner_now, own_table[depth_position_number])
    dyn_grad = dyn_grad.reshape(micro_count * sequence_length, STREAM_COUNT * slot_count)
    act_part = precise(dyn_grad, mixer_output_wide.T)
    mix_out_grad = precise(kept_mix[4].T, dyn_grad)
    act_grad = lax.psum(act_part.astype(jnp.bfloat16), "hist").astype(jnp.float32)
    on_root = (hist_place == root).astype(jnp.float32)
    latest_grad, gain_zero, mix_in_grad = mix_backward(kept_mix, act_grad, gains_all[0], mix_in_all)
    gain_zero = gain_zero * on_root
    mix_in_grad = mix_in_grad * on_root
    latest_grad = latest_grad.reshape(micro_count, sequence_length, features)
    marked = []
    for depth_position_number in range(local_slots):
        is_latest = (hist_place * local_slots + depth_position_number == newest_output).astype(
            jnp.float32
        )
        marked.append(slot_grads[depth_position_number] + latest_grad * is_latest)
    history_grad = jnp.stack(marked).astype(jnp.bfloat16)
    gains_grad_full = jnp.stack(
        [gain_zero, gain_grads[0], gain_grads[1], gain_grads[2], gain_grads[3]]
    )
    share_rows = w_out.shape[0]
    per_device = mix_width // dp_count
    mix_out_padded = jnp.pad(
        mix_out_grad.reshape(dp_count, per_device, mix_width),
        ((0, 0), (0, share_rows - per_device), (0, 0)),
    ).reshape(dp_count * share_rows, mix_width)
    small_wide = jnp.concatenate([mix_in_grad, gains_grad_full.T, mix_out_padded], axis=1)
    attn_lefts = (normed[0], normed[1], normed[2], attended_low)
    attn_rights = (projection_grads[0], projection_grads[1], projection_grads[2], grad_low)
    attn_share = lax.psum_scatter(
        jnp.concatenate(
            [
                lax.dot_general(
                    left_side, right_side, contract_rows, preferred_element_type=jnp.float32
                )
                for left_side, right_side in zip(attn_lefts, attn_rights)
            ],
            axis=1,
        ).astype(jnp.bfloat16),
        "dp",
        scatter_dimension=0,
        tiled=True,
    )
    up_term = lax.dot_general(normed[3], up_grad, contract_rows, preferred_element_type=jnp.float32)
    down_term = lax.dot_general(
        hidden, grad_low, contract_rows, preferred_element_type=jnp.float32
    ).reshape(share_rows * lax.axis_size("dp"), ratio * features)
    ffn_share = lax.psum_scatter(
        jnp.concatenate([up_term, down_term, small_wide], axis=1).astype(jnp.bfloat16),
        "dp",
        scatter_dimension=0,
        tiled=True,
    )
    attn_total, ffn_total = (
        lax.psum(attn_share, "hist").astype(jnp.float32),
        lax.psum(ffn_share, "hist").astype(jnp.float32),
    )
    ff_width = ratio * features
    w_attn_grad = jnp.stack(
        [
            attn_total[:, 0:features],
            attn_total[:, features : 2 * features],
            attn_total[:, 2 * features : 3 * features],
        ]
    )
    w_out_grad = attn_total[:, 3 * features : 4 * features]
    w_up_grad = ffn_total[:, 0:ff_width]
    w_down_grad = ffn_total[:, ff_width : 2 * ff_width].reshape(share_rows * ratio, features)
    mix_in_share = ffn_total[:, 2 * ff_width : 2 * ff_width + mix_width]
    gains_share = ffn_total[:, 2 * ff_width + mix_width : 2 * ff_width + mix_width + 5].T
    mix_out_share = ffn_total[0:per_device, 2 * ff_width + mix_width + 5 :]
    return (
        block_out,
        history_grad,
        gains_share,
        mix_in_share,
        mix_out_share,
        w_attn_grad,
        w_out_grad,
        w_up_grad,
        w_down_grad,
    )


DEVICE_MESH = pl.DeviceIdType.MESH
CORE, ACROSS_X, ACROSS_Y = 1, 2, 4


def partner(column, mask):
    moved = column
    for bit in (1, 2, 4):
        if mask & bit:
            on = lax.rem(lax.div(moved, bit), 2)
            moved = moved + bit - 2 * bit * on
    return moved


def push(source, target, send_sem, recv_sem, place):
    copy = pltpu.make_async_remote_copy(
        src_ref=source,
        dst_ref=target,
        send_sem=send_sem,
        recv_sem=recv_sem,
        device_id={"dp": place},
        device_id_type=DEVICE_MESH,
    )
    copy.start()
    return copy


def z_place(plane):
    return {"hist": plane}


class PlaneGatherSteps:

    def __init__(self, column, own, whole, send_sem, recv_sem, local_sem):
        self.column, self.own, self.whole = column, own, whole
        self.send_sem, self.recv_sem, self.local_sem = send_sem, recv_sem, local_sem
        self.rows = own.shape[0]
        self.half = self.rows // 2
        self.across = partner(column, ACROSS_X)
        self.along = partner(column, ACROSS_Y)
        self.beside = partner(column, CORE)
        self.corner = partner(column, ACROSS_X + ACROSS_Y)
        self.copies = []

    def place(self, owner, part):
        start = owner * self.rows + (self.half if part == 1 else 0)
        count = self.rows if part is None else self.half
        return self.whole.at[pl.ds(pl.multiple_of(start, 16), count)]

    def mine(self, part):
        start = self.half if part == 1 else 0
        return self.own.at[pl.ds(start, self.rows if part is None else self.half)]

    def send(self, source, owner, part, to):
        index = len(self.copies)
        copy = push(
            source, self.place(owner, part), self.send_sem.at[index], self.recv_sem.at[index], to
        )
        self.copies.append(copy)

    def begin(self):
        me = self.column
        self.local = pltpu.make_async_copy(self.mine(None), self.place(me, None), self.local_sem)
        self.local.start()
        self.send(self.mine(1), me, 1, self.across)
        self.send(self.mine(0), me, 0, self.along)
        self.send(self.mine(0), me, 0, self.across)
        self.send(self.mine(1), me, 1, self.along)
        self.send(self.mine(None), me, None, self.beside)

    def corners(self):
        self.copies[1].wait_recv()
        self.send(self.place(self.along, 0), self.along, 0, self.across)
        self.copies[0].wait_recv()
        self.send(self.place(self.across, 1), self.across, 1, self.along)

    def siblings(self):
        self.copies[2].wait_recv()
        self.send(self.place(self.across, None), self.across, None, self.beside)
        self.copies[3].wait_recv()
        self.send(self.place(self.along, None), self.along, None, self.beside)

    def rest(self):
        self.copies[5].wait_recv()
        self.send(self.place(self.corner, 0), self.corner, 0, self.beside)
        self.copies[6].wait_recv()
        self.send(self.place(self.corner, 1), self.corner, 1, self.beside)

    def finish(self):
        for index in (4, 7, 8, 9, 10):
            self.copies[index].wait_recv()
        for copy in self.copies:
            copy.wait_send()
        self.local.wait()


class PlaneScatterSteps:
    def __init__(self, column, product, refs, send_sem, recv_sem):
        self.column, self.product = column, product
        self.out_buf, self.side, self.chip, self.from_x, self.from_y, self.last = refs
        self.send_sem, self.recv_sem = send_sem, recv_sem
        rows = self.chip.shape[1]
        self.first, self.second = pl.ds(0, rows // 2), pl.ds(rows // 2, rows // 2)
        self.across = partner(column, ACROSS_X)
        self.along = partner(column, ACROSS_Y)
        self.beside = partner(column, CORE)
        self.pair, self.sends = [], []

    def block(self, i):
        mask = (6, 2, 4, 0)[i]
        if i >= 2:
            self.pair[i - 2].wait_send()
        self.product(partner(self.column, mask + CORE), self.out_buf.at[i % 2])
        self.pair.append(
            push(
                self.out_buf.at[i % 2],
                self.side.at[i],
                self.send_sem.at[i],
                self.recv_sem.at[i],
                self.beside,
            )
        )
        self.product(partner(self.column, mask), self.chip.at[i])
        self.pair[i].wait_recv()
        add_into(self.chip.at[i], self.side.at[i])
        if i == 0:
            self.send(self.chip.at[0, self.first], self.from_x.at[0], self.across)
            self.send(self.chip.at[0, self.second], self.from_y.at[0], self.along)
        if i == 1:
            self.send(self.chip.at[1, self.first], self.from_x.at[1], self.across)
        if i == 2:
            self.send(self.chip.at[2, self.second], self.from_y.at[1], self.along)

    def send(self, source, target, to):
        index = 4 + len(self.sends)
        self.sends.append(
            push(source, target, self.send_sem.at[index], self.recv_sem.at[index], to)
        )

    def turn(self):
        self.sends[0].wait_recv()
        add_into(self.chip.at[2, self.first], self.from_x.at[0])
        self.send(self.chip.at[2, self.first], self.last.at[0], self.along)
        self.sends[1].wait_recv()
        add_into(self.chip.at[1, self.second], self.from_y.at[0])
        self.send(self.chip.at[1, self.second], self.last.at[1], self.across)

    def finish(self, out_ref):
        self.sends[2].wait_recv()
        add_into(self.chip.at[3, self.first], self.from_x.at[1])
        self.sends[3].wait_recv()
        add_into(self.chip.at[3, self.second], self.from_y.at[1])
        self.sends[4].wait_recv()
        add_into(self.chip.at[3, self.first], self.last.at[0])
        self.sends[5].wait_recv()
        add_into(self.chip.at[3, self.second], self.last.at[1])
        if out_ref is not None:
            out_ref[...] = self.chip[3]
        for copy in self.pair[2:] + self.sends:
            copy.wait_send()


def add_into(target, other):
    rows = target.shape[0]
    step = 32 if rows % 32 == 0 else 16

    def some_rows(r, carry):
        piece = pl.ds(pl.multiple_of(r * step, step), step)
        target[piece, :] = (
            target[piece, :].astype(jnp.float32) + other[piece, :].astype(jnp.float32)
        ).astype(jnp.bfloat16)
        return carry

    lax.fori_loop(0, rows // step, some_rows, 0)


class LineSums:

    def __init__(self, plane, parts, arrived, own, last, held, send_sem, recv_sem, load_sem):
        self.plane, self.parts, self.arrived = plane, parts, arrived
        self.own, self.last, self.held = own, last, held
        self.send_sem, self.recv_sem, self.load_sem = send_sem, recv_sem, load_sem
        self.rows = own.shape[0]

    def part(self, way, item, b):
        place = b if way == 0 else 3 - b
        return self.parts.at[pl.ds((item * 4 + place) * self.rows, self.rows)]

    def message(self, way, turn, a, source):
        to = a + 1 if way == 0 else 2 - a
        return pltpu.make_async_remote_copy(
            src_ref=source,
            dst_ref=self.arrived.at[way * 12 + turn],
            send_sem=self.send_sem.at[way * 12 + turn],
            recv_sem=self.recv_sem.at[way * 12 + turn],
            device_id=z_place(to),
            device_id_type=DEVICE_MESH,
        )

    def origin(self, way, turn):
        item, t = divmod(turn, 3)
        return self.message(way, turn, 0, self.part(way, item, 3 - t))

    def slot(self, way, a, turn):
        item, t = divmod(turn, 3)
        return way * 2 + (item * (3 - a) + t) % 2

    def relay(self, way, turn, a):
        return self.message(way, turn, a, self.held.at[self.slot(way, a, turn)])

    def start(self, turn):
        for place in (0, 3):

            @pl.when(self.plane == place)
            def _():
                self.origin(0 if place == 0 else 1, turn).start()

    def load(self, source, target, index):
        return pltpu.make_async_copy(source, target, self.load_sem.at[index])

    def service(self, sigma):
        for place in range(4):

            @pl.when(self.plane == place)
            def _():
                for way in (0, 1):
                    a = place if way == 0 else 3 - place
                    if a == 0:
                        if sigma < 12:
                            self.origin(way, sigma).wait_send()
                        if sigma + 2 < 12:
                            self.origin(way, sigma + 2).start()
                        continue
                    turn = sigma - a + 1
                    if turn < 0 or turn >= 12:
                        continue
                    item, t = divmod(turn, 3)
                    b = 3 - t
                    if b < a:
                        continue
                    if b > a:
                        slot = self.slot(way, a, turn)
                        sent = [
                            earlier
                            for earlier in range(turn)
                            if 3 - earlier % 3 > a and self.slot(way, a, earlier) == slot
                        ]
                        if sent:
                            self.relay(way, sent[-1], a).wait_send()
                        target = self.held.at[slot]
                        mine = self.load(self.part(way, item, b), self.own, 0)
                        mine.start()
                        self.relay(way, turn, a).wait_recv()
                        came = self.load(self.arrived.at[way * 12 + turn], target, 1)
                        came.start()
                        mine.wait()
                        came.wait()
                        add_into(target, self.own)
                        self.relay(way, turn, a).start()
                    else:
                        self.message(way, turn, a - 1, self.own).wait_recv()
                        came = self.load(self.arrived.at[way * 12 + turn], self.last.at[way], 1)
                        came.start()
                        came.wait()
                if sigma % 3 == 2:
                    item = sigma // 3
                    mine = self.load(self.part(0, item, place), self.own, 0)
                    mine.start()
                    mine.wait()

    def drain(self):
        for place in range(4):

            @pl.when(self.plane == place)
            def _():
                for way in (0, 1):
                    a = place if way == 0 else 3 - place
                    if a == 0 or a == 3:
                        continue
                    for slot in (way * 2, way * 2 + 1):
                        sent = [
                            turn
                            for turn in range(12)
                            if 3 - turn % 3 > a and self.slot(way, a, turn) == slot
                        ]
                        self.relay(way, sent[-1], a).wait_send()


class LineSum:

    def __init__(
        self, plane, parts, arrived, own, last, held, send_sem, recv_sem, load_sem, stride, first
    ):
        self.plane, self.parts, self.arrived = plane, parts, arrived
        self.own, self.last, self.held = own, last, held
        self.send_sem, self.recv_sem, self.load_sem = send_sem, recv_sem, load_sem
        self.rows, self.stride, self.first = own.shape[0], stride, first

    def part(self, way, b):
        place = b if way == 0 else 3 - b
        return self.parts.at[pl.ds(place * self.stride + self.first, self.rows)]

    def message(self, way, t, a, source):
        return pltpu.make_async_remote_copy(
            src_ref=source,
            dst_ref=self.arrived.at[way * 3 + t],
            send_sem=self.send_sem.at[way * 3 + t],
            recv_sem=self.recv_sem.at[way * 3 + t],
            device_id=z_place(a + 1 if way == 0 else 2 - a),
            device_id_type=DEVICE_MESH,
        )

    def origin(self, way, t):
        return self.message(way, t, 0, self.part(way, 3 - t))

    def relay(self, way, t, a):
        return self.message(way, t, a, self.held.at[t if a == 1 else 2])

    def start(self):
        for place in (0, 3):

            @pl.when(self.plane == place)
            def _():
                way = 0 if place == 0 else 1
                self.origin(way, 0).start()
                self.origin(way, 1).start()

    def load(self, source, target, index):
        copy = pltpu.make_async_copy(source, target, self.load_sem.at[index])
        copy.start()
        return copy

    def service(self, sigma):
        for place in range(4):

            @pl.when(self.plane == place)
            def _():
                for way in (0, 1):
                    a = place if way == 0 else 3 - place
                    if a == 0:
                        self.origin(way, sigma).wait_send()
                        if sigma == 0:
                            self.origin(way, 2).start()
                        continue
                    t = sigma - a + 1
                    if t < 0 or 3 - t < a:
                        continue
                    b = 3 - t
                    source = self.arrived.at[way * 3 + t]
                    if b > a:
                        relay = self.relay(way, t, a)
                        target = self.held.at[t if a == 1 else 2]
                        mine = self.load(self.part(way, b), self.own, 0)
                        relay.wait_recv()
                        came = self.load(source, target, 1)
                        mine.wait()
                        came.wait()
                        add_into(target, self.own)
                        relay.start()
                    else:
                        self.message(way, t, a - 1, self.own).wait_recv()
                        self.load(source, self.last.at[way], 1).wait()
                if sigma == 2:
                    self.load(self.part(0, place), self.own, 0).wait()

    def finish(self, target):
        step = 16

        def some_rows(r, carry):
            piece = pl.ds(pl.multiple_of(r * step, step), step)
            total = self.own[piece, :].astype(jnp.float32)
            total = total + self.last[0, piece, :].astype(jnp.float32)
            total = total + self.last[1, piece, :].astype(jnp.float32)
            target[piece, :] = total.astype(jnp.bfloat16)
            return carry

        lax.fori_loop(0, self.rows // step, some_rows, 0)
        for place in (1, 2):

            @pl.when(self.plane == place)
            def _():
                for way in (0, 1):
                    a = place if way == 0 else 3 - place
                    for t in range(3 - a):
                        self.relay(way, t, a).wait_send()


class LineGather:

    def __init__(self, plane, own, slot, send_sem, recv_sem, local_sem):
        self.plane, self.own, self.slot = plane, own, slot
        self.send_sem, self.recv_sem, self.local_sem = send_sem, recv_sem, local_sem

    def message(self, way, a, distance):
        origin = a - distance
        plane_of_origin = origin if way == 0 else 3 - origin
        target = self.slot(plane_of_origin)
        return pltpu.make_async_remote_copy(
            src_ref=self.own if distance == 0 else target,
            dst_ref=target,
            send_sem=self.send_sem.at[way * 3 + distance],
            recv_sem=self.recv_sem.at[way * 3 + distance],
            device_id=z_place(a + 1 if way == 0 else 2 - a),
            device_id_type=DEVICE_MESH,
        )

    def service(self, step):
        for place in range(4):

            @pl.when(self.plane == place)
            def _():
                if step == 0:
                    pltpu.make_async_copy(self.own, self.slot(place), self.local_sem).start()
                for way in (0, 1):
                    a = place if way == 0 else 3 - place
                    if step > a:
                        continue
                    if step > 0:
                        self.message(way, a - 1, step - 1).wait_recv()
                    if a < 3:
                        self.message(way, a, step).start()

    def placed(self):
        for place in range(4):

            @pl.when(self.plane == place)
            def _():
                pltpu.make_async_copy(self.own, self.slot(place), self.local_sem).wait()

    def finish(self):
        for place in range(4):

            @pl.when(self.plane == place)
            def _():
                for way in (0, 1):
                    a = place if way == 0 else 3 - place
                    if a < 3:
                        for distance in range(a + 1):
                            self.message(way, a, distance).wait_send()


GAIN_ROW = (4, 1, 2, 3)


def norm_rows_back(x_buf, back, gain_ref, gain_grad_ref, item, extra, target):
    gain = gain_ref[pl.ds(GAIN_ROW[item], 1), :]
    rows, features = target.shape

    def some_rows(r, gain_sum):
        piece = pl.ds(pl.multiple_of(r * 16, 16), 16)
        x = x_buf[piece, :]
        inverse = lax.rsqrt(jnp.mean(x * x, axis=-1, keepdims=True) + epsilon)
        grad = back[piece, :].astype(jnp.float32)
        scaled = grad * gain
        mean = jnp.mean(scaled * x, axis=-1, keepdims=True)
        result = inverse * scaled - x * (inverse * inverse * inverse) * mean
        if extra is not None:
            result = result + extra[piece, :].astype(jnp.float32)
        target[piece, :] = result.astype(jnp.bfloat16)
        return gain_sum + jnp.sum(grad * x * inverse, axis=0, keepdims=True)

    gain_grad_ref[pl.ds(item, 1), :] = lax.fori_loop(
        0, rows // 16, some_rows, jnp.zeros((1, features), jnp.float32)
    )


def forward_kernel(
    length_ref,
    pack_ref,
    latest_ref,
    history_ref,
    select_ref,
    root_ref,
    cotangent_ref,
    w_up_ref,
    w_attn_ref,
    w_down_ref,
    w_out_ref,
    cos_ref,
    sin_ref,
    packed_ref,
    gain_ref,
    pre_ref,
    factor_ref,
    x_ref,
    normed_ref,
    grad_all_ref,
    hidden_ref,
    up_term_ref,
    down_sum_ref,
    full3_ref,
    gain_grad_ref,
    attn_columns,
    q_ref,
    k_ref,
    v_ref,
    out_grad_ref,
    key_before_ref,
    part_ref,
    down_term_ref,
    arrived_ref,
    arrived_down_ref,
    normed3,
    grads,
    up_columns,
    up_grad,
    out_buf,
    side,
    chip,
    from_x,
    from_y,
    last,
    own,
    ends,
    held,
    x_buf,
    normed_buf,
    term_buf,
    grad_own,
    stream_own,
    mix_out_buf,
    dyn_got,
    gather_send,
    gather_recv,
    gather_local,
    scatter_send,
    scatter_recv,
    line_send,
    line_recv,
    line_load,
    swap_send,
    swap_recv,
    swap_local,
    out_sem,
    small_send,
    small_recv,
    dyn_send,
    dyn_recv,
    route_send,
    route_recv,
    block_sem,
    spread_send,
    spread_recv,
    sum_send,
    sum_recv,
    key_send,
    key_recv,
    ready_sem,
    *,
    micro_count,
    sequence_length,
):
    column = lax.axis_index("dp")
    plane = lax.axis_index("hist")
    rows, features = grad_own.shape
    total = 8 * rows
    share = w_up_ref.shape[0]
    ff_share = w_down_ref.shape[0]
    width = share
    tile = 256
    mix_rows = pack_ref.shape[0] - share - 32 + 8
    every_mask = (6, 7, 2, 3, 4, 5, 1)

    barrier = pltpu.get_barrier_semaphore()
    for mask in every_mask:
        pl.semaphore_signal(
            barrier, inc=1, device_id={"dp": partner(column, mask)}, device_id_type=DEVICE_MESH
        )
    for place in range(4):

        @pl.when(plane == place)
        def _():
            for p in range(4):
                if p != place:
                    pl.semaphore_signal(
                        barrier, inc=1, device_id=z_place(p), device_id_type=DEVICE_MESH
                    )

    pl.semaphore_wait(barrier, 10)

    def block_load(source, target, index):
        copy = pltpu.make_async_copy(source, target, block_sem.at[index])
        copy.start()
        return copy

    small_copies = [
        push(
            pack_ref,
            packed_ref.at[column],
            small_send.at[mask],
            small_recv.at[mask],
            partner(column, mask),
        )
        for mask in every_mask
    ]
    small_local = pltpu.make_async_copy(pack_ref, packed_ref.at[column], small_send.at[0])
    small_local.start()
    latest_loads = [
        block_load(latest_ref.at[pl.ds(q * rows, rows)], normed_buf.at[q], 8 + q) for q in range(4)
    ]

    my_rows = pl.ds(pl.multiple_of(column * share, 16), share)

    def up_piece(owner):
        return w_up_ref.at[:, pl.ds(pl.multiple_of(owner * ff_share, 128), ff_share)]

    up_local = pltpu.make_async_copy(up_piece(column), up_columns.at[my_rows], swap_local.at[0])
    up_local.start()
    up_swaps = [
        push(
            up_piece(partner(column, mask)),
            up_columns.at[my_rows],
            swap_send.at[mask],
            swap_recv.at[mask],
            partner(column, mask),
        )
        for mask in every_mask
    ]

    chunk = rows // micro_count

    def route_source(place, s):
        return cotangent_ref.at[pl.ds(s * chunk, chunk)]

    def route_copy(place, s, target_place, slot):
        return pltpu.make_async_remote_copy(
            src_ref=route_source(place, s),
            dst_ref=grad_own.at[pl.ds(slot * chunk, chunk)],
            send_sem=route_send.at[s],
            recv_sem=route_recv.at[slot],
            device_id=z_place(target_place),
            device_id_type=DEVICE_MESH,
        )

    def route_local(place, s, slot):
        return pltpu.make_async_copy(
            route_source(place, s), grad_own.at[pl.ds(slot * chunk, chunk)], route_recv.at[slot]
        )

    for place in range(4):

        @pl.when(plane == place)
        def _():
            for s in range(micro_count):
                target_place, slot = divmod(s * 4 + place, micro_count)
                if target_place == place:
                    route_local(place, s, slot).start()
                else:
                    route_copy(place, s, target_place, slot).start()

    block_order = (3, 0, 2, 1)

    def history_loads(i):
        p, h = block_order[i], i % 2
        return [
            block_load(
                history_ref.at[pl.ds((slot * 4 + p) * rows, rows)],
                normed3.at[pl.ds((h * 4 + slot) * rows, rows)],
                h * 4 + slot,
            )
            for slot in range(4)
        ]

    loads = [history_loads(0), history_loads(1)]
    zeros = jnp.zeros((16, features), jnp.bfloat16)

    def clear(r, carry):
        ends[0, pl.ds(pl.multiple_of(r * 16, 16), 16), :] = zeros
        ends[1, pl.ds(pl.multiple_of(r * 16, 16), 16), :] = zeros
        return carry

    lax.fori_loop(0, ends.shape[1] // 16, clear, 0)

    small_local.wait()
    for copy in small_copies:
        copy.wait_recv()
    for d in range(8):
        gains = packed_ref[d, pl.ds(share + 16, 16), :].astype(jnp.float32)
        gain_ref[:, pl.ds(d * share, share // 2)] = gains[:8]
        gain_ref[:, pl.ds(d * share + share // 2, share // 2)] = gains[8:]
        mix_out_buf[pl.ds(d * mix_rows, mix_rows), :] = packed_ref[
            d, pl.ds(share, 16), :
        ].astype(jnp.float32)[:mix_rows]
    for copy in latest_loads:
        copy.wait()
    for q in range(4):

        def norm_rows(r, carry):
            piece = pl.ds(pl.multiple_of(r * 16, 16), 16)
            x = normed_buf[q, piece, :].astype(jnp.float32)
            inverse = lax.rsqrt(jnp.mean(x * x, axis=-1, keepdims=True) + epsilon)
            normed_buf[q, piece, :] = (x * inverse * gain_ref[pl.ds(0, 1), :]).astype(jnp.bfloat16)
            return carry

        lax.fori_loop(0, rows // 16, norm_rows, 0)
        pre = None
        for d in range(8):
            term = matmul(normed_buf[q, :, d * share : (d + 1) * share], packed_ref[d, :share, :])
            pre = term if pre is None else pre + term
        pre_ref[pl.ds(q * rows, rows), :] = pre
    pre = pre_ref[...]
    act = 0.5 * pre * (1.0 + lax.erf(pre * (1.0 / math.sqrt(2.0))))
    dyn = precise(act[:, : 8 * mix_rows], mix_out_buf[...])
    dyn_columns = (jnp.transpose(dyn)[: 8 * mix_rows] * root_ref[pl.ds(0, 1), :]).astype(jnp.bfloat16)

    def dyn_copy(source_place, target_place):
        return pltpu.make_async_remote_copy(
            src_ref=dyn_got.at[source_place],
            dst_ref=dyn_got.at[source_place],
            send_sem=dyn_send.at[target_place],
            recv_sem=dyn_recv.at[source_place],
            device_id=z_place(target_place),
            device_id_type=DEVICE_MESH,
        )

    for place in range(4):

        @pl.when(plane == place)
        def _():
            dyn_got[place] = dyn_columns
            for p in range(4):
                if p != place:
                    dyn_copy(place, p).start()
            for p in range(4):
                if p != place:
                    dyn_copy(p, place).wait_recv()

    dyn_sum = dyn_got[0] + dyn_got[1] + dyn_got[2] + dyn_got[3]
    factor_ref[...] = lax.dot_general(
        dyn_sum, select_ref[...], contract_rows, preferred_element_type=jnp.float32
    )

    block = pl.ds(0, rows)
    line = LineSums(
        plane,
        part_ref,
        arrived_ref,
        own.at[block],
        ends.at[:, block],
        held.at[:, block],
        line_send,
        line_recv,
        line_load,
    )
    stores = [None, None]
    for i, p in enumerate(block_order):
        h = i % 2
        for copy in loads[i]:
            copy.wait()
        if stores[h] is not None:
            for copy in stores[h]:
                copy.wait()

        def mix_rows_of(r, carry):
            factors = factor_ref[pl.ds(pl.multiple_of(p * rows + r * 16, 16), 16), :]
            for lane in range(0, features, 512):
                slots = [
                    normed3[
                        pl.ds(pl.multiple_of((h * 4 + slot) * rows + r * 16, 16), 16),
                        lane : lane + 512,
                    ].astype(jnp.float32)
                    for slot in range(4)
                ]
                for item in range(4):
                    mixed = None
                    for slot in range(4):
                        one = item * 4 + slot
                        term = factors[:, one : one + 1] * slots[slot]
                        mixed = term if mixed is None else mixed + term
                    grads[
                        pl.ds(pl.multiple_of((h * 4 + item) * rows + r * 16, 16), 16),
                        lane : lane + 512,
                    ] = mixed.astype(jnp.bfloat16)
            return carry

        lax.fori_loop(0, rows // 16, mix_rows_of, 0)
        stores[h] = [
            pltpu.make_async_copy(
                grads.at[pl.ds((h * 4 + item) * rows, rows)],
                part_ref.at[pl.ds((item * 4 + p) * rows, rows)],
                block_sem.at[12 + h * 4 + item],
            )
            for item in range(4)
        ]
        for copy in stores[h]:
            copy.start()
        if i + 2 < 4:
            loads.append(history_loads(i + 2))
        if i % 2 == 1:
            for copies in stores:
                for copy in copies:
                    copy.wait()
            stores = [None, None]
        if i == 1:
            line.start(0)

    line.start(1)
    for mask in (CORE, ACROSS_X, ACROSS_Y):
        pl.semaphore_signal(
            ready_sem, inc=1, device_id={"dp": partner(column, mask)}, device_id_type=DEVICE_MESH
        )

    def attn_piece(stream, owner):
        return w_attn_ref.at[stream, :, pl.ds(pl.multiple_of(owner * share, 128), share)]

    def gather(index, own_rows, whole):
        return PlaneGatherSteps(
            column,
            own_rows,
            whole,
            gather_send.at[index],
            gather_recv.at[index],
            gather_local.at[index],
        )

    for place in range(4):

        @pl.when(plane == place)
        def _():
            for slot in range(micro_count):
                s, source_place = divmod(place * micro_count + slot, 4)
                if source_place == place:
                    route_local(place, s, slot).wait()
                else:
                    route_copy(source_place, s, place, slot).wait_recv()

    def mask_rows(r, carry):
        piece = pl.ds(pl.multiple_of(r * 16, 16), 16)
        row = plane * rows + r * 16 + lax.broadcasted_iota(jnp.int32, (16, 1), 0)
        limit = jnp.zeros((16, 1), jnp.int32)
        for m in range(micro_count):
            inside = (row >= m * sequence_length) & (row < (m + 1) * sequence_length)
            limit = jnp.where(inside, m * sequence_length + length_ref[m], limit)
        kept = jnp.where(row < limit, grad_own[piece, :].astype(jnp.float32), 0.0)
        grad_own[piece, :] = kept.astype(jnp.bfloat16)
        return carry

    lax.fori_loop(0, rows // 16, mask_rows, 0)
    pl.semaphore_wait(ready_sem, 3)
    grad_gather = gather(4, grad_own, grads)
    grad_gather.begin()

    x_copies = []

    def combine(item):
        if x_copies:
            x_copies[-1].wait()

        def some_rows(r, carry):
            piece = pl.ds(pl.multiple_of(r * 16, 16), 16)
            x = (
                own[piece, :].astype(jnp.float32)
                + ends[0, piece, :].astype(jnp.float32)
                + ends[1, piece, :].astype(jnp.float32)
            )
            x_buf[piece, :] = x
            inverse = lax.rsqrt(jnp.mean(x * x, axis=-1, keepdims=True) + epsilon)
            normed_buf[item, piece, :] = (
                x * inverse * gain_ref[pl.ds(GAIN_ROW[item], 1), :]
            ).astype(jnp.bfloat16)
            return carry

        lax.fori_loop(0, rows // 16, some_rows, 0)
        copy = pltpu.make_async_copy(x_buf, x_ref.at[item], out_sem.at[0])
        copy.start()
        x_copies.append(copy)
        steps = gather(
            item, normed_buf.at[item], normed3 if item == 0 else normed_ref.at[item - 1]
        )
        steps.begin()
        return steps

    line.service(0)
    line.service(1)
    grad_gather.corners()
    grad_gather.siblings()
    line.service(2)
    gather3 = combine(0)
    grad_gather.rest()
    grad_gather.finish()
    grads_out = pltpu.make_async_copy(grads, grad_all_ref, out_sem.at[2])
    grads_out.start()
    gather3.corners()
    line.service(3)
    gather3.siblings()
    gather3.rest()
    line.service(4)
    for copy in up_swaps:
        copy.wait_recv()
    up_local.wait()
    gather3.finish()
    attn_swaps, attn_locals = [], []
    for stream in range(3):
        local = pltpu.make_async_copy(
            attn_piece(stream, column),
            attn_columns.at[stream, my_rows],
            swap_local.at[1 + stream],
        )
        local.start()
        attn_locals.append(local)
        for mask in every_mask:
            attn_swaps.append(
                push(
                    attn_piece(stream, partner(column, mask)),
                    attn_columns.at[stream, my_rows],
                    swap_send.at[8 * (stream + 1) + mask],
                    swap_recv.at[8 * (stream + 1) + mask],
                    partner(column, mask),
                )
            )

    def feed(first_block, count):
        def one_tile(step, carry):
            piece = pl.ds(pl.multiple_of((step // (ff_share // tile)) * rows, 16), rows)
            lanes = pl.ds(pl.multiple_of((step % (ff_share // tile)) * tile, tile), tile)
            up = jnp.dot(normed3[piece, :], up_columns[:, lanes], preferred_element_type=jnp.float32)
            spread = 0.5 * (1.0 + lax.erf(up * (1.0 / math.sqrt(2.0))))
            hidden_ref[piece, lanes] = (up * spread).astype(jnp.bfloat16)
            slope = spread + up * jnp.exp(-0.5 * up * up) * (1.0 / math.sqrt(2.0 * math.pi))
            hidden_grad = lax.dot_general(
                grads[piece, :],
                w_down_ref[lanes, :],
                contract_cols,
                preferred_element_type=jnp.float32,
            )
            up_grad[piece, lanes] = (hidden_grad * slope).astype(jnp.bfloat16)
            return carry

        per_block = ff_share // tile
        lax.fori_loop(first_block * per_block, (first_block + count) * per_block, one_tile, 0)

    def back_product(owner, target):
        left_rows = pl.ds(pl.multiple_of(owner * rows, 16), rows)

        def one_tile(t, carry):
            lanes = pl.ds(pl.multiple_of(t * 2 * tile, 2 * tile), 2 * tile)
            target[:, lanes] = lax.dot_general(
                up_grad[left_rows, :],
                up_columns[lanes, :],
                contract_cols,
                preferred_element_type=jnp.float32,
            ).astype(jnp.bfloat16)
            return carry

        lax.fori_loop(0, features // (2 * tile), one_tile, 0)

    term_slots = 2
    part = share // 4

    def term_copies(kind, slot, index):
        if kind == 0:
            return [
                pltpu.make_async_copy(
                    term_buf.at[slot, pl.ds(h * part, part), pl.ds(0, ff_share)],
                    up_term_ref.at[
                        pl.ds(h * 4 * part + index % 4 * part, part),
                        pl.ds(index // 4 * ff_share, ff_share),
                    ],
                    out_sem.at[3 + 4 * slot + h],
                )
                for h in range(4)
            ]
        return [
            pltpu.make_async_copy(
                term_buf.at[slot],
                down_term_ref.at[pl.ds(index * tile, tile)],
                out_sem.at[3 + 4 * slot],
            )
        ]

    def terms(kind, first, count):
        term_width = ff_share if kind == 0 else features
        pending = []
        for index in range(first, first + count):
            slot = index % term_slots
            if len(pending) >= term_slots:
                for copy in pending[-term_slots]:
                    copy.wait()

            def one_tile(t, carry):
                lanes = pl.ds(pl.multiple_of(t * 2 * tile, 2 * tile), 2 * tile)
                if kind == 0:
                    left, right = normed3[:, index * tile : (index + 1) * tile], up_grad[:, lanes]
                else:
                    left, right = hidden_ref[:, index * tile : (index + 1) * tile], grads[:, lanes]
                term_buf[slot, :, lanes] = lax.dot_general(
                    left, right, contract_rows, preferred_element_type=jnp.float32
                ).astype(jnp.bfloat16)
                return carry

            lax.fori_loop(0, term_width // (2 * tile), one_tile, 0)
            copies = term_copies(kind, slot, index)
            for copy in copies:
                copy.start()
            pending.append(copies)
        for copies in pending[-term_slots:]:
            for copy in copies:
                copy.wait()

    def project(stream, target):
        def one_block(b, carry):
            piece = pl.ds(pl.multiple_of(b * rows, 16), rows)
            value = matmul(normed3[piece, :], attn_columns[stream])
            if stream < 2:
                parts = []
                for head in range(width // HEAD_DIM):
                    one = value[:, head * HEAD_DIM : (head + 1) * HEAD_DIM]
                    swapped = jnp.concatenate(
                        [one[:, HEAD_DIM // 2 :], one[:, : HEAD_DIM // 2]], axis=1
                    )
                    parts.append(one * cos_ref[...] + swapped * sin_ref[...])
                value = jnp.concatenate(parts, axis=1)
            target[piece, :] = value.astype(jnp.bfloat16)
            return carry

        lax.fori_loop(0, 8, one_block, 0)

    def out_grads(b, carry):
        piece = pl.ds(pl.multiple_of(b * rows, 16), rows)
        out_grad_ref[piece, :] = lax.dot_general(
            grads[piece, :], w_out_ref[...], contract_cols, preferred_element_type=jnp.float32
        ).astype(jnp.bfloat16)
        return carry

    def key_copy(place):
        return pltpu.make_async_remote_copy(
            src_ref=k_ref,
            dst_ref=key_before_ref,
            send_sem=key_send.at[0],
            recv_sem=key_recv.at[0],
            device_id=z_place(place + 1),
            device_id_type=DEVICE_MESH,
        )

    feed(0, 2)
    line.service(5)
    gather0 = combine(1)
    feed(2, 2)
    line.service(6)
    gather0.corners()
    feed(4, 2)
    line.service(7)
    gather0.siblings()
    feed(6, 2)
    gather0.rest()
    scatter = PlaneScatterSteps(
        column,
        back_product,
        (out_buf, side, chip, from_x, from_y, last),
        scatter_send,
        scatter_recv,
    )
    scatter.block(0)
    line.service(8)
    gather1 = combine(2)
    scatter.block(1)
    scatter.block(2)
    scatter.block(3)
    gather0.finish()
    terms(1, 0, 2)
    line.service(9)
    scatter.turn()
    gather1.corners()
    terms(1, 2, ff_share // tile - 2)
    line.service(10)
    scatter.finish(None)
    x_copies[-1].wait()
    x_load = pltpu.make_async_copy(x_ref.at[0], x_buf, out_sem.at[1])
    x_load.start()
    x_load.wait()
    norm_rows_back(x_buf, chip.at[3], gain_ref, gain_grad_ref, 0, grad_own, stream_own)
    x_copies.clear()
    spread3 = LineGather(
        plane,
        stream_own,
        lambda p: full3_ref.at[pl.ds(p * rows, rows)],
        spread_send,
        spread_recv,
        out_sem.at[11],
    )
    spread3.service(0)
    gather1.siblings()
    down_line = LineSum(
        plane,
        down_term_ref,
        arrived_down_ref,
        own,
        ends,
        held,
        sum_send,
        sum_recv,
        line_load,
        share,
        0,
    )
    line.service(11)
    gather2 = combine(3)
    down_line.start()
    gather1.rest()
    terms(0, 0, features // tile)
    line.drain()
    gather1.finish()
    load = block_load(normed_ref.at[1], normed3, 0)
    gather2.corners()
    for copy in attn_swaps:
        copy.wait_recv()
    for copy in attn_locals:
        copy.wait()
    spread3.service(1)
    load.wait()
    project(1, k_ref)
    for place in range(3):

        @pl.when(plane == place)
        def _():
            key_copy(place).start()

    load = block_load(normed_ref.at[0], normed3, 0)
    down_line.service(0)
    gather2.siblings()
    gather2.rest()
    load.wait()
    project(0, q_ref)
    spread3.service(2)
    lax.fori_loop(0, 8, out_grads, 0)
    gather2.finish()
    load = block_load(normed_ref.at[2], normed3, 0)
    down_line.service(1)
    load.wait()
    project(2, v_ref)
    spread3.service(3)
    for copy in small_copies + up_swaps + attn_swaps:
        copy.wait_send()
    grads_out.wait()
    x_copies[-1].wait()
    for place in range(4):

        @pl.when(plane == place)
        def _():
            for p in range(4):
                if p != place:
                    dyn_copy(place, p).wait_send()
            for s in range(micro_count):
                target_place, slot = divmod(s * 4 + place, micro_count)
                if target_place != place:
                    route_copy(place, s, target_place, slot).wait_send()

    down_line.service(2)
    down_line.finish(down_sum_ref)
    spread3.placed()
    spread3.finish()
    for place in range(4):

        @pl.when(plane == place)
        def _():
            if place > 0:
                key_copy(place - 1).wait_recv()
            if place < 3:
                key_copy(place).wait_send()


def forward_and_feed(
    lengths,
    pack,
    latest,
    history,
    select,
    root,
    cotangent,
    w_up,
    w_attn,
    w_down,
    w_out,
    cosine,
    sine_part,
    sequence_length,
):
    rows, features = cotangent.shape
    micro_count = lengths.shape[0]
    total = 8 * rows
    share = w_up.shape[0]
    ff_share = w_down.shape[0]
    mix_width = select.shape[0]
    block = (rows, features)
    piece = (share, features)
    half = (2, rows // 2, features)
    anywhere = pl.BlockSpec(memory_space=pl.ANY)
    near = pl.BlockSpec(memory_space=pltpu.VMEM)
    shape = jax.ShapeDtypeStruct
    low_type = jnp.bfloat16
    some = lambda *dims: pltpu.VMEM(dims, low_type)
    wide = lambda *dims: pltpu.VMEM(dims, jnp.float32)
    dma = pltpu.SemaphoreType.DMA
    outputs = [
        (near, shape((8,) + pack.shape, low_type)),
        (near, shape((8, features), jnp.float32)),
        (near, shape((4 * rows, 128), jnp.float32)),
        (near, shape((4 * rows, 128), jnp.float32)),
        (anywhere, shape((4,) + block, jnp.float32)),
        (anywhere, shape((3, total, features), low_type)),
        (anywhere, shape((total, features), low_type)),
        (near, shape((total, ff_share), low_type)),
        (anywhere, shape((ff_share, features), low_type)),
        (near, shape(piece, low_type)),
        (anywhere, shape((4 * rows, features), low_type)),
        (near, shape((8, features), jnp.float32)),
        (near, shape((3, features, share), low_type)),
        (near, shape((total, share), low_type)),
        (near, shape((total, share), low_type)),
        (near, shape((total, share), low_type)),
        (near, shape((total, share), low_type)),
        (anywhere, shape((total, share), low_type)),
        (anywhere, shape((16 * rows, features), low_type)),
        (anywhere, shape((ff_share, features), low_type)),
        (anywhere, shape((24,) + block, low_type)),
        (anywhere, shape((6,) + piece, low_type)),
    ]
    return pl.pallas_call(
        functools.partial(
            forward_kernel, micro_count=micro_count, sequence_length=sequence_length
        ),
        in_specs=[pl.BlockSpec(memory_space=pltpu.SMEM), near, anywhere, anywhere]
        + [near, near, anywhere, anywhere, anywhere]
        + [near] * 4,
        out_specs=[spec for spec, _ in outputs],
        out_shape=[out for _, out in outputs],
        scratch_shapes=[
            some(total, features),
            some(total, features),
            some(features, ff_share),
            some(total, ff_share),
            some(2, *block),
            some(4, *block),
            some(4, *block),
            some(*half),
            some(*half),
            some(*half),
            some(*piece),
            some(2, *piece),
            some(4, *piece),
            wide(*block),
            some(4, *block),
            some(2, 256, features),
            some(*block),
            some(*block),
            wide(mix_width, 128),
            some(4, mix_width, 4 * rows),
            dma((5, 11)),
            dma((5, 11)),
            dma((5,)),
            dma((10,)),
            dma((10,)),
            dma((24,)),
            dma((24,)),
            dma((2,)),
            dma((32,)),
            dma((32,)),
            dma((4,)),
            dma((12,)),
            dma((8,)),
            dma((8,)),
            dma((4,)),
            dma((4,)),
            dma((micro_count,)),
            dma((micro_count,)),
            dma((20,)),
            dma((6,)),
            dma((6,)),
            dma((6,)),
            dma((6,)),
            dma((1,)),
            dma((1,)),
            pltpu.SemaphoreType.REGULAR,
        ],
        compiler_params=pltpu.CompilerParams(
            collective_id=5, has_side_effects=True, vmem_limit_bytes=63 * 1024 * 1024
        ),
        cost_estimate=pl.CostEstimate(
            flops=12 * total * features * ff_share,
            bytes_accessed=600 * 1000 * 1000,
            transcendentals=0,
        ),
    )(
        lengths,
        pack,
        latest,
        history,
        select,
        root,
        cotangent,
        w_up,
        w_attn,
        w_down,
        w_out,
        cosine,
        sine_part,
    )


def small_sum_kernel(parts_ref, out_ref, got, sums, send_sem, recv_sem, z_send, z_recv):
    column = lax.axis_index("dp")
    plane = lax.axis_index("hist")
    every_mask = (6, 7, 2, 3, 4, 5, 1)
    barrier = pltpu.get_barrier_semaphore()
    for mask in every_mask:
        pl.semaphore_signal(
            barrier, inc=1, device_id={"dp": partner(column, mask)}, device_id_type=DEVICE_MESH
        )
    for place in range(4):

        @pl.when(plane == place)
        def _():
            for p in range(4):
                if p != place:
                    pl.semaphore_signal(
                        barrier, inc=1, device_id=z_place(p), device_id_type=DEVICE_MESH
                    )

    pl.semaphore_wait(barrier, 10)
    copies = [
        push(
            parts_ref.at[partner(column, mask)],
            got.at[mask],
            send_sem.at[mask],
            recv_sem.at[mask],
            partner(column, mask),
        )
        for mask in every_mask
    ]
    total = parts_ref[column].astype(jnp.float32)
    for mask, copy in zip(every_mask, copies):
        copy.wait_recv()
        total = total + got[mask].astype(jnp.float32)

    def line_copy(source_place, target_place):
        return pltpu.make_async_remote_copy(
            src_ref=sums.at[source_place],
            dst_ref=sums.at[source_place],
            send_sem=z_send.at[target_place],
            recv_sem=z_recv.at[source_place],
            device_id=z_place(target_place),
            device_id_type=DEVICE_MESH,
        )

    for place in range(4):

        @pl.when(plane == place)
        def _():
            others = [p for p in range(4) if p != place]
            sums[place] = total.astype(jnp.bfloat16)
            for p in others:
                line_copy(place, p).start()
            for p in others:
                line_copy(p, place).wait_recv()
            for p in others:
                line_copy(place, p).wait_send()

    out_ref[...] = (sums[0].astype(jnp.float32) + sums[1].astype(jnp.float32)) + (
        sums[2].astype(jnp.float32) + sums[3].astype(jnp.float32)
    )
    for copy in copies:
        copy.wait_send()


def small_sums(parts):
    dims = parts.shape[1:]
    dma = pltpu.SemaphoreType.DMA
    return pl.pallas_call(
        small_sum_kernel,
        out_shape=jax.ShapeDtypeStruct(dims, jnp.float32),
        in_specs=[pl.BlockSpec(memory_space=pltpu.VMEM)],
        out_specs=pl.BlockSpec(memory_space=pltpu.VMEM),
        scratch_shapes=[
            pltpu.VMEM((8,) + dims, jnp.bfloat16),
            pltpu.VMEM((4,) + dims, jnp.bfloat16),
            dma((8,)),
            dma((8,)),
            dma((4,)),
            dma((4,)),
        ],
        compiler_params=pltpu.CompilerParams(collective_id=7, has_side_effects=True),
        cost_estimate=pl.CostEstimate(
            flops=0, bytes_accessed=40 * 1000 * 1000, transcendentals=0
        ),
    )(parts)


def slot_grad_kernel(
    flag_ref,
    factor_ref,
    first_ref,
    rest_ref,
    latest_ref,
    pre_grad_ref,
    mix_in_ref,
    gain_ref,
    out_ref,
    gain_grad_ref,
):
    x = latest_ref[...].astype(jnp.float32)
    inverse = lax.rsqrt(jnp.mean(x * x, axis=-1, keepdims=True) + epsilon)
    grad = precise(pre_grad_ref[...], mix_in_ref[...])
    scaled = grad * gain_ref[pl.ds(0, 1), :]
    mean = jnp.mean(scaled * x, axis=-1, keepdims=True)
    latest_grad = inverse * scaled - x * (inverse * inverse * inverse) * mean
    gain_sum = jnp.sum(grad * x * inverse, axis=0, keepdims=True)

    @pl.when(pl.program_id(0) == 0)
    def _():
        gain_grad_ref[...] = jnp.zeros_like(gain_grad_ref)

    gain_grad_ref[pl.ds(0, 1), :] += gain_sum
    grads = [first_ref[...].astype(jnp.float32)] + [
        rest_ref[i].astype(jnp.float32) for i in range(3)
    ]
    factors = factor_ref[...]
    for slot in range(4):
        total = latest_grad * flag_ref[slot]
        for item in range(4):
            one = item * 4 + slot
            total = total + factors[:, one : one + 1] * grads[item]
        out_ref[slot] = total.astype(jnp.bfloat16)


def slot_grads_of(latest_here, factors, first, rest, latest, pre_grad, mix_in_columns, gains):
    total, features = first.shape
    step = 64
    mix_width = pre_grad.shape[1]
    rows_of = lambda *lead: pl.BlockSpec(
        lead + (step, features), lambda r: (0,) * len(lead) + (r, 0)
    )
    whole = lambda *dims: pl.BlockSpec(dims, lambda r: (0, 0))
    return pl.pallas_call(
        slot_grad_kernel,
        grid=(total // step,),
        in_specs=[
            pl.BlockSpec(memory_space=pltpu.SMEM),
            pl.BlockSpec((step, 128), lambda r: (r, 0)),
            rows_of(),
            rows_of(3),
            rows_of(),
            pl.BlockSpec((step, mix_width), lambda r: (r, 0)),
            whole(mix_width, features),
            whole(8, features),
        ],
        out_specs=[rows_of(4), whole(8, features)],
        out_shape=[
            jax.ShapeDtypeStruct((4, total, features), jnp.bfloat16),
            jax.ShapeDtypeStruct((8, features), jnp.float32),
        ],
        compiler_params=pltpu.CompilerParams(vmem_limit_bytes=56 * 1024 * 1024),
        cost_estimate=pl.CostEstimate(
            flops=40 * total * features, bytes_accessed=20 * total * features, transcendentals=0
        ),
    )(latest_here, factors, first, rest, latest, pre_grad, mix_in_columns, gains)


def lay_out_kernel(part_ref, attn_ref, out_ref):
    quarter = out_ref.shape[0]
    for stream in range(3):
        attn_ref[stream] = part_ref[stream * quarter : (stream + 1) * quarter, :].astype(
            jnp.float32
        )
    out_ref[...] = part_ref[3 * quarter :, :].astype(jnp.float32)


def lay_out(parts):
    total, features = parts.shape
    step = total // 4
    quarter = step // 4
    return pl.pallas_call(
        lay_out_kernel,
        grid=(4,),
        in_specs=[pl.BlockSpec((step, features), lambda p: (p, 0))],
        out_specs=[
            pl.BlockSpec((3, quarter, features), lambda p: (0, p, 0)),
            pl.BlockSpec((quarter, features), lambda p: (p, 0)),
        ],
        out_shape=[
            jax.ShapeDtypeStruct((3, step, features), jnp.float32),
            jax.ShapeDtypeStruct((step, features), jnp.float32),
        ],
        compiler_params=pltpu.CompilerParams(vmem_limit_bytes=56 * 1024 * 1024),
        cost_estimate=pl.CostEstimate(
            flops=0, bytes_accessed=6 * total * features, transcendentals=0
        ),
    )(parts)


def attend_column(
    column,
    plane,
    length_ref,
    cosine,
    sine_part,
    q_ref,
    k_ref,
    v_ref,
    kv_before_ref,
    out_grad_ref,
    att_ref,
    q_grad_ref,
    kv_grad_ref,
    kv_before_grad_ref,
    rows,
    micro_count,
    sequence_length,
):
    here = pl.ds(pl.multiple_of(column * rows, 16), rows)
    width = q_ref.shape[1]
    scale = 1.0 / math.sqrt(HEAD_DIM)
    row = plane * rows + lax.broadcasted_iota(jnp.int32, (rows, 1), 0)
    start = jnp.zeros((rows, 1), jnp.int32)
    limit = jnp.zeros((rows, 1), jnp.int32)
    for m in range(micro_count):
        inside = (row >= m * sequence_length) & (row < (m + 1) * sequence_length)
        start = jnp.where(inside, m * sequence_length, start)
        limit = jnp.where(inside, m * sequence_length + length_ref[column * micro_count + m], limit)
    limit = jnp.minimum(limit, row + 1)
    key_row = (plane - 1) * rows + lax.broadcasted_iota(jnp.int32, (1, 2 * rows), 1)
    allowed = (key_row >= start) & (key_row < limit)
    for head in range(width // HEAD_DIM):
        lanes = slice(head * HEAD_DIM, (head + 1) * HEAD_DIM)
        value_lanes = slice(width + head * HEAD_DIM, width + (head + 1) * HEAD_DIM)
        query = q_ref[here, lanes]
        keys = jnp.concatenate([kv_before_ref[here, lanes], k_ref[here, lanes]], axis=0)
        values = jnp.concatenate([kv_before_ref[here, value_lanes], v_ref[here, lanes]], axis=0)
        out_grad = out_grad_ref[here, lanes]
        scores = (
            lax.dot_general(query, keys, contract_cols, preferred_element_type=jnp.float32) * scale
        )
        scores = jnp.where(allowed, scores, masked_out)
        raised = jnp.exp(scores - jnp.max(scores, axis=-1, keepdims=True))
        weights = raised / jnp.sum(raised, axis=-1, keepdims=True)
        weights_low = weights.astype(jnp.bfloat16)
        att_ref[here, lanes] = matmul(weights_low, values).astype(jnp.bfloat16)
        weight_grad = lax.dot_general(
            out_grad, values, contract_cols, preferred_element_type=jnp.float32
        )
        inner = jnp.sum(weights * weight_grad, axis=-1, keepdims=True)
        score_grad = (weights * (weight_grad - inner) * scale).astype(jnp.bfloat16)
        query_grad = matmul(score_grad, keys)
        swapped = jnp.concatenate(
            [query_grad[:, HEAD_DIM // 2 :], query_grad[:, : HEAD_DIM // 2]], axis=1
        )
        q_grad_ref[here, lanes] = (query_grad * cosine - swapped * sine_part).astype(jnp.bfloat16)
        key_grad = lax.dot_general(
            score_grad, query, contract_rows, preferred_element_type=jnp.float32
        )
        value_grad = lax.dot_general(
            weights_low, out_grad, contract_rows, preferred_element_type=jnp.float32
        )
        kv_before_grad_ref[here, lanes] = key_grad[:rows].astype(jnp.bfloat16)
        kv_before_grad_ref[here, value_lanes] = value_grad[:rows].astype(jnp.bfloat16)
        kv_grad_ref[here, lanes] = key_grad[rows:]
        kv_grad_ref[here, value_lanes] = value_grad[rows:]


def backward_kernel(
    length_ref,
    cos_ref,
    sin_ref,
    q_ref,
    k_ref,
    v_ref,
    out_grad_ref,
    normed_ref,
    grad_all_ref,
    hidden_ref,
    w_out_ref,
    w_down_ref,
    attn_columns_ref,
    x_ref,
    gain_ref,
    down_own,
    up_term_ref,
    full3_ref,
    history_ref,
    key_before_ref,
    full_ref,
    down_all_ref,
    up_all_ref,
    inner_columns,
    quarter_ref,
    branch_ref,
    gain_grad_ref,
    attn_parts_ref,
    arrived_ref,
    big,
    att,
    q_grad,
    kv_grad,
    kv_before,
    kv_before_grad,
    kv_after,
    out_buf,
    side,
    chip,
    from_x,
    from_y,
    last,
    line_own,
    line_ends,
    line_held,
    up_sum,
    up_own,
    stream_own,
    back_buf,
    x_buf,
    stage,
    scatter_send,
    scatter_recv,
    sum_send,
    sum_recv,
    load_sem,
    spread_send,
    spread_recv,
    spread_local,
    key_send,
    key_recv,
    swap_send,
    swap_recv,
    local_sem,
    inner_sem,
    *,
    micro_count,
    sequence_length,
):
    column = lax.axis_index("dp")
    plane = lax.axis_index("hist")
    total, width = q_ref.shape
    rows, features = total // 8, w_down_ref.shape[1]
    ff_share = w_down_ref.shape[0]
    quarter = features // 8 // 4
    v_grad = kv_before.at[:, pl.ds(0, width)]
    k_grad = kv_before.at[:, pl.ds(width, width)]
    attn_sum = up_sum
    tile = 512

    barrier = pltpu.get_barrier_semaphore()
    for mask in range(1, 8):
        pl.semaphore_signal(
            barrier, inc=1, device_id={"dp": partner(column, mask)}, device_id_type=DEVICE_MESH
        )
    for place in range(4):

        @pl.when(plane == place)
        def _():
            for p in range(4):
                if p != place:
                    pl.semaphore_signal(
                        barrier, inc=1, device_id=z_place(p), device_id_type=DEVICE_MESH
                    )

    pl.semaphore_wait(barrier, 10)

    def value_copy(place):
        return pltpu.make_async_remote_copy(
            src_ref=v_ref,
            dst_ref=kv_before.at[:, pl.ds(width, width)],
            send_sem=key_send.at[1],
            recv_sem=key_recv.at[1],
            device_id=z_place(place + 1),
            device_id_type=DEVICE_MESH,
        )

    for place in range(3):

        @pl.when(plane == place)
        def _():
            value_copy(place).start()

    def back_copy(place):
        return pltpu.make_async_remote_copy(
            src_ref=kv_before_grad,
            dst_ref=kv_after,
            send_sem=key_send.at[0],
            recv_sem=key_recv.at[0],
            device_id=z_place(place - 1),
            device_id_type=DEVICE_MESH,
        )

    def clear(target):
        step = 64

        def some_rows(r, carry):
            target[pl.ds(pl.multiple_of(r * step, step), step), :] = jnp.zeros(
                (step, target.shape[1]), jnp.bfloat16
            )
            return carry

        lax.fori_loop(0, target.shape[0] // step, some_rows, 0)

    line_sums = [
        LineSum(
            plane,
            parts,
            arrived_ref.at[pl.ds(6 * i, 6)],
            line_own,
            line_ends,
            line_held,
            sum_send.at[i],
            sum_recv.at[i],
            load_sem,
            4 * quarter,
            0,
        )
        for i, parts in enumerate((up_term_ref, attn_parts_ref))
    ]
    up_line, attn_line = line_sums

    def spread(index, own, slot):
        return LineGather(
            plane, own, slot, spread_send.at[index], spread_recv.at[index], spread_local.at[index]
        )

    def stream_spread(item):
        return spread(
            item,
            stream_own.at[item - 1],
            lambda p: full_ref.at[pl.ds(((item - 1) * 4 + p) * rows, rows)],
        )

    def norm_back(item, back):
        load = pltpu.make_async_copy(x_ref.at[item], x_buf, local_sem.at[0])
        load.start()
        load.wait()
        norm_rows_back(
            x_buf, back, gain_ref, gain_grad_ref, item, None, stream_own.at[item - 1]
        )

    def scatter_of(product, index):
        return PlaneScatterSteps(
            column,
            product,
            (out_buf, side, chip)
            + tuple(arriving.at[pl.ds(2 * (index % 2), 2)] for arriving in (from_x, from_y, last)),
            scatter_send.at[index],
            scatter_recv.at[index],
        )

    def projection_product(stream, grad):
        def product(owner, target):
            left = pl.ds(pl.multiple_of(owner * rows, 16), rows)

            def one_tile(t, carry):
                lanes = pl.ds(pl.multiple_of(t * tile, tile), tile)
                target[:, lanes] = lax.dot_general(
                    grad[left, :],
                    attn_columns_ref[stream, lanes, :],
                    contract_cols,
                    preferred_element_type=jnp.float32,
                ).astype(jnp.bfloat16)
                return carry

            lax.fori_loop(0, features // tile, one_tile, 0)

        return product

    def branch_product(owner, target):
        left = pl.ds(pl.multiple_of(owner * rows, 16), rows)

        def one_tile(t, carry):
            lanes = pl.ds(pl.multiple_of(t * tile, tile), tile)
            target[:, lanes] = (
                matmul(att[left, :], w_out_ref[:, lanes])
                + matmul(hidden_ref[left, :], w_down_ref[:, lanes])
            ).astype(jnp.bfloat16)
            return carry

        lax.fori_loop(0, features // tile, one_tile, 0)

    def attend(first, count):
        def one_column(m, carry):
            attend_column(
                m,
                plane,
                length_ref,
                cos_ref[...],
                sin_ref[...],
                q_ref,
                k_ref,
                v_ref,
                kv_before,
                out_grad_ref,
                att,
                q_grad,
                kv_grad,
                kv_before_grad,
                rows,
                micro_count,
                sequence_length,
            )
            return carry

        lax.fori_loop(first, first + count, one_column, 0)

    step_rows = rows // 2

    def inner_loads(item, i):
        source = full3_ref if item == 0 else full_ref
        first = 0 if item == 0 else (item - 1) * 4 * rows
        base = (i % 2) * 5 * step_rows
        copies = [
            pltpu.make_async_copy(
                source.at[pl.ds(first + i * step_rows, step_rows)],
                big.at[pl.ds(base + 4 * step_rows, step_rows)],
                inner_sem.at[(i % 2) * 5 + 4],
            )
        ] + [
            pltpu.make_async_copy(
                history_ref.at[pl.ds(slot * 4 * rows + i * step_rows, step_rows)],
                big.at[pl.ds(base + slot * step_rows, step_rows)],
                inner_sem.at[(i % 2) * 5 + slot],
            )
            for slot in range(4)
        ]
        for copy in copies:
            copy.start()
        return copies

    def inner_products(item):
        loads = [inner_loads(item, 0)]
        for i in range(8):
            if i + 1 < 8:
                loads.append(inner_loads(item, i + 1))
            for copy in loads[i]:
                copy.wait()
            base = (i % 2) * 5 * step_rows

            def some_rows(r, carry):
                grad = big[
                    pl.ds(pl.multiple_of(base + 4 * step_rows + r * 16, 16), 16), :
                ].astype(jnp.float32)
                for slot in range(4):
                    values = big[
                        pl.ds(pl.multiple_of(base + slot * step_rows + r * 16, 16), 16), :
                    ].astype(jnp.float32)
                    one = item * 4 + slot
                    inner_columns[
                        pl.ds(pl.multiple_of(i * step_rows + r * 16, 16), 16), one : one + 1
                    ] = jnp.sum(grad * values, axis=-1, keepdims=True)
                return carry

            lax.fori_loop(0, step_rows // 16, some_rows, 0)

    def part_copies(first_row):
        return [
            pltpu.make_async_copy(
                stage.at[pl.ds(p * quarter, quarter)],
                attn_parts_ref.at[pl.ds(p * 4 * quarter + first_row, quarter)],
                local_sem.at[4 + p],
            )
            for p in range(4)
        ]

    def load_big(source):
        copy = pltpu.make_async_copy(source, big, local_sem.at[2])
        copy.start()
        return copy

    def attn_term(stream, grad):
        def one_owner(d, carry):
            lanes = pl.ds(pl.multiple_of(d * width, width), width)
            stage[:, lanes] = lax.dot_general(
                big[:, lanes], grad[...], contract_rows, preferred_element_type=jnp.float32
            ).astype(jnp.bfloat16)
            return carry

        lax.fori_loop(0, 8, one_owner, 0)
        copies = part_copies(stream * quarter)
        for copy in copies:
            copy.start()
        return copies

    def out_term():
        def one_tile(t, carry):
            lanes = pl.ds(pl.multiple_of(t * tile, tile), tile)
            stage[:, lanes] = lax.dot_general(
                att[...], big[:, lanes], contract_rows, preferred_element_type=jnp.float32
            ).astype(jnp.bfloat16)
            return carry

        lax.fori_loop(0, features // tile, one_tile, 0)
        copies = part_copies(3 * quarter)
        for copy in copies:
            copy.start()
        return copies

    def swap(kind):
        copies = []
        for mask in (6, 7, 2, 3, 4, 5, 1):
            owner = partner(column, mask)
            if kind == 0:
                source, target = up_piece(owner), up_target()
            else:
                source, target = attn_piece(owner), attn_target()
            copies.append(
                push(
                    source,
                    target,
                    swap_send.at[8 * kind + mask],
                    swap_recv.at[8 * kind + mask],
                    owner,
                )
            )
        if kind == 0:
            source, target = up_piece(column), up_target()
        else:
            source, target = attn_piece(column), attn_target()
        local = pltpu.make_async_copy(source, target, local_sem.at[3])
        local.start()
        return copies, local

    def up_piece(owner):
        return up_sum.at[
            pl.ds(pl.multiple_of(lax.rem(owner, 4) * quarter, 16), quarter),
            pl.ds(pl.multiple_of(lax.div(owner, 4) * ff_share, 128), ff_share),
        ]

    def up_target():
        return up_own.at[:, pl.ds(pl.multiple_of(column * ff_share, 128), ff_share)]

    def attn_piece(owner):
        return attn_sum.at[
            pl.ds(0, 3 * quarter), pl.ds(pl.multiple_of(owner * width, 128), width)
        ]

    def attn_target():
        return quarter_ref.at[
            pl.ds(0, 3 * quarter), pl.ds(pl.multiple_of(column * width, 128), width)
        ]

    def swapped_in(swapping):
        copies, local = swapping
        for copy in copies:
            copy.wait_recv()
        local.wait()
        for copy in copies:
            copy.wait_send()

    up_line.start()
    down_spread = spread(4, down_own, lambda p: down_all_ref.at[pl.ds(p * 4 * quarter, 4 * quarter)])
    down_spread.service(0)

    @pl.when(plane == 0)
    def _():
        clear(kv_before)
        clear(line_ends.at[0])

    @pl.when(plane > 0)
    def _():
        load = pltpu.make_async_copy(
            key_before_ref, kv_before.at[:, pl.ds(0, width)], local_sem.at[0]
        )
        load.start()
        load.wait()

    @pl.when(plane == 3)
    def _():
        clear(kv_after)
        clear(line_ends.at[1])

    def key_value(m, carry):
        here = pl.ds(pl.multiple_of(m * rows, 16), rows)
        for head in range(width // HEAD_DIM):
            lanes = slice(head * HEAD_DIM, (head + 1) * HEAD_DIM)
            value_lanes = slice(width + head * HEAD_DIM, width + (head + 1) * HEAD_DIM)
            grad = kv_grad[here, lanes] + kv_after[here, lanes].astype(jnp.float32)
            turned_half = jnp.concatenate(
                [grad[:, HEAD_DIM // 2 :], grad[:, : HEAD_DIM // 2]], axis=1
            )
            k_grad[here, lanes] = (grad * cos_ref[...] - turned_half * sin_ref[...]).astype(
                jnp.bfloat16
            )
            v_grad[here, lanes] = (
                kv_grad[here, value_lanes] + kv_after[here, value_lanes].astype(jnp.float32)
            ).astype(jnp.bfloat16)
        return carry

    for place in range(1, 4):

        @pl.when(plane == place)
        def _():
            value_copy(place - 1).wait_recv()

    attend(0, 8)
    for place in range(1, 4):

        @pl.when(plane == place)
        def _():
            back_copy(place).start()

    loading = load_big(grad_all_ref)
    query_scatter = scatter_of(projection_product(0, q_grad), 0)
    query_scatter.block(0)
    query_scatter.block(1)
    query_scatter.block(2)
    query_scatter.block(3)
    up_line.service(0)
    query_scatter.turn()
    loading.wait()
    parts_out = out_term()
    query_scatter.finish(back_buf)
    norm_back(1, back_buf)
    query_spread = stream_spread(1)
    query_spread.service(0)
    down_spread.service(1)
    up_line.service(1)
    for copy in parts_out:
        copy.wait()
    loading = load_big(normed_ref.at[0])

    for place in range(3):

        @pl.when(plane == place)
        def _():
            back_copy(place + 1).wait_recv()

    lax.fori_loop(0, 8, key_value, 0)
    key_scatter = scatter_of(projection_product(1, k_grad), 1)
    key_scatter.block(0)
    key_scatter.block(1)
    key_scatter.block(2)
    key_scatter.block(3)
    down_spread.service(2)
    loading.wait()
    parts_out = attn_term(0, q_grad)
    key_scatter.turn()
    key_scatter.finish(back_buf)
    norm_back(2, back_buf)
    key_spread = stream_spread(2)
    key_spread.service(0)
    up_line.service(2)
    up_line.finish(up_sum)
    up_swap = swap(0)
    for copy in parts_out:
        copy.wait()
    loading = load_big(normed_ref.at[1])
    value_scatter = scatter_of(projection_product(2, v_grad), 2)
    value_scatter.block(0)
    value_scatter.block(1)
    value_scatter.block(2)
    value_scatter.block(3)
    down_spread.service(3)
    query_spread.service(1)
    loading.wait()
    parts_out = attn_term(1, k_grad)
    value_scatter.turn()
    swapped_in(up_swap)
    up_spread = spread(5, up_own, lambda p: up_all_ref.at[pl.ds(p * quarter, quarter)])
    up_spread.service(0)
    value_scatter.finish(back_buf)
    norm_back(3, back_buf)
    value_spread = stream_spread(3)
    for copy in parts_out:
        copy.wait()
    loading = load_big(normed_ref.at[2])
    loading.wait()
    parts_out = attn_term(2, v_grad)
    for copy in parts_out:
        copy.wait()
    attn_line.start()
    value_spread.service(0)
    query_spread.service(2)
    branch_scatter = scatter_of(branch_product, 3)
    branch_scatter.block(0)
    branch_scatter.block(1)
    key_spread.service(1)
    branch_scatter.block(2)
    branch_scatter.block(3)
    up_spread.service(1)
    query_spread.service(3)
    branch_scatter.turn()
    branch_scatter.finish(branch_ref)
    attn_line.service(0)
    key_spread.service(2)
    up_spread.service(2)
    value_spread.service(1)
    attn_line.service(1)
    key_spread.service(3)
    query_spread.placed()
    inner_products(0)
    inner_products(1)
    up_spread.service(3)
    attn_line.service(2)
    attn_line.finish(attn_sum)
    attn_swap = swap(1)
    quarter_ref[pl.ds(3 * quarter, quarter), :] = attn_sum[pl.ds(3 * quarter, quarter), :]
    value_spread.service(2)
    key_spread.placed()
    inner_products(2)
    down_spread.placed()
    up_spread.placed()
    swapped_in(attn_swap)
    value_spread.service(3)
    value_spread.placed()

    for spreading in (
        down_spread,
        query_spread,
        up_spread,
        key_spread,
        value_spread,
    ):
        spreading.finish()
    for place in range(3):

        @pl.when(plane == place)
        def _():
            value_copy(place).wait_send()

    for place in range(1, 4):

        @pl.when(plane == place)
        def _():
            back_copy(place).wait_send()


def attend_and_back(
    lengths_all,
    cosine,
    sine_part,
    q,
    k,
    v,
    out_grad,
    normed_all,
    grad_all,
    hidden,
    w_out,
    w_down,
    attn_columns,
    x_ordered,
    gains,
    down_own,
    up_term,
    full3,
    history,
    key_before,
    micro_count,
    sequence_length,
):
    total, width = q.shape
    rows, features = total // 8, w_down.shape[1]
    ff_share = w_down.shape[0]
    quarter = features // 32
    block = (rows, features)
    piece = (4 * quarter, features)
    half = (4, rows // 2, features)
    anywhere = pl.BlockSpec(memory_space=pl.ANY)
    near = pl.BlockSpec(memory_space=pltpu.VMEM)
    shape = jax.ShapeDtypeStruct
    low_type = jnp.bfloat16
    some = lambda *dims: pltpu.VMEM(dims, low_type)
    dma = pltpu.SemaphoreType.DMA
    return pl.pallas_call(
        functools.partial(
            backward_kernel, micro_count=micro_count, sequence_length=sequence_length
        ),
        in_specs=[pl.BlockSpec(memory_space=pltpu.SMEM)]
        + [near] * 6
        + [anywhere, anywhere]
        + [near] * 4
        + [anywhere]
        + [near] * 2
        + [anywhere] * 4,
        out_specs=[anywhere] * 3 + [near, near, near, near, anywhere, anywhere],
        out_shape=[
            shape((12 * rows, features), low_type),
            shape((ff_share, features), low_type),
            shape((4 * quarter, 8 * ff_share), low_type),
            shape((4 * rows, 128), jnp.float32),
            shape(piece, low_type),
            shape(block, low_type),
            shape((8, features), jnp.float32),
            shape((16 * quarter, features), low_type),
            shape((12,) + piece, low_type),
        ],
        scratch_shapes=[
            some(total, features),
            some(total, width),
            some(total, width),
            pltpu.VMEM((total, 2 * width), jnp.float32),
            some(total, 2 * width),
            some(total, 2 * width),
            some(total, 2 * width),
            some(2, *block),
            some(4, *block),
            some(4, *block),
            some(*half),
            some(*half),
            some(*half),
            some(*piece),
            some(2, *piece),
            some(3, *piece),
            some(*piece),
            some(quarter, 8 * ff_share),
            some(3, *block),
            some(*block),
            pltpu.VMEM(block, jnp.float32),
            some(*piece),
            dma((4, 10)),
            dma((4, 10)),
            dma((3, 6)),
            dma((3, 6)),
            dma((2,)),
            dma((6, 6)),
            dma((6, 6)),
            dma((6,)),
            dma((3,)),
            dma((3,)),
            dma((16,)),
            dma((16,)),
            dma((8,)),
            dma((10,)),
        ],
        compiler_params=pltpu.CompilerParams(
            collective_id=6, has_side_effects=True, vmem_limit_bytes=63 * 1024 * 1024
        ),
        cost_estimate=pl.CostEstimate(
            flops=20 * total * features * width,
            bytes_accessed=1000 * 1000 * 1000,
            transcendentals=0,
        ),
    )(
        lengths_all,
        cosine,
        sine_part,
        q,
        k,
        v,
        out_grad,
        normed_all,
        grad_all,
        hidden,
        w_out,
        w_down,
        attn_columns,
        x_ordered,
        gains,
        down_own,
        up_term,
        full3,
        history,
        key_before,
    )


def last_products_kernel(
    columns_ref,
    full_ref,
    history_ref,
    inner_ref,
    inner_columns,
    big,
    inner_sem,
    share_send,
    share_recv,
):
    plane = lax.axis_index("hist")
    inner_columns[...] = columns_ref[...]

    def barrier_line(plane):
        barrier = pltpu.get_barrier_semaphore()
        for place in range(4):

            @pl.when(plane == place)
            def _():
                for p in range(4):
                    if p != place:
                        pl.semaphore_signal(
                            barrier, inc=1, device_id=z_place(p), device_id_type=DEVICE_MESH
                        )

        pl.semaphore_wait(barrier, 3)

    rows = full_ref.shape[0] // 12
    step_rows = rows // 2

    def inner_loads(item, i):
        source = full_ref
        first = (item - 1) * 4 * rows
        base = (i % 2) * 5 * step_rows
        copies = [
            pltpu.make_async_copy(
                source.at[pl.ds(first + i * step_rows, step_rows)],
                big.at[pl.ds(base + 4 * step_rows, step_rows)],
                inner_sem.at[(i % 2) * 5 + 4],
            )
        ] + [
            pltpu.make_async_copy(
                history_ref.at[pl.ds(slot * 4 * rows + i * step_rows, step_rows)],
                big.at[pl.ds(base + slot * step_rows, step_rows)],
                inner_sem.at[(i % 2) * 5 + slot],
            )
            for slot in range(4)
        ]
        for copy in copies:
            copy.start()
        return copies

    def inner_products(item):
        loads = [inner_loads(item, 0)]
        for i in range(8):
            if i + 1 < 8:
                loads.append(inner_loads(item, i + 1))
            for copy in loads[i]:
                copy.wait()
            base = (i % 2) * 5 * step_rows

            def some_rows(r, carry):
                grad = big[
                    pl.ds(pl.multiple_of(base + 4 * step_rows + r * 16, 16), 16), :
                ].astype(jnp.float32)
                for slot in range(4):
                    values = big[
                        pl.ds(pl.multiple_of(base + slot * step_rows + r * 16, 16), 16), :
                    ].astype(jnp.float32)
                    one = item * 4 + slot
                    inner_columns[
                        pl.ds(pl.multiple_of(i * step_rows + r * 16, 16), 16), one : one + 1
                    ] = jnp.sum(grad * values, axis=-1, keepdims=True)
                return carry

            lax.fori_loop(0, step_rows // 16, some_rows, 0)

    barrier_line(plane)
    inner_products(3)

    def share_copy(source_place, target_place):
        return pltpu.make_async_remote_copy(
            src_ref=inner_ref.at[source_place],
            dst_ref=inner_ref.at[source_place],
            send_sem=share_send.at[target_place],
            recv_sem=share_recv.at[source_place],
            device_id=z_place(target_place),
            device_id_type=DEVICE_MESH,
        )

    for place in range(4):

        @pl.when(plane == place)
        def _():
            others = [p for p in range(4) if p != place]
            inner_ref[place] = jnp.transpose(inner_columns[...])[:16]
            for p in others:
                share_copy(place, p).start()
            for p in others:
                share_copy(p, place).wait_recv()
            for p in others:
                share_copy(place, p).wait_send()


def last_products(columns, full, history):
    rows, features = full.shape[0] // 12, full.shape[1]
    anywhere = pl.BlockSpec(memory_space=pl.ANY)
    near = pl.BlockSpec(memory_space=pltpu.VMEM)
    dma = pltpu.SemaphoreType.DMA
    return pl.pallas_call(
        last_products_kernel,
        in_specs=[near, anywhere, anywhere],
        out_specs=near,
        out_shape=jax.ShapeDtypeStruct((4, 16, 4 * rows), jnp.float32),
        scratch_shapes=[
            pltpu.VMEM((4 * rows, 128), jnp.float32),
            pltpu.VMEM((5 * rows, features), jnp.bfloat16),
            dma((10,)),
            dma((4,)),
            dma((4,)),
        ],
        compiler_params=pltpu.CompilerParams(
            collective_id=8, has_side_effects=True, vmem_limit_bytes=56 * 1024 * 1024
        ),
        cost_estimate=pl.CostEstimate(
            flops=0, bytes_accessed=40 * 1000 * 1000, transcendentals=0
        ),
    )(columns, full, history)


def rotary_table(row_positions, head_dim):
    half_dim = head_dim // 2
    frequency = jnp.exp(
        jnp.arange(half_dim, dtype=jnp.float32) * (-2.0 * math.log(10000.0) / head_dim)
    )
    angles = row_positions.astype(jnp.float32)[:, None] * frequency[None, :]
    cosine = jnp.cos(angles)
    sine_part = jnp.sin(angles)
    return (
        jnp.concatenate([cosine, cosine], axis=-1),
        jnp.concatenate([-sine_part, sine_part], axis=-1),
    )


def shards_split(
    history,
    history_layer_index,
    lengths,
    norm_gains,
    mix_in,
    mix_out,
    w_attn,
    w_out,
    w_up,
    w_down,
    cotangent,
):
    local_slots, micro_count, sequence_length, features = history.shape
    planes = lax.axis_size("hist")
    columns = lax.axis_size("dp")
    plane = lax.axis_index("hist")
    slot_count = local_slots * planes
    all_rows = micro_count * sequence_length
    rows = all_rows // planes
    share = features // columns
    mix_width = mix_in.shape[1]
    mix_rows = mix_out.shape[0]
    low = lambda values: values.astype(jnp.bfloat16)
    order = (3, 0, 1, 2)

    spare = 128 - mix_width
    middle = jnp.concatenate(
        [
            jnp.pad(mix_out, ((0, 8 - mix_rows), (0, spare))),
            jnp.pad(low(lengths)[None, :], ((0, 7), (0, 128 - micro_count))),
        ],
        axis=0,
    )
    gain_rows = jnp.pad(norm_gains, ((0, 3), (0, 0))).reshape(8, 2, share // 2)
    pack = jnp.concatenate(
        [
            jnp.pad(mix_in, ((0, 0), (0, spare))),
            middle,
            gain_rows.transpose(1, 0, 2).reshape(16, share // 2),
        ],
        axis=0,
    )

    layer_lookup = (
        history_layer_index[:, None] == jnp.arange(slot_count, dtype=jnp.int32)[None, :]
    ).astype(jnp.float32)
    newest_output = jnp.sum(
        jnp.arange(slot_count, dtype=jnp.int32)
        * (history_layer_index == slot_count - 1).astype(jnp.int32)
    )
    root = newest_output // local_slots
    on_root = (plane == root).astype(jnp.float32)
    latest_rows = lax.dynamic_index_in_dim(
        history, newest_output % local_slots, 0, keepdims=False
    ).reshape(all_rows, features)
    latest_rows = lax.optimization_barrier(latest_rows)
    own_table = lax.dynamic_slice_in_dim(layer_lookup, plane * local_slots, local_slots, 0)
    ordered = jnp.eye(STREAM_COUNT, dtype=jnp.float32)[:, jnp.array(order)]
    select = jnp.einsum("ci,sj->cjis", ordered, own_table).reshape(
        STREAM_COUNT * slot_count, STREAM_COUNT * local_slots
    )
    select = low(jnp.pad(select, ((0, 0), (0, 128 - STREAM_COUNT * local_slots))))

    my_row = plane * rows + jnp.arange(rows, dtype=jnp.int32)
    my_position = lax.rem(my_row, sequence_length)
    my_sequence = lax.div(my_row, sequence_length)
    my_length = jnp.sum(
        jnp.where(
            my_sequence[:, None] == jnp.arange(micro_count, dtype=jnp.int32)[None, :],
            lengths[None, :],
            0,
        ),
        axis=1,
    )
    valid_rows = (my_position < my_length).astype(jnp.float32)[:, None]
    cosine, sine_part = rotary_table(my_position, HEAD_DIM)

    (
        packed,
        gains,
        pre,
        factors,
        x_ordered,
        normed_all,
        grad_all,
        hidden,
        up_term,
        down_own,
        full3,
        gain_sum3,
        attn_columns,
        q,
        k,
        v,
        out_grad,
        key_before,
        _,
        _,
        _,
        _,
    ) = forward_and_feed(
        lengths,
        pack,
        latest_rows,
        history.reshape(local_slots * all_rows, features),
        select,
        jnp.broadcast_to(on_root, (8, all_rows)),
        cotangent.reshape(rows, features),
        w_up,
        w_attn,
        w_down,
        w_out,
        cosine,
        sine_part,
        sequence_length,
    )
    lengths_all = packed[:, share + 8, :micro_count].reshape(-1).astype(jnp.int32)
    (
        full,
        down_all,
        up_all,
        inner_columns,
        attn_quarter,
        branch,
        gain_sums,
        _,
        _,
    ) = attend_and_back(
        lengths_all,
        cosine,
        sine_part,
        q,
        k,
        v,
        out_grad,
        normed_all,
        grad_all,
        hidden,
        w_out,
        w_down,
        attn_columns,
        x_ordered,
        gains,
        down_own,
        up_term,
        full3,
        history.reshape(local_slots * all_rows, features),
        key_before,
        micro_count,
        sequence_length,
    )
    attn_every = lax.all_gather(attn_quarter, "hist", axis=0, tiled=True)

    chunk = sequence_length // planes
    inverse_step = pow(micro_count, -1, planes)
    block_rows = low((x_ordered[0] + branch.astype(jnp.float32)) * valid_rows)
    block_out = jnp.zeros((micro_count, chunk, features), jnp.bfloat16)
    for i in range(micro_count):
        pairs = [(p, (micro_count * p + i) % planes) for p in range(planes)]
        piece = lax.ppermute(block_rows[i * chunk : (i + 1) * chunk], "hist", pairs)
        source = lax.rem((plane - i + planes * micro_count) * inverse_step, planes)
        which = lax.div(source * micro_count + i, planes)
        block_out = lax.dynamic_update_index_in_dim(block_out, piece, which, 0)

    inner_all = last_products(
        inner_columns, full, history.reshape(local_slots * all_rows, features)
    )
    mixer_output_wide = (
        packed[:, share : share + mix_rows, :mix_width]
        .reshape(mix_width, mix_width)
        .astype(jnp.float32)
    )
    mix_in_all = packed[:, :share, :mix_width].reshape(features, mix_width)
    tables = layer_lookup.reshape(planes, local_slots, slot_count)
    dyn_grad = jnp.einsum(
        "pist,ic,psj->tcj",
        inner_all.reshape(planes, STREAM_COUNT, local_slots, all_rows),
        ordered.T,
        tables,
        precision=highest,
    ).reshape(all_rows, STREAM_COUNT * slot_count)
    mixer_preactivation = pre[:, :mix_width]
    mix_act = jax.nn.gelu(mixer_preactivation, approximate=False)
    act_grad = precise(dyn_grad, mixer_output_wide.T)
    mix_out_grad = precise(mix_act.T, dyn_grad) * on_root
    pre_grad = act_grad * gelu_slope(mixer_preactivation)
    latest_scaled, _ = rms_scale(latest_rows.astype(jnp.float32), gains[0])
    mix_in_grad = precise(low(latest_scaled).astype(jnp.float32).T, pre_grad)
    latest_here = (plane * local_slots + jnp.arange(local_slots) == newest_output).astype(
        jnp.float32
    )
    history_grad, gain_zero = slot_grads_of(
        latest_here,
        factors,
        full3,
        full.reshape(3, all_rows, features),
        latest_rows,
        pre_grad,
        mix_in_all.astype(jnp.float32).T,
        gains,
    )
    history_grad = history_grad.reshape(history.shape)

    gain_rows = jnp.stack(
        [gain_zero[0] * on_root, gain_sums[1], gain_sums[2], gain_sums[3], gain_sum3[0]]
    )
    counts = (share * mix_width // 128, 5 * share // 128, mix_rows * mix_width // 128)
    dense = jnp.concatenate(
        [
            (mix_in_grad * on_root).reshape(columns, counts[0], 128),
            gain_rows.reshape(5, columns, share).transpose(1, 0, 2).reshape(columns, counts[1], 128),
            mix_out_grad.reshape(columns, counts[2], 128),
        ],
        axis=1,
    )
    used = sum(counts)
    small = small_sums(low(jnp.pad(dense, ((0, 0), (0, -used % 16), (0, 0)))))
    w_attn_grad, w_out_grad = lay_out(attn_every)
    return (
        block_out,
        history_grad,
        small[counts[0] : counts[0] + counts[1]].reshape(5, share),
        small[: counts[0]].reshape(share, mix_width),
        small[counts[0] + counts[1] : used].reshape(mix_rows, mix_width),
        w_attn_grad,
        w_out_grad,
        up_all.astype(jnp.float32),
        down_all.astype(jnp.float32),
    )


def splits_by_heads(mesh, micro_count, sequence_length):
    columns, planes = mesh.shape["dp"], mesh.shape["hist"]
    all_rows = micro_count * sequence_length
    rows = all_rows // planes
    return (
        columns == 8
        and planes == 4
        and HEADS % columns == 0
        and all_rows % planes == 0
        and sequence_length % planes == 0
        and rows % 64 == 0
        and math.gcd(micro_count, planes) == 1
        and all(
            (p * rows) // sequence_length * sequence_length >= (p - 1) * rows
            for p in range(planes)
        )
    )


def solution(mesh):
    placed = (
        P("hist", "dp", None, None),
        P(),
        P("dp"),
        P(None, "dp"),
        P("dp", None),
        P("dp", None),
        P(None, "dp", None),
        P("dp", None),
        P("dp", None),
        P("dp", None),
        P("dp", "hist", None),
    )
    def plan(*arrays):
        micro_count = arrays[2].shape[0]
        if splits_by_heads(mesh, micro_count, arrays[0].shape[2]):
            return shards_split(*arrays)
        return shards(*arrays)

    return jax.shard_map(
        plan,
        mesh=mesh,
        in_specs=placed,
        out_specs=(
            P("dp", "hist", None),
            P("hist", "dp", None, None),
            P(None, "dp"),
            P("dp", None),
            P("dp", None),
            P(None, "dp", None),
            P("dp", None),
            P("dp", None),
            P("dp", None),
        ),
        check_vma=False,
    )
```

```python
import functools
import math

import jax
import jax.numpy as jnp
from jax import lax
from jax.experimental import pallas as pl
from jax.experimental.pallas import tpu as pltpu
from jax.sharding import PartitionSpec as P

MODEL_WIDTH = 2048
HEADS = 16
HEAD_DIM = 128
FF = 8192
STREAM_COUNT = 4


epsilon = 1e-06
masked_out = -1e30
highest = lax.Precision.HIGHEST
contract_rows = (((0,), (0,)), ((), ()))
contract_cols = (((1,), (1,)), ((), ()))


def broadcast(value, axis, source):
    kept = jnp.where(lax.axis_index(axis) == source, value, 0).astype(value.dtype)
    return lax.psum(kept, axis)


def matmul(left_side, right_side):
    return jnp.dot(left_side, right_side, preferred_element_type=jnp.float32)


def precise(left_side, right_side):
    return jnp.dot(left_side, right_side, precision=highest, preferred_element_type=jnp.float32)


def gelu_slope(values):
    return 0.5 * (1.0 + lax.erf(values * (1.0 / math.sqrt(2.0)))) + values * jnp.exp(
        -0.5 * values * values
    ) * (1.0 / math.sqrt(2.0 * math.pi))


def rms_scale(values, gain_row):
    inverse = lax.rsqrt(jnp.mean(values * values, axis=-1, keepdims=True) + epsilon)
    return (values * inverse * gain_row, inverse)


def rms_back(values, inverse, gain_row, grad_in):
    scaled = grad_in * gain_row
    gain_grad = jnp.sum(grad_in * values * inverse, axis=0)
    inner_mean = jnp.mean(scaled * values, axis=-1, keepdims=True)
    return (inverse * scaled - values * (inverse * inverse * inverse) * inner_mean, gain_grad)


def rotate(values, positions, turn_sign):
    half_dim = values.shape[-1] // 2
    frequency = jnp.exp(
        jnp.arange(half_dim, dtype=jnp.float32) * (-2.0 * math.log(10000.0) / values.shape[-1])
    )
    angles = positions.astype(jnp.float32)[:, None] * frequency[None, :]
    cosine = jnp.cos(angles)[:, None, :]
    sine_part = jnp.sin(angles)[:, None, :] * turn_sign
    lower_half = values[..., :half_dim]
    upper_half = values[..., half_dim:]
    return jnp.concatenate(
        [
            lower_half * cosine - upper_half * sine_part,
            upper_half * cosine + lower_half * sine_part,
        ],
        axis=-1,
    )


def first_rows(weights, lefts):

    def add_piece(totals, pieces, start_at):
        return tuple(
            (matmul(left_side, piece_rows) for left_side, piece_rows in zip(lefts, pieces))
        )

    initial = tuple(
        (jnp.zeros((lefts[0].shape[0], weight.shape[1]), jnp.float32) for weight in weights)
    )
    return add_piece(
        initial,
        (
            lax.all_gather(weights[0], "dp", axis=0, tiled=True),
            lax.all_gather(weights[1], "dp", axis=0, tiled=True),
            lax.all_gather(weights[2], "dp", axis=0, tiled=True),
            lax.all_gather(weights[3], "dp", axis=0, tiled=True),
        ),
        jnp.int32(0),
    )


def second_rows(w_out, down_folded, attended_low, hidden, ratio):

    def add_piece(total_sum, pieces, start_at):
        count = pieces[0].shape[0]
        down_rows = pieces[1].reshape(count * ratio, pieces[1].shape[1] // ratio)
        return matmul(attended_low, pieces[0]) + matmul(hidden, down_rows)

    initial = jnp.zeros((attended_low.shape[0], w_out.shape[1]), jnp.float32)
    return add_piece(
        initial,
        (
            lax.all_gather(w_out, "dp", axis=0, tiled=True),
            lax.all_gather(down_folded, "dp", axis=0, tiled=True),
        ),
        jnp.int32(0),
    )


def back_first(w_out, down_folded, grad_low, ratio):

    def add_piece(totals, pieces, start_at):
        count = pieces[0].shape[0]
        out_part = lax.dot_general(
            grad_low, pieces[0], contract_cols, preferred_element_type=jnp.float32
        )
        down_rows = pieces[1].reshape(count * ratio, pieces[1].shape[1] // ratio)
        down_part = lax.dot_general(
            grad_low, down_rows, contract_cols, preferred_element_type=jnp.float32
        )
        return (out_part, down_part)

    features = w_out.shape[1]
    initial = (
        jnp.zeros((grad_low.shape[0], features), jnp.float32),
        jnp.zeros((grad_low.shape[0], features * ratio), jnp.float32),
    )
    return add_piece(
        initial,
        (
            lax.all_gather(w_out, "dp", axis=0, tiled=True),
            lax.all_gather(down_folded, "dp", axis=0, tiled=True),
        ),
        jnp.int32(0),
    )


def back_second(weights, rights):

    def add_piece(totals, pieces, start_at):
        return tuple(
            (
                lax.dot_general(
                    right_side, piece_rows, contract_cols, preferred_element_type=jnp.float32
                )
                for right_side, piece_rows in zip(rights, pieces)
            )
        )

    features = weights[1].shape[1]
    initial = tuple((jnp.zeros((rights[0].shape[0], features), jnp.float32) for weight in weights))
    return add_piece(
        initial,
        (
            lax.all_gather(weights[0], "dp", axis=0, tiled=True),
            lax.all_gather(weights[1], "dp", axis=0, tiled=True),
            lax.all_gather(weights[2], "dp", axis=0, tiled=True),
            lax.all_gather(weights[3], "dp", axis=0, tiled=True),
        ),
        jnp.int32(0),
    )


def mix_forward(values_low, gain_row, mix_in_all, mixer_output_wide):
    values = values_low.astype(jnp.float32)
    scaled, inverse = rms_scale(values, gain_row)
    normed_mix = scaled.astype(jnp.bfloat16)
    mixer_preactivation = matmul(normed_mix, mix_in_all)
    mix_act = jax.nn.gelu(mixer_preactivation, approximate=False)
    return (
        precise(mix_act, mixer_output_wide),
        (values, inverse, normed_mix, mixer_preactivation, mix_act),
    )


def mix_backward(kept_mix, act_grad, gain_row, mix_in_all):
    values, inverse, normed_mix, mixer_preactivation, mix_act = kept_mix
    pre_grad = act_grad * gelu_slope(mixer_preactivation)
    in_grad = precise(normed_mix.astype(jnp.float32).T, pre_grad)
    normed_grad = precise(pre_grad, mix_in_all.astype(jnp.float32).T)
    latest_grad, gain_grad = rms_back(values, inverse, gain_row, normed_grad)
    return (latest_grad, gain_grad, in_grad)


def shards(
    history,
    history_layer_index,
    lengths,
    norm_gains,
    mix_in,
    mix_out,
    w_attn,
    w_out,
    w_up,
    w_down,
    cotangent,
):
    local_slots, micro_count, sequence_length, features = history.shape
    hist_count = lax.axis_size("hist")
    dp_count = lax.axis_size("dp")
    hist_place = lax.axis_index("hist")
    slot_count = local_slots * hist_count
    ratio = FF // MODEL_WIDTH
    gains_all, mix_in_all, mix_out_all = (
        lax.all_gather(norm_gains, "dp", axis=1, tiled=True),
        lax.all_gather(mix_in, "dp", axis=0, tiled=True),
        lax.all_gather(mix_out, "dp", axis=0, tiled=True),
    )
    gains_all = gains_all.astype(jnp.float32)
    mixer_output_wide = mix_out_all.astype(jnp.float32)
    mix_width = mixer_output_wide.shape[0]
    layer_lookup = (
        history_layer_index[:, None] == jnp.arange(slot_count, dtype=jnp.int32)[None, :]
    ).astype(jnp.float32)
    newest_output = jnp.sum(
        jnp.arange(slot_count, dtype=jnp.int32)
        * (history_layer_index == slot_count - 1).astype(jnp.int32)
    )
    down_folded = w_down.reshape(w_down.shape[0] // ratio, ratio * w_down.shape[1])
    quarter = cotangent.shape[1]
    own_rows = micro_count * quarter
    positions = hist_place * quarter + jnp.arange(quarter, dtype=jnp.int32)
    valid_rows = (positions[None, :] < lengths[:, None]).astype(jnp.float32).reshape(own_rows, 1)
    root = newest_output // local_slots
    latest_local = lax.dynamic_index_in_dim(history, newest_output % local_slots, 0, keepdims=False)
    latest_rows = broadcast(latest_local, "hist", root)
    dynamic_weights, kept_mix = mix_forward(
        latest_rows.reshape(micro_count * sequence_length, features),
        gains_all[0],
        mix_in_all,
        mixer_output_wide,
    )
    dynamic_weights = dynamic_weights.reshape(
        micro_count, sequence_length, STREAM_COUNT, slot_count
    )
    own_table = lax.dynamic_slice_in_dim(layer_lookup, hist_place * local_slots, local_slots, 0)
    depth_combination_factors = jnp.einsum(
        "mtcj,sj->scmt", dynamic_weights, own_table, precision=highest
    )
    partial_sums = jnp.zeros((STREAM_COUNT, micro_count, sequence_length, features), jnp.float32)
    for depth_position_number in range(local_slots):
        partial_sums = (
            partial_sums
            + depth_combination_factors[depth_position_number][..., None]
            * history[depth_position_number].astype(jnp.float32)[None]
        )
    blended_residual_inputs = lax.psum_scatter(
        partial_sums, "hist", scatter_dimension=2, tiled=True
    )
    stream_rows = blended_residual_inputs.reshape(STREAM_COUNT, own_rows, features)
    normed = []
    inverses = []
    for stream_idx in range(STREAM_COUNT):
        scaled, inverse = rms_scale(stream_rows[stream_idx], gains_all[stream_idx + 1])
        normed.append(scaled.astype(jnp.bfloat16))
        inverses.append(inverse)
    head_shape = (micro_count, quarter, HEADS, HEAD_DIM)
    query_pre, key_pre, value_pre, up_pre = first_rows(
        (w_attn[0], w_attn[1], w_attn[2], w_up), (normed[0], normed[1], normed[2], normed[3])
    )
    attention_asker_vectors = rotate(query_pre.reshape(head_shape), positions, 1.0).astype(
        jnp.bfloat16
    )
    keys_rot = rotate(key_pre.reshape(head_shape), positions, 1.0).astype(jnp.bfloat16)
    values_low = value_pre.astype(jnp.bfloat16)
    keys_all, values_all = (
        lax.all_gather(
            keys_rot.reshape(micro_count, quarter, features), "hist", axis=1, tiled=True
        ),
        lax.all_gather(
            values_low.reshape(micro_count, quarter, features), "hist", axis=1, tiled=True
        ),
    )
    key_heads = keys_all.reshape(micro_count, sequence_length, HEADS, HEAD_DIM)
    value_wide = values_all.reshape(micro_count, sequence_length, HEADS, HEAD_DIM).astype(
        jnp.float32
    )
    score_scale = 1.0 / math.sqrt(HEAD_DIM)
    scores = (
        jnp.einsum(
            "mqhd,mkhd->mhqk",
            attention_asker_vectors,
            key_heads,
            preferred_element_type=jnp.float32,
        )
        * score_scale
    )
    key_positions = jnp.arange(sequence_length, dtype=jnp.int32)
    allowed = (key_positions[None, None, :] <= positions[None, :, None]) & (
        key_positions[None, None, :] < lengths[:, None, None]
    )
    scores = jnp.where(allowed[:, None], scores, masked_out)
    row_top = jnp.max(scores, axis=-1, keepdims=True)
    raised = jnp.exp(scores - row_top)
    soft_weights = raised / jnp.sum(raised, axis=-1, keepdims=True)
    attended = jnp.einsum("mhqk,mkhd->mqhd", soft_weights, value_wide, precision=highest)
    attended_low = attended.reshape(own_rows, features).astype(jnp.bfloat16)
    hidden = jax.nn.gelu(up_pre, approximate=False).astype(jnp.bfloat16)
    branch = second_rows(w_out, down_folded, attended_low, hidden, ratio)
    block_out = (
        ((stream_rows[3] + branch) * valid_rows)
        .astype(jnp.bfloat16)
        .reshape(micro_count, quarter, features)
    )
    grad_rows = cotangent.reshape(own_rows, features).astype(jnp.float32) * valid_rows
    grad_low = grad_rows.astype(jnp.bfloat16)
    attended_back, hidden_grad = back_first(w_out, down_folded, grad_low, ratio)
    up_grad = (hidden_grad * gelu_slope(up_pre)).astype(jnp.bfloat16)
    attended_grad = attended_back.astype(jnp.bfloat16)
    attended_wide = attended_grad.astype(jnp.float32).reshape(head_shape)
    prob_grad = jnp.einsum("mqhd,mkhd->mhqk", attended_wide, value_wide, precision=highest)
    inner_rows = jnp.sum(attended_wide * attended, axis=-1)
    logit_derivative = (
        soft_weights * (prob_grad - jnp.transpose(inner_rows, (0, 2, 1))[..., None]) * score_scale
    )
    query_grad = jnp.einsum(
        "mhqk,mkhd->mqhd", logit_derivative, key_heads.astype(jnp.float32), precision=highest
    )
    key_grad_all = jnp.einsum(
        "mhqk,mqhd->mkhd",
        logit_derivative,
        attention_asker_vectors.astype(jnp.float32),
        precision=highest,
    )
    value_grad_all = jnp.einsum("mhqk,mqhd->mkhd", soft_weights, attended_wide, precision=highest)
    key_grad, value_grad = (
        lax.psum_scatter(
            key_grad_all.reshape(micro_count, sequence_length, features).astype(jnp.bfloat16),
            "hist",
            scatter_dimension=1,
            tiled=True,
        ).astype(jnp.float32),
        lax.psum_scatter(
            value_grad_all.reshape(micro_count, sequence_length, features).astype(jnp.bfloat16),
            "hist",
            scatter_dimension=1,
            tiled=True,
        ).astype(jnp.float32),
    )
    projection_grads = [
        rotate(query_grad, positions, -1.0).reshape(own_rows, features).astype(jnp.bfloat16),
        rotate(key_grad.reshape(head_shape), positions, -1.0)
        .reshape(own_rows, features)
        .astype(jnp.bfloat16),
        value_grad.reshape(own_rows, features).astype(jnp.bfloat16),
    ]
    resid_normed_grad, query_normed_grad, key_normed_grad, value_normed_grad = back_second(
        (w_up, w_attn[0], w_attn[1], w_attn[2]),
        (up_grad, projection_grads[0], projection_grads[1], projection_grads[2]),
    )
    normed_grads = [query_normed_grad, key_normed_grad, value_normed_grad]
    stream_grads = []
    gain_grads = []
    for stream_idx in range(3):
        stream_grad, gain_grad = rms_back(
            stream_rows[stream_idx],
            inverses[stream_idx],
            gains_all[stream_idx + 1],
            normed_grads[stream_idx],
        )
        stream_grads.append(stream_grad)
        gain_grads.append(gain_grad)
    resid_grad, skip_scaling_derivative = rms_back(
        stream_rows[3], inverses[3], gains_all[4], resid_normed_grad
    )
    stream_grads.append(resid_grad + grad_rows)
    gain_grads.append(skip_scaling_derivative)
    stream_grads_all = jnp.stack(stream_grads).reshape(STREAM_COUNT, micro_count, quarter, features)
    full_grads = lax.all_gather(
        stream_grads_all.astype(jnp.bfloat16), "hist", axis=2, tiled=True
    ).astype(stream_grads_all.dtype)
    slot_grads = []
    dyn_grad = jnp.zeros((micro_count, sequence_length, STREAM_COUNT, slot_count), jnp.float32)
    for depth_position_number in range(local_slots):
        rows_now = history[depth_position_number].astype(jnp.float32)
        slot_grads.append(
            jnp.sum(
                depth_combination_factors[depth_position_number][..., None] * full_grads, axis=0
            )
        )
        inner_now = jnp.sum(full_grads * rows_now[None], axis=-1)
        dyn_grad = dyn_grad + jnp.einsum("cmt,j->mtcj", inner_now, own_table[depth_position_number])
    dyn_grad = dyn_grad.reshape(micro_count * sequence_length, STREAM_COUNT * slot_count)
    act_part = precise(dyn_grad, mixer_output_wide.T)
    mix_out_grad = precise(kept_mix[4].T, dyn_grad)
    act_grad = lax.psum(act_part.astype(jnp.bfloat16), "hist").astype(jnp.float32)
    on_root = (hist_place == root).astype(jnp.float32)
    latest_grad, gain_zero, mix_in_grad = mix_backward(kept_mix, act_grad, gains_all[0], mix_in_all)
    gain_zero = gain_zero * on_root
    mix_in_grad = mix_in_grad * on_root
    latest_grad = latest_grad.reshape(micro_count, sequence_length, features)
    marked = []
    for depth_position_number in range(local_slots):
        is_latest = (hist_place * local_slots + depth_position_number == newest_output).astype(
            jnp.float32
        )
        marked.append(slot_grads[depth_position_number] + latest_grad * is_latest)
    history_grad = jnp.stack(marked).astype(jnp.bfloat16)
    gains_grad_full = jnp.stack(
        [gain_zero, gain_grads[0], gain_grads[1], gain_grads[2], gain_grads[3]]
    )
    share_rows = w_out.shape[0]
    per_device = mix_width // dp_count
    mix_out_padded = jnp.pad(
        mix_out_grad.reshape(dp_count, per_device, mix_width),
        ((0, 0), (0, share_rows - per_device), (0, 0)),
    ).reshape(dp_count * share_rows, mix_width)
    small_wide = jnp.concatenate([mix_in_grad, gains_grad_full.T, mix_out_padded], axis=1)
    attn_lefts = (normed[0], normed[1], normed[2], attended_low)
    attn_rights = (projection_grads[0], projection_grads[1], projection_grads[2], grad_low)
    attn_share = lax.psum_scatter(
        jnp.concatenate(
            [
                lax.dot_general(
                    left_side, right_side, contract_rows, preferred_element_type=jnp.float32
                )
                for left_side, right_side in zip(attn_lefts, attn_rights)
            ],
            axis=1,
        ).astype(jnp.bfloat16),
        "dp",
        scatter_dimension=0,
        tiled=True,
    )
    up_term = lax.dot_general(normed[3], up_grad, contract_rows, preferred_element_type=jnp.float32)
    down_term = lax.dot_general(
        hidden, grad_low, contract_rows, preferred_element_type=jnp.float32
    ).reshape(share_rows * lax.axis_size("dp"), ratio * features)
    ffn_share = lax.psum_scatter(
        jnp.concatenate([up_term, down_term, small_wide], axis=1).astype(jnp.bfloat16),
        "dp",
        scatter_dimension=0,
        tiled=True,
    )
    attn_total, ffn_total = (
        lax.psum(attn_share, "hist").astype(jnp.float32),
        lax.psum(ffn_share, "hist").astype(jnp.float32),
    )
    ff_width = ratio * features
    w_attn_grad = jnp.stack(
        [
            attn_total[:, 0:features],
            attn_total[:, features : 2 * features],
            attn_total[:, 2 * features : 3 * features],
        ]
    )
    w_out_grad = attn_total[:, 3 * features : 4 * features]
    w_up_grad = ffn_total[:, 0:ff_width]
    w_down_grad = ffn_total[:, ff_width : 2 * ff_width].reshape(share_rows * ratio, features)
    mix_in_share = ffn_total[:, 2 * ff_width : 2 * ff_width + mix_width]
    gains_share = ffn_total[:, 2 * ff_width + mix_width : 2 * ff_width + mix_width + 5].T
    mix_out_share = ffn_total[0:per_device, 2 * ff_width + mix_width + 5 :]
    return (
        block_out,
        history_grad,
        gains_share,
        mix_in_share,
        mix_out_share,
        w_attn_grad,
        w_out_grad,
        w_up_grad,
        w_down_grad,
    )


DEVICE_MESH = pl.DeviceIdType.MESH
CORE, ACROSS_X, ACROSS_Y = 1, 2, 4


def partner(column, mask):
    moved = column
    for bit in (1, 2, 4):
        if mask & bit:
            on = lax.rem(lax.div(moved, bit), 2)
            moved = moved + bit - 2 * bit * on
    return moved


def push(source, target, send_sem, recv_sem, place):
    copy = pltpu.make_async_remote_copy(
        src_ref=source,
        dst_ref=target,
        send_sem=send_sem,
        recv_sem=recv_sem,
        device_id={"dp": place},
        device_id_type=DEVICE_MESH,
    )
    copy.start()
    return copy


def z_place(plane):
    return {"hist": plane}


class PlaneGatherSteps:

    def __init__(self, column, own, whole, send_sem, recv_sem, local_sem):
        self.column, self.own, self.whole = column, own, whole
        self.send_sem, self.recv_sem, self.local_sem = send_sem, recv_sem, local_sem
        self.rows = own.shape[0]
        self.half = self.rows // 2
        self.across = partner(column, ACROSS_X)
        self.along = partner(column, ACROSS_Y)
        self.beside = partner(column, CORE)
        self.corner = partner(column, ACROSS_X + ACROSS_Y)
        self.copies = []

    def place(self, owner, part):
        start = owner * self.rows + (self.half if part == 1 else 0)
        count = self.rows if part is None else self.half
        return self.whole.at[pl.ds(pl.multiple_of(start, 16), count)]

    def mine(self, part):
        start = self.half if part == 1 else 0
        return self.own.at[pl.ds(start, self.rows if part is None else self.half)]

    def send(self, source, owner, part, to):
        index = len(self.copies)
        copy = push(
            source, self.place(owner, part), self.send_sem.at[index], self.recv_sem.at[index], to
        )
        self.copies.append(copy)

    def begin(self):
        me = self.column
        self.local = pltpu.make_async_copy(self.mine(None), self.place(me, None), self.local_sem)
        self.local.start()
        self.send(self.mine(1), me, 1, self.across)
        self.send(self.mine(0), me, 0, self.along)
        self.send(self.mine(0), me, 0, self.across)
        self.send(self.mine(1), me, 1, self.along)
        self.send(self.mine(None), me, None, self.beside)

    def corners(self):
        self.copies[1].wait_recv()
        self.send(self.place(self.along, 0), self.along, 0, self.across)
        self.copies[0].wait_recv()
        self.send(self.place(self.across, 1), self.across, 1, self.along)

    def siblings(self):
        self.copies[2].wait_recv()
        self.send(self.place(self.across, None), self.across, None, self.beside)
        self.copies[3].wait_recv()
        self.send(self.place(self.along, None), self.along, None, self.beside)

    def rest(self):
        self.copies[5].wait_recv()
        self.send(self.place(self.corner, 0), self.corner, 0, self.beside)
        self.copies[6].wait_recv()
        self.send(self.place(self.corner, 1), self.corner, 1, self.beside)

    def finish(self):
        for index in (4, 7, 8, 9, 10):
            self.copies[index].wait_recv()
        for copy in self.copies:
            copy.wait_send()
        self.local.wait()


class PlaneScatterSteps:
    def __init__(self, column, product, refs, send_sem, recv_sem):
        self.column, self.product = column, product
        self.out_buf, self.side, self.chip, self.from_x, self.from_y, self.last = refs
        self.send_sem, self.recv_sem = send_sem, recv_sem
        rows = self.chip.shape[1]
        self.first, self.second = pl.ds(0, rows // 2), pl.ds(rows // 2, rows // 2)
        self.across = partner(column, ACROSS_X)
        self.along = partner(column, ACROSS_Y)
        self.beside = partner(column, CORE)
        self.pair, self.sends = [], []

    def block(self, i):
        mask = (6, 2, 4, 0)[i]
        if i >= 2:
            self.pair[i - 2].wait_send()
        self.product(partner(self.column, mask + CORE), self.out_buf.at[i % 2])
        self.pair.append(
            push(
                self.out_buf.at[i % 2],
                self.side.at[i],
                self.send_sem.at[i],
                self.recv_sem.at[i],
                self.beside,
            )
        )
        self.product(partner(self.column, mask), self.chip.at[i])
        self.pair[i].wait_recv()
        add_into(self.chip.at[i], self.side.at[i])
        if i == 0:
            self.send(self.chip.at[0, self.first], self.from_x.at[0], self.across)
            self.send(self.chip.at[0, self.second], self.from_y.at[0], self.along)
        if i == 1:
            self.send(self.chip.at[1, self.first], self.from_x.at[1], self.across)
        if i == 2:
            self.send(self.chip.at[2, self.second], self.from_y.at[1], self.along)

    def send(self, source, target, to):
        index = 4 + len(self.sends)
        self.sends.append(
            push(source, target, self.send_sem.at[index], self.recv_sem.at[index], to)
        )

    def turn(self):
        self.sends[0].wait_recv()
        add_into(self.chip.at[2, self.first], self.from_x.at[0])
        self.send(self.chip.at[2, self.first], self.last.at[0], self.along)
        self.sends[1].wait_recv()
        add_into(self.chip.at[1, self.second], self.from_y.at[0])
        self.send(self.chip.at[1, self.second], self.last.at[1], self.across)

    def finish(self, out_ref):
        self.sends[2].wait_recv()
        add_into(self.chip.at[3, self.first], self.from_x.at[1])
        self.sends[3].wait_recv()
        add_into(self.chip.at[3, self.second], self.from_y.at[1])
        self.sends[4].wait_recv()
        add_into(self.chip.at[3, self.first], self.last.at[0])
        self.sends[5].wait_recv()
        add_into(self.chip.at[3, self.second], self.last.at[1])
        if out_ref is not None:
            out_ref[...] = self.chip[3]
        for copy in self.pair[2:] + self.sends:
            copy.wait_send()


def add_into(target, other):
    rows = target.shape[0]
    step = 32 if rows % 32 == 0 else 16

    def some_rows(r, carry):
        piece = pl.ds(pl.multiple_of(r * step, step), step)
        target[piece, :] = (
            target[piece, :].astype(jnp.float32) + other[piece, :].astype(jnp.float32)
        ).astype(jnp.bfloat16)
        return carry

    lax.fori_loop(0, rows // step, some_rows, 0)


class LineSums:

    def __init__(self, plane, parts, arrived, own, last, held, send_sem, recv_sem, load_sem):
        self.plane, self.parts, self.arrived = plane, parts, arrived
        self.own, self.last, self.held = own, last, held
        self.send_sem, self.recv_sem, self.load_sem = send_sem, recv_sem, load_sem
        self.rows = own.shape[0]

    def part(self, way, item, b):
        place = b if way == 0 else 3 - b
        return self.parts.at[pl.ds((item * 4 + place) * self.rows, self.rows)]

    def message(self, way, turn, a, source):
        to = a + 1 if way == 0 else 2 - a
        return pltpu.make_async_remote_copy(
            src_ref=source,
            dst_ref=self.arrived.at[way * 12 + turn],
            send_sem=self.send_sem.at[way * 12 + turn],
            recv_sem=self.recv_sem.at[way * 12 + turn],
            device_id=z_place(to),
            device_id_type=DEVICE_MESH,
        )

    def origin(self, way, turn):
        item, t = divmod(turn, 3)
        return self.message(way, turn, 0, self.part(way, item, 3 - t))

    def slot(self, way, a, turn):
        item, t = divmod(turn, 3)
        return way * 2 + (item * (3 - a) + t) % 2

    def relay(self, way, turn, a):
        return self.message(way, turn, a, self.held.at[self.slot(way, a, turn)])

    def start(self, turn):
        for place in (0, 3):

            @pl.when(self.plane == place)
            def _():
                self.origin(0 if place == 0 else 1, turn).start()

    def load(self, source, target, index):
        return pltpu.make_async_copy(source, target, self.load_sem.at[index])

    def service(self, sigma):
        for place in range(4):

            @pl.when(self.plane == place)
            def _():
                for way in (0, 1):
                    a = place if way == 0 else 3 - place
                    if a == 0:
                        if sigma < 12:
                            self.origin(way, sigma).wait_send()
                        if sigma + 2 < 12:
                            self.origin(way, sigma + 2).start()
                        continue
                    turn = sigma - a + 1
                    if turn < 0 or turn >= 12:
                        continue
                    item, t = divmod(turn, 3)
                    b = 3 - t
                    if b < a:
                        continue
                    if b > a:
                        slot = self.slot(way, a, turn)
                        sent = [
                            earlier
                            for earlier in range(turn)
                            if 3 - earlier % 3 > a and self.slot(way, a, earlier) == slot
                        ]
                        if sent:
                            self.relay(way, sent[-1], a).wait_send()
                        target = self.held.at[slot]
                        mine = self.load(self.part(way, item, b), self.own, 0)
                        mine.start()
                        self.relay(way, turn, a).wait_recv()
                        came = self.load(self.arrived.at[way * 12 + turn], target, 1)
                        came.start()
                        mine.wait()
                        came.wait()
                        add_into(target, self.own)
                        self.relay(way, turn, a).start()
                    else:
                        self.message(way, turn, a - 1, self.own).wait_recv()
                        came = self.load(self.arrived.at[way * 12 + turn], self.last.at[way], 1)
                        came.start()
                        came.wait()
                if sigma % 3 == 2:
                    item = sigma // 3
                    mine = self.load(self.part(0, item, place), self.own, 0)
                    mine.start()
                    mine.wait()

    def drain(self):
        for place in range(4):

            @pl.when(self.plane == place)
            def _():
                for way in (0, 1):
                    a = place if way == 0 else 3 - place
                    if a == 0 or a == 3:
                        continue
                    for slot in (way * 2, way * 2 + 1):
                        sent = [
                            turn
                            for turn in range(12)
                            if 3 - turn % 3 > a and self.slot(way, a, turn) == slot
                        ]
                        self.relay(way, sent[-1], a).wait_send()


class LineSum:

    def __init__(
        self, plane, parts, arrived, own, last, held, send_sem, recv_sem, load_sem, stride, first
    ):
        self.plane, self.parts, self.arrived = plane, parts, arrived
        self.own, self.last, self.held = own, last, held
        self.send_sem, self.recv_sem, self.load_sem = send_sem, recv_sem, load_sem
        self.rows, self.stride, self.first = own.shape[0], stride, first

    def part(self, way, b):
        place = b if way == 0 else 3 - b
        return self.parts.at[pl.ds(place * self.stride + self.first, self.rows)]

    def message(self, way, t, a, source):
        return pltpu.make_async_remote_copy(
            src_ref=source,
            dst_ref=self.arrived.at[way * 3 + t],
            send_sem=self.send_sem.at[way * 3 + t],
            recv_sem=self.recv_sem.at[way * 3 + t],
            device_id=z_place(a + 1 if way == 0 else 2 - a),
            device_id_type=DEVICE_MESH,
        )

    def origin(self, way, t):
        return self.message(way, t, 0, self.part(way, 3 - t))

    def relay(self, way, t, a):
        return self.message(way, t, a, self.held.at[t if a == 1 else 2])

    def start(self):
        for place in (0, 3):

            @pl.when(self.plane == place)
            def _():
                way = 0 if place == 0 else 1
                self.origin(way, 0).start()
                self.origin(way, 1).start()

    def load(self, source, target, index):
        copy = pltpu.make_async_copy(source, target, self.load_sem.at[index])
        copy.start()
        return copy

    def service(self, sigma):
        for place in range(4):

            @pl.when(self.plane == place)
            def _():
                for way in (0, 1):
                    a = place if way == 0 else 3 - place
                    if a == 0:
                        self.origin(way, sigma).wait_send()
                        if sigma == 0:
                            self.origin(way, 2).start()
                        continue
                    t = sigma - a + 1
                    if t < 0 or 3 - t < a:
                        continue
                    b = 3 - t
                    source = self.arrived.at[way * 3 + t]
                    if b > a:
                        relay = self.relay(way, t, a)
                        target = self.held.at[t if a == 1 else 2]
                        mine = self.load(self.part(way, b), self.own, 0)
                        relay.wait_recv()
                        came = self.load(source, target, 1)
                        mine.wait()
                        came.wait()
                        add_into(target, self.own)
                        relay.start()
                    else:
                        self.message(way, t, a - 1, self.own).wait_recv()
                        self.load(source, self.last.at[way], 1).wait()
                if sigma == 2:
                    self.load(self.part(0, place), self.own, 0).wait()

    def finish(self, target):
        step = 16

        def some_rows(r, carry):
            piece = pl.ds(pl.multiple_of(r * step, step), step)
            total = self.own[piece, :].astype(jnp.float32)
            total = total + self.last[0, piece, :].astype(jnp.float32)
            total = total + self.last[1, piece, :].astype(jnp.float32)
            target[piece, :] = total.astype(jnp.bfloat16)
            return carry

        lax.fori_loop(0, self.rows // step, some_rows, 0)
        for place in (1, 2):

            @pl.when(self.plane == place)
            def _():
                for way in (0, 1):
                    a = place if way == 0 else 3 - place
                    for t in range(3 - a):
                        self.relay(way, t, a).wait_send()


class LineGather:

    def __init__(self, plane, own, slot, send_sem, recv_sem, local_sem):
        self.plane, self.own, self.slot = plane, own, slot
        self.send_sem, self.recv_sem, self.local_sem = send_sem, recv_sem, local_sem

    def message(self, way, a, distance):
        origin = a - distance
        plane_of_origin = origin if way == 0 else 3 - origin
        target = self.slot(plane_of_origin)
        return pltpu.make_async_remote_copy(
            src_ref=self.own if distance == 0 else target,
            dst_ref=target,
            send_sem=self.send_sem.at[way * 3 + distance],
            recv_sem=self.recv_sem.at[way * 3 + distance],
            device_id=z_place(a + 1 if way == 0 else 2 - a),
            device_id_type=DEVICE_MESH,
        )

    def service(self, step):
        for place in range(4):

            @pl.when(self.plane == place)
            def _():
                if step == 0:
                    pltpu.make_async_copy(self.own, self.slot(place), self.local_sem).start()
                for way in (0, 1):
                    a = place if way == 0 else 3 - place
                    if step > a:
                        continue
                    if step > 0:
                        self.message(way, a - 1, step - 1).wait_recv()
                    if a < 3:
                        self.message(way, a, step).start()

    def placed(self):
        for place in range(4):

            @pl.when(self.plane == place)
            def _():
                pltpu.make_async_copy(self.own, self.slot(place), self.local_sem).wait()

    def finish(self):
        for place in range(4):

            @pl.when(self.plane == place)
            def _():
                for way in (0, 1):
                    a = place if way == 0 else 3 - place
                    if a < 3:
                        for distance in range(a + 1):
                            self.message(way, a, distance).wait_send()


GAIN_ROW = (4, 1, 2, 3)


def norm_rows_back(x_buf, back, gain_ref, gain_grad_ref, item, extra, target):
    gain = gain_ref[pl.ds(GAIN_ROW[item], 1), :]
    rows, features = target.shape

    def some_rows(r, gain_sum):
        piece = pl.ds(pl.multiple_of(r * 16, 16), 16)
        x = x_buf[piece, :]
        inverse = lax.rsqrt(jnp.mean(x * x, axis=-1, keepdims=True) + epsilon)
        grad = back[piece, :].astype(jnp.float32)
        scaled = grad * gain
        mean = jnp.mean(scaled * x, axis=-1, keepdims=True)
        result = inverse * scaled - x * (inverse * inverse * inverse) * mean
        if extra is not None:
            result = result + extra[piece, :].astype(jnp.float32)
        target[piece, :] = result.astype(jnp.bfloat16)
        return gain_sum + jnp.sum(grad * x * inverse, axis=0, keepdims=True)

    gain_grad_ref[pl.ds(item, 1), :] = lax.fori_loop(
        0, rows // 16, some_rows, jnp.zeros((1, features), jnp.float32)
    )


def forward_kernel(
    length_ref,
    pack_ref,
    latest_ref,
    history_ref,
    select_ref,
    root_ref,
    cotangent_ref,
    w_up_ref,
    w_attn_ref,
    w_down_ref,
    w_out_ref,
    cos_ref,
    sin_ref,
    packed_ref,
    gain_ref,
    pre_ref,
    factor_ref,
    x_ref,
    normed_ref,
    grad_all_ref,
    hidden_ref,
    up_term_ref,
    down_sum_ref,
    full3_ref,
    gain_grad_ref,
    attn_columns,
    q_ref,
    k_ref,
    v_ref,
    out_grad_ref,
    key_before_ref,
    part_ref,
    down_term_ref,
    arrived_ref,
    arrived_down_ref,
    normed3,
    grads,
    up_columns,
    up_grad,
    out_buf,
    side,
    chip,
    from_x,
    from_y,
    last,
    own,
    ends,
    held,
    x_buf,
    normed_buf,
    term_buf,
    grad_own,
    stream_own,
    mix_out_buf,
    dyn_got,
    gather_send,
    gather_recv,
    gather_local,
    scatter_send,
    scatter_recv,
    line_send,
    line_recv,
    line_load,
    swap_send,
    swap_recv,
    swap_local,
    out_sem,
    small_send,
    small_recv,
    dyn_send,
    dyn_recv,
    route_send,
    route_recv,
    block_sem,
    spread_send,
    spread_recv,
    sum_send,
    sum_recv,
    key_send,
    key_recv,
    ready_sem,
    *,
    micro_count,
    sequence_length,
):
    column = lax.axis_index("dp")
    plane = lax.axis_index("hist")
    rows, features = grad_own.shape
    total = 8 * rows
    share = w_up_ref.shape[0]
    ff_share = w_down_ref.shape[0]
    width = share
    tile = 256
    mix_rows = pack_ref.shape[0] - share - 32 + 8
    every_mask = (6, 7, 2, 3, 4, 5, 1)

    barrier = pltpu.get_barrier_semaphore()
    for mask in every_mask:
        pl.semaphore_signal(
            barrier, inc=1, device_id={"dp": partner(column, mask)}, device_id_type=DEVICE_MESH
        )
    for place in range(4):

        @pl.when(plane == place)
        def _():
            for p in range(4):
                if p != place:
                    pl.semaphore_signal(
                        barrier, inc=1, device_id=z_place(p), device_id_type=DEVICE_MESH
                    )

    pl.semaphore_wait(barrier, 10)

    def block_load(source, target, index):
        copy = pltpu.make_async_copy(source, target, block_sem.at[index])
        copy.start()
        return copy

    small_copies = [
        push(
            pack_ref,
            packed_ref.at[column],
            small_send.at[mask],
            small_recv.at[mask],
            partner(column, mask),
        )
        for mask in every_mask
    ]
    small_local = pltpu.make_async_copy(pack_ref, packed_ref.at[column], small_send.at[0])
    small_local.start()
    latest_loads = [
        block_load(latest_ref.at[pl.ds(q * rows, rows)], normed_buf.at[q], 8 + q) for q in range(4)
    ]

    my_rows = pl.ds(pl.multiple_of(column * share, 16), share)

    def up_piece(owner):
        return w_up_ref.at[:, pl.ds(pl.multiple_of(owner * ff_share, 128), ff_share)]

    up_local = pltpu.make_async_copy(up_piece(column), up_columns.at[my_rows], swap_local.at[0])
    up_local.start()
    up_swaps = [
        push(
            up_piece(partner(column, mask)),
            up_columns.at[my_rows],
            swap_send.at[mask],
            swap_recv.at[mask],
            partner(column, mask),
        )
        for mask in every_mask
    ]

    chunk = rows // micro_count

    def route_source(place, s):
        return cotangent_ref.at[pl.ds(s * chunk, chunk)]

    def route_copy(place, s, target_place, slot):
        return pltpu.make_async_remote_copy(
            src_ref=route_source(place, s),
            dst_ref=grad_own.at[pl.ds(slot * chunk, chunk)],
            send_sem=route_send.at[s],
            recv_sem=route_recv.at[slot],
            device_id=z_place(target_place),
            device_id_type=DEVICE_MESH,
        )

    def route_local(place, s, slot):
        return pltpu.make_async_copy(
            route_source(place, s), grad_own.at[pl.ds(slot * chunk, chunk)], route_recv.at[slot]
        )

    for place in range(4):

        @pl.when(plane == place)
        def _():
            for s in range(micro_count):
                target_place, slot = divmod(s * 4 + place, micro_count)
                if target_place == place:
                    route_local(place, s, slot).start()
                else:
                    route_copy(place, s, target_place, slot).start()

    block_order = (3, 0, 2, 1)

    def history_loads(i):
        p, h = block_order[i], i % 2
        return [
            block_load(
                history_ref.at[pl.ds((slot * 4 + p) * rows, rows)],
                normed3.at[pl.ds((h * 4 + slot) * rows, rows)],
                h * 4 + slot,
            )
            for slot in range(4)
        ]

    loads = [history_loads(0), history_loads(1)]
    zeros = jnp.zeros((16, features), jnp.bfloat16)

    def clear(r, carry):
        ends[0, pl.ds(pl.multiple_of(r * 16, 16), 16), :] = zeros
        ends[1, pl.ds(pl.multiple_of(r * 16, 16), 16), :] = zeros
        return carry

    lax.fori_loop(0, ends.shape[1] // 16, clear, 0)

    small_local.wait()
    for copy in small_copies:
        copy.wait_recv()
    for d in range(8):
        gains = packed_ref[d, pl.ds(share + 16, 16), :].astype(jnp.float32)
        gain_ref[:, pl.ds(d * share, share // 2)] = gains[:8]
        gain_ref[:, pl.ds(d * share + share // 2, share // 2)] = gains[8:]
        mix_out_buf[pl.ds(d * mix_rows, mix_rows), :] = packed_ref[
            d, pl.ds(share, 16), :
        ].astype(jnp.float32)[:mix_rows]
    for copy in latest_loads:
        copy.wait()
    for q in range(4):

        def norm_rows(r, carry):
            piece = pl.ds(pl.multiple_of(r * 16, 16), 16)
            x = normed_buf[q, piece, :].astype(jnp.float32)
            inverse = lax.rsqrt(jnp.mean(x * x, axis=-1, keepdims=True) + epsilon)
            normed_buf[q, piece, :] = (x * inverse * gain_ref[pl.ds(0, 1), :]).astype(jnp.bfloat16)
            return carry

        lax.fori_loop(0, rows // 16, norm_rows, 0)
        pre = None
        for d in range(8):
            term = matmul(normed_buf[q, :, d * share : (d + 1) * share], packed_ref[d, :share, :])
            pre = term if pre is None else pre + term
        pre_ref[pl.ds(q * rows, rows), :] = pre
    pre = pre_ref[...]
    act = 0.5 * pre * (1.0 + lax.erf(pre * (1.0 / math.sqrt(2.0))))
    dyn = precise(act[:, : 8 * mix_rows], mix_out_buf[...])
    dyn_columns = (jnp.transpose(dyn)[: 8 * mix_rows] * root_ref[pl.ds(0, 1), :]).astype(jnp.bfloat16)

    def dyn_copy(source_place, target_place):
        return pltpu.make_async_remote_copy(
            src_ref=dyn_got.at[source_place],
            dst_ref=dyn_got.at[source_place],
            send_sem=dyn_send.at[target_place],
            recv_sem=dyn_recv.at[source_place],
            device_id=z_place(target_place),
            device_id_type=DEVICE_MESH,
        )

    for place in range(4):

        @pl.when(plane == place)
        def _():
            dyn_got[place] = dyn_columns
            for p in range(4):
                if p != place:
                    dyn_copy(place, p).start()
            for p in range(4):
                if p != place:
                    dyn_copy(p, place).wait_recv()

    dyn_sum = dyn_got[0] + dyn_got[1] + dyn_got[2] + dyn_got[3]
    factor_ref[...] = lax.dot_general(
        dyn_sum, select_ref[...], contract_rows, preferred_element_type=jnp.float32
    )

    block = pl.ds(0, rows)
    line = LineSums(
        plane,
        part_ref,
        arrived_ref,
        own.at[block],
        ends.at[:, block],
        held.at[:, block],
        line_send,
        line_recv,
        line_load,
    )
    stores = [None, None]
    for i, p in enumerate(block_order):
        h = i % 2
        for copy in loads[i]:
            copy.wait()
        if stores[h] is not None:
            for copy in stores[h]:
                copy.wait()

        def mix_rows_of(r, carry):
            factors = factor_ref[pl.ds(pl.multiple_of(p * rows + r * 16, 16), 16), :]
            for lane in range(0, features, 512):
                slots = [
                    normed3[
                        pl.ds(pl.multiple_of((h * 4 + slot) * rows + r * 16, 16), 16),
                        lane : lane + 512,
                    ].astype(jnp.float32)
                    for slot in range(4)
                ]
                for item in range(4):
                    mixed = None
                    for slot in range(4):
                        one = item * 4 + slot
                        term = factors[:, one : one + 1] * slots[slot]
                        mixed = term if mixed is None else mixed + term
                    grads[
                        pl.ds(pl.multiple_of((h * 4 + item) * rows + r * 16, 16), 16),
                        lane : lane + 512,
                    ] = mixed.astype(jnp.bfloat16)
            return carry

        lax.fori_loop(0, rows // 16, mix_rows_of, 0)
        stores[h] = [
            pltpu.make_async_copy(
                grads.at[pl.ds((h * 4 + item) * rows, rows)],
                part_ref.at[pl.ds((item * 4 + p) * rows, rows)],
                block_sem.at[12 + h * 4 + item],
            )
            for item in range(4)
        ]
        for copy in stores[h]:
            copy.start()
        if i + 2 < 4:
            loads.append(history_loads(i + 2))
        if i % 2 == 1:
            for copies in stores:
                for copy in copies:
                    copy.wait()
            stores = [None, None]
        if i == 1:
            line.start(0)

    line.start(1)
    for mask in (CORE, ACROSS_X, ACROSS_Y):
        pl.semaphore_signal(
            ready_sem, inc=1, device_id={"dp": partner(column, mask)}, device_id_type=DEVICE_MESH
        )

    def attn_piece(stream, owner):
        return w_attn_ref.at[stream, :, pl.ds(pl.multiple_of(owner * share, 128), share)]

    def gather(index, own_rows, whole):
        return PlaneGatherSteps(
            column,
            own_rows,
            whole,
            gather_send.at[index],
            gather_recv.at[index],
            gather_local.at[index],
        )

    for place in range(4):

        @pl.when(plane == place)
        def _():
            for slot in range(micro_count):
                s, source_place = divmod(place * micro_count + slot, 4)
                if source_place == place:
                    route_local(place, s, slot).wait()
                else:
                    route_copy(source_place, s, place, slot).wait_recv()

    def mask_rows(r, carry):
        piece = pl.ds(pl.multiple_of(r * 16, 16), 16)
        row = plane * rows + r * 16 + lax.broadcasted_iota(jnp.int32, (16, 1), 0)
        limit = jnp.zeros((16, 1), jnp.int32)
        for m in range(micro_count):
            inside = (row >= m * sequence_length) & (row < (m + 1) * sequence_length)
            limit = jnp.where(inside, m * sequence_length + length_ref[m], limit)
        kept = jnp.where(row < limit, grad_own[piece, :].astype(jnp.float32), 0.0)
        grad_own[piece, :] = kept.astype(jnp.bfloat16)
        return carry

    lax.fori_loop(0, rows // 16, mask_rows, 0)
    pl.semaphore_wait(ready_sem, 3)
    grad_gather = gather(4, grad_own, grads)
    grad_gather.begin()

    x_copies = []

    def combine(item):
        if x_copies:
            x_copies[-1].wait()

        def some_rows(r, carry):
            piece = pl.ds(pl.multiple_of(r * 16, 16), 16)
            x = (
                own[piece, :].astype(jnp.float32)
                + ends[0, piece, :].astype(jnp.float32)
                + ends[1, piece, :].astype(jnp.float32)
            )
            x_buf[piece, :] = x
            inverse = lax.rsqrt(jnp.mean(x * x, axis=-1, keepdims=True) + epsilon)
            normed_buf[item, piece, :] = (
                x * inverse * gain_ref[pl.ds(GAIN_ROW[item], 1), :]
            ).astype(jnp.bfloat16)
            return carry

        lax.fori_loop(0, rows // 16, some_rows, 0)
        copy = pltpu.make_async_copy(x_buf, x_ref.at[item], out_sem.at[0])
        copy.start()
        x_copies.append(copy)
        steps = gather(
            item, normed_buf.at[item], normed3 if item == 0 else normed_ref.at[item - 1]
        )
        steps.begin()
        return steps

    line.service(0)
    line.service(1)
    grad_gather.corners()
    grad_gather.siblings()
    line.service(2)
    gather3 = combine(0)
    grad_gather.rest()
    grad_gather.finish()
    grads_out = pltpu.make_async_copy(grads, grad_all_ref, out_sem.at[2])
    grads_out.start()
    gather3.corners()
    line.service(3)
    gather3.siblings()
    gather3.rest()
    line.service(4)
    for copy in up_swaps:
        copy.wait_recv()
    up_local.wait()
    gather3.finish()
    attn_swaps, attn_locals = [], []
    for stream in range(3):
        local = pltpu.make_async_copy(
            attn_piece(stream, column),
            attn_columns.at[stream, my_rows],
            swap_local.at[1 + stream],
        )
        local.start()
        attn_locals.append(local)
        for mask in every_mask:
            attn_swaps.append(
                push(
                    attn_piece(stream, partner(column, mask)),
                    attn_columns.at[stream, my_rows],
                    swap_send.at[8 * (stream + 1) + mask],
                    swap_recv.at[8 * (stream + 1) + mask],
                    partner(column, mask),
                )
            )

    def feed(first_block, count):
        def one_tile(step, carry):
            piece = pl.ds(pl.multiple_of((step // (ff_share // tile)) * rows, 16), rows)
            lanes = pl.ds(pl.multiple_of((step % (ff_share // tile)) * tile, tile), tile)
            up = jnp.dot(normed3[piece, :], up_columns[:, lanes], preferred_element_type=jnp.float32)
            spread = 0.5 * (1.0 + lax.erf(up * (1.0 / math.sqrt(2.0))))
            hidden_ref[piece, lanes] = (up * spread).astype(jnp.bfloat16)
            slope = spread + up * jnp.exp(-0.5 * up * up) * (1.0 / math.sqrt(2.0 * math.pi))
            hidden_grad = lax.dot_general(
                grads[piece, :],
                w_down_ref[lanes, :],
                contract_cols,
                preferred_element_type=jnp.float32,
            )
            up_grad[piece, lanes] = (hidden_grad * slope).astype(jnp.bfloat16)
            return carry

        per_block = ff_share // tile
        lax.fori_loop(first_block * per_block, (first_block + count) * per_block, one_tile, 0)

    def back_product(owner, target):
        left_rows = pl.ds(pl.multiple_of(owner * rows, 16), rows)

        def one_tile(t, carry):
            lanes = pl.ds(pl.multiple_of(t * 2 * tile, 2 * tile), 2 * tile)
            target[:, lanes] = lax.dot_general(
                up_grad[left_rows, :],
                up_columns[lanes, :],
                contract_cols,
                preferred_element_type=jnp.float32,
            ).astype(jnp.bfloat16)
            return carry

        lax.fori_loop(0, features // (2 * tile), one_tile, 0)

    term_slots = 2
    part = share // 4

    def term_copies(kind, slot, index):
        if kind == 0:
            return [
                pltpu.make_async_copy(
                    term_buf.at[slot, pl.ds(h * part, part), pl.ds(0, ff_share)],
                    up_term_ref.at[
                        pl.ds(h * 4 * part + index % 4 * part, part),
                        pl.ds(index // 4 * ff_share, ff_share),
                    ],
                    out_sem.at[3 + 4 * slot + h],
                )
                for h in range(4)
            ]
        return [
            pltpu.make_async_copy(
                term_buf.at[slot],
                down_term_ref.at[pl.ds(index * tile, tile)],
                out_sem.at[3 + 4 * slot],
            )
        ]

    def terms(kind, first, count):
        term_width = ff_share if kind == 0 else features
        pending = []
        for index in range(first, first + count):
            slot = index % term_slots
            if len(pending) >= term_slots:
                for copy in pending[-term_slots]:
                    copy.wait()

            def one_tile(t, carry):
                lanes = pl.ds(pl.multiple_of(t * 2 * tile, 2 * tile), 2 * tile)
                if kind == 0:
                    left, right = normed3[:, index * tile : (index + 1) * tile], up_grad[:, lanes]
                else:
                    left, right = hidden_ref[:, index * tile : (index + 1) * tile], grads[:, lanes]
                term_buf[slot, :, lanes] = lax.dot_general(
                    left, right, contract_rows, preferred_element_type=jnp.float32
                ).astype(jnp.bfloat16)
                return carry

            lax.fori_loop(0, term_width // (2 * tile), one_tile, 0)
            copies = term_copies(kind, slot, index)
            for copy in copies:
                copy.start()
            pending.append(copies)
        for copies in pending[-term_slots:]:
            for copy in copies:
                copy.wait()

    def project(stream, target):
        def one_block(b, carry):
            piece = pl.ds(pl.multiple_of(b * rows, 16), rows)
            value = matmul(normed3[piece, :], attn_columns[stream])
            if stream < 2:
                parts = []
                for head in range(width // HEAD_DIM):
                    one = value[:, head * HEAD_DIM : (head + 1) * HEAD_DIM]
                    swapped = jnp.concatenate(
                        [one[:, HEAD_DIM // 2 :], one[:, : HEAD_DIM // 2]], axis=1
                    )
                    parts.append(one * cos_ref[...] + swapped * sin_ref[...])
                value = jnp.concatenate(parts, axis=1)
            target[piece, :] = value.astype(jnp.bfloat16)
            return carry

        lax.fori_loop(0, 8, one_block, 0)

    def out_grads(b, carry):
        piece = pl.ds(pl.multiple_of(b * rows, 16), rows)
        out_grad_ref[piece, :] = lax.dot_general(
            grads[piece, :], w_out_ref[...], contract_cols, preferred_element_type=jnp.float32
        ).astype(jnp.bfloat16)
        return carry

    def key_copy(place):
        return pltpu.make_async_remote_copy(
            src_ref=k_ref,
            dst_ref=key_before_ref,
            send_sem=key_send.at[0],
            recv_sem=key_recv.at[0],
            device_id=z_place(place + 1),
            device_id_type=DEVICE_MESH,
        )

    feed(0, 2)
    line.service(5)
    gather0 = combine(1)
    feed(2, 2)
    line.service(6)
    gather0.corners()
    feed(4, 2)
    line.service(7)
    gather0.siblings()
    feed(6, 2)
    gather0.rest()
    scatter = PlaneScatterSteps(
        column,
        back_product,
        (out_buf, side, chip, from_x, from_y, last),
        scatter_send,
        scatter_recv,
    )
    scatter.block(0)
    line.service(8)
    gather1 = combine(2)
    scatter.block(1)
    scatter.block(2)
    scatter.block(3)
    gather0.finish()
    terms(1, 0, 2)
    line.service(9)
    scatter.turn()
    gather1.corners()
    terms(1, 2, ff_share // tile - 2)
    line.service(10)
    scatter.finish(None)
    x_copies[-1].wait()
    x_load = pltpu.make_async_copy(x_ref.at[0], x_buf, out_sem.at[1])
    x_load.start()
    x_load.wait()
    norm_rows_back(x_buf, chip.at[3], gain_ref, gain_grad_ref, 0, grad_own, stream_own)
    x_copies.clear()
    spread3 = LineGather(
        plane,
        stream_own,
        lambda p: full3_ref.at[pl.ds(p * rows, rows)],
        spread_send,
        spread_recv,
        out_sem.at[11],
    )
    spread3.service(0)
    gather1.siblings()
    down_line = LineSum(
        plane,
        down_term_ref,
        arrived_down_ref,
        own,
        ends,
        held,
        sum_send,
        sum_recv,
        line_load,
        share,
        0,
    )
    line.service(11)
    gather2 = combine(3)
    down_line.start()
    gather1.rest()
    terms(0, 0, features // tile)
    line.drain()
    gather1.finish()
    load = block_load(normed_ref.at[1], normed3, 0)
    gather2.corners()
    for copy in attn_swaps:
        copy.wait_recv()
    for copy in attn_locals:
        copy.wait()
    spread3.service(1)
    load.wait()
    project(1, k_ref)
    for place in range(3):

        @pl.when(plane == place)
        def _():
            key_copy(place).start()

    load = block_load(normed_ref.at[0], normed3, 0)
    down_line.service(0)
    gather2.siblings()
    gather2.rest()
    load.wait()
    project(0, q_ref)
    spread3.service(2)
    lax.fori_loop(0, 8, out_grads, 0)
    gather2.finish()
    load = block_load(normed_ref.at[2], normed3, 0)
    down_line.service(1)
    load.wait()
    project(2, v_ref)
    spread3.service(3)
    for copy in small_copies + up_swaps + attn_swaps:
        copy.wait_send()
    grads_out.wait()
    x_copies[-1].wait()
    for place in range(4):

        @pl.when(plane == place)
        def _():
            for p in range(4):
                if p != place:
                    dyn_copy(place, p).wait_send()
            for s in range(micro_count):
                target_place, slot = divmod(s * 4 + place, micro_count)
                if target_place != place:
                    route_copy(place, s, target_place, slot).wait_send()

    down_line.service(2)
    down_line.finish(down_sum_ref)
    spread3.placed()
    spread3.finish()
    for place in range(4):

        @pl.when(plane == place)
        def _():
            if place > 0:
                key_copy(place - 1).wait_recv()
            if place < 3:
                key_copy(place).wait_send()


def forward_and_feed(
    lengths,
    pack,
    latest,
    history,
    select,
    root,
    cotangent,
    w_up,
    w_attn,
    w_down,
    w_out,
    cosine,
    sine_part,
    sequence_length,
):
    rows, features = cotangent.shape
    micro_count = lengths.shape[0]
    total = 8 * rows
    share = w_up.shape[0]
    ff_share = w_down.shape[0]
    mix_width = select.shape[0]
    block = (rows, features)
    piece = (share, features)
    half = (2, rows // 2, features)
    anywhere = pl.BlockSpec(memory_space=pl.ANY)
    near = pl.BlockSpec(memory_space=pltpu.VMEM)
    shape = jax.ShapeDtypeStruct
    low_type = jnp.bfloat16
    some = lambda *dims: pltpu.VMEM(dims, low_type)
    wide = lambda *dims: pltpu.VMEM(dims, jnp.float32)
    dma = pltpu.SemaphoreType.DMA
    outputs = [
        (near, shape((8,) + pack.shape, low_type)),
        (near, shape((8, features), jnp.float32)),
        (near, shape((4 * rows, 128), jnp.float32)),
        (near, shape((4 * rows, 128), jnp.float32)),
        (anywhere, shape((4,) + block, jnp.float32)),
        (anywhere, shape((3, total, features), low_type)),
        (anywhere, shape((total, features), low_type)),
        (near, shape((total, ff_share), low_type)),
        (anywhere, shape((ff_share, features), low_type)),
        (near, shape(piece, low_type)),
        (anywhere, shape((4 * rows, features), low_type)),
        (near, shape((8, features), jnp.float32)),
        (near, shape((3, features, share), low_type)),
        (near, shape((total, share), low_type)),
        (near, shape((total, share), low_type)),
        (near, shape((total, share), low_type)),
        (near, shape((total, share), low_type)),
        (anywhere, shape((total, share), low_type)),
        (anywhere, shape((16 * rows, features), low_type)),
        (anywhere, shape((ff_share, features), low_type)),
        (anywhere, shape((24,) + block, low_type)),
        (anywhere, shape((6,) + piece, low_type)),
    ]
    return pl.pallas_call(
        functools.partial(
            forward_kernel, micro_count=micro_count, sequence_length=sequence_length
        ),
        in_specs=[pl.BlockSpec(memory_space=pltpu.SMEM), near, anywhere, anywhere]
        + [near, near, anywhere, anywhere, anywhere]
        + [near] * 4,
        out_specs=[spec for spec, _ in outputs],
        out_shape=[out for _, out in outputs],
        scratch_shapes=[
            some(total, features),
            some(total, features),
            some(features, ff_share),
            some(total, ff_share),
            some(2, *block),
            some(4, *block),
            some(4, *block),
            some(*half),
            some(*half),
            some(*half),
            some(*piece),
            some(2, *piece),
            some(4, *piece),
            wide(*block),
            some(4, *block),
            some(2, 256, features),
            some(*block),
            some(*block),
            wide(mix_width, 128),
            some(4, mix_width, 4 * rows),
            dma((5, 11)),
            dma((5, 11)),
            dma((5,)),
            dma((10,)),
            dma((10,)),
            dma((24,)),
            dma((24,)),
            dma((2,)),
            dma((32,)),
            dma((32,)),
            dma((4,)),
            dma((12,)),
            dma((8,)),
            dma((8,)),
            dma((4,)),
            dma((4,)),
            dma((micro_count,)),
            dma((micro_count,)),
            dma((20,)),
            dma((6,)),
            dma((6,)),
            dma((6,)),
            dma((6,)),
            dma((1,)),
            dma((1,)),
            pltpu.SemaphoreType.REGULAR,
        ],
        compiler_params=pltpu.CompilerParams(
            collective_id=5, has_side_effects=True, vmem_limit_bytes=63 * 1024 * 1024
        ),
        cost_estimate=pl.CostEstimate(
            flops=12 * total * features * ff_share,
            bytes_accessed=600 * 1000 * 1000,
            transcendentals=0,
        ),
    )(
        lengths,
        pack,
        latest,
        history,
        select,
        root,
        cotangent,
        w_up,
        w_attn,
        w_down,
        w_out,
        cosine,
        sine_part,
    )


def small_sum_kernel(parts_ref, out_ref, got, sums, send_sem, recv_sem, z_send, z_recv):
    column = lax.axis_index("dp")
    plane = lax.axis_index("hist")
    every_mask = (6, 7, 2, 3, 4, 5, 1)
    barrier = pltpu.get_barrier_semaphore()
    for mask in every_mask:
        pl.semaphore_signal(
            barrier, inc=1, device_id={"dp": partner(column, mask)}, device_id_type=DEVICE_MESH
        )
    for place in range(4):

        @pl.when(plane == place)
        def _():
            for p in range(4):
                if p != place:
                    pl.semaphore_signal(
                        barrier, inc=1, device_id=z_place(p), device_id_type=DEVICE_MESH
                    )

    pl.semaphore_wait(barrier, 10)
    copies = [
        push(
            parts_ref.at[partner(column, mask)],
            got.at[mask],
            send_sem.at[mask],
            recv_sem.at[mask],
            partner(column, mask),
        )
        for mask in every_mask
    ]
    total = parts_ref[column].astype(jnp.float32)
    for mask, copy in zip(every_mask, copies):
        copy.wait_recv()
        total = total + got[mask].astype(jnp.float32)

    def line_copy(source_place, target_place):
        return pltpu.make_async_remote_copy(
            src_ref=sums.at[source_place],
            dst_ref=sums.at[source_place],
            send_sem=z_send.at[target_place],
            recv_sem=z_recv.at[source_place],
            device_id=z_place(target_place),
            device_id_type=DEVICE_MESH,
        )

    for place in range(4):

        @pl.when(plane == place)
        def _():
            others = [p for p in range(4) if p != place]
            sums[place] = total.astype(jnp.bfloat16)
            for p in others:
                line_copy(place, p).start()
            for p in others:
                line_copy(p, place).wait_recv()
            for p in others:
                line_copy(place, p).wait_send()

    out_ref[...] = (sums[0].astype(jnp.float32) + sums[1].astype(jnp.float32)) + (
        sums[2].astype(jnp.float32) + sums[3].astype(jnp.float32)
    )
    for copy in copies:
        copy.wait_send()


def small_sums(parts):
    dims = parts.shape[1:]
    dma = pltpu.SemaphoreType.DMA
    return pl.pallas_call(
        small_sum_kernel,
        out_shape=jax.ShapeDtypeStruct(dims, jnp.float32),
        in_specs=[pl.BlockSpec(memory_space=pltpu.VMEM)],
        out_specs=pl.BlockSpec(memory_space=pltpu.VMEM),
        scratch_shapes=[
            pltpu.VMEM((8,) + dims, jnp.bfloat16),
            pltpu.VMEM((4,) + dims, jnp.bfloat16),
            dma((8,)),
            dma((8,)),
            dma((4,)),
            dma((4,)),
        ],
        compiler_params=pltpu.CompilerParams(collective_id=7, has_side_effects=True),
        cost_estimate=pl.CostEstimate(
            flops=0, bytes_accessed=40 * 1000 * 1000, transcendentals=0
        ),
    )(parts)


def slot_grad_kernel(
    flag_ref,
    factor_ref,
    first_ref,
    rest_ref,
    latest_ref,
    pre_grad_ref,
    mix_in_ref,
    gain_ref,
    out_ref,
    gain_grad_ref,
):
    x = latest_ref[...].astype(jnp.float32)
    inverse = lax.rsqrt(jnp.mean(x * x, axis=-1, keepdims=True) + epsilon)
    grad = precise(pre_grad_ref[...], mix_in_ref[...])
    scaled = grad * gain_ref[pl.ds(0, 1), :]
    mean = jnp.mean(scaled * x, axis=-1, keepdims=True)
    latest_grad = inverse * scaled - x * (inverse * inverse * inverse) * mean
    gain_sum = jnp.sum(grad * x * inverse, axis=0, keepdims=True)

    @pl.when(pl.program_id(0) == 0)
    def _():
        gain_grad_ref[...] = jnp.zeros_like(gain_grad_ref)

    gain_grad_ref[pl.ds(0, 1), :] += gain_sum
    grads = [first_ref[...].astype(jnp.float32)] + [
        rest_ref[i].astype(jnp.float32) for i in range(3)
    ]
    factors = factor_ref[...]
    for slot in range(4):
        total = latest_grad * flag_ref[slot]
        for item in range(4):
            one = item * 4 + slot
            total = total + factors[:, one : one + 1] * grads[item]
        out_ref[slot] = total.astype(jnp.bfloat16)


def slot_grads_of(latest_here, factors, first, rest, latest, pre_grad, mix_in_columns, gains):
    total, features = first.shape
    step = 64
    mix_width = pre_grad.shape[1]
    rows_of = lambda *lead: pl.BlockSpec(
        lead + (step, features), lambda r: (0,) * len(lead) + (r, 0)
    )
    whole = lambda *dims: pl.BlockSpec(dims, lambda r: (0, 0))
    return pl.pallas_call(
        slot_grad_kernel,
        grid=(total // step,),
        in_specs=[
            pl.BlockSpec(memory_space=pltpu.SMEM),
            pl.BlockSpec((step, 128), lambda r: (r, 0)),
            rows_of(),
            rows_of(3),
            rows_of(),
            pl.BlockSpec((step, mix_width), lambda r: (r, 0)),
            whole(mix_width, features),
            whole(8, features),
        ],
        out_specs=[rows_of(4), whole(8, features)],
        out_shape=[
            jax.ShapeDtypeStruct((4, total, features), jnp.bfloat16),
            jax.ShapeDtypeStruct((8, features), jnp.float32),
        ],
        compiler_params=pltpu.CompilerParams(vmem_limit_bytes=56 * 1024 * 1024),
        cost_estimate=pl.CostEstimate(
            flops=40 * total * features, bytes_accessed=20 * total * features, transcendentals=0
        ),
    )(latest_here, factors, first, rest, latest, pre_grad, mix_in_columns, gains)


def lay_out_kernel(part_ref, attn_ref, out_ref):
    quarter = out_ref.shape[0]
    for stream in range(3):
        attn_ref[stream] = part_ref[stream * quarter : (stream + 1) * quarter, :].astype(
            jnp.float32
        )
    out_ref[...] = part_ref[3 * quarter :, :].astype(jnp.float32)


def lay_out(parts):
    total, features = parts.shape
    step = total // 4
    quarter = step // 4
    return pl.pallas_call(
        lay_out_kernel,
        grid=(4,),
        in_specs=[pl.BlockSpec((step, features), lambda p: (p, 0))],
        out_specs=[
            pl.BlockSpec((3, quarter, features), lambda p: (0, p, 0)),
            pl.BlockSpec((quarter, features), lambda p: (p, 0)),
        ],
        out_shape=[
            jax.ShapeDtypeStruct((3, step, features), jnp.float32),
            jax.ShapeDtypeStruct((step, features), jnp.float32),
        ],
        compiler_params=pltpu.CompilerParams(vmem_limit_bytes=56 * 1024 * 1024),
        cost_estimate=pl.CostEstimate(
            flops=0, bytes_accessed=6 * total * features, transcendentals=0
        ),
    )(parts)


def attend_column(
    column,
    plane,
    length_ref,
    cosine,
    sine_part,
    q_ref,
    k_ref,
    v_ref,
    kv_before_ref,
    out_grad_ref,
    att_ref,
    q_grad_ref,
    kv_grad_ref,
    kv_before_grad_ref,
    rows,
    micro_count,
    sequence_length,
):
    here = pl.ds(pl.multiple_of(column * rows, 16), rows)
    width = q_ref.shape[1]
    scale = 1.0 / math.sqrt(HEAD_DIM)
    row = plane * rows + lax.broadcasted_iota(jnp.int32, (rows, 1), 0)
    start = jnp.zeros((rows, 1), jnp.int32)
    limit = jnp.zeros((rows, 1), jnp.int32)
    for m in range(micro_count):
        inside = (row >= m * sequence_length) & (row < (m + 1) * sequence_length)
        start = jnp.where(inside, m * sequence_length, start)
        limit = jnp.where(inside, m * sequence_length + length_ref[column * micro_count + m], limit)
    limit = jnp.minimum(limit, row + 1)
    key_row = (plane - 1) * rows + lax.broadcasted_iota(jnp.int32, (1, 2 * rows), 1)
    allowed = (key_row >= start) & (key_row < limit)
    for head in range(width // HEAD_DIM):
        lanes = slice(head * HEAD_DIM, (head + 1) * HEAD_DIM)
        value_lanes = slice(width + head * HEAD_DIM, width + (head + 1) * HEAD_DIM)
        query = q_ref[here, lanes]
        keys = jnp.concatenate([kv_before_ref[here, lanes], k_ref[here, lanes]], axis=0)
        values = jnp.concatenate([kv_before_ref[here, value_lanes], v_ref[here, lanes]], axis=0)
        out_grad = out_grad_ref[here, lanes]
        scores = (
            lax.dot_general(query, keys, contract_cols, preferred_element_type=jnp.float32) * scale
        )
        scores = jnp.where(allowed, scores, masked_out)
        raised = jnp.exp(scores - jnp.max(scores, axis=-1, keepdims=True))
        weights = raised / jnp.sum(raised, axis=-1, keepdims=True)
        weights_low = weights.astype(jnp.bfloat16)
        att_ref[here, lanes] = matmul(weights_low, values).astype(jnp.bfloat16)
        weight_grad = lax.dot_general(
            out_grad, values, contract_cols, preferred_element_type=jnp.float32
        )
        inner = jnp.sum(weights * weight_grad, axis=-1, keepdims=True)
        score_grad = (weights * (weight_grad - inner) * scale).astype(jnp.bfloat16)
        query_grad = matmul(score_grad, keys)
        swapped = jnp.concatenate(
            [query_grad[:, HEAD_DIM // 2 :], query_grad[:, : HEAD_DIM // 2]], axis=1
        )
        q_grad_ref[here, lanes] = (query_grad * cosine - swapped * sine_part).astype(jnp.bfloat16)
        key_grad = lax.dot_general(
            score_grad, query, contract_rows, preferred_element_type=jnp.float32
        )
        value_grad = lax.dot_general(
            weights_low, out_grad, contract_rows, preferred_element_type=jnp.float32
        )
        kv_before_grad_ref[here, lanes] = key_grad[:rows].astype(jnp.bfloat16)
        kv_before_grad_ref[here, value_lanes] = value_grad[:rows].astype(jnp.bfloat16)
        kv_grad_ref[here, lanes] = key_grad[rows:]
        kv_grad_ref[here, value_lanes] = value_grad[rows:]


def backward_kernel(
    length_ref,
    cos_ref,
    sin_ref,
    q_ref,
    k_ref,
    v_ref,
    out_grad_ref,
    normed_ref,
    grad_all_ref,
    hidden_ref,
    w_out_ref,
    w_down_ref,
    attn_columns_ref,
    x_ref,
    gain_ref,
    down_own,
    up_term_ref,
    full3_ref,
    history_ref,
    key_before_ref,
    full_ref,
    down_all_ref,
    up_all_ref,
    down_wide_ref,
    up_wide_ref,
    inner_columns,
    quarter_ref,
    branch_ref,
    gain_grad_ref,
    attn_parts_ref,
    arrived_ref,
    big,
    att,
    q_grad,
    kv_grad,
    kv_before,
    kv_before_grad,
    kv_after,
    out_buf,
    side,
    chip,
    from_x,
    from_y,
    last,
    line_own,
    line_ends,
    line_held,
    up_sum,
    up_own,
    stream_own,
    back_buf,
    x_buf,
    stage,
    scatter_send,
    scatter_recv,
    sum_send,
    sum_recv,
    load_sem,
    spread_send,
    spread_recv,
    spread_local,
    key_send,
    key_recv,
    swap_send,
    swap_recv,
    local_sem,
    inner_sem,
    wide_sem,
    *,
    micro_count,
    sequence_length,
):
    column = lax.axis_index("dp")
    plane = lax.axis_index("hist")
    total, width = q_ref.shape
    rows, features = total // 8, w_down_ref.shape[1]
    ff_share = w_down_ref.shape[0]
    quarter = features // 8 // 4
    v_grad = kv_before.at[:, pl.ds(0, width)]
    k_grad = kv_before.at[:, pl.ds(width, width)]
    attn_sum = up_sum
    tile = 512

    barrier = pltpu.get_barrier_semaphore()
    for mask in range(1, 8):
        pl.semaphore_signal(
            barrier, inc=1, device_id={"dp": partner(column, mask)}, device_id_type=DEVICE_MESH
        )
    for place in range(4):

        @pl.when(plane == place)
        def _():
            for p in range(4):
                if p != place:
                    pl.semaphore_signal(
                        barrier, inc=1, device_id=z_place(p), device_id_type=DEVICE_MESH
                    )

    pl.semaphore_wait(barrier, 10)

    def value_copy(place):
        return pltpu.make_async_remote_copy(
            src_ref=v_ref,
            dst_ref=kv_before.at[:, pl.ds(width, width)],
            send_sem=key_send.at[1],
            recv_sem=key_recv.at[1],
            device_id=z_place(place + 1),
            device_id_type=DEVICE_MESH,
        )

    for place in range(3):

        @pl.when(plane == place)
        def _():
            value_copy(place).start()

    def back_copy(place):
        return pltpu.make_async_remote_copy(
            src_ref=kv_before_grad,
            dst_ref=kv_after,
            send_sem=key_send.at[0],
            recv_sem=key_recv.at[0],
            device_id=z_place(place - 1),
            device_id_type=DEVICE_MESH,
        )

    def clear(target):
        step = 64

        def some_rows(r, carry):
            target[pl.ds(pl.multiple_of(r * step, step), step), :] = jnp.zeros(
                (step, target.shape[1]), jnp.bfloat16
            )
            return carry

        lax.fori_loop(0, target.shape[0] // step, some_rows, 0)

    line_sums = [
        LineSum(
            plane,
            parts,
            arrived_ref.at[pl.ds(6 * i, 6)],
            line_own,
            line_ends,
            line_held,
            sum_send.at[i],
            sum_recv.at[i],
            load_sem,
            4 * quarter,
            0,
        )
        for i, parts in enumerate((up_term_ref, attn_parts_ref))
    ]
    up_line, attn_line = line_sums

    def spread(index, own, slot):
        return LineGather(
            plane, own, slot, spread_send.at[index], spread_recv.at[index], spread_local.at[index]
        )

    def stream_spread(item):
        return spread(
            item,
            stream_own.at[item - 1],
            lambda p: full_ref.at[pl.ds(((item - 1) * 4 + p) * rows, rows)],
        )

    def norm_back(item, back):
        load = pltpu.make_async_copy(x_ref.at[item], x_buf, local_sem.at[0])
        load.start()
        load.wait()
        norm_rows_back(
            x_buf, back, gain_ref, gain_grad_ref, item, None, stream_own.at[item - 1]
        )

    def scatter_of(product, index):
        return PlaneScatterSteps(
            column,
            product,
            (out_buf, side, chip)
            + tuple(arriving.at[pl.ds(2 * (index % 2), 2)] for arriving in (from_x, from_y, last)),
            scatter_send.at[index],
            scatter_recv.at[index],
        )

    def projection_product(stream, grad):
        def product(owner, target):
            left = pl.ds(pl.multiple_of(owner * rows, 16), rows)

            def one_tile(t, carry):
                lanes = pl.ds(pl.multiple_of(t * tile, tile), tile)
                target[:, lanes] = lax.dot_general(
                    grad[left, :],
                    attn_columns_ref[stream, lanes, :],
                    contract_cols,
                    preferred_element_type=jnp.float32,
                ).astype(jnp.bfloat16)
                return carry

            lax.fori_loop(0, features // tile, one_tile, 0)

        return product

    def branch_product(owner, target):
        left = pl.ds(pl.multiple_of(owner * rows, 16), rows)

        def one_tile(t, carry):
            lanes = pl.ds(pl.multiple_of(t * tile, tile), tile)
            target[:, lanes] = (
                matmul(att[left, :], w_out_ref[:, lanes])
                + matmul(hidden_ref[left, :], w_down_ref[:, lanes])
            ).astype(jnp.bfloat16)
            return carry

        lax.fori_loop(0, features // tile, one_tile, 0)

    def attend(first, count):
        def one_column(m, carry):
            attend_column(
                m,
                plane,
                length_ref,
                cos_ref[...],
                sin_ref[...],
                q_ref,
                k_ref,
                v_ref,
                kv_before,
                out_grad_ref,
                att,
                q_grad,
                kv_grad,
                kv_before_grad,
                rows,
                micro_count,
                sequence_length,
            )
            return carry

        lax.fori_loop(first, first + count, one_column, 0)

    step_rows = rows // 2

    def inner_loads(item, i):
        source = full3_ref if item == 0 else full_ref
        first = 0 if item == 0 else (item - 1) * 4 * rows
        base = (i % 2) * 5 * step_rows
        copies = [
            pltpu.make_async_copy(
                source.at[pl.ds(first + i * step_rows, step_rows)],
                big.at[pl.ds(base + 4 * step_rows, step_rows)],
                inner_sem.at[(i % 2) * 5 + 4],
            )
        ] + [
            pltpu.make_async_copy(
                history_ref.at[pl.ds(slot * 4 * rows + i * step_rows, step_rows)],
                big.at[pl.ds(base + slot * step_rows, step_rows)],
                inner_sem.at[(i % 2) * 5 + slot],
            )
            for slot in range(4)
        ]
        for copy in copies:
            copy.start()
        return copies

    def inner_products(item):
        loads = [inner_loads(item, 0)]
        for i in range(8):
            if i + 1 < 8:
                loads.append(inner_loads(item, i + 1))
            for copy in loads[i]:
                copy.wait()
            base = (i % 2) * 5 * step_rows

            def some_rows(r, carry):
                grad = big[
                    pl.ds(pl.multiple_of(base + 4 * step_rows + r * 16, 16), 16), :
                ].astype(jnp.float32)
                for slot in range(4):
                    values = big[
                        pl.ds(pl.multiple_of(base + slot * step_rows + r * 16, 16), 16), :
                    ].astype(jnp.float32)
                    one = item * 4 + slot
                    inner_columns[
                        pl.ds(pl.multiple_of(i * step_rows + r * 16, 16), 16), one : one + 1
                    ] = jnp.sum(grad * values, axis=-1, keepdims=True)
                return carry

            lax.fori_loop(0, step_rows // 16, some_rows, 0)

    def widen(kind):
        if kind == 0:
            pieces = [(down_all_ref, down_wide_ref, i * 64, 0) for i in range(ff_share // 64)]
        else:
            pieces = [
                (up_all_ref, up_wide_ref, i * 64, c * features)
                for i in range(4 * quarter // 64)
                for c in range(8 * ff_share // features)
            ]
        low_at = lambda n: big.at[pl.ds(64 * (n % 3), 64)]
        wide_at = lambda n: x_buf.at[pl.ds(64 * (n % 3), 64)]

        def load(n):
            source, _, row, lane = pieces[n]
            return pltpu.make_async_copy(
                source.at[pl.ds(row, 64), pl.ds(lane, features)], low_at(n), wide_sem.at[n % 3]
            )

        def store(n):
            _, target, row, lane = pieces[n]
            return pltpu.make_async_copy(
                wide_at(n), target.at[pl.ds(row, 64), pl.ds(lane, features)], wide_sem.at[3 + n % 3]
            )

        load(0).start()
        load(1).start()
        for n in range(len(pieces)):
            if n + 2 < len(pieces):
                load(n + 2).start()
            load(n).wait()
            if n >= 3:
                store(n - 3).wait()

            def some_rows(r, carry):
                x_buf[pl.ds(pl.multiple_of(64 * (n % 3) + r * 16, 16), 16), :] = big[
                    pl.ds(pl.multiple_of(64 * (n % 3) + r * 16, 16), 16), :
                ].astype(jnp.float32)
                return carry

            lax.fori_loop(0, 4, some_rows, 0)
            store(n).start()
        for n in range(len(pieces) - 3, len(pieces)):
            store(n).wait()

    def part_copies(first_row):
        return [
            pltpu.make_async_copy(
                stage.at[pl.ds(p * quarter, quarter)],
                attn_parts_ref.at[pl.ds(p * 4 * quarter + first_row, quarter)],
                local_sem.at[4 + p],
            )
            for p in range(4)
        ]

    def load_big(source):
        copy = pltpu.make_async_copy(source, big, local_sem.at[2])
        copy.start()
        return copy

    def attn_term(stream, grad):
        def one_owner(d, carry):
            lanes = pl.ds(pl.multiple_of(d * width, width), width)
            stage[:, lanes] = lax.dot_general(
                big[:, lanes], grad[...], contract_rows, preferred_element_type=jnp.float32
            ).astype(jnp.bfloat16)
            return carry

        lax.fori_loop(0, 8, one_owner, 0)
        copies = part_copies(stream * quarter)
        for copy in copies:
            copy.start()
        return copies

    def out_term():
        def one_tile(t, carry):
            lanes = pl.ds(pl.multiple_of(t * tile, tile), tile)
            stage[:, lanes] = lax.dot_general(
                att[...], big[:, lanes], contract_rows, preferred_element_type=jnp.float32
            ).astype(jnp.bfloat16)
            return carry

        lax.fori_loop(0, features // tile, one_tile, 0)
        copies = part_copies(3 * quarter)
        for copy in copies:
            copy.start()
        return copies

    def swap(kind):
        copies = []
        for mask in (6, 7, 2, 3, 4, 5, 1):
            owner = partner(column, mask)
            if kind == 0:
                source, target = up_piece(owner), up_target()
            else:
                source, target = attn_piece(owner), attn_target()
            copies.append(
                push(
                    source,
                    target,
                    swap_send.at[8 * kind + mask],
                    swap_recv.at[8 * kind + mask],
                    owner,
                )
            )
        if kind == 0:
            source, target = up_piece(column), up_target()
        else:
            source, target = attn_piece(column), attn_target()
        local = pltpu.make_async_copy(source, target, local_sem.at[3])
        local.start()
        return copies, local

    def up_piece(owner):
        return up_sum.at[
            pl.ds(pl.multiple_of(lax.rem(owner, 4) * quarter, 16), quarter),
            pl.ds(pl.multiple_of(lax.div(owner, 4) * ff_share, 128), ff_share),
        ]

    def up_target():
        return up_own.at[:, pl.ds(pl.multiple_of(column * ff_share, 128), ff_share)]

    def attn_piece(owner):
        return attn_sum.at[
            pl.ds(0, 3 * quarter), pl.ds(pl.multiple_of(owner * width, 128), width)
        ]

    def attn_target():
        return quarter_ref.at[
            pl.ds(0, 3 * quarter), pl.ds(pl.multiple_of(column * width, 128), width)
        ]

    def swapped_in(swapping):
        copies, local = swapping
        for copy in copies:
            copy.wait_recv()
        local.wait()
        for copy in copies:
            copy.wait_send()

    up_line.start()
    down_spread = spread(4, down_own, lambda p: down_all_ref.at[pl.ds(p * 4 * quarter, 4 * quarter)])
    down_spread.service(0)

    @pl.when(plane == 0)
    def _():
        clear(kv_before)
        clear(line_ends.at[0])

    @pl.when(plane > 0)
    def _():
        load = pltpu.make_async_copy(
            key_before_ref, kv_before.at[:, pl.ds(0, width)], local_sem.at[0]
        )
        load.start()
        load.wait()

    @pl.when(plane == 3)
    def _():
        clear(kv_after)
        clear(line_ends.at[1])

    def key_value(m, carry):
        here = pl.ds(pl.multiple_of(m * rows, 16), rows)
        for head in range(width // HEAD_DIM):
            lanes = slice(head * HEAD_DIM, (head + 1) * HEAD_DIM)
            value_lanes = slice(width + head * HEAD_DIM, width + (head + 1) * HEAD_DIM)
            grad = kv_grad[here, lanes] + kv_after[here, lanes].astype(jnp.float32)
            turned_half = jnp.concatenate(
                [grad[:, HEAD_DIM // 2 :], grad[:, : HEAD_DIM // 2]], axis=1
            )
            k_grad[here, lanes] = (grad * cos_ref[...] - turned_half * sin_ref[...]).astype(
                jnp.bfloat16
            )
            v_grad[here, lanes] = (
                kv_grad[here, value_lanes] + kv_after[here, value_lanes].astype(jnp.float32)
            ).astype(jnp.bfloat16)
        return carry

    for place in range(1, 4):

        @pl.when(plane == place)
        def _():
            value_copy(place - 1).wait_recv()

    attend(0, 8)
    for place in range(1, 4):

        @pl.when(plane == place)
        def _():
            back_copy(place).start()

    loading = load_big(grad_all_ref)
    query_scatter = scatter_of(projection_product(0, q_grad), 0)
    query_scatter.block(0)
    query_scatter.block(1)
    query_scatter.block(2)
    query_scatter.block(3)
    up_line.service(0)
    query_scatter.turn()
    loading.wait()
    parts_out = out_term()
    query_scatter.finish(back_buf)
    norm_back(1, back_buf)
    query_spread = stream_spread(1)
    query_spread.service(0)
    down_spread.service(1)
    up_line.service(1)
    for copy in parts_out:
        copy.wait()
    loading = load_big(normed_ref.at[0])

    for place in range(3):

        @pl.when(plane == place)
        def _():
            back_copy(place + 1).wait_recv()

    lax.fori_loop(0, 8, key_value, 0)
    key_scatter = scatter_of(projection_product(1, k_grad), 1)
    key_scatter.block(0)
    key_scatter.block(1)
    key_scatter.block(2)
    key_scatter.block(3)
    down_spread.service(2)
    loading.wait()
    parts_out = attn_term(0, q_grad)
    key_scatter.turn()
    key_scatter.finish(back_buf)
    norm_back(2, back_buf)
    key_spread = stream_spread(2)
    key_spread.service(0)
    up_line.service(2)
    up_line.finish(up_sum)
    up_swap = swap(0)
    for copy in parts_out:
        copy.wait()
    loading = load_big(normed_ref.at[1])
    value_scatter = scatter_of(projection_product(2, v_grad), 2)
    value_scatter.block(0)
    value_scatter.block(1)
    value_scatter.block(2)
    value_scatter.block(3)
    down_spread.service(3)
    query_spread.service(1)
    loading.wait()
    parts_out = attn_term(1, k_grad)
    value_scatter.turn()
    swapped_in(up_swap)
    up_spread = spread(5, up_own, lambda p: up_all_ref.at[pl.ds(p * quarter, quarter)])
    up_spread.service(0)
    value_scatter.finish(back_buf)
    norm_back(3, back_buf)
    value_spread = stream_spread(3)
    for copy in parts_out:
        copy.wait()
    loading = load_big(normed_ref.at[2])
    loading.wait()
    parts_out = attn_term(2, v_grad)
    for copy in parts_out:
        copy.wait()
    attn_line.start()
    value_spread.service(0)
    query_spread.service(2)
    branch_scatter = scatter_of(branch_product, 3)
    branch_scatter.block(0)
    branch_scatter.block(1)
    key_spread.service(1)
    branch_scatter.block(2)
    branch_scatter.block(3)
    up_spread.service(1)
    query_spread.service(3)
    branch_scatter.turn()
    branch_scatter.finish(branch_ref)
    attn_line.service(0)
    key_spread.service(2)
    up_spread.service(2)
    value_spread.service(1)
    attn_line.service(1)
    key_spread.service(3)
    query_spread.placed()
    inner_products(0)
    inner_products(1)
    down_spread.placed()
    widen(0)
    up_spread.service(3)
    attn_line.service(2)
    attn_line.finish(attn_sum)
    attn_swap = swap(1)
    quarter_ref[pl.ds(3 * quarter, quarter), :] = attn_sum[pl.ds(3 * quarter, quarter), :]
    value_spread.service(2)
    key_spread.placed()
    inner_products(2)
    up_spread.placed()
    swapped_in(attn_swap)
    widen(1)
    value_spread.service(3)
    value_spread.placed()

    for spreading in (
        down_spread,
        query_spread,
        up_spread,
        key_spread,
        value_spread,
    ):
        spreading.finish()
    for place in range(3):

        @pl.when(plane == place)
        def _():
            value_copy(place).wait_send()

    for place in range(1, 4):

        @pl.when(plane == place)
        def _():
            back_copy(place).wait_send()


def attend_and_back(
    lengths_all,
    cosine,
    sine_part,
    q,
    k,
    v,
    out_grad,
    normed_all,
    grad_all,
    hidden,
    w_out,
    w_down,
    attn_columns,
    x_ordered,
    gains,
    down_own,
    up_term,
    full3,
    history,
    key_before,
    micro_count,
    sequence_length,
):
    total, width = q.shape
    rows, features = total // 8, w_down.shape[1]
    ff_share = w_down.shape[0]
    quarter = features // 32
    block = (rows, features)
    piece = (4 * quarter, features)
    half = (4, rows // 2, features)
    anywhere = pl.BlockSpec(memory_space=pl.ANY)
    near = pl.BlockSpec(memory_space=pltpu.VMEM)
    shape = jax.ShapeDtypeStruct
    low_type = jnp.bfloat16
    some = lambda *dims: pltpu.VMEM(dims, low_type)
    dma = pltpu.SemaphoreType.DMA
    return pl.pallas_call(
        functools.partial(
            backward_kernel, micro_count=micro_count, sequence_length=sequence_length
        ),
        in_specs=[pl.BlockSpec(memory_space=pltpu.SMEM)]
        + [near] * 6
        + [anywhere, anywhere]
        + [near] * 4
        + [anywhere]
        + [near] * 2
        + [anywhere] * 4,
        out_specs=[anywhere] * 5 + [near, near, near, near, anywhere, anywhere],
        out_shape=[
            shape((12 * rows, features), low_type),
            shape((ff_share, features), low_type),
            shape((4 * quarter, 8 * ff_share), low_type),
            shape((ff_share, features), jnp.float32),
            shape((4 * quarter, 8 * ff_share), jnp.float32),
            shape((4 * rows, 128), jnp.float32),
            shape(piece, low_type),
            shape(block, low_type),
            shape((8, features), jnp.float32),
            shape((16 * quarter, features), low_type),
            shape((12,) + piece, low_type),
        ],
        scratch_shapes=[
            some(total, features),
            some(total, width),
            some(total, width),
            pltpu.VMEM((total, 2 * width), jnp.float32),
            some(total, 2 * width),
            some(total, 2 * width),
            some(total, 2 * width),
            some(2, *block),
            some(4, *block),
            some(4, *block),
            some(*half),
            some(*half),
            some(*half),
            some(*piece),
            some(2, *piece),
            some(3, *piece),
            some(*piece),
            some(quarter, 8 * ff_share),
            some(3, *block),
            some(*block),
            pltpu.VMEM(block, jnp.float32),
            some(*piece),
            dma((4, 10)),
            dma((4, 10)),
            dma((3, 6)),
            dma((3, 6)),
            dma((2,)),
            dma((6, 6)),
            dma((6, 6)),
            dma((6,)),
            dma((3,)),
            dma((3,)),
            dma((16,)),
            dma((16,)),
            dma((8,)),
            dma((10,)),
            dma((6,)),
        ],
        compiler_params=pltpu.CompilerParams(
            collective_id=6, has_side_effects=True, vmem_limit_bytes=63 * 1024 * 1024
        ),
        cost_estimate=pl.CostEstimate(
            flops=20 * total * features * width,
            bytes_accessed=1000 * 1000 * 1000,
            transcendentals=0,
        ),
    )(
        lengths_all,
        cosine,
        sine_part,
        q,
        k,
        v,
        out_grad,
        normed_all,
        grad_all,
        hidden,
        w_out,
        w_down,
        attn_columns,
        x_ordered,
        gains,
        down_own,
        up_term,
        full3,
        history,
        key_before,
    )


def last_products_kernel(
    columns_ref,
    full_ref,
    history_ref,
    inner_ref,
    inner_columns,
    big,
    inner_sem,
    share_send,
    share_recv,
):
    plane = lax.axis_index("hist")
    inner_columns[...] = columns_ref[...]

    def barrier_line(plane):
        barrier = pltpu.get_barrier_semaphore()
        for place in range(4):

            @pl.when(plane == place)
            def _():
                for p in range(4):
                    if p != place:
                        pl.semaphore_signal(
                            barrier, inc=1, device_id=z_place(p), device_id_type=DEVICE_MESH
                        )

        pl.semaphore_wait(barrier, 3)

    rows = full_ref.shape[0] // 12
    step_rows = rows // 2

    def inner_loads(item, i):
        source = full_ref
        first = (item - 1) * 4 * rows
        base = (i % 2) * 5 * step_rows
        copies = [
            pltpu.make_async_copy(
                source.at[pl.ds(first + i * step_rows, step_rows)],
                big.at[pl.ds(base + 4 * step_rows, step_rows)],
                inner_sem.at[(i % 2) * 5 + 4],
            )
        ] + [
            pltpu.make_async_copy(
                history_ref.at[pl.ds(slot * 4 * rows + i * step_rows, step_rows)],
                big.at[pl.ds(base + slot * step_rows, step_rows)],
                inner_sem.at[(i % 2) * 5 + slot],
            )
            for slot in range(4)
        ]
        for copy in copies:
            copy.start()
        return copies

    def inner_products(item):
        loads = [inner_loads(item, 0)]
        for i in range(8):
            if i + 1 < 8:
                loads.append(inner_loads(item, i + 1))
            for copy in loads[i]:
                copy.wait()
            base = (i % 2) * 5 * step_rows

            def some_rows(r, carry):
                grad = big[
                    pl.ds(pl.multiple_of(base + 4 * step_rows + r * 16, 16), 16), :
                ].astype(jnp.float32)
                for slot in range(4):
                    values = big[
                        pl.ds(pl.multiple_of(base + slot * step_rows + r * 16, 16), 16), :
                    ].astype(jnp.float32)
                    one = item * 4 + slot
                    inner_columns[
                        pl.ds(pl.multiple_of(i * step_rows + r * 16, 16), 16), one : one + 1
                    ] = jnp.sum(grad * values, axis=-1, keepdims=True)
                return carry

            lax.fori_loop(0, step_rows // 16, some_rows, 0)

    barrier_line(plane)
    inner_products(3)

    def share_copy(source_place, target_place):
        return pltpu.make_async_remote_copy(
            src_ref=inner_ref.at[source_place],
            dst_ref=inner_ref.at[source_place],
            send_sem=share_send.at[target_place],
            recv_sem=share_recv.at[source_place],
            device_id=z_place(target_place),
            device_id_type=DEVICE_MESH,
        )

    for place in range(4):

        @pl.when(plane == place)
        def _():
            others = [p for p in range(4) if p != place]
            inner_ref[place] = jnp.transpose(inner_columns[...])[:16]
            for p in others:
                share_copy(place, p).start()
            for p in others:
                share_copy(p, place).wait_recv()
            for p in others:
                share_copy(place, p).wait_send()


def last_products(columns, full, history):
    rows, features = full.shape[0] // 12, full.shape[1]
    anywhere = pl.BlockSpec(memory_space=pl.ANY)
    near = pl.BlockSpec(memory_space=pltpu.VMEM)
    dma = pltpu.SemaphoreType.DMA
    return pl.pallas_call(
        last_products_kernel,
        in_specs=[near, anywhere, anywhere],
        out_specs=near,
        out_shape=jax.ShapeDtypeStruct((4, 16, 4 * rows), jnp.float32),
        scratch_shapes=[
            pltpu.VMEM((4 * rows, 128), jnp.float32),
            pltpu.VMEM((5 * rows, features), jnp.bfloat16),
            dma((10,)),
            dma((4,)),
            dma((4,)),
        ],
        compiler_params=pltpu.CompilerParams(
            collective_id=8, has_side_effects=True, vmem_limit_bytes=56 * 1024 * 1024
        ),
        cost_estimate=pl.CostEstimate(
            flops=0, bytes_accessed=40 * 1000 * 1000, transcendentals=0
        ),
    )(columns, full, history)


def rotary_table(row_positions, head_dim):
    half_dim = head_dim // 2
    frequency = jnp.exp(
        jnp.arange(half_dim, dtype=jnp.float32) * (-2.0 * math.log(10000.0) / head_dim)
    )
    angles = row_positions.astype(jnp.float32)[:, None] * frequency[None, :]
    cosine = jnp.cos(angles)
    sine_part = jnp.sin(angles)
    return (
        jnp.concatenate([cosine, cosine], axis=-1),
        jnp.concatenate([-sine_part, sine_part], axis=-1),
    )


def shards_split(
    history,
    history_layer_index,
    lengths,
    norm_gains,
    mix_in,
    mix_out,
    w_attn,
    w_out,
    w_up,
    w_down,
    cotangent,
):
    local_slots, micro_count, sequence_length, features = history.shape
    planes = lax.axis_size("hist")
    columns = lax.axis_size("dp")
    plane = lax.axis_index("hist")
    slot_count = local_slots * planes
    all_rows = micro_count * sequence_length
    rows = all_rows // planes
    share = features // columns
    mix_width = mix_in.shape[1]
    mix_rows = mix_out.shape[0]
    low = lambda values: values.astype(jnp.bfloat16)
    order = (3, 0, 1, 2)

    spare = 128 - mix_width
    middle = jnp.concatenate(
        [
            jnp.pad(mix_out, ((0, 8 - mix_rows), (0, spare))),
            jnp.pad(low(lengths)[None, :], ((0, 7), (0, 128 - micro_count))),
        ],
        axis=0,
    )
    gain_rows = jnp.pad(norm_gains, ((0, 3), (0, 0))).reshape(8, 2, share // 2)
    pack = jnp.concatenate(
        [
            jnp.pad(mix_in, ((0, 0), (0, spare))),
            middle,
            gain_rows.transpose(1, 0, 2).reshape(16, share // 2),
        ],
        axis=0,
    )

    layer_lookup = (
        history_layer_index[:, None] == jnp.arange(slot_count, dtype=jnp.int32)[None, :]
    ).astype(jnp.float32)
    newest_output = jnp.sum(
        jnp.arange(slot_count, dtype=jnp.int32)
        * (history_layer_index == slot_count - 1).astype(jnp.int32)
    )
    root = newest_output // local_slots
    on_root = (plane == root).astype(jnp.float32)
    latest_rows = lax.dynamic_index_in_dim(
        history, newest_output % local_slots, 0, keepdims=False
    ).reshape(all_rows, features)
    latest_rows = lax.optimization_barrier(latest_rows)
    own_table = lax.dynamic_slice_in_dim(layer_lookup, plane * local_slots, local_slots, 0)
    ordered = jnp.eye(STREAM_COUNT, dtype=jnp.float32)[:, jnp.array(order)]
    select = jnp.einsum("ci,sj->cjis", ordered, own_table).reshape(
        STREAM_COUNT * slot_count, STREAM_COUNT * local_slots
    )
    select = low(jnp.pad(select, ((0, 0), (0, 128 - STREAM_COUNT * local_slots))))

    my_row = plane * rows + jnp.arange(rows, dtype=jnp.int32)
    my_position = lax.rem(my_row, sequence_length)
    my_sequence = lax.div(my_row, sequence_length)
    my_length = jnp.sum(
        jnp.where(
            my_sequence[:, None] == jnp.arange(micro_count, dtype=jnp.int32)[None, :],
            lengths[None, :],
            0,
        ),
        axis=1,
    )
    valid_rows = (my_position < my_length).astype(jnp.float32)[:, None]
    cosine, sine_part = rotary_table(my_position, HEAD_DIM)

    (
        packed,
        gains,
        pre,
        factors,
        x_ordered,
        normed_all,
        grad_all,
        hidden,
        up_term,
        down_own,
        full3,
        gain_sum3,
        attn_columns,
        q,
        k,
        v,
        out_grad,
        key_before,
        _,
        _,
        _,
        _,
    ) = forward_and_feed(
        lengths,
        pack,
        latest_rows,
        history.reshape(local_slots * all_rows, features),
        select,
        jnp.broadcast_to(on_root, (8, all_rows)),
        cotangent.reshape(rows, features),
        w_up,
        w_attn,
        w_down,
        w_out,
        cosine,
        sine_part,
        sequence_length,
    )
    lengths_all = packed[:, share + 8, :micro_count].reshape(-1).astype(jnp.int32)
    (
        full,
        _,
        _,
        w_down_grad,
        w_up_grad,
        inner_columns,
        attn_quarter,
        branch,
        gain_sums,
        _,
        _,
    ) = attend_and_back(
        lengths_all,
        cosine,
        sine_part,
        q,
        k,
        v,
        out_grad,
        normed_all,
        grad_all,
        hidden,
        w_out,
        w_down,
        attn_columns,
        x_ordered,
        gains,
        down_own,
        up_term,
        full3,
        history.reshape(local_slots * all_rows, features),
        key_before,
        micro_count,
        sequence_length,
    )
    attn_every = lax.all_gather(attn_quarter, "hist", axis=0, tiled=True)

    chunk = sequence_length // planes
    inverse_step = pow(micro_count, -1, planes)
    block_rows = low((x_ordered[0] + branch.astype(jnp.float32)) * valid_rows)
    block_out = jnp.zeros((micro_count, chunk, features), jnp.bfloat16)
    for i in range(micro_count):
        pairs = [(p, (micro_count * p + i) % planes) for p in range(planes)]
        piece = lax.ppermute(block_rows[i * chunk : (i + 1) * chunk], "hist", pairs)
        source = lax.rem((plane - i + planes * micro_count) * inverse_step, planes)
        which = lax.div(source * micro_count + i, planes)
        block_out = lax.dynamic_update_index_in_dim(block_out, piece, which, 0)

    inner_all = last_products(
        inner_columns, full, history.reshape(local_slots * all_rows, features)
    )
    mixer_output_wide = (
        packed[:, share : share + mix_rows, :mix_width]
        .reshape(mix_width, mix_width)
        .astype(jnp.float32)
    )
    mix_in_all = packed[:, :share, :mix_width].reshape(features, mix_width)
    tables = layer_lookup.reshape(planes, local_slots, slot_count)
    dyn_grad = jnp.einsum(
        "pist,ic,psj->tcj",
        inner_all.reshape(planes, STREAM_COUNT, local_slots, all_rows),
        ordered.T,
        tables,
        precision=highest,
    ).reshape(all_rows, STREAM_COUNT * slot_count)
    mixer_preactivation = pre[:, :mix_width]
    mix_act = jax.nn.gelu(mixer_preactivation, approximate=False)
    act_grad = precise(dyn_grad, mixer_output_wide.T)
    mix_out_grad = precise(mix_act.T, dyn_grad) * on_root
    pre_grad = act_grad * gelu_slope(mixer_preactivation)
    latest_scaled, _ = rms_scale(latest_rows.astype(jnp.float32), gains[0])
    mix_in_grad = precise(low(latest_scaled).astype(jnp.float32).T, pre_grad)
    latest_here = (plane * local_slots + jnp.arange(local_slots) == newest_output).astype(
        jnp.float32
    )
    history_grad, gain_zero = slot_grads_of(
        latest_here,
        factors,
        full3,
        full.reshape(3, all_rows, features),
        latest_rows,
        pre_grad,
        mix_in_all.astype(jnp.float32).T,
        gains,
    )
    history_grad = history_grad.reshape(history.shape)

    gain_rows = jnp.stack(
        [gain_zero[0] * on_root, gain_sums[1], gain_sums[2], gain_sums[3], gain_sum3[0]]
    )
    counts = (share * mix_width // 128, 5 * share // 128, mix_rows * mix_width // 128)
    dense = jnp.concatenate(
        [
            (mix_in_grad * on_root).reshape(columns, counts[0], 128),
            gain_rows.reshape(5, columns, share).transpose(1, 0, 2).reshape(columns, counts[1], 128),
            mix_out_grad.reshape(columns, counts[2], 128),
        ],
        axis=1,
    )
    used = sum(counts)
    small = small_sums(low(jnp.pad(dense, ((0, 0), (0, -used % 16), (0, 0)))))
    w_attn_grad, w_out_grad = lay_out(attn_every)
    return (
        block_out,
        history_grad,
        small[counts[0] : counts[0] + counts[1]].reshape(5, share),
        small[: counts[0]].reshape(share, mix_width),
        small[counts[0] + counts[1] : used].reshape(mix_rows, mix_width),
        w_attn_grad,
        w_out_grad,
        w_up_grad,
        w_down_grad,
    )


def splits_by_heads(mesh, micro_count, sequence_length):
    columns, planes = mesh.shape["dp"], mesh.shape["hist"]
    all_rows = micro_count * sequence_length
    rows = all_rows // planes
    return (
        columns == 8
        and planes == 4
        and HEADS % columns == 0
        and all_rows % planes == 0
        and sequence_length % planes == 0
        and rows % 64 == 0
        and math.gcd(micro_count, planes) == 1
        and all(
            (p * rows) // sequence_length * sequence_length >= (p - 1) * rows
            for p in range(planes)
        )
    )


def solution(mesh):
    placed = (
        P("hist", "dp", None, None),
        P(),
        P("dp"),
        P(None, "dp"),
        P("dp", None),
        P("dp", None),
        P(None, "dp", None),
        P("dp", None),
        P("dp", None),
        P("dp", None),
        P("dp", "hist", None),
    )
    def plan(*arrays):
        micro_count = arrays[2].shape[0]
        if splits_by_heads(mesh, micro_count, arrays[0].shape[2]):
            return shards_split(*arrays)
        return shards(*arrays)

    return jax.shard_map(
        plan,
        mesh=mesh,
        in_specs=placed,
        out_specs=(
            P("dp", "hist", None),
            P("hist", "dp", None, None),
            P(None, "dp"),
            P("dp", None),
            P("dp", None),
            P(None, "dp", None),
            P("dp", None),
            P("dp", None),
            P("dp", None),
        ),
        check_vma=False,
    )
```
